32 devices in a mesh: seq: 8 (over z, y), batch: 4 (over x, core).
Axes of the slice: x: 2, y: 2, z: 4, core: 2. Of those that a mesh axis runs over, the one named last changes fastest.
Arguments:
- inputs: bfloat16 [8, 2048, 768], P('batch', 'seq'), may hold values from -6 to 6
- history: bfloat16 [5, 8, 2048, 768], P(None, 'batch', 'seq'), may hold values from -6 to 6
- seq_lengths: int32 [8], P('batch'), may hold values from 256 to 1024, as said below
- attn_gain: bfloat16 [768], P(('seq', 'batch')), may hold values from 0.5 to 1.5
- attn_shift: bfloat16 [768], P(('seq', 'batch')), may hold values from -3 to 3
- qkv_weight: bfloat16 [768, 2304], P(('seq', 'batch')), may hold values from -0.21875 to 0.21875
- qkv_bias: bfloat16 [2304], P(('seq', 'batch')), may hold values from -3 to 3
- out_weight: bfloat16 [768, 768], P(('seq', 'batch')), may hold values from -1.75 to 1.75
- out_bias: bfloat16 [768], P(('seq', 'batch')), may hold values from -3 to 3
- mlp_gain: bfloat16 [768], P(('seq', 'batch')), may hold values from 0.5 to 1.5
- mlp_shift: bfloat16 [768], P(('seq', 'batch')), may hold values from -3 to 3
- up_weight: bfloat16 [768, 3072], P(('seq', 'batch')), may hold values from -0.21875 to 0.21875
- up_bias: bfloat16 [3072], P(('seq', 'batch')), may hold values from -3 to 3
- down_weight: bfloat16 [3072, 768], P(('seq', 'batch')), may hold values from -0.109375 to 0.109375
- down_bias: bfloat16 [768], P(('seq', 'batch')), may hold values from -3 to 3
- mix_weights: float32 [6], replicated, may hold values from 0.2 to 1
- cotangent: bfloat16 [8, 2048, 768], P('batch', 'seq'), may hold values from -6 to 6
Outputs:
- layer_out: bfloat16 [8, 2048, 768], P('batch', 'seq')
- grad_inputs: bfloat16 [8, 2048, 768], P('batch', 'seq')
- grad_history: bfloat16 [5, 8, 2048, 768], P(None, 'batch', 'seq')
- grad_attn_gain: float32 [768], P(('seq', 'batch'))
- grad_attn_shift: float32 [768], P(('seq', 'batch'))
- grad_qkv_weight: float32 [768, 2304], P(('seq', 'batch'))
- grad_qkv_bias: float32 [2304], P(('seq', 'batch'))
- grad_out_weight: float32 [768, 768], P(('seq', 'batch'))
- grad_out_bias: float32 [768], P(('seq', 'batch'))
- grad_mlp_gain: float32 [768], P(('seq', 'batch'))
- grad_mlp_shift: float32 [768], P(('seq', 'batch'))
- grad_up_weight: float32 [768, 3072], P(('seq', 'batch'))
- grad_up_bias: float32 [3072], P(('seq', 'batch'))
- grad_down_weight: float32 [3072, 768], P(('seq', 'batch'))
- grad_down_bias: float32 [768], P(('seq', 'batch'))
- grad_mix_weights: float32 [6], replicated
The draws below stay inside these ranges and needn't reach their ends.
Inputs may be any that keep to these rules, and one draw needn't show every extreme that they name: `seq_lengths`: each entry is 1024 or 256; both values occur in every draw.
All inputs are finite; a program needn't handle non-finite values.
Results may differ from the reference program's by a relative error of at most 0.028.
Values may be sent and summed in bfloat16 or wider, within the bound.
A program may use at most 320 MiB of HBM per device.

```python
import math
import jax
import jax.numpy as jnp
from jax import lax

D = 768
HEADS = 12
HEAD_DIM = 64
FF = 3072
TOK_DEV = 256
LONG_LEN = 1024
SHORT_LEN = 256
HIST = 5
SLICE = 128
GROUP_TOK = 2048
GROUPS = 8


def draw_seq_lengths(key, part):
    key = jax.random.fold_in(key, 11)
    first_key, second_key, third_key = jax.random.split(key, 3)
    picked = jax.random.randint(first_key, (GROUPS,), 0, 3)
    long_index = jax.random.randint(second_key, (), 0, GROUPS)
    short_index = (long_index + 1 + jax.random.randint(third_key, (), 0, GROUPS - 1)) % GROUPS
    positions = jnp.arange(GROUPS)
    is_long = picked < 2
    is_long = jnp.where(positions == long_index, True, is_long)
    is_long = jnp.where(positions == short_index, False, is_long)
    return jnp.where(is_long, LONG_LEN, SHORT_LEN).astype(jnp.int32)


def block_scale(key, extent, cuts, smallest, top_value):
    loudness = 1.0
    for dim, blocks in cuts:
        heights = jax.random.uniform(jax.random.fold_in(jax.random.fold_in(key, 6), dim), (blocks,), jnp.float32, smallest / len(cuts), top_value / len(cuts))
        loudness = loudness * jnp.repeat(jnp.exp(heights), extent[dim] // blocks).reshape((-1,) + (1,) * (len(extent) - 1 - dim))
    return loudness


def bell_draw(key, dims, width, limit, shards=(), held_as=jnp.bfloat16):
    values = jax.random.normal(key, dims, jnp.float32) * width
    if len(shards) > 0:
        values = block_scale(key, dims, shards, -0.22, 0.18) * values
    return jnp.clip(values, min=-limit, max=limit).astype(held_as)


def setup_inputs(seed: int = 0) -> dict:
    seeds = jax.random.split(jax.random.key(seed), 18)
    inputs = bell_draw(seeds[0], (GROUPS, GROUP_TOK, D), 1.0, 6.0, ((0, 4), (1, 8)))
    history = bell_draw(seeds[1], (HIST, GROUPS, GROUP_TOK, D), 1.0, 6.0, ((1, 4), (2, 8)))
    seq_lengths = draw_seq_lengths(jax.random.fold_in(seeds[17], 71), 0)
    attn_gain = jnp.clip(1.0 + 0.1 * jax.random.normal(seeds[3], (D,), jnp.float32), 0.5, 1.5).astype(jnp.bfloat16)
    attn_shift = bell_draw(seeds[4], (D,), 0.3, 3.0, ((0, 32),))
    qkv_weight = bell_draw(seeds[5], (D, 3 * D), D ** -0.5, 0.21875, ((0, 32),))
    qkv_bias = bell_draw(seeds[6], (3 * D,), 0.3, 3.0, ((0, 32),))
    out_weight = bell_draw(seeds[7], (D, D), (D // 64) ** -0.5, 1.75, ((0, 32),))
    out_bias = bell_draw(seeds[8], (D,), 0.3, 3.0, ((0, 32),))
    mlp_gain = jnp.clip(1.0 + 0.1 * jax.random.normal(seeds[9], (D,), jnp.float32), 0.5, 1.5).astype(jnp.bfloat16)
    mlp_shift = bell_draw(seeds[10], (D,), 0.3, 3.0, ((0, 32),))
    up_weight = bell_draw(seeds[11], (D, FF), D ** -0.5, 0.21875, ((0, 32),))
    up_bias = bell_draw(seeds[12], (FF,), 0.3, 3.0, ((0, 32),))
    down_weight = bell_draw(seeds[13], (FF, D), FF ** -0.5, 0.109375, ((0, 32),))
    down_bias = bell_draw(seeds[14], (D,), 0.3, 3.0, ((0, 32),))
    mix_weights = jnp.clip(jax.random.uniform(seeds[15], (HIST + 1,), jnp.float32, 0.2, 1.0), 0.2, 1.0)
    cotangent = bell_draw(seeds[16], (GROUPS, GROUP_TOK, D), 1.0, 6.0, ((0, 4), (1, 8)))
    return {"inputs": inputs, "history": history, "seq_lengths": seq_lengths, "attn_gain": attn_gain, "attn_shift": attn_shift, "qkv_weight": qkv_weight, "qkv_bias": qkv_bias, "out_weight": out_weight, "out_bias": out_bias, "mlp_gain": mlp_gain, "mlp_shift": mlp_shift, "up_weight": up_weight, "up_bias": up_bias, "down_weight": down_weight, "down_bias": down_bias, "mix_weights": mix_weights, "cotangent": cotangent}


eps = 1e-05
masked = -1e+30

@jax.custom_vjp
def low(v):
    return lax.optimization_barrier(v.astype(jnp.bfloat16)).astype(jnp.float32)

@jax.custom_vjp
def low_back(v):
    return v

def low_keep(v):
    return (low(v), None)

def low_pass(kept, grad):
    return (grad,)

def back_keep(v):
    return (v, None)

def back_low(kept, grad):
    return (low(grad),)
low.defvjp(low_keep, low_pass)
low_back.defvjp(back_keep, back_low)

def layer_norm(values, norm_gain, norm_shift):
    average = lax.optimization_barrier(jnp.mean(values, axis=-1, keepdims=True))
    centred = values - average
    inverse = lax.rsqrt(lax.optimization_barrier(jnp.mean(centred * centred, axis=-1, keepdims=True)) + eps)
    return centred * inverse * norm_gain + norm_shift

def token_layout(index, seq_len):
    is_long = seq_len == LONG_LEN
    offset = index % TOK_DEV
    device = index // TOK_DEV
    doc_ids = jnp.where(is_long, offset // SLICE, index // SHORT_LEN).astype(jnp.int32)
    relative = jnp.where(is_long, device * SLICE + offset % SLICE, index % SHORT_LEN).astype(jnp.int32)
    return (doc_ids, relative)

def rotary_tables(relative):
    half_dim = HEAD_DIM // 2
    frequency = jnp.exp(-math.log(10000.0) * (2.0 * jnp.arange(half_dim, dtype=jnp.float32) / HEAD_DIM))
    angles = relative.astype(jnp.float32)[:, None] * frequency[None, :]
    return (jnp.cos(angles)[:, None, :], jnp.sin(angles)[:, None, :])

def rotate(values, cosine, sine_table):
    half_dim = values.shape[-1] // 2
    lower_half = values[..., :half_dim]
    upper_half = values[..., half_dim:]
    return jnp.concatenate([lower_half * cosine - upper_half * sine_table, upper_half * cosine + lower_half * sine_table], axis=-1)

def attend_group(queries, key_heads, values, relative, doc_ids):
    total_rows = queries.shape[0]
    block_rows = min(512, total_rows)
    factor = HEAD_DIM ** (-0.5)

    def one_block(block_index):
        first_row = block_index * block_rows
        query_block = lax.dynamic_slice_in_dim(queries, first_row, block_rows, 0)
        query_rel = lax.dynamic_slice_in_dim(relative, first_row, block_rows, 0)
        query_docs = lax.dynamic_slice_in_dim(doc_ids, first_row, block_rows, 0)
        scores = jnp.einsum('qhd,khd->hqk', query_block, key_heads, precision=lax.Precision.HIGHEST) * factor
        scores = low_back(scores)
        allowed = (doc_ids[None, :] == query_docs[:, None]) & (relative[None, :] <= query_rel[:, None])
        scores = jnp.where(allowed[None], scores, masked)
        probabilities = low(jax.nn.softmax(scores, axis=-1))
        return jnp.einsum('hqk,khd->qhd', probabilities, values, precision=lax.Precision.HIGHEST)
    blocks = lax.map(jax.checkpoint(one_block), jnp.arange(total_rows // block_rows, dtype=jnp.int32))
    return blocks.reshape(total_rows, HEADS * HEAD_DIM)

def block_group(block_in, seq_len, params):
    attn_gain, attn_shift, qkv_weight, qkv_bias, out_weight, out_bias, mlp_gain, mlp_shift, up_weight, up_bias, down_weight, down_bias = params
    total_rows = block_in.shape[0]
    model_width = HEADS * HEAD_DIM
    places = jnp.arange(total_rows, dtype=jnp.int32)
    doc_ids, relative = token_layout(places, seq_len)
    cosine, sine_table = rotary_tables(relative)
    normed_one = low(layer_norm(block_in, attn_gain, attn_shift))
    projected = low_back(jnp.dot(normed_one, qkv_weight, precision=lax.Precision.HIGHEST) + qkv_bias)
    queries = low(rotate(projected[:, :model_width].reshape(total_rows, HEADS, HEAD_DIM), cosine, sine_table))
    key_heads = low(rotate(projected[:, model_width:2 * model_width].reshape(total_rows, HEADS, HEAD_DIM), cosine, sine_table))
    values = low(projected[:, 2 * model_width:].reshape(total_rows, HEADS, HEAD_DIM))
    attended = low(low_back(attend_group(queries, key_heads, values, relative, doc_ids)))
    middle = block_in + low_back(jnp.dot(attended, out_weight, precision=lax.Precision.HIGHEST) + out_bias)
    normed_two = low(layer_norm(middle, mlp_gain, mlp_shift))
    upward = low_back(jnp.dot(normed_two, up_weight, precision=lax.Precision.HIGHEST) + up_bias)
    activated = low(jax.nn.gelu(upward, approximate=False))
    return middle + low_back(jnp.dot(activated, down_weight, precision=lax.Precision.HIGHEST) + down_bias)

def reference(inputs, history, seq_lengths, attn_gain, attn_shift, qkv_weight, qkv_bias, out_weight, out_bias, mlp_gain, mlp_shift, up_weight, up_bias, down_weight, down_bias, mix_weights, cotangent):
    weights = (attn_gain.astype(jnp.float32), attn_shift.astype(jnp.float32), qkv_weight.astype(jnp.float32), qkv_bias.astype(jnp.float32), out_weight.astype(jnp.float32), out_bias.astype(jnp.float32), mlp_gain.astype(jnp.float32), mlp_shift.astype(jnp.float32), up_weight.astype(jnp.float32), up_bias.astype(jnp.float32), down_weight.astype(jnp.float32), down_bias.astype(jnp.float32))

    def forward(block_in, earlier, mixing, params):

        def per_group(group_pair):
            return block_group(group_pair[0], group_pair[1], params)
        outputs = lax.map(per_group, (block_in, seq_lengths))
        return lax.optimization_barrier(jnp.sum(mixing[:HIST, None, None, None] * earlier, axis=0)) + mixing[HIST] * outputs
    mixed_out, pullback = jax.vjp(forward, inputs.astype(jnp.float32), history.astype(jnp.float32), mix_weights, weights)
    grad_in, grad_earlier, grad_mix, grad_params = pullback(cotangent.astype(jnp.float32))
    return (mixed_out.astype(jnp.bfloat16), grad_in.astype(jnp.bfloat16), grad_earlier.astype(jnp.bfloat16), grad_params[0], grad_params[1], grad_params[2], grad_params[3], grad_params[4], grad_params[5], grad_params[6], grad_params[7], grad_params[8], grad_params[9], grad_params[10], grad_params[11], grad_mix)
```

```python
import functools
import math

import jax
import jax.numpy as jnp
import numpy as np
from jax import lax
from jax.experimental import pallas as pl
from jax.experimental.pallas import tpu as pltpu
from jax.sharding import PartitionSpec as P

HEADS = 12
HEAD_DIM = 64
LONG_LEN = 1024
SHORT_LEN = 256


eps = 1e-05
masked = -1e30


def block_size(row_count):
    chosen = 1
    for candidate in range(1, min(row_count, 512) + 1):
        if row_count % candidate == 0:
            chosen = candidate
    return chosen


def exact_gelu(values):
    return jax.nn.gelu(values, approximate=False)


def layer_norm(values, norm_gain, norm_shift):
    average = jnp.mean(values, axis=-1, keepdims=True)
    centred = values - average
    inverse = lax.rsqrt(jnp.mean(centred * centred, axis=-1, keepdims=True) + eps)
    normed = centred * inverse
    return (normed * norm_gain + norm_shift, normed, inverse)


def norm_back(grad_out, normed, inverse, norm_gain):
    grad_normed = grad_out * norm_gain
    mean_grad = jnp.mean(grad_normed, axis=-1, keepdims=True)
    mean_cross = jnp.mean(grad_normed * normed, axis=-1, keepdims=True)
    grad_in = inverse * (grad_normed - mean_grad - normed * mean_cross)
    return (grad_in, jnp.sum(grad_out * normed, axis=0), jnp.sum(grad_out, axis=0))


def token_layout(index, info):
    seq_len, tok_count, slice_len = info
    is_long = seq_len == LONG_LEN
    offset = index % tok_count
    device = index // tok_count
    doc_ids = jnp.where(is_long, offset // slice_len, index // SHORT_LEN).astype(jnp.int32)
    relative = jnp.where(
        is_long, device * slice_len + offset % slice_len, index % SHORT_LEN
    ).astype(jnp.int32)
    return (doc_ids, relative)


def rotary_tables(relative):
    half_dim = HEAD_DIM // 2
    frequency = jnp.exp(
        -math.log(10000.0) * (2.0 * jnp.arange(half_dim, dtype=jnp.float32) / HEAD_DIM)
    )
    angles = relative.astype(jnp.float32)[:, None] * frequency[None, :]
    return (jnp.cos(angles)[:, None, :], jnp.sin(angles)[:, None, :])


def rotate(values, cosine, sine_table):
    half_dim = values.shape[-1] // 2
    lower_half = values[..., :half_dim]
    upper_half = values[..., half_dim:]
    return jnp.concatenate(
        [
            lower_half * cosine - upper_half * sine_table,
            upper_half * cosine + lower_half * sine_table,
        ],
        axis=-1,
    )


def allowed_mask(query_places, key_places, info):
    query_docs, query_rel = token_layout(query_places, info)
    key_docs, key_rel = token_layout(key_places, info)
    return (key_docs[None, :] == query_docs[:, None]) & (key_rel[None, :] <= query_rel[:, None])


def online_block(current, query_b, key_block, value_block, query_places, key_places, info):
    running, denominator, weighted = current
    key_count = key_block.shape[0]
    allowed = allowed_mask(query_places, key_places, info)
    key_heads = key_block.reshape(key_count, HEADS, HEAD_DIM)
    scores = jnp.einsum(
        "qhd,khd->hqk", query_b, key_heads, preferred_element_type=jnp.float32
    ) * HEAD_DIM ** (-0.5)
    scores = jnp.where(allowed[None], scores, masked)
    new_max = jnp.maximum(running, jnp.max(scores, axis=-1))
    exp_scores = jnp.where(allowed[None], jnp.exp(scores - new_max[..., None]), 0.0)
    rescale = jnp.exp(running - new_max)
    denominator = denominator * rescale + jnp.sum(exp_scores, axis=-1)
    value_heads = value_block.reshape(key_count, HEADS, HEAD_DIM)
    weighted = weighted * rescale[..., None] + jnp.einsum(
        "hqk,khd->hqd",
        exp_scores.astype(jnp.bfloat16),
        value_heads,
        preferred_element_type=jnp.float32,
    )
    return (new_max, denominator, weighted)


def attend_rows(current, query_b, key_rows, value_rows, first_row, query_places, info, last_place):
    key_count = key_rows.shape[0]
    block_rows = block_size(key_count)

    def one_block(carried, block_index):
        start_place = first_row + block_index * block_rows
        key_block = lax.dynamic_slice_in_dim(key_rows, block_index * block_rows, block_rows, 0)
        value_block = lax.dynamic_slice_in_dim(value_rows, block_index * block_rows, block_rows, 0)
        key_places = start_place + jnp.arange(block_rows, dtype=jnp.int32)

        def one_compute(state_in):
            return online_block(
                state_in, query_b, key_block, value_block, query_places, key_places, info
            )

        def unchanged(state_in):
            return state_in

        return (lax.cond(start_place > last_place, unchanged, one_compute, carried), None)

    result, unused = lax.scan(
        one_block, current, jnp.arange(key_count // block_rows, dtype=jnp.int32)
    )
    return result


def block_probs(query_b, key_b, query_places, key_places, info, lse_rows):
    allowed = allowed_mask(query_places, key_places, info)
    scores = jnp.einsum(
        "qhd,khd->hqk", query_b, key_b, preferred_element_type=jnp.float32
    ) * HEAD_DIM ** (-0.5)
    return jnp.exp(jnp.where(allowed[None], scores - lse_rows[..., None], masked))


def block_dscores(probabilities, grad_b, value_b, delta_rows):
    dprobs = jnp.einsum("qhd,khd->hqk", grad_b, value_b, preferred_element_type=jnp.float32)
    return (probabilities * (dprobs - delta_rows[..., None])).astype(jnp.bfloat16)


def shards(
    inputs,
    history,
    seq_lengths,
    attn_gain,
    attn_shift,
    qkv_weight,
    qkv_bias,
    out_weight,
    out_bias,
    mlp_gain,
    mlp_shift,
    up_weight,
    up_bias,
    down_weight,
    down_bias,
    mix_weights,
    cotangent,
):
    group_count = inputs.shape[0]
    tok_count = inputs.shape[1]
    model_width = inputs.shape[2]
    seq_count = lax.axis_size("seq")
    group_rows = tok_count * seq_count
    slice_len = LONG_LEN // seq_count
    factor = HEAD_DIM ** (-0.5)
    seq_index = lax.axis_index("seq")
    first_place = seq_index * tok_count
    last_place = first_place + tok_count - 1
    places = first_place + jnp.arange(tok_count, dtype=jnp.int32)
    gathered = (
        lax.all_gather(attn_gain, ("seq", "batch"), axis=0, tiled=True),
        lax.all_gather(attn_shift, ("seq", "batch"), axis=0, tiled=True),
        lax.all_gather(qkv_weight, ("seq", "batch"), axis=0, tiled=True),
        lax.all_gather(qkv_bias, ("seq", "batch"), axis=0, tiled=True),
        lax.all_gather(out_weight, ("seq", "batch"), axis=0, tiled=True),
        lax.all_gather(out_bias, ("seq", "batch"), axis=0, tiled=True),
        lax.all_gather(mlp_gain, ("seq", "batch"), axis=0, tiled=True),
        lax.all_gather(mlp_shift, ("seq", "batch"), axis=0, tiled=True),
        lax.all_gather(up_weight, ("seq", "batch"), axis=0, tiled=True),
        lax.all_gather(up_bias, ("seq", "batch"), axis=0, tiled=True),
        lax.all_gather(down_weight, ("seq", "batch"), axis=0, tiled=True),
        lax.all_gather(down_bias, ("seq", "batch"), axis=0, tiled=True),
    )
    (
        gain_one,
        shift_one,
        qkv_full,
        qkv_vec,
        out_full,
        out_vec,
        gain_two,
        shift_two,
        up_full,
        up_vec,
        down_full,
        down_vec,
    ) = gathered
    saved = []
    block_outs = []
    for group in range(group_count):
        info = (seq_lengths[group], tok_count, slice_len)
        doc_ids, relative = token_layout(places, info)
        cosine, sine_table = rotary_tables(relative)
        residual_in = inputs[group].astype(jnp.float32)
        normed_out, normed_one, inverse_one = layer_norm(
            residual_in, gain_one.astype(jnp.float32), shift_one.astype(jnp.float32)
        )
        acts_one = normed_out.astype(jnp.bfloat16)
        projected = jnp.dot(
            acts_one, qkv_full, preferred_element_type=jnp.float32
        ) + qkv_vec.astype(jnp.float32)
        queries = rotate(
            projected[:, :model_width].reshape(tok_count, HEADS, HEAD_DIM), cosine, sine_table
        ).astype(jnp.bfloat16)
        key_flat = (
            rotate(
                projected[:, model_width : 2 * model_width].reshape(tok_count, HEADS, HEAD_DIM),
                cosine,
                sine_table,
            )
            .reshape(tok_count, model_width)
            .astype(jnp.bfloat16)
        )
        value_flat = projected[:, 2 * model_width :].astype(jnp.bfloat16)
        start_state = (
            jnp.full((HEADS, tok_count), masked, jnp.float32),
            jnp.zeros((HEADS, tok_count), jnp.float32),
            jnp.zeros((HEADS, tok_count, HEAD_DIM), jnp.float32),
        )
        key_all = None
        value_all = None
        running, denominator, weighted = attend_rows(
            start_state,
            queries,
            lax.all_gather(key_flat, "seq", axis=0, tiled=True),
            lax.all_gather(value_flat, "seq", axis=0, tiled=True),
            jnp.int32(0),
            places,
            info,
            last_place,
        )
        attended = jnp.transpose(weighted / denominator[..., None], (1, 0, 2))
        lse_rows = running + jnp.log(denominator)
        attended_b = attended.reshape(tok_count, model_width).astype(jnp.bfloat16)
        middle = (
            residual_in
            + jnp.dot(attended_b, out_full, preferred_element_type=jnp.float32)
            + out_vec.astype(jnp.float32)
        )
        normed_out_two, normed_two, inverse_two = layer_norm(
            middle, gain_two.astype(jnp.float32), shift_two.astype(jnp.float32)
        )
        acts_two = normed_out_two.astype(jnp.bfloat16)
        upward = jnp.dot(acts_two, up_full, preferred_element_type=jnp.float32) + up_vec.astype(
            jnp.float32
        )
        activated, gelu_back = jax.vjp(exact_gelu, upward)
        activated_b = activated.astype(jnp.bfloat16)
        block_out = (
            middle
            + jnp.dot(activated_b, down_full, preferred_element_type=jnp.float32)
            + down_vec.astype(jnp.float32)
        )
        block_outs.append(block_out)
        saved.append(
            (
                info,
                cosine,
                sine_table,
                normed_one,
                inverse_one,
                acts_one,
                queries,
                key_flat,
                value_flat,
                key_all,
                value_all,
                attended,
                lse_rows,
                attended_b,
                normed_two,
                inverse_two,
                acts_two,
                gelu_back,
                activated_b,
            )
        )
    block_stack = jnp.stack(block_outs, axis=0)
    earlier = history.astype(jnp.float32)
    grad_out_all = cotangent.astype(jnp.float32)
    mixed_out = (
        jnp.sum(mix_weights[:-1, None, None, None] * earlier, axis=0)
        + mix_weights[-1] * block_stack
    )
    mix_terms = jnp.concatenate(
        [
            jnp.sum(earlier * grad_out_all[None], axis=(1, 2, 3)),
            jnp.sum(block_stack * grad_out_all)[None],
        ]
    )
    grad_history = (mix_weights[:-1, None, None, None] * grad_out_all[None]).astype(jnp.bfloat16)
    back_gain_one, back_qkv, back_out, back_gain_two, back_up, back_down = (
        lax.all_gather(attn_gain, ("seq", "batch"), axis=0, tiled=True),
        lax.all_gather(qkv_weight, ("seq", "batch"), axis=0, tiled=True),
        lax.all_gather(out_weight, ("seq", "batch"), axis=0, tiled=True),
        lax.all_gather(mlp_gain, ("seq", "batch"), axis=0, tiled=True),
        lax.all_gather(up_weight, ("seq", "batch"), axis=0, tiled=True),
        lax.all_gather(down_weight, ("seq", "batch"), axis=0, tiled=True),
    )
    totals = None
    grad_input_list = []
    for group in range(group_count):
        (
            info,
            cosine,
            sine_table,
            normed_one,
            inverse_one,
            acts_one,
            queries,
            key_flat,
            value_flat,
            key_all,
            value_all,
            attended,
            lse_rows,
            attended_b,
            normed_two,
            inverse_two,
            acts_two,
            gelu_back,
            activated_b,
        ) = saved[group]
        grad_block = mix_weights[-1] * grad_out_all[group]
        down_grad_b = grad_block.astype(jnp.bfloat16)
        grad_w_down = jnp.einsum(
            "tf,td->fd", activated_b, down_grad_b, preferred_element_type=jnp.float32
        )
        grad_b_down = jnp.sum(down_grad_b.astype(jnp.float32), axis=0)
        grad_act = jnp.einsum(
            "td,fd->tf", down_grad_b, back_down, preferred_element_type=jnp.float32
        )
        up_grad_b = gelu_back(grad_act)[0].astype(jnp.bfloat16)
        grad_w_up = jnp.einsum("td,tf->df", acts_two, up_grad_b, preferred_element_type=jnp.float32)
        grad_b_up = jnp.sum(up_grad_b.astype(jnp.float32), axis=0)
        grad_acts_two = jnp.einsum(
            "tf,df->td", up_grad_b, back_up, preferred_element_type=jnp.float32
        )
        grad_middle_norm, grad_gain_two, grad_shift_two = norm_back(
            grad_acts_two, normed_two, inverse_two, back_gain_two.astype(jnp.float32)
        )
        grad_middle = grad_block + grad_middle_norm
        attn_grad_b = grad_middle.astype(jnp.bfloat16)
        grad_w_out = jnp.einsum(
            "te,td->ed", attended_b, attn_grad_b, preferred_element_type=jnp.float32
        )
        grad_b_out = jnp.sum(attn_grad_b.astype(jnp.float32), axis=0)
        grad_heads = (
            jnp.einsum("td,ed->te", attn_grad_b, back_out, preferred_element_type=jnp.float32)
            .astype(jnp.bfloat16)
            .reshape(tok_count, HEADS, HEAD_DIM)
        )
        delta_rows = jnp.transpose(jnp.sum(grad_heads.astype(jnp.float32) * attended, axis=-1))
        key_all, value_all = (
            lax.all_gather(key_flat, "seq", axis=0, tiled=True),
            lax.all_gather(value_flat, "seq", axis=0, tiled=True),
        )
        key_block_rows = block_size(group_rows)

        def query_grad_block(carried, block_index):
            start_place = block_index * key_block_rows
            key_block = lax.dynamic_slice_in_dim(key_all, start_place, key_block_rows, 0).reshape(
                key_block_rows, HEADS, HEAD_DIM
            )
            value_block = lax.dynamic_slice_in_dim(
                value_all, start_place, key_block_rows, 0
            ).reshape(key_block_rows, HEADS, HEAD_DIM)
            key_places = start_place + jnp.arange(key_block_rows, dtype=jnp.int32)

            def query_compute(summed):
                probabilities = block_probs(queries, key_block, places, key_places, info, lse_rows)
                dscores = block_dscores(probabilities, grad_heads, value_block, delta_rows)
                return (
                    summed
                    + jnp.einsum(
                        "hqk,khd->qhd", dscores, key_block, preferred_element_type=jnp.float32
                    )
                    * factor
                )

            return (
                lax.cond(start_place > last_place, lambda summed: summed, query_compute, carried),
                None,
            )

        grad_queries, unused = lax.scan(
            query_grad_block,
            jnp.zeros((tok_count, HEADS, HEAD_DIM), jnp.float32),
            jnp.arange(group_rows // key_block_rows, dtype=jnp.int32),
        )
        key_first_row = jnp.int32(0)
        key_rows = key_all
        value_rows = value_all
        inner_rows = block_size(lax.axis_size("seq") * tok_count)

        def key_grad_block(carried, block_index):
            offset = block_index * inner_rows
            start_place = key_first_row + offset
            key_block = lax.dynamic_slice_in_dim(key_rows, offset, inner_rows, 0).reshape(
                inner_rows, HEADS, HEAD_DIM
            )
            value_block = lax.dynamic_slice_in_dim(value_rows, offset, inner_rows, 0).reshape(
                inner_rows, HEADS, HEAD_DIM
            )
            key_places = start_place + jnp.arange(inner_rows, dtype=jnp.int32)

            def key_compute(unused_in):
                probabilities = block_probs(queries, key_block, places, key_places, info, lse_rows)
                dscores = block_dscores(probabilities, grad_heads, value_block, delta_rows)
                grad_keys = (
                    jnp.einsum("hqk,qhd->khd", dscores, queries, preferred_element_type=jnp.float32)
                    * factor
                )
                grad_values = jnp.einsum(
                    "hqk,qhd->khd",
                    probabilities.astype(jnp.bfloat16),
                    grad_heads,
                    preferred_element_type=jnp.float32,
                )
                return jnp.concatenate(
                    [
                        grad_keys.reshape(inner_rows, model_width),
                        grad_values.reshape(inner_rows, model_width),
                    ],
                    axis=1,
                )

            def nothing(unused_in):
                return jnp.zeros((inner_rows, 2 * model_width), jnp.float32)

            return (carried, lax.cond(start_place > last_place, nothing, key_compute, carried))

        unused_out, blocks = lax.scan(
            key_grad_block,
            jnp.int32(0),
            jnp.arange(lax.axis_size("seq") * tok_count // inner_rows, dtype=jnp.int32),
        )
        key_grads = lax.psum_scatter(
            blocks.reshape(lax.axis_size("seq") * tok_count, 2 * model_width).astype(jnp.bfloat16),
            "seq",
            scatter_dimension=0,
            tiled=True,
        ).astype(jnp.float32)
        grad_keys_own = key_grads[:, :model_width]
        grad_values_own = key_grads[:, model_width:]
        grad_q_turned = rotate(grad_queries, cosine, -sine_table).reshape(tok_count, model_width)
        grad_k_turned = rotate(
            grad_keys_own.reshape(tok_count, HEADS, HEAD_DIM), cosine, -sine_table
        ).reshape(tok_count, model_width)
        qkv_grad_b = jnp.concatenate(
            [grad_q_turned, grad_k_turned, grad_values_own], axis=1
        ).astype(jnp.bfloat16)
        grad_w_qkv = jnp.einsum(
            "td,te->de", acts_one, qkv_grad_b, preferred_element_type=jnp.float32
        )
        grad_b_qkv = jnp.sum(qkv_grad_b.astype(jnp.float32), axis=0)
        grad_acts_one = jnp.einsum(
            "te,de->td", qkv_grad_b, back_qkv, preferred_element_type=jnp.float32
        )
        grad_in_norm, grad_gain_one, grad_shift_one = norm_back(
            grad_acts_one, normed_one, inverse_one, back_gain_one.astype(jnp.float32)
        )
        grad_input_list.append((grad_middle + grad_in_norm).astype(jnp.bfloat16))
        terms = [
            grad_gain_one,
            grad_shift_one,
            grad_w_qkv,
            grad_b_qkv,
            grad_w_out,
            grad_b_out,
            grad_gain_two,
            grad_shift_two,
            grad_w_up,
            grad_b_up,
            grad_w_down,
            grad_b_down,
        ]
        if totals is None:
            totals = terms
        else:
            totals = [older + newer for older, newer in zip(totals, terms)]
    shares = (
        lax.psum_scatter(totals[0], ("seq", "batch"), scatter_dimension=0, tiled=True),
        lax.psum_scatter(totals[1], ("seq", "batch"), scatter_dimension=0, tiled=True),
        lax.psum_scatter(totals[2], ("seq", "batch"), scatter_dimension=0, tiled=True),
        lax.psum_scatter(totals[3], ("seq", "batch"), scatter_dimension=0, tiled=True),
        lax.psum_scatter(totals[4], ("seq", "batch"), scatter_dimension=0, tiled=True),
        lax.psum_scatter(totals[5], ("seq", "batch"), scatter_dimension=0, tiled=True),
        lax.psum_scatter(totals[6], ("seq", "batch"), scatter_dimension=0, tiled=True),
        lax.psum_scatter(totals[7], ("seq", "batch"), scatter_dimension=0, tiled=True),
        lax.psum_scatter(totals[8], ("seq", "batch"), scatter_dimension=0, tiled=True),
        lax.psum_scatter(totals[9], ("seq", "batch"), scatter_dimension=0, tiled=True),
        lax.psum_scatter(totals[10], ("seq", "batch"), scatter_dimension=0, tiled=True),
        lax.psum_scatter(totals[11], ("seq", "batch"), scatter_dimension=0, tiled=True),
    )
    grad_mix = lax.psum(mix_terms, ("seq", "batch"))
    grad_inputs = jnp.stack(grad_input_list, axis=0)
    return (
        mixed_out.astype(jnp.bfloat16),
        grad_inputs,
        grad_history,
        shares[0],
        shares[1],
        shares[2],
        shares[3],
        shares[4],
        shares[5],
        shares[6],
        shares[7],
        shares[8],
        shares[9],
        shares[10],
        shares[11],
        grad_mix,
    )


def placed(mesh, body):
    return jax.shard_map(
        body,
        mesh=mesh,
        in_specs=(
            P("batch", "seq", None),
            P(None, "batch", "seq", None),
            P("batch"),
            P(("seq", "batch")),
            P(("seq", "batch")),
            P(("seq", "batch"), None),
            P(("seq", "batch")),
            P(("seq", "batch"), None),
            P(("seq", "batch")),
            P(("seq", "batch")),
            P(("seq", "batch")),
            P(("seq", "batch"), None),
            P(("seq", "batch")),
            P(("seq", "batch"), None),
            P(("seq", "batch")),
            P(),
            P("batch", "seq", None),
        ),
        out_specs=(
            P("batch", "seq", None),
            P("batch", "seq", None),
            P(None, "batch", "seq", None),
            P(("seq", "batch")),
            P(("seq", "batch")),
            P(("seq", "batch"), None),
            P(("seq", "batch")),
            P(("seq", "batch"), None),
            P(("seq", "batch")),
            P(("seq", "batch")),
            P(("seq", "batch")),
            P(("seq", "batch"), None),
            P(("seq", "batch")),
            P(("seq", "batch"), None),
            P(("seq", "batch")),
            P(),
        ),
        check_vma=False,
    )

MESH = pl.DeviceIdType.MESH
BF, F32 = jnp.bfloat16, jnp.float32


def where_am_i():
    seq, batch = lax.axis_index("seq"), lax.axis_index("batch")
    return seq // 2, seq % 2, batch // 2, batch % 2


def dev(z, y, x, k):
    return (z * 2 + y, x * 2 + k)


def remote(src, dst, ssem, rsem, device):
    return pltpu.make_async_remote_copy(src_ref=src, dst_ref=dst, send_sem=ssem, recv_sem=rsem,
                                        device_id=device, device_id_type=MESH)


def greet(z, y, x, k):
    barrier = pltpu.get_barrier_semaphore()
    mine = (z * 2 + y) * 2 + k
    for step in range(1, 16):
        other = lax.rem(mine + step, 16)
        pl.semaphore_signal(barrier, inc=1, device_id=dev(other // 4, (other // 2) % 2, x, other % 2), device_id_type=MESH)
    pl.semaphore_signal(barrier, inc=1, device_id=dev(z, y, 1 - x, k), device_id_type=MESH)
    pl.semaphore_wait(barrier, 16)


class Gather:
    def __init__(self, part, send, recv, pos):
        self.part, self.send, self.recv, self.pos = part, send, recv, pos
        z, y, x, k = pos
        self.c = []
        p2 = jnp.where(k == 0, 1 - y, y), jnp.where(k == 0, x, 1 - x)
        p3 = jnp.where(k == 0, y, 1 - y), jnp.where(k == 0, 1 - x, x)
        d4 = 1 - y, 1 - x
        own = (y, x)
        zed = lambda i: part((slice(z, z + 1) if False else pl.ds(z, 1)), y, x, k)
        allz = lambda yx: part(slice(None), yx[0], yx[1], k)
        def cp(n, ref, device):
            return remote(ref, ref, send.at[n], recv.at[n], device)
        self.zs = [cp(d - 1, zed(0), dev(lax.rem(z + d, 4), y, x, k)) for d in (1, 2, 3)]
        self.a2 = cp(3, allz(own), dev(z, *p2, k))
        self.a3 = cp(4, allz(own), dev(z, *p3, k))
        self.b3 = cp(5, allz(p2), dev(z, *p3, k))
        sib = dev(z, y, x, 1 - k)
        self.s1 = cp(6, allz(own), sib)
        self.s2 = cp(7, allz(p2), sib)
        self.s3 = cp(8, allz(p3), sib)
        self.s4 = cp(9, allz(d4), sib)

    def stage(self, n):
        if n == 0:
            for c in self.zs: c.start()
        elif n == 1:
            for c in self.zs: c.wait_recv()
            self.a2.start(); self.a3.start(); self.s1.start()
        elif n == 2:
            self.a2.wait_recv()
            self.b3.start(); self.s2.start()
        elif n == 3:
            self.a3.wait_recv()
            self.s3.start()
        elif n == 4:
            self.b3.wait_recv()
            self.s4.start()
        elif n == 5:
            for c in (self.s1, self.s2, self.s3, self.s4): c.wait_recv()
            for c in self.zs + [self.a2, self.a3, self.b3, self.s1, self.s2, self.s3, self.s4]: c.wait_send()
    STAGES = 6


def gather_kernel(cols, qkv, out, up, down, vec, xin, cin,
                  QKV, OUT, UP, DOWN, VEC, XM, XA, CM, CA,
                  f_own, f_sib, block, psend, precv, lsem, gsend, grecv, asend, arecv, aarecv, fsend, frecv):
    pos = z, y, x, k = where_am_i()
    greet(z, y, x, k)
    at = 0
    tot = sum(cols)
    offs = []
    for n, ref in zip(cols, (qkv, out, up)):
        half = n // 2
        f_own[0, :, at:at + half] = ref[:, :half].astype(F32)
        f_own[1, :, at:at + half] = ref[:, half:].astype(F32)
        offs.append((at, half))
        at += half
    pre = remote(f_own.at[1 - k], f_sib, psend, precv, dev(z, y, x, 1 - k))
    pre.start()
    s = 2 * z + y
    own_s = lax.rem(y + z, 2)
    acps = []
    for a, (src, M, A) in enumerate(((xin, XM, XA), (cin, CM, CA))):
        for i in range(2):
            g = 2 * k + i
            lo = src.at[i, pl.ds(pl.multiple_of(y * 128, 128), 128)]
            hi = src.at[i, pl.ds(pl.multiple_of((1 - y) * 128, 128), 128)]
            for n, (ref, dst, rs, d) in enumerate((
                (lo, M.at[s], arecv.at[a, s], (g, y, x, own_s)),
                (hi, M.at[s], arecv.at[a, s], (g, 1 - y, x, own_s)),
                (hi, A.at[z], aarecv.at[a, z], (g, y, x, 1 - own_s)))):
                ss = asend.at[a, i, n]
                me = (g == z) & (d[1] == y) & (d[3] == k)
                cp = remote(ref, dst, ss, rs, dev(*d))
                @pl.when(me)
                def _():
                    pltpu.make_async_copy(ref, dst, rs).start()
                @pl.when(jnp.logical_not(me))
                def _():
                    cp.start()
                acps.append((cp, me))
    pre.wait_recv()
    lcs = []
    for i, ((at, half), W) in enumerate(zip(offs, (QKV, OUT, UP))):
        mine = f_own[k, :, at:at + half]
        theirs = f_sib[:, at:at + half]
        first = jnp.where(k == 0, mine, theirs)
        second = jnp.where(k == 0, theirs, mine)
        block[:, at:at + half] = jnp.concatenate([first, second], axis=0).astype(BF)
        c = pltpu.make_async_copy(block.at[:, at:at + half],
                                  W.at[z, y, x, :, pl.ds(pl.multiple_of(k * half, 128), half)], lsem.at[i])
        c.start(); lcs.append(c)
    for i, (ref, W) in enumerate(((down, DOWN), (vec, VEC))):
        c = pltpu.make_async_copy(ref, W.at[z, y, x, k], lsem.at[3 + i])
        c.start(); lcs.append(c)
    def colpart(W, half):
        return lambda zz, yy, xx, kk: W.at[zz, yy, xx, :, pl.ds(pl.multiple_of(kk * half, 128), half)]
    def rowpart(W):
        return lambda zz, yy, xx, kk: W.at[zz, yy, xx, kk]
    parts = [rowpart(VEC), colpart(QKV, offs[0][1]), colpart(OUT, offs[1][1]), colpart(UP, offs[2][1]), rowpart(DOWN)]
    for c in lcs: c.wait()
    gs = [Gather(p, gsend.at[i], grecv.at[i], pos) for i, p in enumerate(parts)]
    fw = []
    def tokens_forward():
        for zz in range(4):
            j = 2 * zz + lax.rem(zz + k, 2)
            cp = remote(XM.at[j], XM.at[j], fsend.at[zz], frecv.at[zz], dev(z, y, x, 1 - k))
            remote(XM.at[j], XM.at[j], fsend.at[zz], arecv.at[0, j], dev(z, y, x, 1 - k)).wait_recv()
            cp.start(); fw.append(cp)
        for e in range(2):
            zz = lax.rem(1 - y + k, 2) + 2 * e
            cp = remote(XA.at[zz], XA.at[zz], fsend.at[4 + e], frecv.at[4 + e], dev(z, y, x, 1 - k))
            remote(XA.at[zz], XA.at[zz], fsend.at[4 + e], aarecv.at[0, zz], dev(z, y, x, 1 - k)).wait_recv()
            cp.start(); fw.append(cp)
    for tick in range(len(gs) + Gather.STAGES - 1):
        for i, g in enumerate(gs):
            n = tick - i
            if 0 <= n < Gather.STAGES:
                g.stage(n)
        if tick == 2:
            tokens_forward()
    for zz in range(4):
        j = 2 * zz + lax.rem(zz + k, 2)
        remote(CM.at[j], CM.at[j], fsend.at[zz], arecv.at[1, j], dev(z, y, x, 1 - k)).wait_recv()
    for e in range(2):
        zz = lax.rem(1 - y + k, 2) + 2 * e
        remote(CA.at[zz], CA.at[zz], fsend.at[4 + e], aarecv.at[1, zz], dev(z, y, x, 1 - k)).wait_recv()
    for c in fw: c.wait()
    for cp, me in acps:
        @pl.when(jnp.logical_not(me))
        def _():
            cp.wait_send()
    pre.wait_send()


def gather_call(qkv, out, up, down, vec, xin, cin):
    D = xin.shape[-1]
    cols = (qkv.shape[1], out.shape[1], up.shape[1])
    H = sum(cols) // 2
    sd = jax.ShapeDtypeStruct
    outs = [sd((4, 2, 2, 48, n), BF) for n in cols] + [sd((4, 2, 2, 2) + down.shape, BF), sd((4, 2, 2, 2) + vec.shape, F32),
            sd((8, 128, D), BF), sd((4, 128, D), BF), sd((8, 128, D), BF), sd((4, 128, D), BF)]
    V, A = pl.BlockSpec(memory_space=pltpu.VMEM), pl.BlockSpec(memory_space=pl.ANY)
    S = pltpu.SemaphoreType.DMA
    return pl.pallas_call(
        functools.partial(gather_kernel, cols),
        out_shape=outs,
        in_specs=[V, V, V, A, A, A, A],
        out_specs=[A] * 9,
        scratch_shapes=[pltpu.VMEM((2, 24, H), F32), pltpu.VMEM((24, H), F32), pltpu.VMEM((48, H), BF),
                        S, S, S((5,)), S((5, 10)), S((5, 10)), S((2, 2, 3)), S((2, 8)), S((2, 4)), S((6,)), S((6,))],
        compiler_params=pltpu.CompilerParams(collective_id=0, has_side_effects=True, vmem_limit_bytes=32 * 2**20),
    )(qkv, out, up, down, vec, xin, cin)

EPS = 1e-5
NT = (((1,), (1,)), ((), ()))


def nt(a, b):
    return lax.dot_general(a, b, NT, preferred_element_type=F32)


def nn(a, b):
    return jnp.dot(a, b, preferred_element_type=F32)


def rope_tables():
    freq = np.exp(-math.log(10000.0) * (2.0 * np.arange(32, dtype=np.float32) / 64)).astype(np.float32)
    ang = np.arange(1024, dtype=np.float32)[:, None] * freq[None, :]
    c, s = np.cos(ang.astype(np.float64)), np.sin(ang.astype(np.float64))
    return (np.concatenate([c, c, c, c], 1).astype(np.float32), np.concatenate([-s, s, -s, s], 1).astype(np.float32))


def swap(u):
    low = lax.broadcasted_iota(jnp.int32, u.shape, 1) % 64 < 32
    return jnp.where(low, pltpu.roll(u, 96, 1), pltpu.roll(u, 32, 1))


def norm(v):
    mean = jnp.mean(v, axis=-1, keepdims=True)
    cen = v - mean
    inv = lax.rsqrt(jnp.mean(cen * cen, axis=-1, keepdims=True) + EPS)
    return cen * inv, inv


def norm_grad(e, n, inv, gain):
    g = e * gain
    return inv * (g - jnp.mean(g, axis=-1, keepdims=True) - n * jnp.mean(g * n, axis=-1, keepdims=True))


def own_block(i, k):
    return 2 * i + lax.rem(i + k, 2)


def rows(i, n=128):
    return pl.ds(pl.multiple_of(i * n, n), n)


def spread(p):
    low = lax.broadcasted_iota(jnp.int32, p.shape, 1) < 64
    zero = jnp.zeros_like(p)
    return jnp.concatenate([jnp.where(low, p, zero), jnp.where(low, zero, p)], axis=0)


def pick(o):
    low = lax.broadcasted_iota(jnp.int32, (128, 128), 0) < 64
    return jnp.where(low, o[:, :128], o[:, 128:]).T


def fill_bias(bias, is_long, k):
    at = 0
    for i in range(4):
        kk = 256 * (i + 1)
        key = lax.broadcasted_iota(jnp.int32, (kk, 256), 0)
        q = own_block(i, k) * 128 + lax.broadcasted_iota(jnp.int32, (kk, 256), 1) % 128
        first = jnp.where(is_long, 0, q - q % 256)
        bias[at:at + kk, :] = jnp.where((key <= q) & (key >= first), 0.0, -1e30)
        at += kk


def attn_fwd(flag, XM, XA, wqkv, wout, gain, shift, bqkv, bout, COS, SIN,
             acts, Q, K, V, att, lse, middle, bias, VT):
    z, y, x, k = where_am_i()
    is_long = flag[0] != 0
    fill_bias(bias, is_long, k)
    for j in range(8):
        alt = jnp.logical_and(jnp.logical_not(is_long), lax.rem(jnp.int32(j), 2) != y)
        blk = jnp.where(alt, XA[j // 2], XM[j]).astype(F32)
        n, _ = norm(blk)
        acts[j * 128:(j + 1) * 128, :] = (n * gain[...] + shift[...]).astype(BF)

    def tables(j):
        off = jnp.where(is_long, j, lax.rem(j, 2))
        return COS[rows(off), :], SIN[rows(off), :]

    @pl.loop(0, 8)
    def _(j):
        a = acts[rows(j), :]
        c, s = tables(j)
        for t in range(6):
            u = nn(a, wqkv[:, 768 + t * 128:896 + t * 128]) + bqkv[:, 768 + t * 128:896 + t * 128]
            K[rows(j), t * 128:(t + 1) * 128] = (u * c + swap(u) * s).astype(BF)
        V[rows(j), :] = (nn(a, wqkv[:, 1536:]) + bqkv[:, 1536:]).astype(BF)

    @pl.loop(0, 4)
    def _(i):
        j = own_block(i, k)
        a = acts[rows(j), :]
        c, s = tables(j)
        for t in range(6):
            u = nn(a, wqkv[:, t * 128:(t + 1) * 128]) + bqkv[:, t * 128:(t + 1) * 128]
            Q[rows(i), t * 128:(t + 1) * 128] = (u * c + swap(u) * s).astype(BF) * jnp.asarray(0.125, BF)

    @pl.loop(0, 6)
    def _(h):
        lanes = rows(h)
        VT[...] = V[:, lanes].T
        at = 0
        for i in range(4):
            kk = 256 * (i + 1)
            qb = spread(Q[i * 128:(i + 1) * 128, lanes])
            st = nt(K[0:kk, lanes], qb) + bias[at:at + kk, :]
            top = jnp.max(st, axis=0, keepdims=True)
            p = jnp.exp(st - top)
            den = jnp.sum(p, axis=0, keepdims=True)
            o = nn(VT[:, 0:kk], p.astype(BF)) * (1.0 / den)
            att[i * 128:(i + 1) * 128, lanes] = pick(o)
            lse[h, i:i + 1, :] = top + jnp.log(den)
            at += kk

    @pl.loop(0, 4)
    def _(i):
        j = own_block(i, k)
        alt = jnp.logical_and(jnp.logical_not(is_long), lax.rem(j, 2) != y)
        xb = jnp.where(alt, XA[i], XM[j]).astype(F32)
        middle[rows(i), :] = xb + (nn(att[rows(i), :].astype(BF), wout[...]) + bout[...])


def mlp(CH, flag, mix, middle, CM, CA, wup, wdown, gain, shift, bup, bdown,
        block, gmid, gup, gdown, g_gain, g_shift, g_bup, g_bdown, mixsum, acts2, actsT, dg, ga, cf):
    z, y, x, k = where_am_i()
    is_long = flag[0] != 0
    m5 = mix[5]
    for i in range(4):
        r = slice(i * 128, (i + 1) * 128)
        mid = middle[r, :]
        n, _ = norm(mid)
        acts2[r, :] = (n * gain[...] + shift[...]).astype(BF)
        j = own_block(jnp.int32(i), k)
        alt = jnp.logical_and(jnp.logical_not(is_long), lax.rem(j, 2) != y)
        c = jnp.where(alt, CA[i], CM[j]).astype(F32)
        cf[r, :] = c
        dg[r, :] = (m5 * c).astype(BF)
        block[r, :] = mid + bdown[...]
        ga[r, :] = jnp.zeros_like(mid)
        actsT[:, r] = acts2[r, :].T
    g_bdown[...] = jnp.sum(dg[...].astype(F32), axis=0, keepdims=True)

    @pl.loop(0, wup.shape[1] // CH)
    def _(f):
        cols = rows(f, CH)
        up = nn(acts2[...], wup[:, cols]) + bup[:, cols]
        half_erf = 0.5 * lax.erf(up * (2.0 ** -0.5)) + 0.5
        slope = half_erf + up * (jnp.exp(up * up * -0.5) * (1.0 / math.sqrt(2 * math.pi)))
        act = (up * half_erf).astype(BF)
        block[...] += nn(act, wdown[cols, :])
        upg = (nt(dg[...], wdown[cols, :]) * slope).astype(BF)
        g_bup[:, cols] = jnp.sum(upg.astype(F32), axis=0, keepdims=True)
        gdown[cols, :] = nn(act.T, dg[...]).astype(BF)
        gup[:, cols] = nn(actsT[...], upg).astype(BF)
        ga[...] += nt(upg, wup[:, cols])

    total = jnp.zeros((1, 768), F32)
    gg = jnp.zeros((1, 768), F32)
    gs = jnp.zeros((1, 768), F32)
    for i in range(4):
        r = slice(i * 128, (i + 1) * 128)
        n, inv = norm(middle[r, :])
        e = ga[r, :]
        gg += jnp.sum(e * n, axis=0, keepdims=True)
        gs += jnp.sum(e, axis=0, keepdims=True)
        gmid[r, :] = m5 * cf[r, :] + norm_grad(e, n, inv, gain[...])
        total += jnp.sum(cf[r, :] * block[r, :], axis=0, keepdims=True)
    g_gain[...] = gg
    g_shift[...] = gs
    mixsum[...] = total


def attn_bwd(flag, gmid, XM, XA, acts, Q, K, V, att, lse, wqkv, wout, gain, COS, SIN,
             e, gqkv, gout, g_bqkv, g_bout, bias, KT, da, dQ, dK, dV, agrad, actsT, actsqT, KG, VG):
    z, y, x, k = where_am_i()
    is_long = flag[0] != 0
    fill_bias(bias, is_long, k)
    agrad[...] = gmid[...].astype(BF)
    g_bout[...] = jnp.sum(agrad[...].astype(F32), axis=0, keepdims=True)

    @pl.loop(0, 4)
    def _(i):
        da[rows(i), :] = nt(agrad[rows(i), :], wout[...]).astype(BF)

    for t in range(6):
        aT = att[:, t * 128:(t + 1) * 128].T.astype(BF)
        gout[t * 128:(t + 1) * 128, :] = nn(aT, agrad[...]).astype(BF)
    dK[...] = jnp.zeros_like(dK)
    dV[...] = jnp.zeros_like(dV)

    @pl.loop(0, 6)
    def _(h):
        lanes = rows(h)
        KT[...] = K[:, lanes].T
        at = 0
        for i in range(4):
            kk = 256 * (i + 1)
            r = slice(i * 128, (i + 1) * 128)
            d = da[r, lanes]
            qb, db = spread(Q[r, lanes]), spread(d)
            prod = (d.astype(F32) * att[r, lanes]).T
            delta = jnp.concatenate([jnp.sum(prod[:64], axis=0, keepdims=True), jnp.sum(prod[64:], axis=0, keepdims=True)], axis=1)
            st = nt(K[0:kk, lanes], qb) + bias[at:at + kk, :]
            p = jnp.exp(st - lse[h, i:i + 1, :])
            ds = (p * (nt(V[0:kk, lanes], db) - delta)).astype(BF)
            dV[0:kk, lanes] += nn(p.astype(BF), db)
            dK[0:kk, lanes] += nn(ds, qb)
            dQ[r, lanes] = pick(nn(KT[:, 0:kk], ds)) * 0.125
            at += kk

    def tables(j):
        off = jnp.where(is_long, j, lax.rem(j, 2))
        return COS[rows(off), :], SIN[rows(off), :]

    for j in range(8):
        actsT[:, j * 128:(j + 1) * 128] = acts[j * 128:(j + 1) * 128, :].T
    for i in range(4):
        j = own_block(jnp.int32(i), k)
        actsqT[:, i * 128:(i + 1) * 128] = acts[rows(j), :].T
        c, s = tables(j)
        for t in range(6):
            u = dQ[i * 128:(i + 1) * 128, t * 128:(t + 1) * 128]
            da[i * 128:(i + 1) * 128, t * 128:(t + 1) * 128] = (u * c - swap(u) * s).astype(BF)

    @pl.loop(0, 8)
    def _(j):
        c, s = tables(j)
        for t in range(6):
            u = dK[rows(j), t * 128:(t + 1) * 128]
            KG[rows(j), t * 128:(t + 1) * 128] = (u * c - swap(u) * s).astype(BF)
        VG[rows(j), :] = dV[rows(j), :].astype(BF)
        e[rows(j), :] = nt(KG[rows(j), :], wqkv[:, 768:1536]) + nt(VG[rows(j), :], wqkv[:, 1536:])

    @pl.loop(0, 4)
    def _(i):
        j = own_block(i, k)
        e[rows(j), :] += nt(da[rows(i), :], wqkv[:, :768])

    g_bqkv[:, :768] = jnp.sum(da[...].astype(F32), axis=0, keepdims=True)
    g_bqkv[:, 768:1536] = jnp.sum(KG[...].astype(F32), axis=0, keepdims=True)
    g_bqkv[:, 1536:] = jnp.sum(VG[...].astype(F32), axis=0, keepdims=True)

    @pl.loop(0, 6)
    def _(t):
        gqkv[rows(t), :768] = nn(actsqT[rows(t), :], da[...]).astype(BF)
        gqkv[rows(t), 768:1536] = nn(actsT[rows(t), :], KG[...]).astype(BF)
        gqkv[rows(t), 1536:] = nn(actsT[rows(t), :], VG[...]).astype(BF)


sd = jax.ShapeDtypeStruct
VM = pltpu.VMEM
vs = pl.BlockSpec(memory_space=pltpu.VMEM)
ss = pl.BlockSpec(memory_space=pltpu.SMEM)
CP = pltpu.CompilerParams(vmem_limit_bytes=60 * 2**20)


def attn_fwd_call(flag, *ins):
    return pl.pallas_call(attn_fwd,
        out_shape=[sd((1024, 768), BF), sd((512, 768), BF), sd((1024, 768), BF), sd((1024, 768), BF),
                   sd((512, 768), F32), sd((6, 4, 256), F32), sd((512, 768), F32)],
        in_specs=[ss] + [vs] * len(ins), out_specs=[vs] * 7,
        scratch_shapes=[VM((2560, 256), F32), VM((128, 1024), BF)],
        compiler_params=CP)(flag, *ins)


def mlp_call(flag, mix, *ins):
    r = sd((1, 768), F32)
    return pl.pallas_call(functools.partial(mlp, 512),
        out_shape=[sd((512, 768), F32), sd((512, 768), F32), sd((768, 3072), BF), sd((3072, 768), BF), r, r, sd((1, 3072), F32), r, r],
        in_specs=[ss, ss] + [vs] * len(ins), out_specs=[vs] * 9,
        scratch_shapes=[VM((512, 768), BF), VM((768, 512), BF), VM((512, 768), BF), VM((512, 768), F32), VM((512, 768), F32)],
        compiler_params=CP)(flag, mix, *ins)


def attn_bwd_call(flag, *ins):
    return pl.pallas_call(attn_bwd,
        out_shape=[sd((1024, 768), F32), sd((768, 2304), BF), sd((768, 768), BF), sd((1, 2304), F32), sd((1, 768), F32)],
        in_specs=[ss] + [vs] * len(ins), out_specs=[vs] * 5,
        scratch_shapes=[VM((2560, 256), F32), VM((128, 1024), BF), VM((512, 768), BF), VM((512, 768), F32), VM((1024, 768), F32),
                        VM((1024, 768), F32), VM((512, 768), BF), VM((768, 1024), BF), VM((768, 512), BF), VM((1024, 768), BF), VM((1024, 768), BF)],
        compiler_params=CP)(flag, *ins)


class Scatter:
    STAGES = 5

    def __init__(self, part, PA, RA, RB, RC, RZ, put, send, recv, pos):
        self.__dict__.update(locals())
        z, y, x, k = pos
        self.own = (y, x)
        self.p2 = jnp.where(k == 0, 1 - y, y), jnp.where(k == 0, x, 1 - x)
        self.p3 = jnp.where(k == 0, y, 1 - y), jnp.where(k == 0, 1 - x, x)
        self.d4 = 1 - y, 1 - x
        blk = lambda yx: PA.at[:, yx[0], yx[1]]
        n3, n2 = dev(z, *self.p3, k), dev(z, *self.p2, k)
        self.pre = remote(part(slice(None), slice(None), slice(None), 1 - k), RA, send.at[0], recv.at[0], dev(z, y, x, 1 - k))
        self.b1 = remote(blk(self.d4), RB.at[1], send.at[1], recv.at[1], n3)
        self.b0 = remote(blk(self.p3), RB.at[0], send.at[2], recv.at[2], n3)
        self.c = remote(blk(self.p2), RC, send.at[3], recv.at[3], n2)
        self.zs = [remote(PA.at[lax.rem(z + d, 4), y, x], RZ.at[d - 1], send.at[3 + d], recv.at[3 + d],
                          dev(lax.rem(z + d, 4), y, x, k)) for d in (1, 2, 3)]

    def add(self, yx, other):
        @pl.loop(0, 4)
        def _(i):
            a = self.PA[i, yx[0], yx[1]].astype(F32) + other[i].astype(F32)
            self.PA[i, yx[0], yx[1]] = a.astype(BF)

    def first(self, yx):
        k = self.pos[3]
        @pl.loop(0, 4)
        def _(i):
            a = self.part(i, yx[0], yx[1], k)[...].astype(F32) + self.RA[i, yx[0], yx[1]].astype(F32)
            self.PA[i, yx[0], yx[1]] = a.astype(BF)

    def stage(self, n):
        z, y, x, k = self.pos
        if n == 0:
            self.pre.start()
        elif n == 1:
            self.pre.wait_recv()
            self.first(self.d4)
            self.b1.start()
            self.first(self.p3)
            self.b0.start()
            self.first(self.p2)
            self.first(self.own)
        elif n == 2:
            self.b1.wait_recv()
            self.add(self.p2, self.RB.at[1])
            self.c.start()
            self.b0.wait_recv()
            self.add(self.own, self.RB.at[0])
        elif n == 3:
            self.c.wait_recv()
            self.add(self.own, self.RC)
            for c in self.zs: c.start()
        elif n == 4:
            for c in self.zs: c.wait_recv()
            tot = self.PA[z, y, x].astype(F32)
            for i in range(3):
                tot = tot + self.RZ[i].astype(F32)
            self.put(tot)
            for c in [self.pre, self.b0, self.b1, self.c] + self.zs: c.wait_send()


def reduce_kernel(cols, flag, gqkv, gout, gup, gdown, e, gmid, block, XM, XA, gain, vin,
                  oq, oo, ou, od, vout, H0, HL, HS,
                  PQ, AQ, BQ, CQ, ZQ, PO, AO, BO, CO, ZO, PU, AU, BU, CU, ZU, PD, AD, BD, CD, ZD,
                  fin, fsib, es, er, gx, bl, vbuf, vrec,
                  ssem, rsem, hsend, h0, hl, hs, misc_s, misc_r, vsend, vrecv):
    pos = z, y, x, k = where_am_i()
    is_long = flag[0] != 0
    greet(z, y, x, k)
    sib = dev(z, y, x, 1 - k)
    for i in range(4):
        es[i] = e[rows(own_block(jnp.int32(i), 1 - k)), :].astype(BF)
    ecp = remote(es, er, misc_s.at[0], misc_r.at[0], sib)
    ecp.start()
    halves = [c // 2 for c in cols]

    def colpart(W, half):
        def f(zz, yy, xx, kk):
            return W.at[zz, yy, xx, :, pl.ds(pl.multiple_of(kk * half, 128), half)]
        return f
    offs = [0, halves[0], halves[0] + halves[1]]
    def put_cols(i):
        def put(t):
            fin[0, :, offs[i]:offs[i] + halves[i]] = t[:24]
            fin[1, :, offs[i]:offs[i] + halves[i]] = t[24:]
        return put
    def put_down(t):
        od[...] = t
    S = lambda a, part, bufs, put: Scatter(part, *bufs, put, ssem.at[a], rsem.at[a], pos)
    gs = [S(0, lambda zz, yy, xx, kk: gdown.at[zz, yy, xx, kk], (PD, AD, BD, CD, ZD), put_down),
          S(1, colpart(gup, halves[2]), (PU, AU, BU, CU, ZU), put_cols(2)),
          S(2, colpart(gout, halves[1]), (PO, AO, BO, CO, ZO), put_cols(1)),
          S(3, colpart(gqkv, halves[0]), (PQ, AQ, BQ, CQ, ZQ), put_cols(0))]
    homes = []
    g = z
    def send_home(a, buf):
        for i in range(4):
            j = own_block(jnp.int32(i), k)
            yj = lax.rem(j, 2)
            zj = jnp.int32(i)
            core = g // 2
            straight = yj == y
            slot = lax.rem(g, 2)
            for n, (dst, rs, yd, cond) in enumerate((
                (H0.at[a, slot], h0.at[a, slot], y, straight),
                (HL.at[a, slot], hl.at[a, slot], 1 - y, jnp.logical_not(straight)),
                (HS.at[a, slot], hs.at[a, slot], y, jnp.logical_not(straight)))):
                me = (zj == z) & (yd == y) & (core == k)
                cp = remote(buf.at[i], dst, hsend.at[a, i, n], rs, dev(zj, yd, x, core))
                @pl.when(cond & me)
                def _():
                    pltpu.make_async_copy(buf.at[i], dst, rs).start()
                @pl.when(cond & jnp.logical_not(me))
                def _():
                    cp.start()
                homes.append((cp, cond & jnp.logical_not(me)))
    for i in range(4):
        bl[i] = block[i * 128:(i + 1) * 128, :].astype(BF)
    send_home(0, bl)

    def token_grads():
        ecp.wait_recv()
        gg = jnp.zeros((1, 768), F32)
        gsh = jnp.zeros((1, 768), F32)
        for i in range(4):
            j = own_block(jnp.int32(i), k)
            alt = jnp.logical_and(jnp.logical_not(is_long), lax.rem(j, 2) != y)
            n, inv = norm(jnp.where(alt, XA[i], XM[j]).astype(F32))
            ee = e[rows(j), :] + er[i].astype(F32)
            gg += jnp.sum(ee * n, axis=0, keepdims=True)
            gsh += jnp.sum(ee, axis=0, keepdims=True)
            gx[i] = (gmid[i * 128:(i + 1) * 128, :] + norm_grad(ee, n, inv, gain[...])).astype(BF)
        send_home(1, gx)
        vbuf[0] = vin[...]
        for t in range(6):
            vbuf[0, t:t + 1, :] = gg[:, t * 128:(t + 1) * 128]
            vbuf[0, 6 + t:7 + t, :] = gsh[:, t * 128:(t + 1) * 128]

    sc = gs[0]
    vec_steps = [[sib], [dev(z, *sc.p2, k)], [dev(z, *sc.p3, k)], [dev(lax.rem(z + d, 4), y, x, k) for d in (1, 2, 3)]]
    vcp = []
    def vec_stage(n):
        if n > 0:
            for c in vcp[-1]: c.wait_recv()
            t = vbuf[n - 1]
            for r in range(len(vcp[-1])):
                t = t + vrec[n - 1 + r]
            if n < 4: vbuf[n] = t
            else: vout[...] = t
        if n < 4:
            vcp.append([remote(vbuf.at[n], vrec.at[n + i], vsend.at[n + i], vrecv.at[n + i], d) for i, d in enumerate(vec_steps[n])])
            for c in vcp[-1]: c.start()

    for tick in range(len(gs) + Scatter.STAGES - 1):
        for i, gg_ in enumerate(gs):
            n = tick - i
            if 0 <= n < Scatter.STAGES:
                gg_.stage(n)
        if tick == 0:
            token_grads()
        if 1 <= tick <= 5:
            vec_stage(tick - 1)
    lst = remote(fin.at[1 - k], fsib, misc_s.at[1], misc_r.at[1], sib)
    lst.start()
    lst.wait_recv()
    for i, o in enumerate((oq, oo, ou)):
        mine = fin[k, :, offs[i]:offs[i] + halves[i]]
        theirs = fsib[:, offs[i]:offs[i] + halves[i]]
        o[:, :halves[i]] = jnp.where(k == 0, mine, theirs)
        o[:, halves[i]:] = jnp.where(k == 0, theirs, mine)
    for a in range(2):
        for i in range(2):
            remote(H0.at[a, i], H0.at[a, i], hsend.at[0, 0, 0], h0.at[a, i], sib).wait_recv()
            remote(HL.at[a, i], HL.at[a, i], hsend.at[0, 0, 0], hl.at[a, i], sib).wait_recv()
            remote(HS.at[a, i], HS.at[a, i], hsend.at[0, 0, 0], hs.at[a, i], sib).wait_recv()
    lst.wait_send()
    ecp.wait_send()
    for cs in vcp:
        for c in cs: c.wait_send()
    for cp, cond in homes:
        @pl.when(cond)
        def _():
            cp.wait_send()


def reduce_call(flag, gqkv, gout, gup, gdown, *ins):
    cols = (gqkv.shape[1], gout.shape[1], gup.shape[1])
    gqkv, gout, gup = (g.reshape(4, 2, 2, 48, g.shape[1]) for g in (gqkv, gout, gup))
    gdown = gdown.reshape(4, 2, 2, 2, 96, 768)
    any_ = pl.BlockSpec(memory_space=pl.ANY)
    bufs = []
    for r, n in ((48, cols[0] // 2), (48, cols[1] // 2), (48, cols[2] // 2), (96, 768)):
        bufs += [VM((4, 2, 2, r, n), BF), VM((4, 2, 2, r, n), BF), VM((2, 4, r, n), BF), VM((4, r, n), BF), VM((3, r, n), BF)]
    H = sum(cols) // 2
    DS = pltpu.SemaphoreType.DMA
    home = sd((2, 2, 128, 768), BF)
    return pl.pallas_call(functools.partial(reduce_kernel, cols),
        out_shape=[sd((24, cols[0]), F32), sd((24, cols[1]), F32), sd((24, cols[2]), F32), sd((96, 768), F32), sd((80, 128), F32), home, home, home],
        in_specs=[ss] + [vs] * (4 + len(ins)), out_specs=[vs] * 5 + [any_] * 3,
        scratch_shapes=bufs + [VM((2, 24, H), F32), VM((24, H), F32), VM((4, 128, 768), BF), VM((4, 128, 768), BF), VM((4, 128, 768), BF),
                               VM((4, 128, 768), BF), VM((4, 80, 128), F32), VM((6, 80, 128), F32),
                               DS((4, 7)), DS((4, 7)), DS((2, 4, 3)), DS((2, 2)), DS((2, 2)), DS((2, 2)), DS((2,)), DS((2,)), DS((6,)), DS((6,))],
        compiler_params=pltpu.CompilerParams(collective_id=1, has_side_effects=True, vmem_limit_bytes=62 * 2**20),
    )(flag, gqkv, gout, gup, gdown, *ins)

def fast_shards(inputs, history, seq_lengths, attn_gain, attn_shift, qkv_weight, qkv_bias, out_weight, out_bias, mlp_gain,
                mlp_shift, up_weight, up_bias, down_weight, down_bias, mix_weights, cotangent):
    seq, batch = lax.axis_index("seq"), lax.axis_index("batch")
    z, y, x, k = seq // 2, seq % 2, batch // 2, batch % 2
    vectors = (attn_gain, attn_shift, qkv_bias, out_bias, mlp_gain, mlp_shift, up_bias, down_bias)
    packed = jnp.concatenate([v.astype(F32) for v in vectors] + [seq_lengths.astype(F32)])
    packed = jnp.pad(packed, (0, 1024 - packed.shape[0])).reshape(8, 128)
    QKV, OUT, UP, DOWN, VEC, XM, XA, CM, CA = gather_call(qkv_weight, out_weight, up_weight, down_weight, packed, inputs, cotangent)
    wqkv, wout, wup = (w.reshape(768, w.shape[-1]) for w in (QKV, OUT, UP))
    wdown = DOWN.reshape(3072, 768)
    flat = VEC.reshape(32, 1024)
    full, at = [], 0
    for v in vectors:
        n = v.shape[0]
        full.append(flat[:, at:at + n].reshape(1, 32 * n))
        at += n
    a_gain, a_shift, bqkv, bout, m_gain, m_shift, bup, bdown = full
    length = VEC[0, 0, :, :, 0, :].reshape(2, 2, 0 + 128)[:, :, 0] if False else flat[:4, at:at + 2].reshape(2, 4)
    lens = lax.dynamic_index_in_dim(length, x, 0, keepdims=False)
    flag = (lax.dynamic_index_in_dim(lens, z, 0, keepdims=True) == LONG_LEN).astype(jnp.int32)
    COS, SIN = (jnp.asarray(t) for t in rope_tables())
    acts, Q, K, V, att, lse, middle = attn_fwd_call(flag, XM, XA, wqkv, wout, a_gain, a_shift, bqkv, bout, COS, SIN)
    block, gmid, gup, gdown, g_mgain, g_mshift, g_bup, g_bdown, mixsum = mlp_call(
        flag, mix_weights, middle, CM, CA, wup, wdown, m_gain, m_shift, bup, bdown)
    e, gqkv, gout, g_bqkv, g_bout = attn_bwd_call(flag, gmid, XM, XA, acts, Q, K, V, att, lse, wqkv, wout, a_gain, COS, SIN)
    earlier, cot = history.astype(F32), cotangent.astype(F32)
    mix_terms = jnp.concatenate([jnp.sum(earlier * cot[None], axis=(1, 2, 3)), jnp.sum(mixsum)[None]])
    grad_history = (mix_weights[:-1, None, None, None] * cot[None]).astype(BF)
    vin = jnp.concatenate([jnp.zeros((1536,), F32)] + [v.reshape(-1) for v in (g_bqkv, g_bout, g_mgain, g_mshift, g_bup, g_bdown)]
                          + [mix_terms, jnp.zeros((250,), F32)]).reshape(80, 128)
    oq, oo, ou, od, vout, H0, HL, HS = reduce_call(flag, gqkv, gout, gup, gdown, e, gmid, block, XM, XA, a_gain, vin)
    is_long = (seq_lengths == LONG_LEN)[None, :, None, None]
    other = jnp.where(is_long, HL, HS)
    home = jnp.where(y == 0, jnp.concatenate([H0, other], axis=2), jnp.concatenate([other, H0], axis=2))
    layer_out = (jnp.sum(mix_weights[:-1, None, None, None] * earlier, axis=0) + mix_weights[-1] * home[0].astype(F32)).astype(BF)
    vflat = vout.reshape(-1)
    me = seq * 4 + batch
    gv, at = [], 0
    for v in vectors:
        n = v.shape[0]
        gv.append(lax.dynamic_slice_in_dim(vflat, at + me * n, n, 0))
        at += 32 * n
    grad_mix = vflat[at:at + 6]
    return (layer_out, home[1], grad_history, gv[0], gv[1], oq, gv[2], oo, gv[3], gv[4], gv[5], ou, gv[6], od, gv[7], grad_mix)


def fits(mesh, inputs):
    shape = dict(mesh.shape)
    return shape == {"seq": 8, "batch": 4} and inputs.shape == (8, 2048, 768)


def solution(mesh):
    def run(*args):
        body = fast_shards if fits(mesh, args[0]) else shards
        return placed(mesh, body)(*args)
    return run
```

```python
import functools
import math

import jax
import jax.numpy as jnp
import numpy as np
from jax import lax
from jax.experimental import pallas as pl
from jax.experimental.pallas import tpu as pltpu
from jax.sharding import PartitionSpec as P

HEADS = 12
HEAD_DIM = 64
LONG_LEN = 1024
SHORT_LEN = 256


eps = 1e-05
masked = -1e30


def block_size(row_count):
    chosen = 1
    for candidate in range(1, min(row_count, 512) + 1):
        if row_count % candidate == 0:
            chosen = candidate
    return chosen


def exact_gelu(values):
    return jax.nn.gelu(values, approximate=False)


def layer_norm(values, norm_gain, norm_shift):
    average = jnp.mean(values, axis=-1, keepdims=True)
    centred = values - average
    inverse = lax.rsqrt(jnp.mean(centred * centred, axis=-1, keepdims=True) + eps)
    normed = centred * inverse
    return (normed * norm_gain + norm_shift, normed, inverse)


def norm_back(grad_out, normed, inverse, norm_gain):
    grad_normed = grad_out * norm_gain
    mean_grad = jnp.mean(grad_normed, axis=-1, keepdims=True)
    mean_cross = jnp.mean(grad_normed * normed, axis=-1, keepdims=True)
    grad_in = inverse * (grad_normed - mean_grad - normed * mean_cross)
    return (grad_in, jnp.sum(grad_out * normed, axis=0), jnp.sum(grad_out, axis=0))


def token_layout(index, info):
    seq_len, tok_count, slice_len = info
    is_long = seq_len == LONG_LEN
    offset = index % tok_count
    device = index // tok_count
    doc_ids = jnp.where(is_long, offset // slice_len, index // SHORT_LEN).astype(jnp.int32)
    relative = jnp.where(
        is_long, device * slice_len + offset % slice_len, index % SHORT_LEN
    ).astype(jnp.int32)
    return (doc_ids, relative)


def rotary_tables(relative):
    half_dim = HEAD_DIM // 2
    frequency = jnp.exp(
        -math.log(10000.0) * (2.0 * jnp.arange(half_dim, dtype=jnp.float32) / HEAD_DIM)
    )
    angles = relative.astype(jnp.float32)[:, None] * frequency[None, :]
    return (jnp.cos(angles)[:, None, :], jnp.sin(angles)[:, None, :])


def rotate(values, cosine, sine_table):
    half_dim = values.shape[-1] // 2
    lower_half = values[..., :half_dim]
    upper_half = values[..., half_dim:]
    return jnp.concatenate(
        [
            lower_half * cosine - upper_half * sine_table,
            upper_half * cosine + lower_half * sine_table,
        ],
        axis=-1,
    )


def allowed_mask(query_places, key_places, info):
    query_docs, query_rel = token_layout(query_places, info)
    key_docs, key_rel = token_layout(key_places, info)
    return (key_docs[None, :] == query_docs[:, None]) & (key_rel[None, :] <= query_rel[:, None])


def online_block(current, query_b, key_block, value_block, query_places, key_places, info):
    running, denominator, weighted = current
    key_count = key_block.shape[0]
    allowed = allowed_mask(query_places, key_places, info)
    key_heads = key_block.reshape(key_count, HEADS, HEAD_DIM)
    scores = jnp.einsum(
        "qhd,khd->hqk", query_b, key_heads, preferred_element_type=jnp.float32
    ) * HEAD_DIM ** (-0.5)
    scores = jnp.where(allowed[None], scores, masked)
    new_max = jnp.maximum(running, jnp.max(scores, axis=-1))
    exp_scores = jnp.where(allowed[None], jnp.exp(scores - new_max[..., None]), 0.0)
    rescale = jnp.exp(running - new_max)
    denominator = denominator * rescale + jnp.sum(exp_scores, axis=-1)
    value_heads = value_block.reshape(key_count, HEADS, HEAD_DIM)
    weighted = weighted * rescale[..., None] + jnp.einsum(
        "hqk,khd->hqd",
        exp_scores.astype(jnp.bfloat16),
        value_heads,
        preferred_element_type=jnp.float32,
    )
    return (new_max, denominator, weighted)


def attend_rows(current, query_b, key_rows, value_rows, first_row, query_places, info, last_place):
    key_count = key_rows.shape[0]
    block_rows = block_size(key_count)

    def one_block(carried, block_index):
        start_place = first_row + block_index * block_rows
        key_block = lax.dynamic_slice_in_dim(key_rows, block_index * block_rows, block_rows, 0)
        value_block = lax.dynamic_slice_in_dim(value_rows, block_index * block_rows, block_rows, 0)
        key_places = start_place + jnp.arange(block_rows, dtype=jnp.int32)

        def one_compute(state_in):
            return online_block(
                state_in, query_b, key_block, value_block, query_places, key_places, info
            )

        def unchanged(state_in):
            return state_in

        return (lax.cond(start_place > last_place, unchanged, one_compute, carried), None)

    result, unused = lax.scan(
        one_block, current, jnp.arange(key_count // block_rows, dtype=jnp.int32)
    )
    return result


def block_probs(query_b, key_b, query_places, key_places, info, lse_rows):
    allowed = allowed_mask(query_places, key_places, info)
    scores = jnp.einsum(
        "qhd,khd->hqk", query_b, key_b, preferred_element_type=jnp.float32
    ) * HEAD_DIM ** (-0.5)
    return jnp.exp(jnp.where(allowed[None], scores - lse_rows[..., None], masked))


def block_dscores(probabilities, grad_b, value_b, delta_rows):
    dprobs = jnp.einsum("qhd,khd->hqk", grad_b, value_b, preferred_element_type=jnp.float32)
    return (probabilities * (dprobs - delta_rows[..., None])).astype(jnp.bfloat16)


def shards(
    inputs,
    history,
    seq_lengths,
    attn_gain,
    attn_shift,
    qkv_weight,
    qkv_bias,
    out_weight,
    out_bias,
    mlp_gain,
    mlp_shift,
    up_weight,
    up_bias,
    down_weight,
    down_bias,
    mix_weights,
    cotangent,
):
    group_count = inputs.shape[0]
    tok_count = inputs.shape[1]
    model_width = inputs.shape[2]
    seq_count = lax.axis_size("seq")
    group_rows = tok_count * seq_count
    slice_len = LONG_LEN // seq_count
    factor = HEAD_DIM ** (-0.5)
    seq_index = lax.axis_index("seq")
    first_place = seq_index * tok_count
    last_place = first_place + tok_count - 1
    places = first_place + jnp.arange(tok_count, dtype=jnp.int32)
    gathered = (
        lax.all_gather(attn_gain, ("seq", "batch"), axis=0, tiled=True),
        lax.all_gather(attn_shift, ("seq", "batch"), axis=0, tiled=True),
        lax.all_gather(qkv_weight, ("seq", "batch"), axis=0, tiled=True),
        lax.all_gather(qkv_bias, ("seq", "batch"), axis=0, tiled=True),
        lax.all_gather(out_weight, ("seq", "batch"), axis=0, tiled=True),
        lax.all_gather(out_bias, ("seq", "batch"), axis=0, tiled=True),
        lax.all_gather(mlp_gain, ("seq", "batch"), axis=0, tiled=True),
        lax.all_gather(mlp_shift, ("seq", "batch"), axis=0, tiled=True),
        lax.all_gather(up_weight, ("seq", "batch"), axis=0, tiled=True),
        lax.all_gather(up_bias, ("seq", "batch"), axis=0, tiled=True),
        lax.all_gather(down_weight, ("seq", "batch"), axis=0, tiled=True),
        lax.all_gather(down_bias, ("seq", "batch"), axis=0, tiled=True),
    )
    (
        gain_one,
        shift_one,
        qkv_full,
        qkv_vec,
        out_full,
        out_vec,
        gain_two,
        shift_two,
        up_full,
        up_vec,
        down_full,
        down_vec,
    ) = gathered
    saved = []
    block_outs = []
    for group in range(group_count):
        info = (seq_lengths[group], tok_count, slice_len)
        doc_ids, relative = token_layout(places, info)
        cosine, sine_table = rotary_tables(relative)
        residual_in = inputs[group].astype(jnp.float32)
        normed_out, normed_one, inverse_one = layer_norm(
            residual_in, gain_one.astype(jnp.float32), shift_one.astype(jnp.float32)
        )
        acts_one = normed_out.astype(jnp.bfloat16)
        projected = jnp.dot(
            acts_one, qkv_full, preferred_element_type=jnp.float32
        ) + qkv_vec.astype(jnp.float32)
        queries = rotate(
            projected[:, :model_width].reshape(tok_count, HEADS, HEAD_DIM), cosine, sine_table
        ).astype(jnp.bfloat16)
        key_flat = (
            rotate(
                projected[:, model_width : 2 * model_width].reshape(tok_count, HEADS, HEAD_DIM),
                cosine,
                sine_table,
            )
            .reshape(tok_count, model_width)
            .astype(jnp.bfloat16)
        )
        value_flat = projected[:, 2 * model_width :].astype(jnp.bfloat16)
        start_state = (
            jnp.full((HEADS, tok_count), masked, jnp.float32),
            jnp.zeros((HEADS, tok_count), jnp.float32),
            jnp.zeros((HEADS, tok_count, HEAD_DIM), jnp.float32),
        )
        key_all = None
        value_all = None
        running, denominator, weighted = attend_rows(
            start_state,
            queries,
            lax.all_gather(key_flat, "seq", axis=0, tiled=True),
            lax.all_gather(value_flat, "seq", axis=0, tiled=True),
            jnp.int32(0),
            places,
            info,
            last_place,
        )
        attended = jnp.transpose(weighted / denominator[..., None], (1, 0, 2))
        lse_rows = running + jnp.log(denominator)
        attended_b = attended.reshape(tok_count, model_width).astype(jnp.bfloat16)
        middle = (
            residual_in
            + jnp.dot(attended_b, out_full, preferred_element_type=jnp.float32)
            + out_vec.astype(jnp.float32)
        )
        normed_out_two, normed_two, inverse_two = layer_norm(
            middle, gain_two.astype(jnp.float32), shift_two.astype(jnp.float32)
        )
        acts_two = normed_out_two.astype(jnp.bfloat16)
        upward = jnp.dot(acts_two, up_full, preferred_element_type=jnp.float32) + up_vec.astype(
            jnp.float32
        )
        activated, gelu_back = jax.vjp(exact_gelu, upward)
        activated_b = activated.astype(jnp.bfloat16)
        block_out = (
            middle
            + jnp.dot(activated_b, down_full, preferred_element_type=jnp.float32)
            + down_vec.astype(jnp.float32)
        )
        block_outs.append(block_out)
        saved.append(
            (
                info,
                cosine,
                sine_table,
                normed_one,
                inverse_one,
                acts_one,
                queries,
                key_flat,
                value_flat,
                key_all,
                value_all,
                attended,
                lse_rows,
                attended_b,
                normed_two,
                inverse_two,
                acts_two,
                gelu_back,
                activated_b,
            )
        )
    block_stack = jnp.stack(block_outs, axis=0)
    earlier = history.astype(jnp.float32)
    grad_out_all = cotangent.astype(jnp.float32)
    mixed_out = (
        jnp.sum(mix_weights[:-1, None, None, None] * earlier, axis=0)
        + mix_weights[-1] * block_stack
    )
    mix_terms = jnp.concatenate(
        [
            jnp.sum(earlier * grad_out_all[None], axis=(1, 2, 3)),
            jnp.sum(block_stack * grad_out_all)[None],
        ]
    )
    grad_history = (mix_weights[:-1, None, None, None] * grad_out_all[None]).astype(jnp.bfloat16)
    back_gain_one, back_qkv, back_out, back_gain_two, back_up, back_down = (
        lax.all_gather(attn_gain, ("seq", "batch"), axis=0, tiled=True),
        lax.all_gather(qkv_weight, ("seq", "batch"), axis=0, tiled=True),
        lax.all_gather(out_weight, ("seq", "batch"), axis=0, tiled=True),
        lax.all_gather(mlp_gain, ("seq", "batch"), axis=0, tiled=True),
        lax.all_gather(up_weight, ("seq", "batch"), axis=0, tiled=True),
        lax.all_gather(down_weight, ("seq", "batch"), axis=0, tiled=True),
    )
    totals = None
    grad_input_list = []
    for group in range(group_count):
        (
            info,
            cosine,
            sine_table,
            normed_one,
            inverse_one,
            acts_one,
            queries,
            key_flat,
            value_flat,
            key_all,
            value_all,
            attended,
            lse_rows,
            attended_b,
            normed_two,
            inverse_two,
            acts_two,
            gelu_back,
            activated_b,
        ) = saved[group]
        grad_block = mix_weights[-1] * grad_out_all[group]
        down_grad_b = grad_block.astype(jnp.bfloat16)
        grad_w_down = jnp.einsum(
            "tf,td->fd", activated_b, down_grad_b, preferred_element_type=jnp.float32
        )
        grad_b_down = jnp.sum(down_grad_b.astype(jnp.float32), axis=0)
        grad_act = jnp.einsum(
            "td,fd->tf", down_grad_b, back_down, preferred_element_type=jnp.float32
        )
        up_grad_b = gelu_back(grad_act)[0].astype(jnp.bfloat16)
        grad_w_up = jnp.einsum("td,tf->df", acts_two, up_grad_b, preferred_element_type=jnp.float32)
        grad_b_up = jnp.sum(up_grad_b.astype(jnp.float32), axis=0)
        grad_acts_two = jnp.einsum(
            "tf,df->td", up_grad_b, back_up, preferred_element_type=jnp.float32
        )
        grad_middle_norm, grad_gain_two, grad_shift_two = norm_back(
            grad_acts_two, normed_two, inverse_two, back_gain_two.astype(jnp.float32)
        )
        grad_middle = grad_block + grad_middle_norm
        attn_grad_b = grad_middle.astype(jnp.bfloat16)
        grad_w_out = jnp.einsum(
            "te,td->ed", attended_b, attn_grad_b, preferred_element_type=jnp.float32
        )
        grad_b_out = jnp.sum(attn_grad_b.astype(jnp.float32), axis=0)
        grad_heads = (
            jnp.einsum("td,ed->te", attn_grad_b, back_out, preferred_element_type=jnp.float32)
            .astype(jnp.bfloat16)
            .reshape(tok_count, HEADS, HEAD_DIM)
        )
        delta_rows = jnp.transpose(jnp.sum(grad_heads.astype(jnp.float32) * attended, axis=-1))
        key_all, value_all = (
            lax.all_gather(key_flat, "seq", axis=0, tiled=True),
            lax.all_gather(value_flat, "seq", axis=0, tiled=True),
        )
        key_block_rows = block_size(group_rows)

        def query_grad_block(carried, block_index):
            start_place = block_index * key_block_rows
            key_block = lax.dynamic_slice_in_dim(key_all, start_place, key_block_rows, 0).reshape(
                key_block_rows, HEADS, HEAD_DIM
            )
            value_block = lax.dynamic_slice_in_dim(
                value_all, start_place, key_block_rows, 0
            ).reshape(key_block_rows, HEADS, HEAD_DIM)
            key_places = start_place + jnp.arange(key_block_rows, dtype=jnp.int32)

            def query_compute(summed):
                probabilities = block_probs(queries, key_block, places, key_places, info, lse_rows)
                dscores = block_dscores(probabilities, grad_heads, value_block, delta_rows)
                return (
                    summed
                    + jnp.einsum(
                        "hqk,khd->qhd", dscores, key_block, preferred_element_type=jnp.float32
                    )
                    * factor
                )

            return (
                lax.cond(start_place > last_place, lambda summed: summed, query_compute, carried),
                None,
            )

        grad_queries, unused = lax.scan(
            query_grad_block,
            jnp.zeros((tok_count, HEADS, HEAD_DIM), jnp.float32),
            jnp.arange(group_rows // key_block_rows, dtype=jnp.int32),
        )
        key_first_row = jnp.int32(0)
        key_rows = key_all
        value_rows = value_all
        inner_rows = block_size(lax.axis_size("seq") * tok_count)

        def key_grad_block(carried, block_index):
            offset = block_index * inner_rows
            start_place = key_first_row + offset
            key_block = lax.dynamic_slice_in_dim(key_rows, offset, inner_rows, 0).reshape(
                inner_rows, HEADS, HEAD_DIM
            )
            value_block = lax.dynamic_slice_in_dim(value_rows, offset, inner_rows, 0).reshape(
                inner_rows, HEADS, HEAD_DIM
            )
            key_places = start_place + jnp.arange(inner_rows, dtype=jnp.int32)

            def key_compute(unused_in):
                probabilities = block_probs(queries, key_block, places, key_places, info, lse_rows)
                dscores = block_dscores(probabilities, grad_heads, value_block, delta_rows)
                grad_keys = (
                    jnp.einsum("hqk,qhd->khd", dscores, queries, preferred_element_type=jnp.float32)
                    * factor
                )
                grad_values = jnp.einsum(
                    "hqk,qhd->khd",
                    probabilities.astype(jnp.bfloat16),
                    grad_heads,
                    preferred_element_type=jnp.float32,
                )
                return jnp.concatenate(
                    [
                        grad_keys.reshape(inner_rows, model_width),
                        grad_values.reshape(inner_rows, model_width),
                    ],
                    axis=1,
                )

            def nothing(unused_in):
                return jnp.zeros((inner_rows, 2 * model_width), jnp.float32)

            return (carried, lax.cond(start_place > last_place, nothing, key_compute, carried))

        unused_out, blocks = lax.scan(
            key_grad_block,
            jnp.int32(0),
            jnp.arange(lax.axis_size("seq") * tok_count // inner_rows, dtype=jnp.int32),
        )
        key_grads = lax.psum_scatter(
            blocks.reshape(lax.axis_size("seq") * tok_count, 2 * model_width).astype(jnp.bfloat16),
            "seq",
            scatter_dimension=0,
            tiled=True,
        ).astype(jnp.float32)
        grad_keys_own = key_grads[:, :model_width]
        grad_values_own = key_grads[:, model_width:]
        grad_q_turned = rotate(grad_queries, cosine, -sine_table).reshape(tok_count, model_width)
        grad_k_turned = rotate(
            grad_keys_own.reshape(tok_count, HEADS, HEAD_DIM), cosine, -sine_table
        ).reshape(tok_count, model_width)
        qkv_grad_b = jnp.concatenate(
            [grad_q_turned, grad_k_turned, grad_values_own], axis=1
        ).astype(jnp.bfloat16)
        grad_w_qkv = jnp.einsum(
            "td,te->de", acts_one, qkv_grad_b, preferred_element_type=jnp.float32
        )
        grad_b_qkv = jnp.sum(qkv_grad_b.astype(jnp.float32), axis=0)
        grad_acts_one = jnp.einsum(
            "te,de->td", qkv_grad_b, back_qkv, preferred_element_type=jnp.float32
        )
        grad_in_norm, grad_gain_one, grad_shift_one = norm_back(
            grad_acts_one, normed_one, inverse_one, back_gain_one.astype(jnp.float32)
        )
        grad_input_list.append((grad_middle + grad_in_norm).astype(jnp.bfloat16))
        terms = [
            grad_gain_one,
            grad_shift_one,
            grad_w_qkv,
            grad_b_qkv,
            grad_w_out,
            grad_b_out,
            grad_gain_two,
            grad_shift_two,
            grad_w_up,
            grad_b_up,
            grad_w_down,
            grad_b_down,
        ]
        if totals is None:
            totals = terms
        else:
            totals = [older + newer for older, newer in zip(totals, terms)]
    shares = (
        lax.psum_scatter(totals[0], ("seq", "batch"), scatter_dimension=0, tiled=True),
        lax.psum_scatter(totals[1], ("seq", "batch"), scatter_dimension=0, tiled=True),
        lax.psum_scatter(totals[2], ("seq", "batch"), scatter_dimension=0, tiled=True),
        lax.psum_scatter(totals[3], ("seq", "batch"), scatter_dimension=0, tiled=True),
        lax.psum_scatter(totals[4], ("seq", "batch"), scatter_dimension=0, tiled=True),
        lax.psum_scatter(totals[5], ("seq", "batch"), scatter_dimension=0, tiled=True),
        lax.psum_scatter(totals[6], ("seq", "batch"), scatter_dimension=0, tiled=True),
        lax.psum_scatter(totals[7], ("seq", "batch"), scatter_dimension=0, tiled=True),
        lax.psum_scatter(totals[8], ("seq", "batch"), scatter_dimension=0, tiled=True),
        lax.psum_scatter(totals[9], ("seq", "batch"), scatter_dimension=0, tiled=True),
        lax.psum_scatter(totals[10], ("seq", "batch"), scatter_dimension=0, tiled=True),
        lax.psum_scatter(totals[11], ("seq", "batch"), scatter_dimension=0, tiled=True),
    )
    grad_mix = lax.psum(mix_terms, ("seq", "batch"))
    grad_inputs = jnp.stack(grad_input_list, axis=0)
    return (
        mixed_out.astype(jnp.bfloat16),
        grad_inputs,
        grad_history,
        shares[0],
        shares[1],
        shares[2],
        shares[3],
        shares[4],
        shares[5],
        shares[6],
        shares[7],
        shares[8],
        shares[9],
        shares[10],
        shares[11],
        grad_mix,
    )


def placed(mesh, body):
    return jax.shard_map(
        body,
        mesh=mesh,
        in_specs=(
            P("batch", "seq", None),
            P(None, "batch", "seq", None),
            P("batch"),
            P(("seq", "batch")),
            P(("seq", "batch")),
            P(("seq", "batch"), None),
            P(("seq", "batch")),
            P(("seq", "batch"), None),
            P(("seq", "batch")),
            P(("seq", "batch")),
            P(("seq", "batch")),
            P(("seq", "batch"), None),
            P(("seq", "batch")),
            P(("seq", "batch"), None),
            P(("seq", "batch")),
            P(),
            P("batch", "seq", None),
        ),
        out_specs=(
            P("batch", "seq", None),
            P("batch", "seq", None),
            P(None, "batch", "seq", None),
            P(("seq", "batch")),
            P(("seq", "batch")),
            P(("seq", "batch"), None),
            P(("seq", "batch")),
            P(("seq", "batch"), None),
            P(("seq", "batch")),
            P(("seq", "batch")),
            P(("seq", "batch")),
            P(("seq", "batch"), None),
            P(("seq", "batch")),
            P(("seq", "batch"), None),
            P(("seq", "batch")),
            P(),
        ),
        check_vma=False,
    )

MESH = pl.DeviceIdType.MESH
BF, F32 = jnp.bfloat16, jnp.float32


def where_am_i():
    seq, batch = lax.axis_index("seq"), lax.axis_index("batch")
    return seq // 2, seq % 2, batch // 2, batch % 2


def dev(z, y, x, k):
    return (z * 2 + y, x * 2 + k)


def remote(src, dst, ssem, rsem, device):
    return pltpu.make_async_remote_copy(src_ref=src, dst_ref=dst, send_sem=ssem, recv_sem=rsem,
                                        device_id=device, device_id_type=MESH)


def greet(z, y, x, k):
    barrier = pltpu.get_barrier_semaphore()
    mine = (z * 2 + y) * 2 + k
    for step in range(1, 16):
        other = lax.rem(mine + step, 16)
        pl.semaphore_signal(barrier, inc=1, device_id=dev(other // 4, (other // 2) % 2, x, other % 2), device_id_type=MESH)
    pl.semaphore_signal(barrier, inc=1, device_id=dev(z, y, 1 - x, k), device_id_type=MESH)
    pl.semaphore_wait(barrier, 16)


class Gather:
    def __init__(self, part, send, recv, pos):
        self.part, self.send, self.recv, self.pos = part, send, recv, pos
        z, y, x, k = pos
        self.c = []
        p2 = jnp.where(k == 0, 1 - y, y), jnp.where(k == 0, x, 1 - x)
        p3 = jnp.where(k == 0, y, 1 - y), jnp.where(k == 0, 1 - x, x)
        d4 = 1 - y, 1 - x
        own = (y, x)
        zed = lambda i: part((slice(z, z + 1) if False else pl.ds(z, 1)), y, x, k)
        allz = lambda yx: part(slice(None), yx[0], yx[1], k)
        def cp(n, ref, device):
            return remote(ref, ref, send.at[n], recv.at[n], device)
        self.zs = [cp(d - 1, zed(0), dev(lax.rem(z + d, 4), y, x, k)) for d in (1, 2, 3)]
        self.a2 = cp(3, allz(own), dev(z, *p2, k))
        self.a3 = cp(4, allz(own), dev(z, *p3, k))
        self.b3 = cp(5, allz(p2), dev(z, *p3, k))
        sib = dev(z, y, x, 1 - k)
        self.s1 = cp(6, allz(own), sib)
        self.s2 = cp(7, allz(p2), sib)
        self.s3 = cp(8, allz(p3), sib)
        self.s4 = cp(9, allz(d4), sib)

    def stage(self, n):
        if n == 0:
            for c in self.zs: c.start()
        elif n == 1:
            for c in self.zs: c.wait_recv()
            self.a2.start(); self.a3.start(); self.s1.start()
        elif n == 2:
            self.a2.wait_recv()
            self.b3.start(); self.s2.start()
        elif n == 3:
            self.a3.wait_recv()
            self.s3.start()
        elif n == 4:
            self.b3.wait_recv()
            self.s4.start()
        elif n == 5:
            for c in (self.s1, self.s2, self.s3, self.s4): c.wait_recv()
            for c in self.zs + [self.a2, self.a3, self.b3, self.s1, self.s2, self.s3, self.s4]: c.wait_send()
    STAGES = 6


def gather_kernel(cols, qkv, out, up, down, vec, xin, cin,
                  QKV, OUT, UP, DOWN, VEC, XM, XA, CM, CA,
                  f_own, f_sib, block, psend, precv, lsem, gsend, grecv, asend, arecv, aarecv, fsend, frecv):
    pos = z, y, x, k = where_am_i()
    greet(z, y, x, k)
    at = 0
    tot = sum(cols)
    offs = []
    for n, ref in zip(cols, (qkv, out, up)):
        half = n // 2
        f_own[0, :, at:at + half] = ref[:, :half].astype(F32)
        f_own[1, :, at:at + half] = ref[:, half:].astype(F32)
        offs.append((at, half))
        at += half
    pre = remote(f_own.at[1 - k], f_sib, psend, precv, dev(z, y, x, 1 - k))
    pre.start()
    s = 2 * z + y
    own_s = lax.rem(y + z, 2)
    acps = []
    for a, (src, M, A) in enumerate(((xin, XM, XA), (cin, CM, CA))):
        for i in range(2):
            g = 2 * k + i
            lo = src.at[i, pl.ds(pl.multiple_of(y * 128, 128), 128)]
            hi = src.at[i, pl.ds(pl.multiple_of((1 - y) * 128, 128), 128)]
            for n, (ref, dst, rs, d) in enumerate((
                (lo, M.at[s], arecv.at[a, s], (g, y, x, own_s)),
                (hi, M.at[s], arecv.at[a, s], (g, 1 - y, x, own_s)),
                (hi, A.at[z], aarecv.at[a, z], (g, y, x, 1 - own_s)))):
                ss = asend.at[a, i, n]
                me = (g == z) & (d[1] == y) & (d[3] == k)
                cp = remote(ref, dst, ss, rs, dev(*d))
                @pl.when(me)
                def _():
                    pltpu.make_async_copy(ref, dst, rs).start()
                @pl.when(jnp.logical_not(me))
                def _():
                    cp.start()
                acps.append((cp, me))
    pre.wait_recv()
    lcs = []
    for i, ((at, half), W) in enumerate(zip(offs, (QKV, OUT, UP))):
        mine = f_own[k, :, at:at + half]
        theirs = f_sib[:, at:at + half]
        first = jnp.where(k == 0, mine, theirs)
        second = jnp.where(k == 0, theirs, mine)
        block[:, at:at + half] = jnp.concatenate([first, second], axis=0).astype(BF)
        c = pltpu.make_async_copy(block.at[:, at:at + half],
                                  W.at[z, y, x, :, pl.ds(pl.multiple_of(k * half, 128), half)], lsem.at[i])
        c.start(); lcs.append(c)
    for i, (ref, W) in enumerate(((down, DOWN), (vec, VEC))):
        c = pltpu.make_async_copy(ref, W.at[z, y, x, k], lsem.at[3 + i])
        c.start(); lcs.append(c)
    def colpart(W, half):
        return lambda zz, yy, xx, kk: W.at[zz, yy, xx, :, pl.ds(pl.multiple_of(kk * half, 128), half)]
    def rowpart(W):
        return lambda zz, yy, xx, kk: W.at[zz, yy, xx, kk]
    parts = [rowpart(VEC), colpart(QKV, offs[0][1]), colpart(OUT, offs[1][1]), colpart(UP, offs[2][1]), rowpart(DOWN)]
    for c in lcs: c.wait()
    gs = [Gather(p, gsend.at[i], grecv.at[i], pos) for i, p in enumerate(parts)]
    fw = []
    def tokens_forward():
        for zz in range(4):
            j = 2 * zz + lax.rem(zz + k, 2)
            cp = remote(XM.at[j], XM.at[j], fsend.at[zz], frecv.at[zz], dev(z, y, x, 1 - k))
            remote(XM.at[j], XM.at[j], fsend.at[zz], arecv.at[0, j], dev(z, y, x, 1 - k)).wait_recv()
            cp.start(); fw.append(cp)
        for e in range(2):
            zz = lax.rem(1 - y + k, 2) + 2 * e
            cp = remote(XA.at[zz], XA.at[zz], fsend.at[4 + e], frecv.at[4 + e], dev(z, y, x, 1 - k))
            remote(XA.at[zz], XA.at[zz], fsend.at[4 + e], aarecv.at[0, zz], dev(z, y, x, 1 - k)).wait_recv()
            cp.start(); fw.append(cp)
    for tick in range(len(gs) + Gather.STAGES - 1):
        for i, g in enumerate(gs):
            n = tick - i
            if 0 <= n < Gather.STAGES:
                g.stage(n)
        if tick == 2:
            tokens_forward()
    for zz in range(4):
        j = 2 * zz + lax.rem(zz + k, 2)
        remote(CM.at[j], CM.at[j], fsend.at[zz], arecv.at[1, j], dev(z, y, x, 1 - k)).wait_recv()
    for e in range(2):
        zz = lax.rem(1 - y + k, 2) + 2 * e
        remote(CA.at[zz], CA.at[zz], fsend.at[4 + e], aarecv.at[1, zz], dev(z, y, x, 1 - k)).wait_recv()
    for c in fw: c.wait()
    for cp, me in acps:
        @pl.when(jnp.logical_not(me))
        def _():
            cp.wait_send()
    pre.wait_send()


def gather_call(qkv, out, up, down, vec, xin, cin):
    D = xin.shape[-1]
    cols = (qkv.shape[1], out.shape[1], up.shape[1])
    H = sum(cols) // 2
    sd = jax.ShapeDtypeStruct
    outs = [sd((4, 2, 2, 48, n), BF) for n in cols] + [sd((4, 2, 2, 2) + down.shape, BF), sd((4, 2, 2, 2) + vec.shape, F32),
            sd((8, 128, D), BF), sd((4, 128, D), BF), sd((8, 128, D), BF), sd((4, 128, D), BF)]
    V, A = pl.BlockSpec(memory_space=pltpu.VMEM), pl.BlockSpec(memory_space=pl.ANY)
    S = pltpu.SemaphoreType.DMA
    return pl.pallas_call(
        functools.partial(gather_kernel, cols),
        out_shape=outs,
        in_specs=[V, V, V, A, A, A, A],
        out_specs=[A] * 9,
        scratch_shapes=[pltpu.VMEM((2, 24, H), F32), pltpu.VMEM((24, H), F32), pltpu.VMEM((48, H), BF),
                        S, S, S((5,)), S((5, 10)), S((5, 10)), S((2, 2, 3)), S((2, 8)), S((2, 4)), S((6,)), S((6,))],
        compiler_params=pltpu.CompilerParams(collective_id=0, has_side_effects=True, vmem_limit_bytes=32 * 2**20),
    )(qkv, out, up, down, vec, xin, cin)

EPS = 1e-5
NT = (((1,), (1,)), ((), ()))


def nt(a, b):
    return lax.dot_general(a, b, NT, preferred_element_type=F32)


def nn(a, b):
    return jnp.dot(a, b, preferred_element_type=F32)


def rope_tables():
    freq = np.exp(-math.log(10000.0) * (2.0 * np.arange(32, dtype=np.float32) / 64)).astype(np.float32)
    ang = np.arange(1024, dtype=np.float32)[:, None] * freq[None, :]
    c, s = np.cos(ang.astype(np.float64)), np.sin(ang.astype(np.float64))
    return (np.concatenate([c, c, c, c], 1).astype(np.float32), np.concatenate([-s, s, -s, s], 1).astype(np.float32))


def swap(u):
    low = lax.broadcasted_iota(jnp.int32, u.shape, 1) % 64 < 32
    return jnp.where(low, pltpu.roll(u, 96, 1), pltpu.roll(u, 32, 1))


def norm(v):
    mean = jnp.mean(v, axis=-1, keepdims=True)
    cen = v - mean
    inv = lax.rsqrt(jnp.mean(cen * cen, axis=-1, keepdims=True) + EPS)
    return cen * inv, inv


def norm_grad(e, n, inv, gain):
    g = e * gain
    return inv * (g - jnp.mean(g, axis=-1, keepdims=True) - n * jnp.mean(g * n, axis=-1, keepdims=True))


def own_block(i, k):
    return 2 * i + lax.rem(i + k, 2)


def rows(i, n=128):
    return pl.ds(pl.multiple_of(i * n, n), n)


def spread(p):
    low = lax.broadcasted_iota(jnp.int32, p.shape, 1) < 64
    zero = jnp.zeros_like(p)
    return jnp.concatenate([jnp.where(low, p, zero), jnp.where(low, zero, p)], axis=0)


def pick(o):
    low = lax.broadcasted_iota(jnp.int32, (128, 128), 0) < 64
    return jnp.where(low, o[:, :128], o[:, 128:]).T


def fill_bias(bias, is_long, k):
    at = 0
    for i in range(4):
        kk = 256 * (i + 1)
        key = lax.broadcasted_iota(jnp.int32, (kk, 256), 0)
        q = own_block(i, k) * 128 + lax.broadcasted_iota(jnp.int32, (kk, 256), 1) % 128
        first = jnp.where(is_long, 0, q - q % 256)
        bias[at:at + kk, :] = jnp.where((key <= q) & (key >= first), 0.0, -1e30)
        at += kk


def attn_fwd(flag, XM, XA, wqkv, wout, gain, shift, bqkv, bout, COS, SIN,
             acts, Q, K, V, att, lse, middle, bias, VT):
    z, y, x, k = where_am_i()
    is_long = flag[0] != 0
    fill_bias(bias, is_long, k)
    for j in range(8):
        alt = jnp.logical_and(jnp.logical_not(is_long), lax.rem(jnp.int32(j), 2) != y)
        blk = jnp.where(alt, XA[j // 2], XM[j]).astype(F32)
        n, _ = norm(blk)
        acts[j * 128:(j + 1) * 128, :] = (n * gain[...] + shift[...]).astype(BF)

    def tables(j):
        off = jnp.where(is_long, j, lax.rem(j, 2))
        return COS[rows(off), :], SIN[rows(off), :]

    @pl.loop(0, 8)
    def _(j):
        a = acts[rows(j), :]
        c, s = tables(j)
        for t in range(6):
            u = nn(a, wqkv[:, 768 + t * 128:896 + t * 128]) + bqkv[:, 768 + t * 128:896 + t * 128]
            K[rows(j), t * 128:(t + 1) * 128] = (u * c + swap(u) * s).astype(BF)
        V[rows(j), :] = (nn(a, wqkv[:, 1536:]) + bqkv[:, 1536:]).astype(BF)

    @pl.loop(0, 4)
    def _(i):
        j = own_block(i, k)
        a = acts[rows(j), :]
        c, s = tables(j)
        for t in range(6):
            u = nn(a, wqkv[:, t * 128:(t + 1) * 128]) + bqkv[:, t * 128:(t + 1) * 128]
            Q[rows(i), t * 128:(t + 1) * 128] = (u * c + swap(u) * s).astype(BF) * jnp.asarray(0.125, BF)

    @pl.loop(0, 6)
    def _(h):
        lanes = rows(h)
        VT[...] = V[:, lanes].T
        at = 0
        for i in range(4):
            kk = 256 * (i + 1)
            qb = spread(Q[i * 128:(i + 1) * 128, lanes])
            st = nt(K[0:kk, lanes], qb) + bias[at:at + kk, :]
            top = jnp.max(st, axis=0, keepdims=True)
            p = jnp.exp(st - top)
            den = jnp.sum(p, axis=0, keepdims=True)
            o = nn(VT[:, 0:kk], p.astype(BF)) * (1.0 / den)
            att[i * 128:(i + 1) * 128, lanes] = pick(o)
            lse[h, i:i + 1, :] = top + jnp.log(den)
            at += kk

    @pl.loop(0, 4)
    def _(i):
        j = own_block(i, k)
        alt = jnp.logical_and(jnp.logical_not(is_long), lax.rem(j, 2) != y)
        xb = jnp.where(alt, XA[i], XM[j]).astype(F32)
        middle[rows(i), :] = xb + (nn(att[rows(i), :].astype(BF), wout[...]) + bout[...])


def mlp(CH, flag, mix, middle, CM, CA, wup, wdown, gain, shift, bup, bdown,
        block, gmid, gup, gdown, g_gain, g_shift, g_bup, g_bdown, mixsum, acts2, actsT, dg, ga, cf):
    z, y, x, k = where_am_i()
    is_long = flag[0] != 0
    m5 = mix[5]
    for i in range(4):
        r = slice(i * 128, (i + 1) * 128)
        mid = middle[r, :]
        n, _ = norm(mid)
        acts2[r, :] = (n * gain[...] + shift[...]).astype(BF)
        j = own_block(jnp.int32(i), k)
        alt = jnp.logical_and(jnp.logical_not(is_long), lax.rem(j, 2) != y)
        c = jnp.where(alt, CA[i], CM[j]).astype(F32)
        cf[r, :] = c
        dg[r, :] = (m5 * c).astype(BF)
        block[r, :] = mid + bdown[...]
        ga[r, :] = jnp.zeros_like(mid)
        actsT[:, r] = acts2[r, :].T
    g_bdown[...] = jnp.sum(dg[...].astype(F32), axis=0, keepdims=True)

    @pl.loop(0, wup.shape[1] // CH)
    def _(f):
        cols = rows(f, CH)
        up = nn(acts2[...], wup[:, cols]) + bup[:, cols]
        half_erf = 0.5 * lax.erf(up * (2.0 ** -0.5)) + 0.5
        slope = half_erf + up * (jnp.exp(up * up * -0.5) * (1.0 / math.sqrt(2 * math.pi)))
        act = (up * half_erf).astype(BF)
        block[...] += nn(act, wdown[cols, :])
        upg = (nt(dg[...], wdown[cols, :]) * slope).astype(BF)
        g_bup[:, cols] = jnp.sum(upg.astype(F32), axis=0, keepdims=True)
        gdown[cols, :] = nn(act.T, dg[...]).astype(BF)
        gup[:, cols] = nn(actsT[...], upg).astype(BF)
        ga[...] += nt(upg, wup[:, cols])

    total = jnp.zeros((1, 768), F32)
    gg = jnp.zeros((1, 768), F32)
    gs = jnp.zeros((1, 768), F32)
    for i in range(4):
        r = slice(i * 128, (i + 1) * 128)
        n, inv = norm(middle[r, :])
        e = ga[r, :]
        gg += jnp.sum(e * n, axis=0, keepdims=True)
        gs += jnp.sum(e, axis=0, keepdims=True)
        gmid[r, :] = m5 * cf[r, :] + norm_grad(e, n, inv, gain[...])
        total += jnp.sum(cf[r, :] * block[r, :], axis=0, keepdims=True)
    g_gain[...] = gg
    g_shift[...] = gs
    mixsum[...] = total


def attn_bwd(flag, gmid, acts, Q, K, V, att, lse, wqkv, wout, COS, SIN,
             e, gqkv, gout, g_bqkv, g_bout, bias, KT, da, dQ, dK, dV, agrad, actsT, actsqT, KG, VG):
    z, y, x, k = where_am_i()
    is_long = flag[0] != 0
    fill_bias(bias, is_long, k)
    agrad[...] = gmid[...].astype(BF)
    g_bout[...] = jnp.sum(agrad[...].astype(F32), axis=0, keepdims=True)

    @pl.loop(0, 4)
    def _(i):
        da[rows(i), :] = nt(agrad[rows(i), :], wout[...]).astype(BF)

    for t in range(6):
        aT = att[:, t * 128:(t + 1) * 128].T.astype(BF)
        gout[t * 128:(t + 1) * 128, :] = nn(aT, agrad[...]).astype(BF)
    dK[...] = jnp.zeros_like(dK)
    dV[...] = jnp.zeros_like(dV)

    @pl.loop(0, 6)
    def _(h):
        lanes = rows(h)
        KT[...] = K[:, lanes].T
        at = 0
        for i in range(4):
            kk = 256 * (i + 1)
            r = slice(i * 128, (i + 1) * 128)
            d = da[r, lanes]
            qb, db = spread(Q[r, lanes]), spread(d)
            prod = (d.astype(F32) * att[r, lanes]).T
            delta = jnp.concatenate([jnp.sum(prod[:64], axis=0, keepdims=True), jnp.sum(prod[64:], axis=0, keepdims=True)], axis=1)
            st = nt(K[0:kk, lanes], qb) + bias[at:at + kk, :]
            p = jnp.exp(st - lse[h, i:i + 1, :])
            ds = (p * (nt(V[0:kk, lanes], db) - delta)).astype(BF)
            dV[0:kk, lanes] += nn(p.astype(BF), db)
            dK[0:kk, lanes] += nn(ds, qb)
            dQ[r, lanes] = pick(nn(KT[:, 0:kk], ds)) * 0.125
            at += kk

    def tables(j):
        off = jnp.where(is_long, j, lax.rem(j, 2))
        return COS[rows(off), :], SIN[rows(off), :]

    for j in range(8):
        actsT[:, j * 128:(j + 1) * 128] = acts[j * 128:(j + 1) * 128, :].T
    for i in range(4):
        j = own_block(jnp.int32(i), k)
        actsqT[:, i * 128:(i + 1) * 128] = acts[rows(j), :].T
        c, s = tables(j)
        for t in range(6):
            u = dQ[i * 128:(i + 1) * 128, t * 128:(t + 1) * 128]
            da[i * 128:(i + 1) * 128, t * 128:(t + 1) * 128] = (u * c - swap(u) * s).astype(BF)

    @pl.loop(0, 8)
    def _(j):
        c, s = tables(j)
        for t in range(6):
            u = dK[rows(j), t * 128:(t + 1) * 128]
            KG[rows(j), t * 128:(t + 1) * 128] = (u * c - swap(u) * s).astype(BF)
        VG[rows(j), :] = dV[rows(j), :].astype(BF)
        e[rows(j), :] = nt(KG[rows(j), :], wqkv[:, 768:1536]) + nt(VG[rows(j), :], wqkv[:, 1536:])

    @pl.loop(0, 4)
    def _(i):
        j = own_block(i, k)
        e[rows(j), :] += nt(da[rows(i), :], wqkv[:, :768])

    g_bqkv[:, :768] = jnp.sum(da[...].astype(F32), axis=0, keepdims=True)
    g_bqkv[:, 768:1536] = jnp.sum(KG[...].astype(F32), axis=0, keepdims=True)
    g_bqkv[:, 1536:] = jnp.sum(VG[...].astype(F32), axis=0, keepdims=True)

    @pl.loop(0, 6)
    def _(t):
        gqkv[rows(t), :768] = nn(actsqT[rows(t), :], da[...]).astype(BF)
        gqkv[rows(t), 768:1536] = nn(actsT[rows(t), :], KG[...]).astype(BF)
        gqkv[rows(t), 1536:] = nn(actsT[rows(t), :], VG[...]).astype(BF)


sd = jax.ShapeDtypeStruct
VM = pltpu.VMEM
vs = pl.BlockSpec(memory_space=pltpu.VMEM)
ss = pl.BlockSpec(memory_space=pltpu.SMEM)
CP = pltpu.CompilerParams(vmem_limit_bytes=60 * 2**20)


def attn_fwd_call(flag, *ins):
    return pl.pallas_call(attn_fwd,
        out_shape=[sd((1024, 768), BF), sd((512, 768), BF), sd((1024, 768), BF), sd((1024, 768), BF),
                   sd((512, 768), F32), sd((6, 4, 256), F32), sd((512, 768), F32)],
        in_specs=[ss] + [vs] * len(ins), out_specs=[vs] * 7,
        scratch_shapes=[VM((2560, 256), F32), VM((128, 1024), BF)],
        compiler_params=CP)(flag, *ins)


def mlp_call(flag, mix, *ins):
    r = sd((1, 768), F32)
    return pl.pallas_call(functools.partial(mlp, 512),
        out_shape=[sd((512, 768), F32), sd((512, 768), F32), sd((768, 3072), BF), sd((3072, 768), BF), r, r, sd((1, 3072), F32), r, r],
        in_specs=[ss, ss] + [vs] * len(ins), out_specs=[vs] * 9,
        scratch_shapes=[VM((512, 768), BF), VM((768, 512), BF), VM((512, 768), BF), VM((512, 768), F32), VM((512, 768), F32)],
        compiler_params=CP)(flag, mix, *ins)


def attn_bwd_call(flag, *ins):
    return pl.pallas_call(attn_bwd,
        out_shape=[sd((1024, 768), F32), sd((768, 2304), BF), sd((768, 768), BF), sd((1, 2304), F32), sd((1, 768), F32)],
        in_specs=[ss] + [vs] * len(ins), out_specs=[vs] * 5,
        scratch_shapes=[VM((2560, 256), F32), VM((128, 1024), BF), VM((512, 768), BF), VM((512, 768), F32), VM((1024, 768), F32),
                        VM((1024, 768), F32), VM((512, 768), BF), VM((768, 1024), BF), VM((768, 512), BF), VM((1024, 768), BF), VM((1024, 768), BF)],
        compiler_params=CP)(flag, *ins)


VROWS = (24, 24, 72, 24, 24, 24, 96, 24)


def widen(vecs, row, n):
    v = vecs[:, row, :].astype(BF)
    wide = 32 * n
    j = lax.broadcasted_iota(jnp.int32, (128, wide), 1)
    i = lax.broadcasted_iota(jnp.int32, (128, wide), 0)
    q = jnp.floor((j.astype(F32) + 0.5) * (1.0 / n)).astype(jnp.int32)
    hot = jnp.where(j - q * n == i, 1.0, 0.0).astype(BF)
    full = nn(v, hot)
    d = lax.broadcasted_iota(jnp.int32, (32, wide), 0)
    return jnp.sum(jnp.where(q[:32] == d, full, 0.0), axis=0, keepdims=True)


def lane(tile, row, at):
    r = lax.broadcasted_iota(jnp.int32, tile.shape, 0)
    c = lax.broadcasted_iota(jnp.int32, tile.shape, 1)
    v = jnp.sum(jnp.where((r == row) & (c == at), tile, 0.0), axis=1, keepdims=True)
    return jnp.sum(v, axis=0, keepdims=True)


def longer(length, shape):
    return jnp.broadcast_to(length, shape) > 512.0


def bias_rows(bias, length, k):
    at = 0
    for i in range(4):
        kk = 256 * (i + 1)
        key = lax.broadcasted_iota(jnp.int32, (kk, 256), 0)
        q = own_block(i, k) * 128 + lax.broadcasted_iota(jnp.int32, (kk, 256), 1) % 128
        first = jnp.where(longer(length, (kk, 256)), 0, q - q % 256)
        bias[at:at + kk, :] = jnp.where((key <= q) & (key >= first), 0.0, -1e30)
        at += kk


def table_rows(COS, SIN, length, j):
    far = longer(length, (128, 128))
    near = lax.rem(j, 2)
    return (jnp.where(far, COS[rows(j), :], COS[rows(near), :]), jnp.where(far, SIN[rows(j), :], SIN[rows(near), :]))


def matrix(W, cols):
    w = W[:, :, :, :, cols]
    return w.reshape(768, w.shape[-1])


def forward_kernel(cols, qkv, out, up, down, vec, xin, cin, COS, SIN, mix,
                   oX, oacts, oQ, oK, oV, oatt, olse, oWQ, oWO, oblock, ogmid, ogup, ogdown, ogain, vgrad,
                   f_own, f_sib, block_w, WQ, WO, WU, WD, VEC, X, C, NB, SB,
                   acts, Q, K, V, att, lse, middle, bias, VT, act, slope, block, ga, acts2, actsT, dg, gup, gdown, gmid,
                   vq, vg, vu,
                   psend, precv, lsem, gsend, grecv, asend, arecv, nsend, nrecv, fsend, frecv, xsem, csem):
    pos = z, y, x, k = where_am_i()
    sib = dev(z, y, x, 1 - k)
    greet(z, y, x, k)
    s = 2 * z + y
    own_s = lax.rem(y + z, 2)
    def neighbour(a, src):
        cps = []
        for i in range(2):
            hi = src.at[i, pl.ds(pl.multiple_of((1 - y) * 128, 128), 128)]
            cp = remote(hi, NB.at[a, i], nsend.at[a, i], nrecv.at[a, i], dev(z, 1 - y, x, k))
            cp.start()
            cps.append(cp)
        return cps

    tokens = []
    def along_z(a, i, n, ref, dst, core):
        g = 2 * k + i
        me = (g == z) & (core == k)
        cp = remote(ref, dst, asend.at[a, i, n], arecv.at[a, z], dev(g, y, x, core))
        @pl.when(me)
        def _():
            pltpu.make_async_copy(ref, dst, arecv.at[a, z]).start()
        @pl.when(jnp.logical_not(me))
        def _():
            cp.start()
        tokens.append((cp, jnp.logical_not(me)))

    def straight(a, src, dst):
        for i in range(2):
            along_z(a, i, 0, src.at[i, pl.ds(pl.multiple_of(y * 128, 128), 128)], dst(s), own_s)

    def crossed(a, src, dst, cps):
        for i in range(2):
            cps[i].wait_recv()
            mine = src[i, pl.ds(pl.multiple_of((1 - y) * 128, 128), 128), :]
            far = longer(lane(vec[...], 0, 64 + i), (128, 768))
            SB[a, i] = jnp.where(far, NB[a, i].astype(F32), mine.astype(F32)).astype(BF)
            along_z(a, i, 1, SB.at[a, i], dst(s + 1 - 2 * y), 1 - own_s)

    def arrived(a, dst, i):
        remote(dst, dst, asend.at[a, 0, 0], arecv.at[a, i], sib).wait_recv()

    to_x = lambda j: X.at[j]
    to_c = lambda j: C.at[j // 2]
    nx = neighbour(0, xin)
    at, offs = 0, []
    for n, ref in zip(cols, (qkv, out, up)):
        half = n // 2
        f_own[0, :, at:at + half] = ref[:, :half].astype(F32)
        f_own[1, :, at:at + half] = ref[:, half:].astype(F32)
        offs.append((at, half))
        at += half
    pre = remote(f_own.at[1 - k], f_sib, psend, precv, sib)
    pre.start()
    straight(0, xin, to_x)
    lcs = [pltpu.make_async_copy(down, WD.at[z, y, x, k], lsem.at[3]), pltpu.make_async_copy(vec, VEC.at[z, y, x, k], lsem.at[4])]
    for c in lcs: c.start()
    pre.wait_recv()
    for i, ((at, half), W) in enumerate(zip(offs, (WQ, WO, WU))):
        mine = f_own[k, :, at:at + half]
        theirs = f_sib[:, at:at + half]
        block_w[:, at:at + half] = jnp.concatenate([jnp.where(k == 0, mine, theirs), jnp.where(k == 0, theirs, mine)], axis=0).astype(BF)
        c = pltpu.make_async_copy(block_w.at[:, at:at + half], W.at[z, y, x, :, pl.ds(pl.multiple_of(k * half, 128), half)], lsem.at[i])
        c.start(); lcs.append(c)

    def colpart(W, half):
        return lambda zz, yy, xx, kk: W.at[zz, yy, xx, :, pl.ds(pl.multiple_of(kk * half, 128), half)]
    def rowpart(W):
        return lambda zz, yy, xx, kk: W.at[zz, yy, xx, kk]
    for c in lcs: c.wait()
    G = [Gather(p, gsend.at[i], grecv.at[i], pos) for i, p in enumerate(
        [rowpart(VEC), colpart(WQ, offs[0][1]), colpart(WO, offs[1][1]), colpart(WU, offs[2][1]), rowpart(WD)])]
    gv, gq, go, gu, gd = G
    gv.stage(0); gq.stage(0)
    crossed(0, xin, to_x, nx)
    nc = neighbour(1, cin)
    gv.stage(1); gq.stage(1)
    gv.stage(2)
    go.stage(0)
    fw = []
    def forward_x(i):
        j = own_block(jnp.int32(i), k)
        arrived(0, X.at[j], i)
        cp = remote(X.at[j], X.at[j], fsend.at[i], frecv.at[i], sib)
        cp.start(); fw.append(cp)
    gv.stage(3)
    gq.stage(2)
    gv.stage(4); gv.stage(5)
    gu.stage(0)
    for i in range(4): forward_x(i)
    tiles = VEC[...].reshape(32, 8, 128)
    at = 0
    length = lane(VEC[0, 0, x, z // 2], 0, 64 + lax.rem(z, 2))
    vq[...] = widen(tiles, 2, 72)
    vu[...] = widen(tiles, 6, 96)
    for n, r in enumerate((0, 1, 3, 4, 5, 7)):
        vg[n:n + 1, :] = widen(tiles, r, 24)
    a_gain, a_shift, bout, m_gain, m_shift, bdown = (vg[n:n + 1, :] for n in range(6))
    bias_rows(bias, length, k)
    go.stage(1)
    gq.stage(3)
    gq.stage(4)
    straight(1, cin, to_c)
    crossed(1, cin, to_c, nc)
    for i in range(4): fw[i].wait_recv()
    for j in range(8):
        n, _ = norm(X[j].astype(F32))
        acts[j * 128:(j + 1) * 128, :] = (n * a_gain + a_shift).astype(BF)
    gq.stage(5)
    go.stage(2)
    gu.stage(1)
    gd.stage(0)
    exports = []
    def export(ref, dst):
        c = pltpu.make_async_copy(ref, dst, xsem.at[len(exports)])
        c.start(); exports.append(c)

    def keys(j):
        a = acts[rows(j), :]
        c, sn = table_rows(COS, SIN, length, j)
        for t in range(3):
            u2 = nn(a, matrix(WQ, slice(768 + t * 256, 1024 + t * 256))) + vq[:, 768 + t * 256:1024 + t * 256]
            for h in range(2):
                u = u2[:, h * 128:(h + 1) * 128]
                K[rows(j), t * 256 + h * 128:t * 256 + (h + 1) * 128] = (u * c + swap(u) * sn).astype(BF)
        V[rows(j), :] = (nn(a, matrix(WQ, slice(1536, 2304))) + vq[:, 1536:]).astype(BF)

    pl.loop(0, 4)(keys)
    go.stage(3); gu.stage(2)
    pl.loop(4, 8)(keys)
    go.stage(4)

    @pl.loop(0, 4)
    def _(i):
        j = own_block(i, k)
        a = acts[rows(j), :]
        c, sn = table_rows(COS, SIN, length, j)
        for t in range(3):
            u2 = nn(a, matrix(WQ, slice(t * 256, 256 + t * 256))) + vq[:, t * 256:256 + t * 256]
            for h in range(2):
                u = u2[:, h * 128:(h + 1) * 128]
                Q[rows(i), t * 256 + h * 128:t * 256 + (h + 1) * 128] = (u * c + swap(u) * sn).astype(BF) * jnp.asarray(0.125, BF)
    gu.stage(3)
    gd.stage(1)
    export(X, oX); export(acts, oacts); export(Q, oQ); export(K, oK); export(V, oV)
    export(WQ, oWQ)

    def heads(h):
        lanes = rows(h)
        VT[...] = V[:, lanes].T
        at = 0
        for i in range(4):
            kk = 256 * (i + 1)
            qb = spread(Q[i * 128:(i + 1) * 128, lanes])
            st = nt(K[0:kk, lanes], qb) + bias[at:at + kk, :]
            top = jnp.max(st, axis=0, keepdims=True)
            p = jnp.exp(st - top)
            den = jnp.sum(p, axis=0, keepdims=True)
            o = nn(VT[:, 0:kk], p.astype(BF)) * (1.0 / den)
            att[i * 128:(i + 1) * 128, lanes] = pick(o)
            lse[h, i:i + 1, :] = top + jnp.log(den)
            at += kk

    pl.loop(0, 2)(heads)
    gu.stage(4); go.stage(5)
    export(WO, oWO)
    pl.loop(2, 4)(heads)
    gd.stage(2)
    pl.loop(4, 6)(heads)
    gd.stage(3)
    export(att, oatt); export(lse, olse)

    @pl.loop(0, 4)
    def _(i):
        j = own_block(i, k)
        middle[rows(i), :] = X[j].astype(F32) + (nn(att[rows(i), :].astype(BF), WO[...].reshape(768, 768)) + bout)
    m5 = mix[5]
    for i in range(4):
        arrived(1, C.at[i], i)
        r = slice(i * 128, (i + 1) * 128)
        mid = middle[r, :]
        n, _ = norm(mid)
        a2 = (n * m_gain + m_shift).astype(BF)
        acts2[r, :] = a2
        actsT[:, r] = a2.T
        dg[r, :] = (m5 * C[i].astype(F32)).astype(BF)
        block[r, :] = mid + bdown
        ga[r, :] = jnp.zeros_like(mid)
    gu.stage(5)
    gd.stage(4)
    vgrad[...] = jnp.zeros_like(vgrad)

    def put_vec(row, v):
        for t in range(v.shape[1] // 128):
            vgrad[row + t:row + t + 1, :] = v[:, t * 128:(t + 1) * 128]
    put_vec(72, jnp.sum(dg[...].astype(F32), axis=0, keepdims=True))

    @pl.loop(0, 8)
    def _(f):
        c = rows(f, 384)
        u = nn(acts2[...], matrix(WU, c)) + vu[:, c]
        half_erf = 0.5 * lax.erf(u * (2.0 ** -0.5)) + 0.5
        slope[:, c] = half_erf + u * (jnp.exp(u * u * -0.5) * (1.0 / math.sqrt(2 * math.pi)))
        act[:, c] = (u * half_erf).astype(BF)
    gd.stage(5)

    @pl.loop(0, 4)
    def _(f):
        c = rows(f, 768)
        wd = WD[f].reshape(768, 768)
        a = act[:, c]
        block[...] += nn(a, wd)
        upg = (nt(dg[...], wd) * slope[:, c]).astype(BF)
        g = jnp.sum(upg.astype(F32), axis=0, keepdims=True)
        for t in range(6):
            vgrad[pl.ds(48 + f * 6 + t, 1), :] = g[:, t * 128:(t + 1) * 128]
        gdown[c, :] = nn(a.T, dg[...]).astype(BF)
        pltpu.make_async_copy(gdown.at[c, :], ogdown.at[c, :], csem.at[0, f]).start()
        gup[:, c] = nn(actsT[...], upg).astype(BF)
        pltpu.make_async_copy(gup.at[:, c], ogup.at[:, c], csem.at[1, f]).start()
        ga[...] += nt(upg, matrix(WU, c))

    total = jnp.zeros((1, 768), F32)
    gg = jnp.zeros((1, 768), F32)
    gs = jnp.zeros((1, 768), F32)
    for i in range(4):
        r = slice(i * 128, (i + 1) * 128)
        n, inv = norm(middle[r, :])
        e = ga[r, :]
        cf = C[i].astype(F32)
        gg += jnp.sum(e * n, axis=0, keepdims=True)
        gs += jnp.sum(e, axis=0, keepdims=True)
        gmid[r, :] = m5 * cf + norm_grad(e, n, inv, m_gain)
        total += jnp.sum(cf * block[r, :], axis=0, keepdims=True)
    put_vec(36, gg); put_vec(42, gs)
    ogain[...] = jnp.broadcast_to(a_gain, (8, 768))
    whole = jnp.sum(total, axis=1, keepdims=True)
    vgrad[78:79, :] = jnp.where(lax.broadcasted_iota(jnp.int32, (1, 128), 1) == 5, jnp.broadcast_to(whole, (1, 128)), 0.0)
    vgrad[79:80, :] = jnp.broadcast_to(length, (1, 128))
    export(gmid, ogmid); export(block, oblock)
    for f in range(4):
        c = slice(f * 768, (f + 1) * 768)
        pltpu.make_async_copy(gdown.at[c, :], ogdown.at[c, :], csem.at[0, f]).wait()
        pltpu.make_async_copy(gup.at[:, c], ogup.at[:, c], csem.at[1, f]).wait()
    for c in exports: c.wait()
    for c in fw + nx + nc: c.wait_send()
    for cp, cond in tokens:
        @pl.when(cond)
        def _():
            cp.wait_send()
    pre.wait_send()


def forward_call(qkv, out, up, down, vec, xin, cin, COS, SIN, mix):
    cols = (qkv.shape[1], out.shape[1], up.shape[1])
    H = sum(cols) // 2
    any_ = pl.BlockSpec(memory_space=pl.ANY)
    T = lambda n, t=BF: ((n, 768), t)
    shapes = [((8, 128, 768), BF), T(1024), T(512), T(1024), T(1024), T(512, F32), ((6, 4, 256), F32),
              ((4, 2, 2, 48, 2304), BF), ((4, 2, 2, 48, 768), BF), T(512, F32), T(512, F32), ((768, 3072), BF), T(3072)]
    DS = pltpu.SemaphoreType.DMA
    return pl.pallas_call(functools.partial(forward_kernel, cols),
        out_shape=[sd(*t) for t in shapes] + [sd((8, 768), F32), sd((80, 128), F32)],
        in_specs=[vs] * 9 + [ss], out_specs=[any_] * len(shapes) + [vs, vs],
        scratch_shapes=[VM((2, 24, H), F32), VM((24, H), F32), VM((48, H), BF),
                        VM((4, 2, 2, 48, 2304), BF), VM((4, 2, 2, 48, 768), BF), VM((4, 2, 2, 48, 3072), BF), VM((4, 2, 2, 2, 96, 768), BF),
                        VM((4, 2, 2, 2, 8, 128), F32), VM((8, 128, 768), BF), VM((4, 128, 768), BF), VM((2, 2, 128, 768), BF), VM((2, 2, 128, 768), BF),
                        VM((1024, 768), BF), VM((512, 768), BF), VM((1024, 768), BF), VM((1024, 768), BF), VM((512, 768), F32),
                        VM((6, 4, 256), F32), VM((512, 768), F32), VM((2560, 256), F32), VM((128, 1024), BF),
                        VM((512, 3072), BF), VM((512, 3072), F32), VM((512, 768), F32), VM((512, 768), F32), VM((512, 768), BF),
                        VM((768, 512), BF), VM((512, 768), BF), VM((768, 3072), BF), VM((3072, 768), BF), VM((512, 768), F32),
                        VM((1, 2304), F32), VM((8, 768), F32), VM((1, 3072), F32),
                        DS, DS, DS((5,)), DS((5, 10)), DS((5, 10)), DS((2, 2, 2)), DS((2, 4)), DS((2, 2)), DS((2, 2)), DS((4,)), DS((4,)),
                        DS((12,)), DS((2, 4))],
        compiler_params=pltpu.CompilerParams(collective_id=0, has_side_effects=True, vmem_limit_bytes=63 * 2**20),
    )(qkv, out, up, down, vec, xin, cin, COS, SIN, mix)


class Scatter:
    STAGES = 5

    def __init__(self, part, PA, RA, RB, RC, RZ, put, send, recv, pos):
        self.__dict__.update(locals())
        z, y, x, k = pos
        self.own = (y, x)
        self.p2 = jnp.where(k == 0, 1 - y, y), jnp.where(k == 0, x, 1 - x)
        self.p3 = jnp.where(k == 0, y, 1 - y), jnp.where(k == 0, 1 - x, x)
        self.d4 = 1 - y, 1 - x
        blk = lambda yx: PA.at[:, yx[0], yx[1]]
        n3, n2 = dev(z, *self.p3, k), dev(z, *self.p2, k)
        self.pre = remote(part(slice(None), slice(None), slice(None), 1 - k), RA, send.at[0], recv.at[0], dev(z, y, x, 1 - k))
        self.b1 = remote(blk(self.d4), RB.at[1], send.at[1], recv.at[1], n3)
        self.b0 = remote(blk(self.p3), RB.at[0], send.at[2], recv.at[2], n3)
        self.c = remote(blk(self.p2), RC, send.at[3], recv.at[3], n2)
        self.zs = [remote(PA.at[lax.rem(z + d, 4), y, x], RZ.at[d - 1], send.at[3 + d], recv.at[3 + d],
                          dev(lax.rem(z + d, 4), y, x, k)) for d in (1, 2, 3)]

    def add(self, yx, other):
        @pl.loop(0, 4)
        def _(i):
            a = self.PA[i, yx[0], yx[1]].astype(F32) + other[i].astype(F32)
            self.PA[i, yx[0], yx[1]] = a.astype(BF)

    def first(self, yx):
        k = self.pos[3]
        @pl.loop(0, 4)
        def _(i):
            a = self.part(i, yx[0], yx[1], k)[...].astype(F32) + self.RA[i, yx[0], yx[1]].astype(F32)
            self.PA[i, yx[0], yx[1]] = a.astype(BF)

    def stage(self, n):
        z, y, x, k = self.pos
        if n == 0:
            self.pre.start()
        elif n == 1:
            self.pre.wait_recv()
            self.first(self.d4)
            self.b1.start()
            self.first(self.p3)
            self.b0.start()
            self.first(self.p2)
            self.first(self.own)
        elif n == 2:
            self.b1.wait_recv()
            self.add(self.p2, self.RB.at[1])
            self.c.start()
            self.b0.wait_recv()
            self.add(self.own, self.RB.at[0])
        elif n == 3:
            self.c.wait_recv()
            self.add(self.own, self.RC)
            for c in self.zs: c.start()
        elif n == 4:
            for c in self.zs: c.wait_recv()
            tot = self.PA[z, y, x].astype(F32)
            for i in range(3):
                tot = tot + self.RZ[i].astype(F32)
            self.put(tot)
            for c in [self.pre, self.b0, self.b1, self.c] + self.zs: c.wait_send()


def reduce_kernel(cols, flag, gqkv, gout, gup, gdown, e, gmid, block, X, gain, vin,
                  oq, oo, ou, od, vout, H0, HL, HS,
                  PQ, AQ, BQ, CQ, ZQ, PO, AO, BO, CO, ZO, PU, AU, BU, CU, ZU, PD, AD, BD, CD, ZD,
                  fin, fsib, es, er, gx, bl, vbuf, vrec,
                  ssem, rsem, hsend, h0, hl, hs, misc_s, misc_r, vsend, vrecv):
    pos = z, y, x, k = where_am_i()
    is_long = flag[0] != 0
    greet(z, y, x, k)
    sib = dev(z, y, x, 1 - k)
    for i in range(4):
        es[i] = e[rows(own_block(jnp.int32(i), 1 - k)), :].astype(BF)
    ecp = remote(es, er, misc_s.at[0], misc_r.at[0], sib)
    ecp.start()
    halves = [c // 2 for c in cols]

    def colpart(W, half):
        def f(zz, yy, xx, kk):
            return W.at[zz, yy, xx, :, pl.ds(pl.multiple_of(kk * half, 128), half)]
        return f
    offs = [0, halves[0], halves[0] + halves[1]]
    def put_cols(i):
        def put(t):
            fin[0, :, offs[i]:offs[i] + halves[i]] = t[:24]
            fin[1, :, offs[i]:offs[i] + halves[i]] = t[24:]
        return put
    def put_down(t):
        od[...] = t
    S = lambda a, part, bufs, put: Scatter(part, *bufs, put, ssem.at[a], rsem.at[a], pos)
    gs = [S(0, lambda zz, yy, xx, kk: gdown.at[zz, yy, xx, kk], (PD, AD, BD, CD, ZD), put_down),
          S(1, colpart(gup, halves[2]), (PU, AU, BU, CU, ZU), put_cols(2)),
          S(2, colpart(gout, halves[1]), (PO, AO, BO, CO, ZO), put_cols(1)),
          S(3, colpart(gqkv, halves[0]), (PQ, AQ, BQ, CQ, ZQ), put_cols(0))]
    homes = []
    g = z
    def send_home(a, buf):
        for i in range(4):
            j = own_block(jnp.int32(i), k)
            yj = lax.rem(j, 2)
            zj = jnp.int32(i)
            core = g // 2
            straight = yj == y
            slot = lax.rem(g, 2)
            for n, (dst, rs, yd, cond) in enumerate((
                (H0.at[a, slot], h0.at[a, slot], y, straight),
                (HL.at[a, slot], hl.at[a, slot], 1 - y, jnp.logical_not(straight)),
                (HS.at[a, slot], hs.at[a, slot], y, jnp.logical_not(straight)))):
                me = (zj == z) & (yd == y) & (core == k)
                cp = remote(buf.at[i], dst, hsend.at[a, i, n], rs, dev(zj, yd, x, core))
                @pl.when(cond & me)
                def _():
                    pltpu.make_async_copy(buf.at[i], dst, rs).start()
                @pl.when(cond & jnp.logical_not(me))
                def _():
                    cp.start()
                homes.append((cp, cond & jnp.logical_not(me)))
    for i in range(4):
        bl[i] = block[i * 128:(i + 1) * 128, :].astype(BF)
    send_home(0, bl)

    def token_grads():
        ecp.wait_recv()
        gg = jnp.zeros((1, 768), F32)
        gsh = jnp.zeros((1, 768), F32)
        for i in range(4):
            j = own_block(jnp.int32(i), k)
            n, inv = norm(X[j].astype(F32))
            ee = e[rows(j), :] + er[i].astype(F32)
            gg += jnp.sum(ee * n, axis=0, keepdims=True)
            gsh += jnp.sum(ee, axis=0, keepdims=True)
            gx[i] = (gmid[i * 128:(i + 1) * 128, :] + norm_grad(ee, n, inv, gain[...])).astype(BF)
        send_home(1, gx)
        vbuf[0] = vin[...]
        for t in range(6):
            vbuf[0, t:t + 1, :] = gg[:, t * 128:(t + 1) * 128]
            vbuf[0, 6 + t:7 + t, :] = gsh[:, t * 128:(t + 1) * 128]

    sc = gs[0]
    vec_steps = [[sib], [dev(z, *sc.p2, k)], [dev(z, *sc.p3, k)], [dev(lax.rem(z + d, 4), y, x, k) for d in (1, 2, 3)]]
    vcp = []
    def vec_stage(n):
        if n > 0:
            for c in vcp[-1]: c.wait_recv()
            t = vbuf[n - 1]
            for r in range(len(vcp[-1])):
                t = t + vrec[n - 1 + r]
            if n < 4: vbuf[n] = t
            else: vout[...] = t
        if n < 4:
            vcp.append([remote(vbuf.at[n], vrec.at[n + i], vsend.at[n + i], vrecv.at[n + i], d) for i, d in enumerate(vec_steps[n])])
            for c in vcp[-1]: c.start()

    for tick in range(len(gs) + Scatter.STAGES - 1):
        for i, gg_ in enumerate(gs):
            n = tick - i
            if 0 <= n < Scatter.STAGES:
                gg_.stage(n)
        if tick == 0:
            token_grads()
        if 1 <= tick <= 5:
            vec_stage(tick - 1)
    lst = remote(fin.at[1 - k], fsib, misc_s.at[1], misc_r.at[1], sib)
    lst.start()
    lst.wait_recv()
    for i, o in enumerate((oq, oo, ou)):
        mine = fin[k, :, offs[i]:offs[i] + halves[i]]
        theirs = fsib[:, offs[i]:offs[i] + halves[i]]
        o[:, :halves[i]] = jnp.where(k == 0, mine, theirs)
        o[:, halves[i]:] = jnp.where(k == 0, theirs, mine)
    for a in range(2):
        for i in range(2):
            remote(H0.at[a, i], H0.at[a, i], hsend.at[0, 0, 0], h0.at[a, i], sib).wait_recv()
            remote(HL.at[a, i], HL.at[a, i], hsend.at[0, 0, 0], hl.at[a, i], sib).wait_recv()
            remote(HS.at[a, i], HS.at[a, i], hsend.at[0, 0, 0], hs.at[a, i], sib).wait_recv()
    lst.wait_send()
    ecp.wait_send()
    for cs in vcp:
        for c in cs: c.wait_send()
    for cp, cond in homes:
        @pl.when(cond)
        def _():
            cp.wait_send()


def reduce_call(flag, gqkv, gout, gup, gdown, *ins):
    cols = (gqkv.shape[1], gout.shape[1], gup.shape[1])
    gqkv, gout, gup = (g.reshape(4, 2, 2, 48, g.shape[1]) for g in (gqkv, gout, gup))
    gdown = gdown.reshape(4, 2, 2, 2, 96, 768)
    any_ = pl.BlockSpec(memory_space=pl.ANY)
    bufs = []
    for r, n in ((48, cols[0] // 2), (48, cols[1] // 2), (48, cols[2] // 2), (96, 768)):
        bufs += [VM((4, 2, 2, r, n), BF), VM((4, 2, 2, r, n), BF), VM((2, 4, r, n), BF), VM((4, r, n), BF), VM((3, r, n), BF)]
    H = sum(cols) // 2
    DS = pltpu.SemaphoreType.DMA
    home = sd((2, 2, 128, 768), BF)
    return pl.pallas_call(functools.partial(reduce_kernel, cols),
        out_shape=[sd((24, cols[0]), F32), sd((24, cols[1]), F32), sd((24, cols[2]), F32), sd((96, 768), F32), sd((80, 128), F32), home, home, home],
        in_specs=[ss] + [vs] * (4 + len(ins)), out_specs=[vs] * 5 + [any_] * 3,
        scratch_shapes=bufs + [VM((2, 24, H), F32), VM((24, H), F32), VM((4, 128, 768), BF), VM((4, 128, 768), BF), VM((4, 128, 768), BF),
                               VM((4, 128, 768), BF), VM((4, 80, 128), F32), VM((6, 80, 128), F32),
                               DS((4, 7)), DS((4, 7)), DS((2, 4, 3)), DS((2, 2)), DS((2, 2)), DS((2, 2)), DS((2,)), DS((2,)), DS((6,)), DS((6,))],
        compiler_params=pltpu.CompilerParams(collective_id=1, has_side_effects=True, vmem_limit_bytes=62 * 2**20),
    )(flag, gqkv, gout, gup, gdown, *ins)

def fast_shards(inputs, history, seq_lengths, attn_gain, attn_shift, qkv_weight, qkv_bias, out_weight, out_bias, mlp_gain,
                mlp_shift, up_weight, up_bias, down_weight, down_bias, mix_weights, cotangent):
    seq, batch = lax.axis_index("seq"), lax.axis_index("batch")
    z, y, x, k = seq // 2, seq % 2, batch // 2, batch % 2
    vectors = (attn_gain, attn_shift, qkv_bias, out_bias, mlp_gain, mlp_shift, up_bias, down_bias)
    lens = seq_lengths.astype(F32)
    packed = jnp.stack([jnp.pad(v.astype(F32), (0, 128 - v.shape[0])) for v in vectors])
    packed = packed.at[0, 64:66].set(lens)
    COS, SIN = (jnp.asarray(t) for t in rope_tables())
    X, acts, Q, K, V, att, lse, WQ, WO, block, gmid, gup, gdown, gain, vgrad = forward_call(
        qkv_weight, out_weight, up_weight, down_weight, packed, inputs, cotangent, COS, SIN, mix_weights)
    wqkv, wout, a_gain = WQ.reshape(768, 2304), WO.reshape(768, 768), gain[:1]
    flag = (vgrad[79, :1] == LONG_LEN).astype(jnp.int32)
    e, gqkv, gout, g_bqkv, g_bout = attn_bwd_call(flag, gmid, acts, Q, K, V, att, lse, wqkv, wout, COS, SIN)
    earlier, cot = history.astype(F32), cotangent.astype(F32)
    mix_terms = jnp.sum(earlier * cot[None], axis=(1, 2, 3))
    grad_history = (mix_weights[:-1, None, None, None] * cot[None]).astype(BF)
    vin = vgrad.at[12:30].set(g_bqkv.reshape(18, 128)).at[30:36].set(g_bout.reshape(6, 128)).at[78, :5].set(mix_terms)
    oq, oo, ou, od, vout, H0, HL, HS = reduce_call(flag, gqkv, gout, gup, gdown, e, gmid, block, X, a_gain, vin)
    is_long = (seq_lengths == LONG_LEN)[None, :, None, None]
    other = jnp.where(is_long, HL, HS)
    home = jnp.where(y == 0, jnp.concatenate([H0, other], axis=2), jnp.concatenate([other, H0], axis=2))
    layer_out = (jnp.sum(mix_weights[:-1, None, None, None] * earlier, axis=0) + mix_weights[-1] * home[0].astype(F32)).astype(BF)
    vflat = vout.reshape(-1)
    me = seq * 4 + batch
    gv, at = [], 0
    for v in vectors:
        n = v.shape[0]
        gv.append(lax.dynamic_slice_in_dim(vflat, at + me * n, n, 0))
        at += 32 * n
    grad_mix = vflat[at:at + 6]
    return (layer_out, home[1], grad_history, gv[0], gv[1], oq, gv[2], oo, gv[3], gv[4], gv[5], ou, gv[6], od, gv[7], grad_mix)


def fits(mesh, inputs):
    shape = dict(mesh.shape)
    return shape == {"seq": 8, "batch": 4} and inputs.shape == (8, 2048, 768)


def solution(mesh):
    def run(*args):
        body = fast_shards if fits(mesh, args[0]) else shards
        return placed(mesh, body)(*args)
    return run
```

```python
import functools
import math

import jax
import jax.numpy as jnp
import numpy as np
from jax import lax
from jax.experimental import pallas as pl
from jax.experimental.pallas import tpu as pltpu
from jax.sharding import PartitionSpec as P

HEADS = 12
HEAD_DIM = 64
LONG_LEN = 1024
SHORT_LEN = 256


eps = 1e-05
masked = -1e30


def block_size(row_count):
    chosen = 1
    for candidate in range(1, min(row_count, 512) + 1):
        if row_count % candidate == 0:
            chosen = candidate
    return chosen


def exact_gelu(values):
    return jax.nn.gelu(values, approximate=False)


def layer_norm(values, norm_gain, norm_shift):
    average = jnp.mean(values, axis=-1, keepdims=True)
    centred = values - average
    inverse = lax.rsqrt(jnp.mean(centred * centred, axis=-1, keepdims=True) + eps)
    normed = centred * inverse
    return (normed * norm_gain + norm_shift, normed, inverse)


def norm_back(grad_out, normed, inverse, norm_gain):
    grad_normed = grad_out * norm_gain
    mean_grad = jnp.mean(grad_normed, axis=-1, keepdims=True)
    mean_cross = jnp.mean(grad_normed * normed, axis=-1, keepdims=True)
    grad_in = inverse * (grad_normed - mean_grad - normed * mean_cross)
    return (grad_in, jnp.sum(grad_out * normed, axis=0), jnp.sum(grad_out, axis=0))


def token_layout(index, info):
    seq_len, tok_count, slice_len = info
    is_long = seq_len == LONG_LEN
    offset = index % tok_count
    device = index // tok_count
    doc_ids = jnp.where(is_long, offset // slice_len, index // SHORT_LEN).astype(jnp.int32)
    relative = jnp.where(
        is_long, device * slice_len + offset % slice_len, index % SHORT_LEN
    ).astype(jnp.int32)
    return (doc_ids, relative)


def rotary_tables(relative):
    half_dim = HEAD_DIM // 2
    frequency = jnp.exp(
        -math.log(10000.0) * (2.0 * jnp.arange(half_dim, dtype=jnp.float32) / HEAD_DIM)
    )
    angles = relative.astype(jnp.float32)[:, None] * frequency[None, :]
    return (jnp.cos(angles)[:, None, :], jnp.sin(angles)[:, None, :])


def rotate(values, cosine, sine_table):
    half_dim = values.shape[-1] // 2
    lower_half = values[..., :half_dim]
    upper_half = values[..., half_dim:]
    return jnp.concatenate(
        [
            lower_half * cosine - upper_half * sine_table,
            upper_half * cosine + lower_half * sine_table,
        ],
        axis=-1,
    )


def allowed_mask(query_places, key_places, info):
    query_docs, query_rel = token_layout(query_places, info)
    key_docs, key_rel = token_layout(key_places, info)
    return (key_docs[None, :] == query_docs[:, None]) & (key_rel[None, :] <= query_rel[:, None])


def online_block(current, query_b, key_block, value_block, query_places, key_places, info):
    running, denominator, weighted = current
    key_count = key_block.shape[0]
    allowed = allowed_mask(query_places, key_places, info)
    key_heads = key_block.reshape(key_count, HEADS, HEAD_DIM)
    scores = jnp.einsum(
        "qhd,khd->hqk", query_b, key_heads, preferred_element_type=jnp.float32
    ) * HEAD_DIM ** (-0.5)
    scores = jnp.where(allowed[None], scores, masked)
    new_max = jnp.maximum(running, jnp.max(scores, axis=-1))
    exp_scores = jnp.where(allowed[None], jnp.exp(scores - new_max[..., None]), 0.0)
    rescale = jnp.exp(running - new_max)
    denominator = denominator * rescale + jnp.sum(exp_scores, axis=-1)
    value_heads = value_block.reshape(key_count, HEADS, HEAD_DIM)
    weighted = weighted * rescale[..., None] + jnp.einsum(
        "hqk,khd->hqd",
        exp_scores.astype(jnp.bfloat16),
        value_heads,
        preferred_element_type=jnp.float32,
    )
    return (new_max, denominator, weighted)


def attend_rows(current, query_b, key_rows, value_rows, first_row, query_places, info, last_place):
    key_count = key_rows.shape[0]
    block_rows = block_size(key_count)

    def one_block(carried, block_index):
        start_place = first_row + block_index * block_rows
        key_block = lax.dynamic_slice_in_dim(key_rows, block_index * block_rows, block_rows, 0)
        value_block = lax.dynamic_slice_in_dim(value_rows, block_index * block_rows, block_rows, 0)
        key_places = start_place + jnp.arange(block_rows, dtype=jnp.int32)

        def one_compute(state_in):
            return online_block(
                state_in, query_b, key_block, value_block, query_places, key_places, info
            )

        def unchanged(state_in):
            return state_in

        return (lax.cond(start_place > last_place, unchanged, one_compute, carried), None)

    result, unused = lax.scan(
        one_block, current, jnp.arange(key_count // block_rows, dtype=jnp.int32)
    )
    return result


def block_probs(query_b, key_b, query_places, key_places, info, lse_rows):
    allowed = allowed_mask(query_places, key_places, info)
    scores = jnp.einsum(
        "qhd,khd->hqk", query_b, key_b, preferred_element_type=jnp.float32
    ) * HEAD_DIM ** (-0.5)
    return jnp.exp(jnp.where(allowed[None], scores - lse_rows[..., None], masked))


def block_dscores(probabilities, grad_b, value_b, delta_rows):
    dprobs = jnp.einsum("qhd,khd->hqk", grad_b, value_b, preferred_element_type=jnp.float32)
    return (probabilities * (dprobs - delta_rows[..., None])).astype(jnp.bfloat16)


def shards(
    inputs,
    history,
    seq_lengths,
    attn_gain,
    attn_shift,
    qkv_weight,
    qkv_bias,
    out_weight,
    out_bias,
    mlp_gain,
    mlp_shift,
    up_weight,
    up_bias,
    down_weight,
    down_bias,
    mix_weights,
    cotangent,
):
    group_count = inputs.shape[0]
    tok_count = inputs.shape[1]
    model_width = inputs.shape[2]
    seq_count = lax.axis_size("seq")
    group_rows = tok_count * seq_count
    slice_len = LONG_LEN // seq_count
    factor = HEAD_DIM ** (-0.5)
    seq_index = lax.axis_index("seq")
    first_place = seq_index * tok_count
    last_place = first_place + tok_count - 1
    places = first_place + jnp.arange(tok_count, dtype=jnp.int32)
    gathered = (
        lax.all_gather(attn_gain, ("seq", "batch"), axis=0, tiled=True),
        lax.all_gather(attn_shift, ("seq", "batch"), axis=0, tiled=True),
        lax.all_gather(qkv_weight, ("seq", "batch"), axis=0, tiled=True),
        lax.all_gather(qkv_bias, ("seq", "batch"), axis=0, tiled=True),
        lax.all_gather(out_weight, ("seq", "batch"), axis=0, tiled=True),
        lax.all_gather(out_bias, ("seq", "batch"), axis=0, tiled=True),
        lax.all_gather(mlp_gain, ("seq", "batch"), axis=0, tiled=True),
        lax.all_gather(mlp_shift, ("seq", "batch"), axis=0, tiled=True),
        lax.all_gather(up_weight, ("seq", "batch"), axis=0, tiled=True),
        lax.all_gather(up_bias, ("seq", "batch"), axis=0, tiled=True),
        lax.all_gather(down_weight, ("seq", "batch"), axis=0, tiled=True),
        lax.all_gather(down_bias, ("seq", "batch"), axis=0, tiled=True),
    )
    (
        gain_one,
        shift_one,
        qkv_full,
        qkv_vec,
        out_full,
        out_vec,
        gain_two,
        shift_two,
        up_full,
        up_vec,
        down_full,
        down_vec,
    ) = gathered
    saved = []
    block_outs = []
    for group in range(group_count):
        info = (seq_lengths[group], tok_count, slice_len)
        doc_ids, relative = token_layout(places, info)
        cosine, sine_table = rotary_tables(relative)
        residual_in = inputs[group].astype(jnp.float32)
        normed_out, normed_one, inverse_one = layer_norm(
            residual_in, gain_one.astype(jnp.float32), shift_one.astype(jnp.float32)
        )
        acts_one = normed_out.astype(jnp.bfloat16)
        projected = jnp.dot(
            acts_one, qkv_full, preferred_element_type=jnp.float32
        ) + qkv_vec.astype(jnp.float32)
        queries = rotate(
            projected[:, :model_width].reshape(tok_count, HEADS, HEAD_DIM), cosine, sine_table
        ).astype(jnp.bfloat16)
        key_flat = (
            rotate(
                projected[:, model_width : 2 * model_width].reshape(tok_count, HEADS, HEAD_DIM),
                cosine,
                sine_table,
            )
            .reshape(tok_count, model_width)
            .astype(jnp.bfloat16)
        )
        value_flat = projected[:, 2 * model_width :].astype(jnp.bfloat16)
        start_state = (
            jnp.full((HEADS, tok_count), masked, jnp.float32),
            jnp.zeros((HEADS, tok_count), jnp.float32),
            jnp.zeros((HEADS, tok_count, HEAD_DIM), jnp.float32),
        )
        key_all = None
        value_all = None
        running, denominator, weighted = attend_rows(
            start_state,
            queries,
            lax.all_gather(key_flat, "seq", axis=0, tiled=True),
            lax.all_gather(value_flat, "seq", axis=0, tiled=True),
            jnp.int32(0),
            places,
            info,
            last_place,
        )
        attended = jnp.transpose(weighted / denominator[..., None], (1, 0, 2))
        lse_rows = running + jnp.log(denominator)
        attended_b = attended.reshape(tok_count, model_width).astype(jnp.bfloat16)
        middle = (
            residual_in
            + jnp.dot(attended_b, out_full, preferred_element_type=jnp.float32)
            + out_vec.astype(jnp.float32)
        )
        normed_out_two, normed_two, inverse_two = layer_norm(
            middle, gain_two.astype(jnp.float32), shift_two.astype(jnp.float32)
        )
        acts_two = normed_out_two.astype(jnp.bfloat16)
        upward = jnp.dot(acts_two, up_full, preferred_element_type=jnp.float32) + up_vec.astype(
            jnp.float32
        )
        activated, gelu_back = jax.vjp(exact_gelu, upward)
        activated_b = activated.astype(jnp.bfloat16)
        block_out = (
            middle
            + jnp.dot(activated_b, down_full, preferred_element_type=jnp.float32)
            + down_vec.astype(jnp.float32)
        )
        block_outs.append(block_out)
        saved.append(
            (
                info,
                cosine,
                sine_table,
                normed_one,
                inverse_one,
                acts_one,
                queries,
                key_flat,
                value_flat,
                key_all,
                value_all,
                attended,
                lse_rows,
                attended_b,
                normed_two,
                inverse_two,
                acts_two,
                gelu_back,
                activated_b,
            )
        )
    block_stack = jnp.stack(block_outs, axis=0)
    earlier = history.astype(jnp.float32)
    grad_out_all = cotangent.astype(jnp.float32)
    mixed_out = (
        jnp.sum(mix_weights[:-1, None, None, None] * earlier, axis=0)
        + mix_weights[-1] * block_stack
    )
    mix_terms = jnp.concatenate(
        [
            jnp.sum(earlier * grad_out_all[None], axis=(1, 2, 3)),
            jnp.sum(block_stack * grad_out_all)[None],
        ]
    )
    grad_history = (mix_weights[:-1, None, None, None] * grad_out_all[None]).astype(jnp.bfloat16)
    back_gain_one, back_qkv, back_out, back_gain_two, back_up, back_down = (
        lax.all_gather(attn_gain, ("seq", "batch"), axis=0, tiled=True),
        lax.all_gather(qkv_weight, ("seq", "batch"), axis=0, tiled=True),
        lax.all_gather(out_weight, ("seq", "batch"), axis=0, tiled=True),
        lax.all_gather(mlp_gain, ("seq", "batch"), axis=0, tiled=True),
        lax.all_gather(up_weight, ("seq", "batch"), axis=0, tiled=True),
        lax.all_gather(down_weight, ("seq", "batch"), axis=0, tiled=True),
    )
    totals = None
    grad_input_list = []
    for group in range(group_count):
        (
            info,
            cosine,
            sine_table,
            normed_one,
            inverse_one,
            acts_one,
            queries,
            key_flat,
            value_flat,
            key_all,
            value_all,
            attended,
            lse_rows,
            attended_b,
            normed_two,
            inverse_two,
            acts_two,
            gelu_back,
            activated_b,
        ) = saved[group]
        grad_block = mix_weights[-1] * grad_out_all[group]
        down_grad_b = grad_block.astype(jnp.bfloat16)
        grad_w_down = jnp.einsum(
            "tf,td->fd", activated_b, down_grad_b, preferred_element_type=jnp.float32
        )
        grad_b_down = jnp.sum(down_grad_b.astype(jnp.float32), axis=0)
        grad_act = jnp.einsum(
            "td,fd->tf", down_grad_b, back_down, preferred_element_type=jnp.float32
        )
        up_grad_b = gelu_back(grad_act)[0].astype(jnp.bfloat16)
        grad_w_up = jnp.einsum("td,tf->df", acts_two, up_grad_b, preferred_element_type=jnp.float32)
        grad_b_up = jnp.sum(up_grad_b.astype(jnp.float32), axis=0)
        grad_acts_two = jnp.einsum(
            "tf,df->td", up_grad_b, back_up, preferred_element_type=jnp.float32
        )
        grad_middle_norm, grad_gain_two, grad_shift_two = norm_back(
            grad_acts_two, normed_two, inverse_two, back_gain_two.astype(jnp.float32)
        )
        grad_middle = grad_block + grad_middle_norm
        attn_grad_b = grad_middle.astype(jnp.bfloat16)
        grad_w_out = jnp.einsum(
            "te,td->ed", attended_b, attn_grad_b, preferred_element_type=jnp.float32
        )
        grad_b_out = jnp.sum(attn_grad_b.astype(jnp.float32), axis=0)
        grad_heads = (
            jnp.einsum("td,ed->te", attn_grad_b, back_out, preferred_element_type=jnp.float32)
            .astype(jnp.bfloat16)
            .reshape(tok_count, HEADS, HEAD_DIM)
        )
        delta_rows = jnp.transpose(jnp.sum(grad_heads.astype(jnp.float32) * attended, axis=-1))
        key_all, value_all = (
            lax.all_gather(key_flat, "seq", axis=0, tiled=True),
            lax.all_gather(value_flat, "seq", axis=0, tiled=True),
        )
        key_block_rows = block_size(group_rows)

        def query_grad_block(carried, block_index):
            start_place = block_index * key_block_rows
            key_block = lax.dynamic_slice_in_dim(key_all, start_place, key_block_rows, 0).reshape(
                key_block_rows, HEADS, HEAD_DIM
            )
            value_block = lax.dynamic_slice_in_dim(
                value_all, start_place, key_block_rows, 0
            ).reshape(key_block_rows, HEADS, HEAD_DIM)
            key_places = start_place + jnp.arange(key_block_rows, dtype=jnp.int32)

            def query_compute(summed):
                probabilities = block_probs(queries, key_block, places, key_places, info, lse_rows)
                dscores = block_dscores(probabilities, grad_heads, value_block, delta_rows)
                return (
                    summed
                    + jnp.einsum(
                        "hqk,khd->qhd", dscores, key_block, preferred_element_type=jnp.float32
                    )
                    * factor
                )

            return (
                lax.cond(start_place > last_place, lambda summed: summed, query_compute, carried),
                None,
            )

        grad_queries, unused = lax.scan(
            query_grad_block,
            jnp.zeros((tok_count, HEADS, HEAD_DIM), jnp.float32),
            jnp.arange(group_rows // key_block_rows, dtype=jnp.int32),
        )
        key_first_row = jnp.int32(0)
        key_rows = key_all
        value_rows = value_all
        inner_rows = block_size(lax.axis_size("seq") * tok_count)

        def key_grad_block(carried, block_index):
            offset = block_index * inner_rows
            start_place = key_first_row + offset
            key_block = lax.dynamic_slice_in_dim(key_rows, offset, inner_rows, 0).reshape(
                inner_rows, HEADS, HEAD_DIM
            )
            value_block = lax.dynamic_slice_in_dim(value_rows, offset, inner_rows, 0).reshape(
                inner_rows, HEADS, HEAD_DIM
            )
            key_places = start_place + jnp.arange(inner_rows, dtype=jnp.int32)

            def key_compute(unused_in):
                probabilities = block_probs(queries, key_block, places, key_places, info, lse_rows)
                dscores = block_dscores(probabilities, grad_heads, value_block, delta_rows)
                grad_keys = (
                    jnp.einsum("hqk,qhd->khd", dscores, queries, preferred_element_type=jnp.float32)
                    * factor
                )
                grad_values = jnp.einsum(
                    "hqk,qhd->khd",
                    probabilities.astype(jnp.bfloat16),
                    grad_heads,
                    preferred_element_type=jnp.float32,
                )
                return jnp.concatenate(
                    [
                        grad_keys.reshape(inner_rows, model_width),
                        grad_values.reshape(inner_rows, model_width),
                    ],
                    axis=1,
                )

            def nothing(unused_in):
                return jnp.zeros((inner_rows, 2 * model_width), jnp.float32)

            return (carried, lax.cond(start_place > last_place, nothing, key_compute, carried))

        unused_out, blocks = lax.scan(
            key_grad_block,
            jnp.int32(0),
            jnp.arange(lax.axis_size("seq") * tok_count // inner_rows, dtype=jnp.int32),
        )
        key_grads = lax.psum_scatter(
            blocks.reshape(lax.axis_size("seq") * tok_count, 2 * model_width).astype(jnp.bfloat16),
            "seq",
            scatter_dimension=0,
            tiled=True,
        ).astype(jnp.float32)
        grad_keys_own = key_grads[:, :model_width]
        grad_values_own = key_grads[:, model_width:]
        grad_q_turned = rotate(grad_queries, cosine, -sine_table).reshape(tok_count, model_width)
        grad_k_turned = rotate(
            grad_keys_own.reshape(tok_count, HEADS, HEAD_DIM), cosine, -sine_table
        ).reshape(tok_count, model_width)
        qkv_grad_b = jnp.concatenate(
            [grad_q_turned, grad_k_turned, grad_values_own], axis=1
        ).astype(jnp.bfloat16)
        grad_w_qkv = jnp.einsum(
            "td,te->de", acts_one, qkv_grad_b, preferred_element_type=jnp.float32
        )
        grad_b_qkv = jnp.sum(qkv_grad_b.astype(jnp.float32), axis=0)
        grad_acts_one = jnp.einsum(
            "te,de->td", qkv_grad_b, back_qkv, preferred_element_type=jnp.float32
        )
        grad_in_norm, grad_gain_one, grad_shift_one = norm_back(
            grad_acts_one, normed_one, inverse_one, back_gain_one.astype(jnp.float32)
        )
        grad_input_list.append((grad_middle + grad_in_norm).astype(jnp.bfloat16))
        terms = [
            grad_gain_one,
            grad_shift_one,
            grad_w_qkv,
            grad_b_qkv,
            grad_w_out,
            grad_b_out,
            grad_gain_two,
            grad_shift_two,
            grad_w_up,
            grad_b_up,
            grad_w_down,
            grad_b_down,
        ]
        if totals is None:
            totals = terms
        else:
            totals = [older + newer for older, newer in zip(totals, terms)]
    shares = (
        lax.psum_scatter(totals[0], ("seq", "batch"), scatter_dimension=0, tiled=True),
        lax.psum_scatter(totals[1], ("seq", "batch"), scatter_dimension=0, tiled=True),
        lax.psum_scatter(totals[2], ("seq", "batch"), scatter_dimension=0, tiled=True),
        lax.psum_scatter(totals[3], ("seq", "batch"), scatter_dimension=0, tiled=True),
        lax.psum_scatter(totals[4], ("seq", "batch"), scatter_dimension=0, tiled=True),
        lax.psum_scatter(totals[5], ("seq", "batch"), scatter_dimension=0, tiled=True),
        lax.psum_scatter(totals[6], ("seq", "batch"), scatter_dimension=0, tiled=True),
        lax.psum_scatter(totals[7], ("seq", "batch"), scatter_dimension=0, tiled=True),
        lax.psum_scatter(totals[8], ("seq", "batch"), scatter_dimension=0, tiled=True),
        lax.psum_scatter(totals[9], ("seq", "batch"), scatter_dimension=0, tiled=True),
        lax.psum_scatter(totals[10], ("seq", "batch"), scatter_dimension=0, tiled=True),
        lax.psum_scatter(totals[11], ("seq", "batch"), scatter_dimension=0, tiled=True),
    )
    grad_mix = lax.psum(mix_terms, ("seq", "batch"))
    grad_inputs = jnp.stack(grad_input_list, axis=0)
    return (
        mixed_out.astype(jnp.bfloat16),
        grad_inputs,
        grad_history,
        shares[0],
        shares[1],
        shares[2],
        shares[3],
        shares[4],
        shares[5],
        shares[6],
        shares[7],
        shares[8],
        shares[9],
        shares[10],
        shares[11],
        grad_mix,
    )


def placed(mesh, body):
    return jax.shard_map(
        body,
        mesh=mesh,
        in_specs=(
            P("batch", "seq", None),
            P(None, "batch", "seq", None),
            P("batch"),
            P(("seq", "batch")),
            P(("seq", "batch")),
            P(("seq", "batch"), None),
            P(("seq", "batch")),
            P(("seq", "batch"), None),
            P(("seq", "batch")),
            P(("seq", "batch")),
            P(("seq", "batch")),
            P(("seq", "batch"), None),
            P(("seq", "batch")),
            P(("seq", "batch"), None),
            P(("seq", "batch")),
            P(),
            P("batch", "seq", None),
        ),
        out_specs=(
            P("batch", "seq", None),
            P("batch", "seq", None),
            P(None, "batch", "seq", None),
            P(("seq", "batch")),
            P(("seq", "batch")),
            P(("seq", "batch"), None),
            P(("seq", "batch")),
            P(("seq", "batch"), None),
            P(("seq", "batch")),
            P(("seq", "batch")),
            P(("seq", "batch")),
            P(("seq", "batch"), None),
            P(("seq", "batch")),
            P(("seq", "batch"), None),
            P(("seq", "batch")),
            P(),
        ),
        check_vma=False,
    )

MESH = pl.DeviceIdType.MESH
BF, F32 = jnp.bfloat16, jnp.float32


def where_am_i():
    seq, batch = lax.axis_index("seq"), lax.axis_index("batch")
    return seq // 2, seq % 2, batch // 2, batch % 2


def dev(z, y, x, k):
    return (z * 2 + y, x * 2 + k)


def remote(src, dst, ssem, rsem, device):
    return pltpu.make_async_remote_copy(src_ref=src, dst_ref=dst, send_sem=ssem, recv_sem=rsem,
                                        device_id=device, device_id_type=MESH)


def greet(z, y, x, k):
    barrier = pltpu.get_barrier_semaphore()
    mine = (z * 2 + y) * 2 + k
    for step in range(1, 16):
        other = lax.rem(mine + step, 16)
        pl.semaphore_signal(barrier, inc=1, device_id=dev(other // 4, (other // 2) % 2, x, other % 2), device_id_type=MESH)
    pl.semaphore_signal(barrier, inc=1, device_id=dev(z, y, 1 - x, k), device_id_type=MESH)
    pl.semaphore_wait(barrier, 16)


class Gather:
    def __init__(self, part, send, recv, pos):
        self.part, self.send, self.recv, self.pos = part, send, recv, pos
        z, y, x, k = pos
        self.c = []
        p2 = jnp.where(k == 0, 1 - y, y), jnp.where(k == 0, x, 1 - x)
        p3 = jnp.where(k == 0, y, 1 - y), jnp.where(k == 0, 1 - x, x)
        d4 = 1 - y, 1 - x
        own = (y, x)
        zed = lambda i: part((slice(z, z + 1) if False else pl.ds(z, 1)), y, x, k)
        allz = lambda yx: part(slice(None), yx[0], yx[1], k)
        def cp(n, ref, device):
            return remote(ref, ref, send.at[n], recv.at[n], device)
        self.zs = [cp(d - 1, zed(0), dev(lax.rem(z + d, 4), y, x, k)) for d in (1, 2, 3)]
        self.a2 = cp(3, allz(own), dev(z, *p2, k))
        self.a3 = cp(4, allz(own), dev(z, *p3, k))
        self.b3 = cp(5, allz(p2), dev(z, *p3, k))
        sib = dev(z, y, x, 1 - k)
        self.s1 = cp(6, allz(own), sib)
        self.s2 = cp(7, allz(p2), sib)
        self.s3 = cp(8, allz(p3), sib)
        self.s4 = cp(9, allz(d4), sib)

    def stage(self, n):
        if n == 0:
            for c in self.zs: c.start()
        elif n == 1:
            for c in self.zs: c.wait_recv()
            self.a2.start(); self.a3.start(); self.s1.start()
        elif n == 2:
            self.a2.wait_recv()
            self.b3.start(); self.s2.start()
        elif n == 3:
            self.a3.wait_recv()
            self.s3.start()
        elif n == 4:
            self.b3.wait_recv()
            self.s4.start()
        elif n == 5:
            for c in (self.s1, self.s2, self.s3, self.s4): c.wait_recv()
            for c in self.zs + [self.a2, self.a3, self.b3, self.s1, self.s2, self.s3, self.s4]: c.wait_send()
    STAGES = 6


def gather_kernel(cols, qkv, out, up, down, vec, xin, cin,
                  QKV, OUT, UP, DOWN, VEC, XM, XA, CM, CA,
                  f_own, f_sib, block, psend, precv, lsem, gsend, grecv, asend, arecv, aarecv, fsend, frecv):
    pos = z, y, x, k = where_am_i()
    greet(z, y, x, k)
    at = 0
    tot = sum(cols)
    offs = []
    for n, ref in zip(cols, (qkv, out, up)):
        half = n // 2
        f_own[0, :, at:at + half] = ref[:, :half].astype(F32)
        f_own[1, :, at:at + half] = ref[:, half:].astype(F32)
        offs.append((at, half))
        at += half
    pre = remote(f_own.at[1 - k], f_sib, psend, precv, dev(z, y, x, 1 - k))
    pre.start()
    s = 2 * z + y
    own_s = lax.rem(y + z, 2)
    acps = []
    for a, (src, M, A) in enumerate(((xin, XM, XA), (cin, CM, CA))):
        for i in range(2):
            g = 2 * k + i
            lo = src.at[i, pl.ds(pl.multiple_of(y * 128, 128), 128)]
            hi = src.at[i, pl.ds(pl.multiple_of((1 - y) * 128, 128), 128)]
            for n, (ref, dst, rs, d) in enumerate((
                (lo, M.at[s], arecv.at[a, s], (g, y, x, own_s)),
                (hi, M.at[s], arecv.at[a, s], (g, 1 - y, x, own_s)),
                (hi, A.at[z], aarecv.at[a, z], (g, y, x, 1 - own_s)))):
                ss = asend.at[a, i, n]
                me = (g == z) & (d[1] == y) & (d[3] == k)
                cp = remote(ref, dst, ss, rs, dev(*d))
                @pl.when(me)
                def _():
                    pltpu.make_async_copy(ref, dst, rs).start()
                @pl.when(jnp.logical_not(me))
                def _():
                    cp.start()
                acps.append((cp, me))
    pre.wait_recv()
    lcs = []
    for i, ((at, half), W) in enumerate(zip(offs, (QKV, OUT, UP))):
        mine = f_own[k, :, at:at + half]
        theirs = f_sib[:, at:at + half]
        first = jnp.where(k == 0, mine, theirs)
        second = jnp.where(k == 0, theirs, mine)
        block[:, at:at + half] = jnp.concatenate([first, second], axis=0).astype(BF)
        c = pltpu.make_async_copy(block.at[:, at:at + half],
                                  W.at[z, y, x, :, pl.ds(pl.multiple_of(k * half, 128), half)], lsem.at[i])
        c.start(); lcs.append(c)
    for i, (ref, W) in enumerate(((down, DOWN), (vec, VEC))):
        c = pltpu.make_async_copy(ref, W.at[z, y, x, k], lsem.at[3 + i])
        c.start(); lcs.append(c)
    def colpart(W, half):
        return lambda zz, yy, xx, kk: W.at[zz, yy, xx, :, pl.ds(pl.multiple_of(kk * half, 128), half)]
    def rowpart(W):
        return lambda zz, yy, xx, kk: W.at[zz, yy, xx, kk]
    parts = [rowpart(VEC), colpart(QKV, offs[0][1]), colpart(OUT, offs[1][1]), colpart(UP, offs[2][1]), rowpart(DOWN)]
    for c in lcs: c.wait()
    gs = [Gather(p, gsend.at[i], grecv.at[i], pos) for i, p in enumerate(parts)]
    fw = []
    def tokens_forward():
        for zz in range(4):
            j = 2 * zz + lax.rem(zz + k, 2)
            cp = remote(XM.at[j], XM.at[j], fsend.at[zz], frecv.at[zz], dev(z, y, x, 1 - k))
            remote(XM.at[j], XM.at[j], fsend.at[zz], arecv.at[0, j], dev(z, y, x, 1 - k)).wait_recv()
            cp.start(); fw.append(cp)
        for e in range(2):
            zz = lax.rem(1 - y + k, 2) + 2 * e
            cp = remote(XA.at[zz], XA.at[zz], fsend.at[4 + e], frecv.at[4 + e], dev(z, y, x, 1 - k))
            remote(XA.at[zz], XA.at[zz], fsend.at[4 + e], aarecv.at[0, zz], dev(z, y, x, 1 - k)).wait_recv()
            cp.start(); fw.append(cp)
    for tick in range(len(gs) + Gather.STAGES - 1):
        for i, g in enumerate(gs):
            n = tick - i
            if 0 <= n < Gather.STAGES:
                g.stage(n)
        if tick == 2:
            tokens_forward()
    for zz in range(4):
        j = 2 * zz + lax.rem(zz + k, 2)
        remote(CM.at[j], CM.at[j], fsend.at[zz], arecv.at[1, j], dev(z, y, x, 1 - k)).wait_recv()
    for e in range(2):
        zz = lax.rem(1 - y + k, 2) + 2 * e
        remote(CA.at[zz], CA.at[zz], fsend.at[4 + e], aarecv.at[1, zz], dev(z, y, x, 1 - k)).wait_recv()
    for c in fw: c.wait()
    for cp, me in acps:
        @pl.when(jnp.logical_not(me))
        def _():
            cp.wait_send()
    pre.wait_send()


def gather_call(qkv, out, up, down, vec, xin, cin):
    D = xin.shape[-1]
    cols = (qkv.shape[1], out.shape[1], up.shape[1])
    H = sum(cols) // 2
    sd = jax.ShapeDtypeStruct
    outs = [sd((4, 2, 2, 48, n), BF) for n in cols] + [sd((4, 2, 2, 2) + down.shape, BF), sd((4, 2, 2, 2) + vec.shape, F32),
            sd((8, 128, D), BF), sd((4, 128, D), BF), sd((8, 128, D), BF), sd((4, 128, D), BF)]
    V, A = pl.BlockSpec(memory_space=pltpu.VMEM), pl.BlockSpec(memory_space=pl.ANY)
    S = pltpu.SemaphoreType.DMA
    return pl.pallas_call(
        functools.partial(gather_kernel, cols),
        out_shape=outs,
        in_specs=[V, V, V, A, A, A, A],
        out_specs=[A] * 9,
        scratch_shapes=[pltpu.VMEM((2, 24, H), F32), pltpu.VMEM((24, H), F32), pltpu.VMEM((48, H), BF),
                        S, S, S((5,)), S((5, 10)), S((5, 10)), S((2, 2, 3)), S((2, 8)), S((2, 4)), S((6,)), S((6,))],
        compiler_params=pltpu.CompilerParams(collective_id=0, has_side_effects=True, vmem_limit_bytes=32 * 2**20),
    )(qkv, out, up, down, vec, xin, cin)

EPS = 1e-5
NT = (((1,), (1,)), ((), ()))


def nt(a, b):
    return lax.dot_general(a, b, NT, preferred_element_type=F32)


def nn(a, b):
    return jnp.dot(a, b, preferred_element_type=F32)


def rope_tables():
    freq = np.exp(-math.log(10000.0) * (2.0 * np.arange(32, dtype=np.float32) / 64)).astype(np.float32)
    ang = np.arange(1024, dtype=np.float32)[:, None] * freq[None, :]
    c, s = np.cos(ang.astype(np.float64)), np.sin(ang.astype(np.float64))
    return (np.concatenate([c, c, c, c], 1).astype(np.float32), np.concatenate([-s, s, -s, s], 1).astype(np.float32))


def swap(u):
    low = lax.broadcasted_iota(jnp.int32, u.shape, 1) % 64 < 32
    return jnp.where(low, pltpu.roll(u, 96, 1), pltpu.roll(u, 32, 1))


def norm(v):
    mean = jnp.mean(v, axis=-1, keepdims=True)
    cen = v - mean
    inv = lax.rsqrt(jnp.mean(cen * cen, axis=-1, keepdims=True) + EPS)
    return cen * inv, inv


def norm_grad(e, n, inv, gain):
    g = e * gain
    return inv * (g - jnp.mean(g, axis=-1, keepdims=True) - n * jnp.mean(g * n, axis=-1, keepdims=True))


def own_block(i, k):
    return 2 * i + lax.rem(i + k, 2)


def rows(i, n=128):
    return pl.ds(pl.multiple_of(i * n, n), n)


def spread(p):
    low = lax.broadcasted_iota(jnp.int32, p.shape, 1) < 64
    zero = jnp.zeros_like(p)
    return jnp.concatenate([jnp.where(low, p, zero), jnp.where(low, zero, p)], axis=0)


def pick(o):
    low = lax.broadcasted_iota(jnp.int32, (128, 128), 0) < 64
    return jnp.where(low, o[:, :128], o[:, 128:]).T


def fill_bias(bias, is_long, k):
    at = 0
    for i in range(4):
        kk = 256 * (i + 1)
        key = lax.broadcasted_iota(jnp.int32, (kk, 256), 0)
        q = own_block(i, k) * 128 + lax.broadcasted_iota(jnp.int32, (kk, 256), 1) % 128
        first = jnp.where(is_long, 0, q - q % 256)
        bias[at:at + kk, :] = jnp.where((key <= q) & (key >= first), 0.0, -1e30)
        at += kk


def attn_fwd(flag, XM, XA, wqkv, wout, gain, shift, bqkv, bout, COS, SIN,
             acts, Q, K, V, att, lse, middle, bias, VT):
    z, y, x, k = where_am_i()
    is_long = flag[0] != 0
    fill_bias(bias, is_long, k)
    for j in range(8):
        alt = jnp.logical_and(jnp.logical_not(is_long), lax.rem(jnp.int32(j), 2) != y)
        blk = jnp.where(alt, XA[j // 2], XM[j]).astype(F32)
        n, _ = norm(blk)
        acts[j * 128:(j + 1) * 128, :] = (n * gain[...] + shift[...]).astype(BF)

    def tables(j):
        off = jnp.where(is_long, j, lax.rem(j, 2))
        return COS[rows(off), :], SIN[rows(off), :]

    @pl.loop(0, 8)
    def _(j):
        a = acts[rows(j), :]
        c, s = tables(j)
        for t in range(6):
            u = nn(a, wqkv[:, 768 + t * 128:896 + t * 128]) + bqkv[:, 768 + t * 128:896 + t * 128]
            K[rows(j), t * 128:(t + 1) * 128] = (u * c + swap(u) * s).astype(BF)
        V[rows(j), :] = (nn(a, wqkv[:, 1536:]) + bqkv[:, 1536:]).astype(BF)

    @pl.loop(0, 4)
    def _(i):
        j = own_block(i, k)
        a = acts[rows(j), :]
        c, s = tables(j)
        for t in range(6):
            u = nn(a, wqkv[:, t * 128:(t + 1) * 128]) + bqkv[:, t * 128:(t + 1) * 128]
            Q[rows(i), t * 128:(t + 1) * 128] = (u * c + swap(u) * s).astype(BF) * jnp.asarray(0.125, BF)

    @pl.loop(0, 6)
    def _(h):
        lanes = rows(h)
        VT[...] = V[:, lanes].T
        at = 0
        for i in range(4):
            kk = 256 * (i + 1)
            qb = spread(Q[i * 128:(i + 1) * 128, lanes])
            st = nt(K[0:kk, lanes], qb) + bias[at:at + kk, :]
            top = jnp.max(st, axis=0, keepdims=True)
            p = jnp.exp(st - top)
            den = jnp.sum(p, axis=0, keepdims=True)
            o = nn(VT[:, 0:kk], p.astype(BF)) * (1.0 / den)
            att[i * 128:(i + 1) * 128, lanes] = pick(o)
            lse[h, i:i + 1, :] = top + jnp.log(den)
            at += kk

    @pl.loop(0, 4)
    def _(i):
        j = own_block(i, k)
        alt = jnp.logical_and(jnp.logical_not(is_long), lax.rem(j, 2) != y)
        xb = jnp.where(alt, XA[i], XM[j]).astype(F32)
        middle[rows(i), :] = xb + (nn(att[rows(i), :].astype(BF), wout[...]) + bout[...])


def mlp(CH, flag, mix, middle, CM, CA, wup, wdown, gain, shift, bup, bdown,
        block, gmid, gup, gdown, g_gain, g_shift, g_bup, g_bdown, mixsum, acts2, actsT, dg, ga, cf):
    z, y, x, k = where_am_i()
    is_long = flag[0] != 0
    m5 = mix[5]
    for i in range(4):
        r = slice(i * 128, (i + 1) * 128)
        mid = middle[r, :]
        n, _ = norm(mid)
        acts2[r, :] = (n * gain[...] + shift[...]).astype(BF)
        j = own_block(jnp.int32(i), k)
        alt = jnp.logical_and(jnp.logical_not(is_long), lax.rem(j, 2) != y)
        c = jnp.where(alt, CA[i], CM[j]).astype(F32)
        cf[r, :] = c
        dg[r, :] = (m5 * c).astype(BF)
        block[r, :] = mid + bdown[...]
        ga[r, :] = jnp.zeros_like(mid)
        actsT[:, r] = acts2[r, :].T
    g_bdown[...] = jnp.sum(dg[...].astype(F32), axis=0, keepdims=True)

    @pl.loop(0, wup.shape[1] // CH)
    def _(f):
        cols = rows(f, CH)
        up = nn(acts2[...], wup[:, cols]) + bup[:, cols]
        half_erf = 0.5 * lax.erf(up * (2.0 ** -0.5)) + 0.5
        slope = half_erf + up * (jnp.exp(up * up * -0.5) * (1.0 / math.sqrt(2 * math.pi)))
        act = (up * half_erf).astype(BF)
        block[...] += nn(act, wdown[cols, :])
        upg = (nt(dg[...], wdown[cols, :]) * slope).astype(BF)
        g_bup[:, cols] = jnp.sum(upg.astype(F32), axis=0, keepdims=True)
        gdown[cols, :] = nn(act.T, dg[...]).astype(BF)
        gup[:, cols] = nn(actsT[...], upg).astype(BF)
        ga[...] += nt(upg, wup[:, cols])

    total = jnp.zeros((1, 768), F32)
    gg = jnp.zeros((1, 768), F32)
    gs = jnp.zeros((1, 768), F32)
    for i in range(4):
        r = slice(i * 128, (i + 1) * 128)
        n, inv = norm(middle[r, :])
        e = ga[r, :]
        gg += jnp.sum(e * n, axis=0, keepdims=True)
        gs += jnp.sum(e, axis=0, keepdims=True)
        gmid[r, :] = m5 * cf[r, :] + norm_grad(e, n, inv, gain[...])
        total += jnp.sum(cf[r, :] * block[r, :], axis=0, keepdims=True)
    g_gain[...] = gg
    g_shift[...] = gs
    mixsum[...] = total


def attn_bwd(flag, gmid, acts, Q, K, V, att, lse, wqkv, wout, COS, SIN,
             e, gqkv, gout, g_bqkv, g_bout, bias, KT, da, dQ, dK, dV, agrad, actsT, actsqT, KG, VG):
    z, y, x, k = where_am_i()
    is_long = flag[0] != 0
    fill_bias(bias, is_long, k)
    agrad[...] = gmid[...].astype(BF)
    g_bout[...] = jnp.sum(agrad[...].astype(F32), axis=0, keepdims=True)

    @pl.loop(0, 4)
    def _(i):
        da[rows(i), :] = nt(agrad[rows(i), :], wout[...]).astype(BF)

    for t in range(6):
        aT = att[:, t * 128:(t + 1) * 128].T.astype(BF)
        gout[t * 128:(t + 1) * 128, :] = nn(aT, agrad[...]).astype(BF)
    dK[...] = jnp.zeros_like(dK)
    dV[...] = jnp.zeros_like(dV)

    @pl.loop(0, 6)
    def _(h):
        lanes = rows(h)
        KT[...] = K[:, lanes].T
        at = 0
        for i in range(4):
            kk = 256 * (i + 1)
            r = slice(i * 128, (i + 1) * 128)
            d = da[r, lanes]
            qb, db = spread(Q[r, lanes]), spread(d)
            prod = (d.astype(F32) * att[r, lanes]).T
            delta = jnp.concatenate([jnp.sum(prod[:64], axis=0, keepdims=True), jnp.sum(prod[64:], axis=0, keepdims=True)], axis=1)
            st = nt(K[0:kk, lanes], qb) + bias[at:at + kk, :]
            p = jnp.exp(st - lse[h, i:i + 1, :])
            ds = (p * (nt(V[0:kk, lanes], db) - delta)).astype(BF)
            dV[0:kk, lanes] += nn(p.astype(BF), db)
            dK[0:kk, lanes] += nn(ds, qb)
            dQ[r, lanes] = pick(nn(KT[:, 0:kk], ds)) * 0.125
            at += kk

    def tables(j):
        off = jnp.where(is_long, j, lax.rem(j, 2))
        return COS[rows(off), :], SIN[rows(off), :]

    for j in range(8):
        actsT[:, j * 128:(j + 1) * 128] = acts[j * 128:(j + 1) * 128, :].T
    for i in range(4):
        j = own_block(jnp.int32(i), k)
        actsqT[:, i * 128:(i + 1) * 128] = acts[rows(j), :].T
        c, s = tables(j)
        for t in range(6):
            u = dQ[i * 128:(i + 1) * 128, t * 128:(t + 1) * 128]
            da[i * 128:(i + 1) * 128, t * 128:(t + 1) * 128] = (u * c - swap(u) * s).astype(BF)

    @pl.loop(0, 8)
    def _(j):
        c, s = tables(j)
        for t in range(6):
            u = dK[rows(j), t * 128:(t + 1) * 128]
            KG[rows(j), t * 128:(t + 1) * 128] = (u * c - swap(u) * s).astype(BF)
        VG[rows(j), :] = dV[rows(j), :].astype(BF)
        e[rows(j), :] = nt(KG[rows(j), :], wqkv[:, 768:1536]) + nt(VG[rows(j), :], wqkv[:, 1536:])

    @pl.loop(0, 4)
    def _(i):
        j = own_block(i, k)
        e[rows(j), :] += nt(da[rows(i), :], wqkv[:, :768])

    g_bqkv[:, :768] = jnp.sum(da[...].astype(F32), axis=0, keepdims=True)
    g_bqkv[:, 768:1536] = jnp.sum(KG[...].astype(F32), axis=0, keepdims=True)
    g_bqkv[:, 1536:] = jnp.sum(VG[...].astype(F32), axis=0, keepdims=True)

    @pl.loop(0, 6)
    def _(t):
        gqkv[rows(t), :768] = nn(actsqT[rows(t), :], da[...]).astype(BF)
        gqkv[rows(t), 768:1536] = nn(actsT[rows(t), :], KG[...]).astype(BF)
        gqkv[rows(t), 1536:] = nn(actsT[rows(t), :], VG[...]).astype(BF)


sd = jax.ShapeDtypeStruct
VM = pltpu.VMEM
vs = pl.BlockSpec(memory_space=pltpu.VMEM)
ss = pl.BlockSpec(memory_space=pltpu.SMEM)
CP = pltpu.CompilerParams(vmem_limit_bytes=60 * 2**20)


def attn_fwd_call(flag, *ins):
    return pl.pallas_call(attn_fwd,
        out_shape=[sd((1024, 768), BF), sd((512, 768), BF), sd((1024, 768), BF), sd((1024, 768), BF),
                   sd((512, 768), F32), sd((6, 4, 256), F32), sd((512, 768), F32)],
        in_specs=[ss] + [vs] * len(ins), out_specs=[vs] * 7,
        scratch_shapes=[VM((2560, 256), F32), VM((128, 1024), BF)],
        compiler_params=CP)(flag, *ins)


def mlp_call(flag, mix, *ins):
    r = sd((1, 768), F32)
    return pl.pallas_call(functools.partial(mlp, 512),
        out_shape=[sd((512, 768), F32), sd((512, 768), F32), sd((768, 3072), BF), sd((3072, 768), BF), r, r, sd((1, 3072), F32), r, r],
        in_specs=[ss, ss] + [vs] * len(ins), out_specs=[vs] * 9,
        scratch_shapes=[VM((512, 768), BF), VM((768, 512), BF), VM((512, 768), BF), VM((512, 768), F32), VM((512, 768), F32)],
        compiler_params=CP)(flag, mix, *ins)


def attn_bwd_call(flag, *ins):
    return pl.pallas_call(attn_bwd,
        out_shape=[sd((1024, 768), F32), sd((768, 2304), BF), sd((768, 768), BF), sd((1, 2304), F32), sd((1, 768), F32)],
        in_specs=[ss] + [vs] * len(ins), out_specs=[vs] * 5,
        scratch_shapes=[VM((2560, 256), F32), VM((128, 1024), BF), VM((512, 768), BF), VM((512, 768), F32), VM((1024, 768), F32),
                        VM((1024, 768), F32), VM((512, 768), BF), VM((768, 1024), BF), VM((768, 512), BF), VM((1024, 768), BF), VM((1024, 768), BF)],
        compiler_params=CP)(flag, *ins)


VROWS = (24, 24, 72, 24, 24, 24, 96, 24)


def widen(vecs, row, n):
    v = vecs[:, row, :].astype(BF)
    wide = 32 * n
    j = lax.broadcasted_iota(jnp.int32, (128, wide), 1)
    i = lax.broadcasted_iota(jnp.int32, (128, wide), 0)
    q = jnp.floor((j.astype(F32) + 0.5) * (1.0 / n)).astype(jnp.int32)
    hot = jnp.where(j - q * n == i, 1.0, 0.0).astype(BF)
    full = nn(v, hot)
    d = lax.broadcasted_iota(jnp.int32, (32, wide), 0)
    return jnp.sum(jnp.where(q[:32] == d, full, 0.0), axis=0, keepdims=True)


def lane(tile, row, at):
    r = lax.broadcasted_iota(jnp.int32, tile.shape, 0)
    c = lax.broadcasted_iota(jnp.int32, tile.shape, 1)
    v = jnp.sum(jnp.where((r == row) & (c == at), tile, 0.0), axis=1, keepdims=True)
    return jnp.sum(v, axis=0, keepdims=True)


def longer(length, shape):
    return jnp.broadcast_to(length, shape) > 512.0


def bias_rows(bias, length, k):
    at = 0
    for i in range(4):
        kk = 256 * (i + 1)
        key = lax.broadcasted_iota(jnp.int32, (kk, 256), 0)
        q = own_block(i, k) * 128 + lax.broadcasted_iota(jnp.int32, (kk, 256), 1) % 128
        first = jnp.where(longer(length, (kk, 256)), 0, q - q % 256)
        bias[at:at + kk, :] = jnp.where((key <= q) & (key >= first), 0.0, -1e30)
        at += kk


def table_rows(COS, SIN, length, j):
    far = longer(length, (128, 128))
    near = lax.rem(j, 2)
    return (jnp.where(far, COS[rows(j), :], COS[rows(near), :]), jnp.where(far, SIN[rows(j), :], SIN[rows(near), :]))


def matrix(W, cols):
    w = W[:, :, :, :, cols]
    return w.reshape(768, w.shape[-1])


def forward_kernel(cols, qkv, out, up, down, vec, xin, cin, COS, SIN, mix,
                   oX, oacts, oQ, oK, oV, oatt, olse, oWQ, oWO, oblock, ogmid, ogup, ogdown, ogain, vgrad,
                   f_own, f_sib, block_w, WQ, WO, WU, WD, VEC, X, C, NB, SB,
                   acts, Q, K, V, att, lse, middle, bias, VT, act, slope, block, ga, acts2, actsT, dg, gup, gdown, a1T, bl,
                   vq, vg, vu,
                   psend, precv, lsem, gsend, grecv, asend, arecv, nsend, nrecv, fsend, frecv, xsem, csem):
    pos = z, y, x, k = where_am_i()
    sib = dev(z, y, x, 1 - k)
    greet(z, y, x, k)
    s = 2 * z + y
    own_s = lax.rem(y + z, 2)
    def neighbour(a, src):
        cps = []
        for i in range(2):
            hi = src.at[i, pl.ds(pl.multiple_of((1 - y) * 128, 128), 128)]
            cp = remote(hi, NB.at[a, i], nsend.at[a, i], nrecv.at[a, i], dev(z, 1 - y, x, k))
            cp.start()
            cps.append(cp)
        return cps

    tokens = []
    def along_z(a, i, n, ref, dst, core):
        g = 2 * k + i
        me = (g == z) & (core == k)
        cp = remote(ref, dst, asend.at[a, i, n], arecv.at[a, z], dev(g, y, x, core))
        @pl.when(me)
        def _():
            pltpu.make_async_copy(ref, dst, arecv.at[a, z]).start()
        @pl.when(jnp.logical_not(me))
        def _():
            cp.start()
        tokens.append((cp, jnp.logical_not(me)))

    def straight(a, src, dst):
        for i in range(2):
            along_z(a, i, 0, src.at[i, pl.ds(pl.multiple_of(y * 128, 128), 128)], dst(s), own_s)

    def crossed(a, src, dst, cps):
        for i in range(2):
            cps[i].wait_recv()
            mine = src[i, pl.ds(pl.multiple_of((1 - y) * 128, 128), 128), :]
            far = longer(lane(vec[...], 0, 64 + i), (128, 768))
            SB[a, i] = jnp.where(far, NB[a, i].astype(F32), mine.astype(F32)).astype(BF)
            along_z(a, i, 1, SB.at[a, i], dst(s + 1 - 2 * y), 1 - own_s)

    def arrived(a, dst, i):
        remote(dst, dst, asend.at[a, 0, 0], arecv.at[a, i], sib).wait_recv()

    to_x = lambda j: X.at[j]
    to_c = lambda j: C.at[j // 2]
    nx = neighbour(0, xin)
    at, offs = 0, []
    for n, ref in zip(cols, (qkv, out, up)):
        half = n // 2
        f_own[0, :, at:at + half] = ref[:, :half].astype(F32)
        f_own[1, :, at:at + half] = ref[:, half:].astype(F32)
        offs.append((at, half))
        at += half
    pre = remote(f_own.at[1 - k], f_sib, psend, precv, sib)
    pre.start()
    straight(0, xin, to_x)
    lcs = [pltpu.make_async_copy(down, WD.at[z, y, x, k], lsem.at[3]), pltpu.make_async_copy(vec, VEC.at[z, y, x, k], lsem.at[4])]
    for c in lcs: c.start()
    pre.wait_recv()
    for i, ((at, half), W) in enumerate(zip(offs, (WQ, WO, WU))):
        mine = f_own[k, :, at:at + half]
        theirs = f_sib[:, at:at + half]
        block_w[:, at:at + half] = jnp.concatenate([jnp.where(k == 0, mine, theirs), jnp.where(k == 0, theirs, mine)], axis=0).astype(BF)
        c = pltpu.make_async_copy(block_w.at[:, at:at + half], W.at[z, y, x, :, pl.ds(pl.multiple_of(k * half, 128), half)], lsem.at[i])
        c.start(); lcs.append(c)

    def colpart(W, half):
        return lambda zz, yy, xx, kk: W.at[zz, yy, xx, :, pl.ds(pl.multiple_of(kk * half, 128), half)]
    def rowpart(W):
        return lambda zz, yy, xx, kk: W.at[zz, yy, xx, kk]
    for c in lcs: c.wait()
    G = [Gather(p, gsend.at[i], grecv.at[i], pos) for i, p in enumerate(
        [rowpart(VEC), colpart(WQ, offs[0][1]), colpart(WO, offs[1][1]), colpart(WU, offs[2][1]), rowpart(WD)])]
    gv, gq, go, gu, gd = G
    gv.stage(0); gq.stage(0)
    crossed(0, xin, to_x, nx)
    nc = neighbour(1, cin)
    gv.stage(1); gq.stage(1)
    gv.stage(2)
    go.stage(0)
    fw = []
    def forward_x(i):
        j = own_block(jnp.int32(i), k)
        arrived(0, X.at[j], i)
        cp = remote(X.at[j], X.at[j], fsend.at[i], frecv.at[i], sib)
        cp.start(); fw.append(cp)
    gv.stage(3)
    gq.stage(2)
    gv.stage(4); gv.stage(5)
    gu.stage(0)
    for i in range(4): forward_x(i)
    tiles = VEC[...].reshape(32, 8, 128)
    at = 0
    length = lane(VEC[0, 0, x, z // 2], 0, 64 + lax.rem(z, 2))
    vq[...] = widen(tiles, 2, 72)
    vu[...] = widen(tiles, 6, 96)
    for n, r in enumerate((0, 1, 3, 4, 5, 7)):
        vg[n:n + 1, :] = widen(tiles, r, 24)
    a_gain, a_shift, bout, m_gain, m_shift, bdown = (vg[n:n + 1, :] for n in range(6))
    bias_rows(bias, length, k)
    go.stage(1)
    gq.stage(3)
    gq.stage(4)
    straight(1, cin, to_c)
    crossed(1, cin, to_c, nc)
    for i in range(4): fw[i].wait_recv()
    for j in range(8):
        n, _ = norm(X[j].astype(F32))
        acts[j * 128:(j + 1) * 128, :] = (n * a_gain + a_shift).astype(BF)
    gq.stage(5)
    go.stage(2)
    gu.stage(1)
    gd.stage(0)
    exports = []
    def export(ref, dst):
        c = pltpu.make_async_copy(ref, dst, xsem.at[len(exports)])
        c.start(); exports.append(c)

    def keys(j):
        a = acts[rows(j), :]
        c, sn = table_rows(COS, SIN, length, j)
        for t in range(3):
            u2 = nn(a, matrix(WQ, slice(768 + t * 256, 1024 + t * 256))) + vq[:, 768 + t * 256:1024 + t * 256]
            for h in range(2):
                u = u2[:, h * 128:(h + 1) * 128]
                K[rows(j), t * 256 + h * 128:t * 256 + (h + 1) * 128] = (u * c + swap(u) * sn).astype(BF)
        V[rows(j), :] = (nn(a, matrix(WQ, slice(1536, 2304))) + vq[:, 1536:]).astype(BF)

    pl.loop(0, 4)(keys)
    go.stage(3); gu.stage(2)
    pl.loop(4, 8)(keys)
    go.stage(4)

    @pl.loop(0, 4)
    def _(i):
        j = own_block(i, k)
        a = acts[rows(j), :]
        c, sn = table_rows(COS, SIN, length, j)
        for t in range(3):
            u2 = nn(a, matrix(WQ, slice(t * 256, 256 + t * 256))) + vq[:, t * 256:256 + t * 256]
            for h in range(2):
                u = u2[:, h * 128:(h + 1) * 128]
                Q[rows(i), t * 256 + h * 128:t * 256 + (h + 1) * 128] = (u * c + swap(u) * sn).astype(BF) * jnp.asarray(0.125, BF)
    gu.stage(3)
    gd.stage(1)
    for i in range(4):
        j = own_block(jnp.int32(i), k)
        export(X.at[j], oX.at[i])
    for j in range(8):
        a1T[:, j * 128:(j + 1) * 128] = acts[j * 128:(j + 1) * 128, :].T
    export(a1T, oacts); export(Q, oQ); export(K, oK); export(V, oV)
    export(WQ, oWQ)

    def heads(h):
        lanes = rows(h)
        VT[...] = V[:, lanes].T
        at = 0
        for i in range(4):
            kk = 256 * (i + 1)
            qb = spread(Q[i * 128:(i + 1) * 128, lanes])
            st = nt(K[0:kk, lanes], qb) + bias[at:at + kk, :]
            top = jnp.max(st, axis=0, keepdims=True)
            p = jnp.exp(st - top)
            den = jnp.sum(p, axis=0, keepdims=True)
            o = nn(VT[:, 0:kk], p.astype(BF)) * (1.0 / den)
            att[i * 128:(i + 1) * 128, lanes] = pick(o)
            lse[h, i:i + 1, :] = top + jnp.log(den)
            at += kk

    pl.loop(0, 2)(heads)
    gu.stage(4); go.stage(5)
    export(WO, oWO)
    pl.loop(2, 4)(heads)
    gd.stage(2)
    pl.loop(4, 6)(heads)
    gd.stage(3)
    export(att, oatt); export(lse, olse)

    @pl.loop(0, 4)
    def _(i):
        j = own_block(i, k)
        middle[rows(i), :] = X[j].astype(F32) + (nn(att[rows(i), :].astype(BF), WO[...].reshape(768, 768)) + bout)
    m5 = mix[5]
    for i in range(4):
        arrived(1, C.at[i], i)
        r = slice(i * 128, (i + 1) * 128)
        mid = middle[r, :]
        n, _ = norm(mid)
        a2 = (n * m_gain + m_shift).astype(BF)
        acts2[r, :] = a2
        actsT[:, r] = a2.T
        dg[r, :] = (m5 * C[i].astype(F32)).astype(BF)
        block[r, :] = mid + bdown
        ga[r, :] = jnp.zeros_like(mid)
    gu.stage(5)
    gd.stage(4)
    vgrad[...] = jnp.zeros_like(vgrad)

    def put_vec(row, v):
        for t in range(v.shape[1] // 128):
            vgrad[row + t:row + t + 1, :] = v[:, t * 128:(t + 1) * 128]
    put_vec(72, jnp.sum(dg[...].astype(F32), axis=0, keepdims=True))

    @pl.loop(0, 8)
    def _(f):
        c = rows(f, 384)
        u = nn(acts2[...], matrix(WU, c)) + vu[:, c]
        half_erf = 0.5 * lax.erf(u * (2.0 ** -0.5)) + 0.5
        slope[:, c] = half_erf + u * (jnp.exp(u * u * -0.5) * (1.0 / math.sqrt(2 * math.pi)))
        act[:, c] = (u * half_erf).astype(BF)
    gd.stage(5)

    @pl.loop(0, 4)
    def _(f):
        c = rows(f, 768)
        wd = WD[f].reshape(768, 768)
        a = act[:, c]
        block[...] += nn(a, wd)
        upg = (nt(dg[...], wd) * slope[:, c]).astype(BF)
        g = jnp.sum(upg.astype(F32), axis=0, keepdims=True)
        for t in range(6):
            vgrad[pl.ds(48 + f * 6 + t, 1), :] = g[:, t * 128:(t + 1) * 128]
        gdown[c, :] = nn(a.T, dg[...]).astype(BF)
        pltpu.make_async_copy(gdown.at[c, :], ogdown.at[c, :], csem.at[0, f]).start()
        gup[:, c] = nn(actsT[...], upg).astype(BF)
        pltpu.make_async_copy(gup.at[:, c], ogup.at[:, c], csem.at[1, f]).start()
        ga[...] += nt(upg, matrix(WU, c))

    total = jnp.zeros((1, 768), F32)
    gg = jnp.zeros((1, 768), F32)
    gs = jnp.zeros((1, 768), F32)
    for i in range(4):
        r = slice(i * 128, (i + 1) * 128)
        n, inv = norm(middle[r, :])
        e = ga[r, :]
        cf = C[i].astype(F32)
        gg += jnp.sum(e * n, axis=0, keepdims=True)
        gs += jnp.sum(e, axis=0, keepdims=True)
        ga[r, :] = m5 * cf + norm_grad(e, n, inv, m_gain)
        total += jnp.sum(cf * block[r, :], axis=0, keepdims=True)
        bl[i] = block[r, :].astype(BF)
    put_vec(36, gg); put_vec(42, gs)
    ogain[...] = jnp.broadcast_to(a_gain, (8, 768))
    whole = jnp.sum(total, axis=1, keepdims=True)
    vgrad[78:79, :] = jnp.where(lax.broadcasted_iota(jnp.int32, (1, 128), 1) == 5, jnp.broadcast_to(whole, (1, 128)), 0.0)
    vgrad[79:80, :] = jnp.broadcast_to(length, (1, 128))
    export(ga, ogmid); export(bl, oblock)
    for f in range(4):
        c = slice(f * 768, (f + 1) * 768)
        pltpu.make_async_copy(gdown.at[c, :], ogdown.at[c, :], csem.at[0, f]).wait()
        pltpu.make_async_copy(gup.at[:, c], ogup.at[:, c], csem.at[1, f]).wait()
    for c in exports: c.wait()
    for c in fw + nx + nc: c.wait_send()
    for cp, cond in tokens:
        @pl.when(cond)
        def _():
            cp.wait_send()
    pre.wait_send()


def forward_call(qkv, out, up, down, vec, xin, cin, COS, SIN, mix):
    cols = (qkv.shape[1], out.shape[1], up.shape[1])
    H = sum(cols) // 2
    any_ = pl.BlockSpec(memory_space=pl.ANY)
    T = lambda n, t=BF: ((n, 768), t)
    shapes = [((4, 128, 768), BF), ((768, 1024), BF), T(512), T(1024), T(1024), T(512, F32), ((6, 4, 256), F32),
              ((4, 2, 2, 48, 2304), BF), ((4, 2, 2, 48, 768), BF), ((4, 128, 768), BF), T(512, F32), ((768, 3072), BF), T(3072)]
    DS = pltpu.SemaphoreType.DMA
    return pl.pallas_call(functools.partial(forward_kernel, cols),
        out_shape=[sd(*t) for t in shapes] + [sd((8, 768), F32), sd((80, 128), F32)],
        in_specs=[vs] * 9 + [ss], out_specs=[any_] * len(shapes) + [vs, vs],
        scratch_shapes=[VM((2, 24, H), F32), VM((24, H), F32), VM((48, H), BF),
                        VM((4, 2, 2, 48, 2304), BF), VM((4, 2, 2, 48, 768), BF), VM((4, 2, 2, 48, 3072), BF), VM((4, 2, 2, 2, 96, 768), BF),
                        VM((4, 2, 2, 2, 8, 128), F32), VM((8, 128, 768), BF), VM((4, 128, 768), BF), VM((2, 2, 128, 768), BF), VM((2, 2, 128, 768), BF),
                        VM((1024, 768), BF), VM((512, 768), BF), VM((1024, 768), BF), VM((1024, 768), BF), VM((512, 768), F32),
                        VM((6, 4, 256), F32), VM((512, 768), F32), VM((2560, 256), F32), VM((128, 1024), BF),
                        VM((512, 3072), BF), VM((512, 3072), F32), VM((512, 768), F32), VM((512, 768), F32), VM((512, 768), BF),
                        VM((768, 512), BF), VM((512, 768), BF), VM((768, 3072), BF), VM((3072, 768), BF), VM((768, 1024), BF), VM((4, 128, 768), BF),
                        VM((1, 2304), F32), VM((8, 768), F32), VM((1, 3072), F32),
                        DS, DS, DS((5,)), DS((5, 10)), DS((5, 10)), DS((2, 2, 2)), DS((2, 4)), DS((2, 2)), DS((2, 2)), DS((4,)), DS((4,)),
                        DS((16,)), DS((2, 4))],
        compiler_params=pltpu.CompilerParams(collective_id=0, has_side_effects=True, vmem_limit_bytes=63 * 2**20),
    )(qkv, out, up, down, vec, xin, cin, COS, SIN, mix)


class Scatter:
    STAGES = 6

    def __init__(self, mine, theirs, RA, RB, RC, RZ, put, finish, send, recv, pos, load=None):
        self.mine, self.RA, self.RB, self.RC, self.RZ, self.put, self.finish, self.pos, self.load = mine, RA, RB, RC, RZ, put, finish, pos, load
        z, y, x, k = pos
        self.own = (y, x)
        self.p2 = jnp.where(k == 0, 1 - y, y), jnp.where(k == 0, x, 1 - x)
        self.p3 = jnp.where(k == 0, y, 1 - y), jnp.where(k == 0, 1 - x, x)
        self.d4 = 1 - y, 1 - x
        blk = lambda yx: mine(slice(None), yx[0], yx[1])
        n3, n2 = dev(z, *self.p3, k), dev(z, *self.p2, k)
        self.pre = remote(theirs, RA, send.at[0], recv.at[0], dev(z, y, x, 1 - k))
        self.b1 = remote(blk(self.d4), RB.at[1], send.at[1], recv.at[1], n3)
        self.b0 = remote(blk(self.p3), RB.at[0], send.at[2], recv.at[2], n3)
        self.c = remote(blk(self.p2), RC, send.at[3], recv.at[3], n2)
        self.zs = [remote(mine(lax.rem(z + d, 4), y, x), RZ.at[d - 1], send.at[3 + d], recv.at[3 + d],
                          dev(lax.rem(z + d, 4), y, x, k)) for d in (1, 2, 3)]
        self.sends = [self.pre, self.b1, self.b0, self.c] + self.zs

    def add(self, yx, other):
        @pl.loop(0, 4)
        def _(i):
            ref = self.mine(i, yx[0], yx[1])
            ref[...] = (ref[...].astype(F32) + other[i].astype(F32)).astype(BF)

    def first(self, yx):
        self.add(yx, self.RA.at[:, yx[0], yx[1]])

    def stage(self, n):
        z, y, x, k = self.pos
        if n == 0:
            if self.load is not None: self.load.start()
            self.pre.start()
        elif n == 1:
            self.pre.wait_recv()
            if self.load is not None: self.load.wait()
            self.first(self.d4)
            self.b1.start()
            self.first(self.p3)
            self.b0.start()
            self.first(self.p2)
            self.first(self.own)
        elif n == 2:
            self.b1.wait_recv()
            self.add(self.p2, self.RB.at[1])
            self.c.start()
            self.b0.wait_recv()
            self.add(self.own, self.RB.at[0])
        elif n == 3:
            self.c.wait_recv()
            self.add(self.own, self.RC)
            for c in self.zs: c.start()
        elif n == 4:
            for c in self.zs: c.wait_recv()
            tot = self.mine(z, y, x)[...].astype(F32)
            for i in range(3):
                tot = tot + self.RZ[i].astype(F32)
            self.put(tot)
        elif n == 5:
            self.finish()
            for c in self.sends: c.wait_send()


def backward_kernel(gup, gdown, block, gmid, X, actsT, Q, Kin, Vin, att, lse, WQ, WO, gain, COS, SIN, vin,
                    oq, oo, ou, od, vout, H0, HL, HS,
                    K, V, bias, KT, da, dQ, dK, dV, agrad, actsqT, GO, GQ, PU, PD,
                    AU, BU, CU, ZU, AD, BD, CD, ZD, AO, BO, CO, ZO, AQ, BQ, CQ, ZQ,
                    fin, fsib, finu, fsibu, es, er, gx, vbuf, vrec,
                    ssem, rsem, ldsem, fsend, frecv, hsend, h0, hl, hs, nsend, esem_s, esem_r, vsend, vrecv, csem):
    pos = z, y, x, k = where_am_i()
    sib = dev(z, y, x, 1 - k)
    greet(z, y, x, k)
    length = vin[79:80, 0:1]
    ck = pltpu.make_async_copy(Kin, K, csem.at[0])
    cv = pltpu.make_async_copy(Vin, V, csem.at[1])
    ck.start(); cv.start()
    half_of = lambda kk, half: pl.ds(pl.multiple_of(kk * half, 128), half)

    def col_scatter(a, G, half, bufs, n, out, at, width, fi, fs, hbm=None):
        def put(t):
            fi[n, 0] = t[:24]
            fi[n, 1] = t[24:]
            last.start()
        last = remote(fi.at[n, 1 - k], fs.at[n], fsend.at[a], frecv.at[a], sib)
        def finish():
            last.wait_recv()
            mine, theirs = fi[n, k], fs[n]
            out[:, at:at + half] = jnp.where(k == 0, mine, theirs)
            out[:, at + half:at + 2 * half] = jnp.where(k == 0, theirs, mine)
            last.wait_send()
        if hbm is None:
            mine = lambda zz, yy, xx: G.at[zz, yy, xx, :, half_of(k, half)]
            theirs = G.at[:, :, :, :, half_of(1 - k, half)]
            load = None
        else:
            mine = lambda zz, yy, xx: G.at[zz, yy, xx]
            theirs = hbm.at[:, :, :, :, half_of(1 - k, half)]
            load = pltpu.make_async_copy(hbm.at[:, :, :, :, half_of(k, half)], G, ldsem.at[a])
        return Scatter(mine, theirs, *bufs, put, finish, ssem.at[a], rsem.at[a], pos, load)

    def put_down(t):
        od[...] = t
    sdn = Scatter(lambda zz, yy, xx: PD.at[zz, yy, xx], gdown.at[:, :, :, 1 - k], AD, BD, CD, ZD, put_down, lambda: None,
                  ssem.at[0], rsem.at[0], pos, pltpu.make_async_copy(gdown.at[:, :, :, k], PD, ldsem.at[0]))
    sup = col_scatter(1, PU, 1536, (AU, BU, CU, ZU), 0, ou, 0, 3072, finu, fsibu, gup)
    sout = col_scatter(2, GO, 384, (AO, BO, CO, ZO), 0, oo, 0, 768, fin, fsib)
    sq, sk, sv = (col_scatter(3 + n, GQ.at[n], 384, (AQ.at[n], BQ.at[n], CQ.at[n], ZQ.at[n]), 1 + n, oq, 768 * n, 768, fin, fsib)
                  for n in range(3))
    sdn.stage(0); sup.stage(0)

    homes = []
    def send_home(a, buf):
        slot = lax.rem(z, 2)
        for i in range(4):
            j = own_block(jnp.int32(i), k)
            straight = lax.rem(j, 2) == y
            me = (i == z) & (z // 2 == k)
            for n, (dst, rs, cond) in enumerate(((H0.at[a, slot], h0.at[a, slot], straight),
                                                 (HS.at[a, slot], hs.at[a, slot], jnp.logical_not(straight)))):
                cp = remote(buf.at[i], dst, hsend.at[a, i, n], rs, dev(jnp.int32(i), y, x, z // 2))
                @pl.when(cond & me)
                def _():
                    pltpu.make_async_copy(buf.at[i], dst, rs).start()
                @pl.when(cond & jnp.logical_not(me))
                def _():
                    cp.start()
                homes.append((cp, cond & jnp.logical_not(me)))

    across = []
    def home_across(a):
        for i in range(2):
            remote(HS.at[a, i], HS.at[a, i], nsend.at[a, i], hs.at[a, i], sib).wait_recv()
            cp = remote(HS.at[a, i], HL.at[a, i], nsend.at[a, i], hl.at[a, i], dev(z, 1 - y, x, k))
            cp.start(); across.append(cp)

    def home_done(a):
        for i in range(2):
            remote(H0.at[a, i], H0.at[a, i], nsend.at[a, i], h0.at[a, i], sib).wait_recv()
            remote(HL.at[a, i], HL.at[a, i], nsend.at[a, i], hl.at[a, i], sib).wait_recv()

    bias_rows(bias, length, k)
    agrad[...] = gmid[...].astype(BF)
    vbuf[0] = vin[...]

    def put_vec(row, v):
        for t in range(v.shape[1] // 128):
            vbuf[0, row + t:row + t + 1, :] = v[:, t * 128:(t + 1) * 128]
    put_vec(30, jnp.sum(agrad[...].astype(F32), axis=0, keepdims=True))
    wo = lambda: WO[...].reshape(768, 768)

    @pl.loop(0, 4)
    def _(i):
        da[rows(i), :] = nt(agrad[rows(i), :], wo()).astype(BF)
        actsqT[:, rows(i)] = actsT[:, rows(own_block(i, k))]

    sdn.stage(1)
    send_home(0, block)
    attT = lambda t: att[:, t * 192:(t + 1) * 192]

    def out_rows(t):
        aT = att[:, t * 384:(t + 1) * 384].T.astype(BF)
        g = nn(aT, agrad[...]).astype(BF)
        GO[2 * t:2 * t + 2] = g.reshape(2, 2, 2, 48, 768)
    for t in range(2): out_rows(t)
    sup.stage(1)
    sout.stage(0)
    dK[...] = jnp.zeros_like(dK)
    dV[...] = jnp.zeros_like(dV)
    ck.wait(); cv.wait()

    def heads(h):
        lanes = rows(h)
        KT[...] = K[:, lanes].T
        at = 0
        for i in range(4):
            kk = 256 * (i + 1)
            r = slice(i * 128, (i + 1) * 128)
            d = da[r, lanes]
            qb, db = spread(Q[r, lanes]), spread(d)
            prod = (d.astype(F32) * att[r, lanes]).T
            delta = jnp.concatenate([jnp.sum(prod[:64], axis=0, keepdims=True), jnp.sum(prod[64:], axis=0, keepdims=True)], axis=1)
            st = nt(K[0:kk, lanes], qb) + bias[at:at + kk, :]
            p = jnp.exp(st - lse[h, i:i + 1, :])
            ds = (p * (nt(V[0:kk, lanes], db) - delta)).astype(BF)
            dV[0:kk, lanes] += nn(p.astype(BF), db)
            dK[0:kk, lanes] += nn(ds, qb)
            dQ[r, lanes] = pick(nn(KT[:, 0:kk], ds)) * 0.125
            at += kk

    pl.loop(0, 1)(heads)
    sdn.stage(2)
    pl.loop(1, 2)(heads)
    sout.stage(1)
    home_across(0)
    pl.loop(2, 3)(heads)
    sdn.stage(3)
    sup.stage(2)
    pl.loop(3, 4)(heads)
    sout.stage(2)
    pl.loop(4, 5)(heads)
    sdn.stage(4)
    sup.stage(3)
    sout.stage(3)
    pl.loop(5, 6)(heads)
    V[...] = dV[...].astype(BF)
    put_vec(24, jnp.sum(V[...].astype(F32), axis=0, keepdims=True))

    def weight_rows(n, lhs, g):
        @pl.loop(0, 4)
        def _(t):
            GQ[n, t] = nn(lhs[rows(t, 192), :], g[...]).astype(BF).reshape(2, 2, 48, 768)
    weight_rows(2, actsT, V)
    sv.stage(0)

    @pl.loop(0, 8)
    def _(j):
        c, s = table_rows(COS, SIN, length, j)
        for t in range(6):
            u = dK[rows(j), t * 128:(t + 1) * 128]
            K[rows(j), t * 128:(t + 1) * 128] = (u * c - swap(u) * s).astype(BF)
        dK[rows(j), :] = nt(K[rows(j), :], matrix(WQ, slice(768, 1536))) + nt(V[rows(j), :], matrix(WQ, slice(1536, 2304)))

    @pl.loop(0, 4)
    def _(i):
        j = own_block(i, k)
        c, s = table_rows(COS, SIN, length, j)
        for t in range(6):
            u = dQ[rows(i), t * 128:(t + 1) * 128]
            da[rows(i), t * 128:(t + 1) * 128] = (u * c - swap(u) * s).astype(BF)
        dK[rows(j), :] += nt(da[rows(i), :], matrix(WQ, slice(0, 768)))
        es[i] = dK[rows(own_block(i, 1 - k)), :].astype(BF)

    ecp = remote(es, er, esem_s, esem_r, sib)
    ecp.start()
    put_vec(18, jnp.sum(K[...].astype(F32), axis=0, keepdims=True))
    put_vec(12, jnp.sum(da[...].astype(F32), axis=0, keepdims=True))
    sv.stage(1)
    weight_rows(1, actsT, K)
    sk.stage(0)
    ecp.wait_recv()
    gg = jnp.zeros((1, 768), F32)
    gsh = jnp.zeros((1, 768), F32)
    for i in range(4):
        n, inv = norm(X[i].astype(F32))
        ee = dK[rows(own_block(jnp.int32(i), k)), :] + er[i].astype(F32)
        gg += jnp.sum(ee * n, axis=0, keepdims=True)
        gsh += jnp.sum(ee, axis=0, keepdims=True)
        gx[i] = (gmid[i * 128:(i + 1) * 128, :] + norm_grad(ee, n, inv, gain[0:1, :])).astype(BF)
    send_home(1, gx)
    put_vec(0, gg); put_vec(6, gsh)

    vec_steps = [[sib], [dev(z, *sq.p2, k)], [dev(z, *sq.p3, k)], [dev(lax.rem(z + d, 4), y, x, k) for d in (1, 2, 3)]]
    vcp = []
    def vec_stage(n):
        if n > 0:
            for c in vcp[-1]: c.wait_recv()
            t = vbuf[n - 1]
            for r in range(len(vcp[-1])):
                t = t + vrec[n - 1 + r]
            if n < 4: vbuf[n] = t
            else: vout[...] = t
        if n < 4:
            vcp.append([remote(vbuf.at[n], vrec.at[n + i], vsend.at[n + i], vrecv.at[n + i], d) for i, d in enumerate(vec_steps[n])])
            for c in vcp[-1]: c.start()

    vec_stage(0)
    weight_rows(0, actsqT, da)
    sq.stage(0)
    sk.stage(1)
    sv.stage(2)
    sq.stage(1)
    sup.stage(4)
    sout.stage(4)
    vec_stage(1)
    home_across(1)
    sk.stage(2)
    sv.stage(3)
    sq.stage(2)
    vec_stage(2)
    sdn.stage(5); sout.stage(5); sup.stage(5)
    sk.stage(3)
    sq.stage(3)
    vec_stage(3)
    sv.stage(4)
    sk.stage(4)
    sq.stage(4)
    vec_stage(4)
    home_done(0)
    sv.stage(5); sk.stage(5); sq.stage(5)
    home_done(1)
    ecp.wait_send()
    for cs in vcp:
        for c in cs: c.wait_send()
    for c in across: c.wait_send()
    for cp, cond in homes:
        @pl.when(cond)
        def _():
            cp.wait_send()


def backward_call(gup, gdown, block, *ins):
    n_up = gup.shape[1]
    gup = gup.reshape(4, 2, 2, 48, n_up)
    gdown = gdown.reshape(4, 2, 2, 2, 96, 768)
    any_ = pl.BlockSpec(memory_space=pl.ANY)
    def bufs(r, n, lead=()):
        return [VM(lead + s + (r, n), BF) for s in ((4, 2, 2), (2, 4), (4,), (3,))]
    DS = pltpu.SemaphoreType.DMA
    home = sd((2, 2, 128, 768), BF)
    return pl.pallas_call(backward_kernel,
        out_shape=[sd((24, 2304), F32), sd((24, 768), F32), sd((24, 3072), F32), sd((96, 768), F32), sd((80, 128), F32), home, home, home],
        in_specs=[any_] * 3 + [vs] * 4 + [any_] * 2 + [vs] * 8, out_specs=[vs] * 5 + [any_] * 3,
        scratch_shapes=[VM((1024, 768), BF), VM((1024, 768), BF), VM((2560, 256), F32), VM((128, 1024), BF), VM((512, 768), BF), VM((512, 768), F32),
                        VM((1024, 768), F32), VM((1024, 768), F32), VM((512, 768), BF), VM((768, 512), BF),
                        VM((4, 2, 2, 48, 768), BF), VM((3, 4, 2, 2, 48, 768), BF), VM((4, 2, 2, 48, 1536), BF), VM((4, 2, 2, 96, 768), BF)]
        + bufs(48, 1536) + bufs(96, 768) + bufs(48, 384) + bufs(48, 384, (3,))
        + [VM((4, 2, 24, 384), F32), VM((4, 24, 384), F32), VM((1, 2, 24, 1536), F32), VM((1, 24, 1536), F32),
           VM((4, 128, 768), BF), VM((4, 128, 768), BF), VM((4, 128, 768), BF), VM((4, 80, 128), F32), VM((6, 80, 128), F32),
           DS((6, 7)), DS((6, 7)), DS((2,)), DS((6,)), DS((6,)), DS((2, 4, 2)), DS((2, 2)), DS((2, 2)), DS((2, 2)), DS((2, 2)), DS, DS, DS((6,)), DS((6,)), DS((2,))],
        compiler_params=pltpu.CompilerParams(collective_id=1, has_side_effects=True, vmem_limit_bytes=63 * 2**20),
    )(gup, gdown, block, *ins)

def fast_shards(inputs, history, seq_lengths, attn_gain, attn_shift, qkv_weight, qkv_bias, out_weight, out_bias, mlp_gain,
                mlp_shift, up_weight, up_bias, down_weight, down_bias, mix_weights, cotangent):
    seq, batch = lax.axis_index("seq"), lax.axis_index("batch")
    z, y, x, k = seq // 2, seq % 2, batch // 2, batch % 2
    vectors = (attn_gain, attn_shift, qkv_bias, out_bias, mlp_gain, mlp_shift, up_bias, down_bias)
    lens = seq_lengths.astype(F32)
    packed = jnp.stack([jnp.pad(v.astype(F32), (0, 128 - v.shape[0])) for v in vectors])
    packed = packed.at[0, 64:66].set(lens)
    COS, SIN = (jnp.asarray(t) for t in rope_tables())
    X, actsT, Q, K, V, att, lse, WQ, WO, block, gmid, gup, gdown, gain, vgrad = forward_call(
        qkv_weight, out_weight, up_weight, down_weight, packed, inputs, cotangent, COS, SIN, mix_weights)
    earlier, cot = history.astype(F32), cotangent.astype(F32)
    mix_terms = jnp.sum(earlier * cot[None], axis=(1, 2, 3))
    grad_history = (mix_weights[:-1, None, None, None] * cot[None]).astype(BF)
    vin = vgrad.at[78, :5].set(mix_terms)
    oq, oo, ou, od, vout, H0, HL, HS = backward_call(gup, gdown, block, gmid, X, actsT, Q, K, V, att, lse, WQ, WO, gain, COS, SIN, vin)
    is_long = (seq_lengths == LONG_LEN)[None, :, None, None]
    other = jnp.where(is_long, HL, HS)
    home = jnp.where(y == 0, jnp.concatenate([H0, other], axis=2), jnp.concatenate([other, H0], axis=2))
    layer_out = (jnp.sum(mix_weights[:-1, None, None, None] * earlier, axis=0) + mix_weights[-1] * home[0].astype(F32)).astype(BF)
    vflat = vout.reshape(-1)
    me = seq * 4 + batch
    gv, at = [], 0
    for v in vectors:
        n = v.shape[0]
        gv.append(lax.dynamic_slice_in_dim(vflat, at + me * n, n, 0))
        at += 32 * n
    grad_mix = vflat[at:at + 6]
    return (layer_out, home[1], grad_history, gv[0], gv[1], oq, gv[2], oo, gv[3], gv[4], gv[5], ou, gv[6], od, gv[7], grad_mix)


def fits(mesh, inputs):
    shape = dict(mesh.shape)
    return shape == {"seq": 8, "batch": 4} and inputs.shape == (8, 2048, 768)


def solution(mesh):
    def run(*args):
        body = fast_shards if fits(mesh, args[0]) else shards
        return placed(mesh, body)(*args)
    return run
```

```python
import functools
import math

import jax
import jax.numpy as jnp
import numpy as np
from jax import lax
from jax.experimental import pallas as pl
from jax.experimental.pallas import tpu as pltpu
from jax.sharding import PartitionSpec as P

HEADS = 12
HEAD_DIM = 64
LONG_LEN = 1024
SHORT_LEN = 256


eps = 1e-05
masked = -1e30


def block_size(row_count):
    chosen = 1
    for candidate in range(1, min(row_count, 512) + 1):
        if row_count % candidate == 0:
            chosen = candidate
    return chosen


def exact_gelu(values):
    return jax.nn.gelu(values, approximate=False)


def layer_norm(values, norm_gain, norm_shift):
    average = jnp.mean(values, axis=-1, keepdims=True)
    centred = values - average
    inverse = lax.rsqrt(jnp.mean(centred * centred, axis=-1, keepdims=True) + eps)
    normed = centred * inverse
    return (normed * norm_gain + norm_shift, normed, inverse)


def norm_back(grad_out, normed, inverse, norm_gain):
    grad_normed = grad_out * norm_gain
    mean_grad = jnp.mean(grad_normed, axis=-1, keepdims=True)
    mean_cross = jnp.mean(grad_normed * normed, axis=-1, keepdims=True)
    grad_in = inverse * (grad_normed - mean_grad - normed * mean_cross)
    return (grad_in, jnp.sum(grad_out * normed, axis=0), jnp.sum(grad_out, axis=0))


def token_layout(index, info):
    seq_len, tok_count, slice_len = info
    is_long = seq_len == LONG_LEN
    offset = index % tok_count
    device = index // tok_count
    doc_ids = jnp.where(is_long, offset // slice_len, index // SHORT_LEN).astype(jnp.int32)
    relative = jnp.where(
        is_long, device * slice_len + offset % slice_len, index % SHORT_LEN
    ).astype(jnp.int32)
    return (doc_ids, relative)


def rotary_tables(relative):
    half_dim = HEAD_DIM // 2
    frequency = jnp.exp(
        -math.log(10000.0) * (2.0 * jnp.arange(half_dim, dtype=jnp.float32) / HEAD_DIM)
    )
    angles = relative.astype(jnp.float32)[:, None] * frequency[None, :]
    return (jnp.cos(angles)[:, None, :], jnp.sin(angles)[:, None, :])


def rotate(values, cosine, sine_table):
    half_dim = values.shape[-1] // 2
    lower_half = values[..., :half_dim]
    upper_half = values[..., half_dim:]
    return jnp.concatenate(
        [
            lower_half * cosine - upper_half * sine_table,
            upper_half * cosine + lower_half * sine_table,
        ],
        axis=-1,
    )


def allowed_mask(query_places, key_places, info):
    query_docs, query_rel = token_layout(query_places, info)
    key_docs, key_rel = token_layout(key_places, info)
    return (key_docs[None, :] == query_docs[:, None]) & (key_rel[None, :] <= query_rel[:, None])


def online_block(current, query_b, key_block, value_block, query_places, key_places, info):
    running, denominator, weighted = current
    key_count = key_block.shape[0]
    allowed = allowed_mask(query_places, key_places, info)
    key_heads = key_block.reshape(key_count, HEADS, HEAD_DIM)
    scores = jnp.einsum(
        "qhd,khd->hqk", query_b, key_heads, preferred_element_type=jnp.float32
    ) * HEAD_DIM ** (-0.5)
    scores = jnp.where(allowed[None], scores, masked)
    new_max = jnp.maximum(running, jnp.max(scores, axis=-1))
    exp_scores = jnp.where(allowed[None], jnp.exp(scores - new_max[..., None]), 0.0)
    rescale = jnp.exp(running - new_max)
    denominator = denominator * rescale + jnp.sum(exp_scores, axis=-1)
    value_heads = value_block.reshape(key_count, HEADS, HEAD_DIM)
    weighted = weighted * rescale[..., None] + jnp.einsum(
        "hqk,khd->hqd",
        exp_scores.astype(jnp.bfloat16),
        value_heads,
        preferred_element_type=jnp.float32,
    )
    return (new_max, denominator, weighted)


def attend_rows(current, query_b, key_rows, value_rows, first_row, query_places, info, last_place):
    key_count = key_rows.shape[0]
    block_rows = block_size(key_count)

    def one_block(carried, block_index):
        start_place = first_row + block_index * block_rows
        key_block = lax.dynamic_slice_in_dim(key_rows, block_index * block_rows, block_rows, 0)
        value_block = lax.dynamic_slice_in_dim(value_rows, block_index * block_rows, block_rows, 0)
        key_places = start_place + jnp.arange(block_rows, dtype=jnp.int32)

        def one_compute(state_in):
            return online_block(
                state_in, query_b, key_block, value_block, query_places, key_places, info
            )

        def unchanged(state_in):
            return state_in

        return (lax.cond(start_place > last_place, unchanged, one_compute, carried), None)

    result, unused = lax.scan(
        one_block, current, jnp.arange(key_count // block_rows, dtype=jnp.int32)
    )
    return result


def block_probs(query_b, key_b, query_places, key_places, info, lse_rows):
    allowed = allowed_mask(query_places, key_places, info)
    scores = jnp.einsum(
        "qhd,khd->hqk", query_b, key_b, preferred_element_type=jnp.float32
    ) * HEAD_DIM ** (-0.5)
    return jnp.exp(jnp.where(allowed[None], scores - lse_rows[..., None], masked))


def block_dscores(probabilities, grad_b, value_b, delta_rows):
    dprobs = jnp.einsum("qhd,khd->hqk", grad_b, value_b, preferred_element_type=jnp.float32)
    return (probabilities * (dprobs - delta_rows[..., None])).astype(jnp.bfloat16)


def shards(
    inputs,
    history,
    seq_lengths,
    attn_gain,
    attn_shift,
    qkv_weight,
    qkv_bias,
    out_weight,
    out_bias,
    mlp_gain,
    mlp_shift,
    up_weight,
    up_bias,
    down_weight,
    down_bias,
    mix_weights,
    cotangent,
):
    group_count = inputs.shape[0]
    tok_count = inputs.shape[1]
    model_width = inputs.shape[2]
    seq_count = lax.axis_size("seq")
    group_rows = tok_count * seq_count
    slice_len = LONG_LEN // seq_count
    factor = HEAD_DIM ** (-0.5)
    seq_index = lax.axis_index("seq")
    first_place = seq_index * tok_count
    last_place = first_place + tok_count - 1
    places = first_place + jnp.arange(tok_count, dtype=jnp.int32)
    gathered = (
        lax.all_gather(attn_gain, ("seq", "batch"), axis=0, tiled=True),
        lax.all_gather(attn_shift, ("seq", "batch"), axis=0, tiled=True),
        lax.all_gather(qkv_weight, ("seq", "batch"), axis=0, tiled=True),
        lax.all_gather(qkv_bias, ("seq", "batch"), axis=0, tiled=True),
        lax.all_gather(out_weight, ("seq", "batch"), axis=0, tiled=True),
        lax.all_gather(out_bias, ("seq", "batch"), axis=0, tiled=True),
        lax.all_gather(mlp_gain, ("seq", "batch"), axis=0, tiled=True),
        lax.all_gather(mlp_shift, ("seq", "batch"), axis=0, tiled=True),
        lax.all_gather(up_weight, ("seq", "batch"), axis=0, tiled=True),
        lax.all_gather(up_bias, ("seq", "batch"), axis=0, tiled=True),
        lax.all_gather(down_weight, ("seq", "batch"), axis=0, tiled=True),
        lax.all_gather(down_bias, ("seq", "batch"), axis=0, tiled=True),
    )
    (
        gain_one,
        shift_one,
        qkv_full,
        qkv_vec,
        out_full,
        out_vec,
        gain_two,
        shift_two,
        up_full,
        up_vec,
        down_full,
        down_vec,
    ) = gathered
    saved = []
    block_outs = []
    for group in range(group_count):
        info = (seq_lengths[group], tok_count, slice_len)
        doc_ids, relative = token_layout(places, info)
        cosine, sine_table = rotary_tables(relative)
        residual_in = inputs[group].astype(jnp.float32)
        normed_out, normed_one, inverse_one = layer_norm(
            residual_in, gain_one.astype(jnp.float32), shift_one.astype(jnp.float32)
        )
        acts_one = normed_out.astype(jnp.bfloat16)
        projected = jnp.dot(
            acts_one, qkv_full, preferred_element_type=jnp.float32
        ) + qkv_vec.astype(jnp.float32)
        queries = rotate(
            projected[:, :model_width].reshape(tok_count, HEADS, HEAD_DIM), cosine, sine_table
        ).astype(jnp.bfloat16)
        key_flat = (
            rotate(
                projected[:, model_width : 2 * model_width].reshape(tok_count, HEADS, HEAD_DIM),
                cosine,
                sine_table,
            )
            .reshape(tok_count, model_width)
            .astype(jnp.bfloat16)
        )
        value_flat = projected[:, 2 * model_width :].astype(jnp.bfloat16)
        start_state = (
            jnp.full((HEADS, tok_count), masked, jnp.float32),
            jnp.zeros((HEADS, tok_count), jnp.float32),
            jnp.zeros((HEADS, tok_count, HEAD_DIM), jnp.float32),
        )
        key_all = None
        value_all = None
        running, denominator, weighted = attend_rows(
            start_state,
            queries,
            lax.all_gather(key_flat, "seq", axis=0, tiled=True),
            lax.all_gather(value_flat, "seq", axis=0, tiled=True),
            jnp.int32(0),
            places,
            info,
            last_place,
        )
        attended = jnp.transpose(weighted / denominator[..., None], (1, 0, 2))
        lse_rows = running + jnp.log(denominator)
        attended_b = attended.reshape(tok_count, model_width).astype(jnp.bfloat16)
        middle = (
            residual_in
            + jnp.dot(attended_b, out_full, preferred_element_type=jnp.float32)
            + out_vec.astype(jnp.float32)
        )
        normed_out_two, normed_two, inverse_two = layer_norm(
            middle, gain_two.astype(jnp.float32), shift_two.astype(jnp.float32)
        )
        acts_two = normed_out_two.astype(jnp.bfloat16)
        upward = jnp.dot(acts_two, up_full, preferred_element_type=jnp.float32) + up_vec.astype(
            jnp.float32
        )
        activated, gelu_back = jax.vjp(exact_gelu, upward)
        activated_b = activated.astype(jnp.bfloat16)
        block_out = (
            middle
            + jnp.dot(activated_b, down_full, preferred_element_type=jnp.float32)
            + down_vec.astype(jnp.float32)
        )
        block_outs.append(block_out)
        saved.append(
            (
                info,
                cosine,
                sine_table,
                normed_one,
                inverse_one,
                acts_one,
                queries,
                key_flat,
                value_flat,
                key_all,
                value_all,
                attended,
                lse_rows,
                attended_b,
                normed_two,
                inverse_two,
                acts_two,
                gelu_back,
                activated_b,
            )
        )
    block_stack = jnp.stack(block_outs, axis=0)
    earlier = history.astype(jnp.float32)
    grad_out_all = cotangent.astype(jnp.float32)
    mixed_out = (
        jnp.sum(mix_weights[:-1, None, None, None] * earlier, axis=0)
        + mix_weights[-1] * block_stack
    )
    mix_terms = jnp.concatenate(
        [
            jnp.sum(earlier * grad_out_all[None], axis=(1, 2, 3)),
            jnp.sum(block_stack * grad_out_all)[None],
        ]
    )
    grad_history = (mix_weights[:-1, None, None, None] * grad_out_all[None]).astype(jnp.bfloat16)
    back_gain_one, back_qkv, back_out, back_gain_two, back_up, back_down = (
        lax.all_gather(attn_gain, ("seq", "batch"), axis=0, tiled=True),
        lax.all_gather(qkv_weight, ("seq", "batch"), axis=0, tiled=True),
        lax.all_gather(out_weight, ("seq", "batch"), axis=0, tiled=True),
        lax.all_gather(mlp_gain, ("seq", "batch"), axis=0, tiled=True),
        lax.all_gather(up_weight, ("seq", "batch"), axis=0, tiled=True),
        lax.all_gather(down_weight, ("seq", "batch"), axis=0, tiled=True),
    )
    totals = None
    grad_input_list = []
    for group in range(group_count):
        (
            info,
            cosine,
            sine_table,
            normed_one,
            inverse_one,
            acts_one,
            queries,
            key_flat,
            value_flat,
            key_all,
            value_all,
            attended,
            lse_rows,
            attended_b,
            normed_two,
            inverse_two,
            acts_two,
            gelu_back,
            activated_b,
        ) = saved[group]
        grad_block = mix_weights[-1] * grad_out_all[group]
        down_grad_b = grad_block.astype(jnp.bfloat16)
        grad_w_down = jnp.einsum(
            "tf,td->fd", activated_b, down_grad_b, preferred_element_type=jnp.float32
        )
        grad_b_down = jnp.sum(down_grad_b.astype(jnp.float32), axis=0)
        grad_act = jnp.einsum(
            "td,fd->tf", down_grad_b, back_down, preferred_element_type=jnp.float32
        )
        up_grad_b = gelu_back(grad_act)[0].astype(jnp.bfloat16)
        grad_w_up = jnp.einsum("td,tf->df", acts_two, up_grad_b, preferred_element_type=jnp.float32)
        grad_b_up = jnp.sum(up_grad_b.astype(jnp.float32), axis=0)
        grad_acts_two = jnp.einsum(
            "tf,df->td", up_grad_b, back_up, preferred_element_type=jnp.float32
        )
        grad_middle_norm, grad_gain_two, grad_shift_two = norm_back(
            grad_acts_two, normed_two, inverse_two, back_gain_two.astype(jnp.float32)
        )
        grad_middle = grad_block + grad_middle_norm
        attn_grad_b = grad_middle.astype(jnp.bfloat16)
        grad_w_out = jnp.einsum(
            "te,td->ed", attended_b, attn_grad_b, preferred_element_type=jnp.float32
        )
        grad_b_out = jnp.sum(attn_grad_b.astype(jnp.float32), axis=0)
        grad_heads = (
            jnp.einsum("td,ed->te", attn_grad_b, back_out, preferred_element_type=jnp.float32)
            .astype(jnp.bfloat16)
            .reshape(tok_count, HEADS, HEAD_DIM)
        )
        delta_rows = jnp.transpose(jnp.sum(grad_heads.astype(jnp.float32) * attended, axis=-1))
        key_all, value_all = (
            lax.all_gather(key_flat, "seq", axis=0, tiled=True),
            lax.all_gather(value_flat, "seq", axis=0, tiled=True),
        )
        key_block_rows = block_size(group_rows)

        def query_grad_block(carried, block_index):
            start_place = block_index * key_block_rows
            key_block = lax.dynamic_slice_in_dim(key_all, start_place, key_block_rows, 0).reshape(
                key_block_rows, HEADS, HEAD_DIM
            )
            value_block = lax.dynamic_slice_in_dim(
                value_all, start_place, key_block_rows, 0
            ).reshape(key_block_rows, HEADS, HEAD_DIM)
            key_places = start_place + jnp.arange(key_block_rows, dtype=jnp.int32)

            def query_compute(summed):
                probabilities = block_probs(queries, key_block, places, key_places, info, lse_rows)
                dscores = block_dscores(probabilities, grad_heads, value_block, delta_rows)
                return (
                    summed
                    + jnp.einsum(
                        "hqk,khd->qhd", dscores, key_block, preferred_element_type=jnp.float32
                    )
                    * factor
                )

            return (
                lax.cond(start_place > last_place, lambda summed: summed, query_compute, carried),
                None,
            )

        grad_queries, unused = lax.scan(
            query_grad_block,
            jnp.zeros((tok_count, HEADS, HEAD_DIM), jnp.float32),
            jnp.arange(group_rows // key_block_rows, dtype=jnp.int32),
        )
        key_first_row = jnp.int32(0)
        key_rows = key_all
        value_rows = value_all
        inner_rows = block_size(lax.axis_size("seq") * tok_count)

        def key_grad_block(carried, block_index):
            offset = block_index * inner_rows
            start_place = key_first_row + offset
            key_block = lax.dynamic_slice_in_dim(key_rows, offset, inner_rows, 0).reshape(
                inner_rows, HEADS, HEAD_DIM
            )
            value_block = lax.dynamic_slice_in_dim(value_rows, offset, inner_rows, 0).reshape(
                inner_rows, HEADS, HEAD_DIM
            )
            key_places = start_place + jnp.arange(inner_rows, dtype=jnp.int32)

            def key_compute(unused_in):
                probabilities = block_probs(queries, key_block, places, key_places, info, lse_rows)
                dscores = block_dscores(probabilities, grad_heads, value_block, delta_rows)
                grad_keys = (
                    jnp.einsum("hqk,qhd->khd", dscores, queries, preferred_element_type=jnp.float32)
                    * factor
                )
                grad_values = jnp.einsum(
                    "hqk,qhd->khd",
                    probabilities.astype(jnp.bfloat16),
                    grad_heads,
                    preferred_element_type=jnp.float32,
                )
                return jnp.concatenate(
                    [
                        grad_keys.reshape(inner_rows, model_width),
                        grad_values.reshape(inner_rows, model_width),
                    ],
                    axis=1,
                )

            def nothing(unused_in):
                return jnp.zeros((inner_rows, 2 * model_width), jnp.float32)

            return (carried, lax.cond(start_place > last_place, nothing, key_compute, carried))

        unused_out, blocks = lax.scan(
            key_grad_block,
            jnp.int32(0),
            jnp.arange(lax.axis_size("seq") * tok_count // inner_rows, dtype=jnp.int32),
        )
        key_grads = lax.psum_scatter(
            blocks.reshape(lax.axis_size("seq") * tok_count, 2 * model_width).astype(jnp.bfloat16),
            "seq",
            scatter_dimension=0,
            tiled=True,
        ).astype(jnp.float32)
        grad_keys_own = key_grads[:, :model_width]
        grad_values_own = key_grads[:, model_width:]
        grad_q_turned = rotate(grad_queries, cosine, -sine_table).reshape(tok_count, model_width)
        grad_k_turned = rotate(
            grad_keys_own.reshape(tok_count, HEADS, HEAD_DIM), cosine, -sine_table
        ).reshape(tok_count, model_width)
        qkv_grad_b = jnp.concatenate(
            [grad_q_turned, grad_k_turned, grad_values_own], axis=1
        ).astype(jnp.bfloat16)
        grad_w_qkv = jnp.einsum(
            "td,te->de", acts_one, qkv_grad_b, preferred_element_type=jnp.float32
        )
        grad_b_qkv = jnp.sum(qkv_grad_b.astype(jnp.float32), axis=0)
        grad_acts_one = jnp.einsum(
            "te,de->td", qkv_grad_b, back_qkv, preferred_element_type=jnp.float32
        )
        grad_in_norm, grad_gain_one, grad_shift_one = norm_back(
            grad_acts_one, normed_one, inverse_one, back_gain_one.astype(jnp.float32)
        )
        grad_input_list.append((grad_middle + grad_in_norm).astype(jnp.bfloat16))
        terms = [
            grad_gain_one,
            grad_shift_one,
            grad_w_qkv,
            grad_b_qkv,
            grad_w_out,
            grad_b_out,
            grad_gain_two,
            grad_shift_two,
            grad_w_up,
            grad_b_up,
            grad_w_down,
            grad_b_down,
        ]
        if totals is None:
            totals = terms
        else:
            totals = [older + newer for older, newer in zip(totals, terms)]
    shares = (
        lax.psum_scatter(totals[0], ("seq", "batch"), scatter_dimension=0, tiled=True),
        lax.psum_scatter(totals[1], ("seq", "batch"), scatter_dimension=0, tiled=True),
        lax.psum_scatter(totals[2], ("seq", "batch"), scatter_dimension=0, tiled=True),
        lax.psum_scatter(totals[3], ("seq", "batch"), scatter_dimension=0, tiled=True),
        lax.psum_scatter(totals[4], ("seq", "batch"), scatter_dimension=0, tiled=True),
        lax.psum_scatter(totals[5], ("seq", "batch"), scatter_dimension=0, tiled=True),
        lax.psum_scatter(totals[6], ("seq", "batch"), scatter_dimension=0, tiled=True),
        lax.psum_scatter(totals[7], ("seq", "batch"), scatter_dimension=0, tiled=True),
        lax.psum_scatter(totals[8], ("seq", "batch"), scatter_dimension=0, tiled=True),
        lax.psum_scatter(totals[9], ("seq", "batch"), scatter_dimension=0, tiled=True),
        lax.psum_scatter(totals[10], ("seq", "batch"), scatter_dimension=0, tiled=True),
        lax.psum_scatter(totals[11], ("seq", "batch"), scatter_dimension=0, tiled=True),
    )
    grad_mix = lax.psum(mix_terms, ("seq", "batch"))
    grad_inputs = jnp.stack(grad_input_list, axis=0)
    return (
        mixed_out.astype(jnp.bfloat16),
        grad_inputs,
        grad_history,
        shares[0],
        shares[1],
        shares[2],
        shares[3],
        shares[4],
        shares[5],
        shares[6],
        shares[7],
        shares[8],
        shares[9],
        shares[10],
        shares[11],
        grad_mix,
    )


def placed(mesh, body):
    return jax.shard_map(
        body,
        mesh=mesh,
        in_specs=(
            P("batch", "seq", None),
            P(None, "batch", "seq", None),
            P("batch"),
            P(("seq", "batch")),
            P(("seq", "batch")),
            P(("seq", "batch"), None),
            P(("seq", "batch")),
            P(("seq", "batch"), None),
            P(("seq", "batch")),
            P(("seq", "batch")),
            P(("seq", "batch")),
            P(("seq", "batch"), None),
            P(("seq", "batch")),
            P(("seq", "batch"), None),
            P(("seq", "batch")),
            P(),
            P("batch", "seq", None),
        ),
        out_specs=(
            P("batch", "seq", None),
            P("batch", "seq", None),
            P(None, "batch", "seq", None),
            P(("seq", "batch")),
            P(("seq", "batch")),
            P(("seq", "batch"), None),
            P(("seq", "batch")),
            P(("seq", "batch"), None),
            P(("seq", "batch")),
            P(("seq", "batch")),
            P(("seq", "batch")),
            P(("seq", "batch"), None),
            P(("seq", "batch")),
            P(("seq", "batch"), None),
            P(("seq", "batch")),
            P(),
        ),
        check_vma=False,
    )

MESH = pl.DeviceIdType.MESH
BF, F32 = jnp.bfloat16, jnp.float32


def where_am_i():
    seq, batch = lax.axis_index("seq"), lax.axis_index("batch")
    return seq // 2, seq % 2, batch // 2, batch % 2


def dev(z, y, x, k):
    return (z * 2 + y, x * 2 + k)


def remote(src, dst, ssem, rsem, device):
    return pltpu.make_async_remote_copy(src_ref=src, dst_ref=dst, send_sem=ssem, recv_sem=rsem,
                                        device_id=device, device_id_type=MESH)


def chips_of(z, y, x):
    mine = (z * 2 + y) * 2 + x
    for step in range(1, 16):
        other = lax.rem(mine + step, 16)
        yield step, (other // 4, (other // 2) % 2, other % 2)


def greet(z, y, x, k):
    barrier = pltpu.get_barrier_semaphore()
    for _, chip in chips_of(z, y, x):
        pl.semaphore_signal(barrier, inc=1, device_id=dev(*chip, k), device_id_type=MESH)
    for step in range(8):
        other = lax.rem(z * 2 + y + step, 8)
        pl.semaphore_signal(barrier, inc=1, device_id=dev(other // 2, other % 2, x, 1 - k), device_id_type=MESH)
    pl.semaphore_wait(barrier, 23)


class Gather:
    STAGES = 7

    def __init__(self, part, send, recv, pos, both, hops):
        z, y, x, k = pos
        self.hops = hops
        turn = (k == 0) | both
        p2 = jnp.where(turn, 1 - y, y), jnp.where(turn, x, 1 - x)
        p3 = jnp.where(turn, y, 1 - y), jnp.where(turn, 1 - x, x)
        d4 = 1 - y, 1 - x
        one = lambda zz: part(pl.ds(zz, 1), y, x, k)
        allz = lambda yx: part(slice(None), yx[0], yx[1], k)
        self.mid = (z == 1) | (z == 2)
        end = jnp.where(z == 1, 0, 3)
        def cp(n, ref, device, r=None):
            return remote(ref, ref, send.at[n], recv.at[n if r is None else r], device)
        others = [lax.rem(z + d, 4) for d in (1, 2, 3)]
        self.three = [cp(d, one(o), dev(o, y, x, k), o) for d, o in enumerate(others)]
        if hops:
            self.direct = [cp(0, one(z), dev(jnp.where(z == 1, 0, 1), y, x, k), z), cp(1, one(z), dev(jnp.where(z == 2, 3, 2), y, x, k), z)]
        else:
            self.direct = [cp(d, one(z), dev(o, y, x, k), z) for d, o in enumerate(others)]
        self.passed = [cp(3 + n, one(f), dev(end, y, x, k), f) for n, f in enumerate((3 - z, 3 - end))]
        self.near = cp(0, one(end), dev(end, y, x, k), end)
        n2, n3 = dev(z, *p2, k), dev(z, *p3, k)
        blocks = [z] + others
        self.a2 = [cp(5 + n, one(b), n2, 4 + b) for n, b in enumerate(blocks)]
        self.a3 = [cp(9 + n, one(b), n3, 8 + b) for n, b in enumerate(blocks)]
        self.b3 = [cp(13 + n, part(pl.ds(b, 1), *p2, k), n3, 12 + b) for n, b in enumerate(blocks)]
        sib = dev(z, y, x, 1 - k)
        self.s = [cp(17 + n, allz(p), sib, 16 + n) for n, p in enumerate(((y, x), p2, p3, d4))]

    def early(self):
        self.a2[0].start(); self.a3[0].start()

    def early_on(self):
        self.a2[0].wait_recv()
        self.b3[0].start()

    def stage(self, n):
        if n == 0:
            for c in self.direct: c.start()
        elif n == 1:
            if self.hops:
                @pl.when(self.mid)
                def _():
                    for c in self.passed:
                        c.wait_recv()
                        c.start()
        elif n == 2:
            if self.hops:
                @pl.when(self.mid)
                def _():
                    self.near.wait_recv()
                @pl.when(jnp.logical_not(self.mid))
                def _():
                    for c in self.three: c.wait_recv()
            else:
                for c in self.three: c.wait_recv()
            for c in self.a2[1:] + self.a3[1:]: c.start()
            self.s[0].start()
        elif n == 3:
            for c in self.a2[1:]: c.wait_recv()
            for c in self.b3[1:]: c.start()
            self.s[1].start()
        elif n == 4:
            for c in self.a3: c.wait_recv()
            self.s[2].start()
        elif n == 5:
            for c in self.b3: c.wait_recv()
            self.s[3].start()
        elif n == 6:
            for c in self.s: c.wait_recv()

    def sent(self):
        for c in self.direct + self.a2 + self.a3 + self.b3 + self.s: c.wait_send()
        if self.hops:
            @pl.when(self.mid)
            def _():
                for c in self.passed: c.wait_send()


class Home:
    def __init__(self, buf, cross, sel, out, length, sems, pos):
        self.__dict__.update(locals())
        z, y, x, k = pos
        self.esend, self.erecv, self.send, self.h0, self.hs = sems
        self.swap = [remote(buf.at[self.crossed(n)], cross.at[n], self.esend.at[n], self.erecv.at[n], dev(z, 1 - y, x, 1 - k)) for n in range(2)]
        self.sent = []

    def crossed(self, n):
        z, y, x, k = self.pos
        return lax.rem(1 - y + k, 2) + 2 * n

    def go(self, ref, i, h, sem, n):
        z, y, x, k = self.pos
        slot = lax.rem(z, 2)
        dst = self.out.at[slot, pl.ds(pl.multiple_of(h * 128, 128), 128)]
        me = (i == z) & (z // 2 == k)
        cp = remote(ref, dst, self.send.at[n], sem.at[slot], dev(i, y, x, z // 2))
        @pl.when(me)
        def _():
            pltpu.make_async_copy(ref, dst, sem.at[slot]).start()
        @pl.when(jnp.logical_not(me))
        def _():
            cp.start()
        self.sent.append((cp, jnp.logical_not(me)))

    def first(self):
        z, y, x, k = self.pos
        for c in self.swap: c.start()
        for n in range(2):
            i = lax.rem(y + k, 2) + 2 * n
            self.go(self.buf.at[i], i, y, self.h0, n)

    def second(self):
        z, y, x, k = self.pos
        for n in range(2):
            self.swap[n].wait_recv()
            i = self.crossed(n)
            far = jnp.broadcast_to(self.length, (128, 768)) > 512.0
            self.sel[n] = jnp.where(far, self.cross[n].astype(F32), self.buf[i].astype(F32)).astype(BF)
            self.go(self.sel.at[n], i, 1 - y, self.hs, 2 + n)

    def done(self):
        z, y, x, k = self.pos
        for g in range(2):
            for h, sem in ((y, self.h0), (1 - y, self.hs)):
                dst = self.out.at[g, pl.ds(pl.multiple_of(h * 128, 128), 128)]
                remote(dst, dst, self.send.at[0], sem.at[g], dev(z, y, x, 1 - k)).wait_recv()
        for c in self.swap: c.wait_send()
        for cp, cond in self.sent:
            @pl.when(cond)
            def _():
                cp.wait_send()

EPS = 1e-5
NT = (((1,), (1,)), ((), ()))


def nt(a, b):
    return lax.dot_general(a, b, NT, preferred_element_type=F32)


def nn(a, b):
    return jnp.dot(a, b, preferred_element_type=F32)


def rope_tables():
    freq = np.exp(-math.log(10000.0) * (2.0 * np.arange(32, dtype=np.float32) / 64)).astype(np.float32)
    ang = np.arange(1024, dtype=np.float32)[:, None] * freq[None, :]
    c, s = np.cos(ang.astype(np.float64)), np.sin(ang.astype(np.float64))
    return (np.concatenate([c, c, c, c], 1).astype(np.float32), np.concatenate([-s, s, -s, s], 1).astype(np.float32))


def swap(u):
    low = lax.broadcasted_iota(jnp.int32, u.shape, 1) % 64 < 32
    return jnp.where(low, pltpu.roll(u, 96, 1), pltpu.roll(u, 32, 1))


def norm(v):
    mean = jnp.mean(v, axis=-1, keepdims=True)
    cen = v - mean
    inv = lax.rsqrt(jnp.mean(cen * cen, axis=-1, keepdims=True) + EPS)
    return cen * inv, inv


def norm_grad(e, n, inv, gain):
    g = e * gain
    return inv * (g - jnp.mean(g, axis=-1, keepdims=True) - n * jnp.mean(g * n, axis=-1, keepdims=True))


def own_block(i, k):
    return 2 * i + lax.rem(i + k, 2)


def rows(i, n=128):
    return pl.ds(pl.multiple_of(i * n, n), n)


def spread(p):
    low = lax.broadcasted_iota(jnp.int32, p.shape, 1) < 64
    zero = jnp.zeros_like(p)
    return jnp.concatenate([jnp.where(low, p, zero), jnp.where(low, zero, p)], axis=0)


def pick(o):
    low = lax.broadcasted_iota(jnp.int32, (128, 128), 0) < 64
    return jnp.where(low, o[:, :128], o[:, 128:]).T


def fill_bias(bias, is_long, k):
    at = 0
    for i in range(4):
        kk = 256 * (i + 1)
        key = lax.broadcasted_iota(jnp.int32, (kk, 256), 0)
        q = own_block(i, k) * 128 + lax.broadcasted_iota(jnp.int32, (kk, 256), 1) % 128
        first = jnp.where(is_long, 0, q - q % 256)
        bias[at:at + kk, :] = jnp.where((key <= q) & (key >= first), 0.0, -1e30)
        at += kk


def attn_fwd(flag, XM, XA, wqkv, wout, gain, shift, bqkv, bout, COS, SIN,
             acts, Q, K, V, att, lse, middle, bias, VT):
    z, y, x, k = where_am_i()
    is_long = flag[0] != 0
    fill_bias(bias, is_long, k)
    for j in range(8):
        alt = jnp.logical_and(jnp.logical_not(is_long), lax.rem(jnp.int32(j), 2) != y)
        blk = jnp.where(alt, XA[j // 2], XM[j]).astype(F32)
        n, _ = norm(blk)
        acts[j * 128:(j + 1) * 128, :] = (n * gain[...] + shift[...]).astype(BF)

    def tables(j):
        off = jnp.where(is_long, j, lax.rem(j, 2))
        return COS[rows(off), :], SIN[rows(off), :]

    @pl.loop(0, 8)
    def _(j):
        a = acts[rows(j), :]
        c, s = tables(j)
        for t in range(6):
            u = nn(a, wqkv[:, 768 + t * 128:896 + t * 128]) + bqkv[:, 768 + t * 128:896 + t * 128]
            K[rows(j), t * 128:(t + 1) * 128] = (u * c + swap(u) * s).astype(BF)
        V[rows(j), :] = (nn(a, wqkv[:, 1536:]) + bqkv[:, 1536:]).astype(BF)

    @pl.loop(0, 4)
    def _(i):
        j = own_block(i, k)
        a = acts[rows(j), :]
        c, s = tables(j)
        for t in range(6):
            u = nn(a, wqkv[:, t * 128:(t + 1) * 128]) + bqkv[:, t * 128:(t + 1) * 128]
            Q[rows(i), t * 128:(t + 1) * 128] = (u * c + swap(u) * s).astype(BF) * jnp.asarray(0.125, BF)

    @pl.loop(0, 6)
    def _(h):
        lanes = rows(h)
        VT[...] = V[:, lanes].T
        at = 0
        for i in range(4):
            kk = 256 * (i + 1)
            qb = spread(Q[i * 128:(i + 1) * 128, lanes])
            st = nt(K[0:kk, lanes], qb) + bias[at:at + kk, :]
            top = jnp.max(st, axis=0, keepdims=True)
            p = jnp.exp(st - top)
            den = jnp.sum(p, axis=0, keepdims=True)
            o = nn(VT[:, 0:kk], p.astype(BF)) * (1.0 / den)
            att[i * 128:(i + 1) * 128, lanes] = pick(o)
            lse[h, i:i + 1, :] = top + jnp.log(den)
            at += kk

    @pl.loop(0, 4)
    def _(i):
        j = own_block(i, k)
        alt = jnp.logical_and(jnp.logical_not(is_long), lax.rem(j, 2) != y)
        xb = jnp.where(alt, XA[i], XM[j]).astype(F32)
        middle[rows(i), :] = xb + (nn(att[rows(i), :].astype(BF), wout[...]) + bout[...])


def mlp(CH, flag, mix, middle, CM, CA, wup, wdown, gain, shift, bup, bdown,
        block, gmid, gup, gdown, g_gain, g_shift, g_bup, g_bdown, mixsum, acts2, actsT, dg, ga, cf):
    z, y, x, k = where_am_i()
    is_long = flag[0] != 0
    m5 = mix[5]
    for i in range(4):
        r = slice(i * 128, (i + 1) * 128)
        mid = middle[r, :]
        n, _ = norm(mid)
        acts2[r, :] = (n * gain[...] + shift[...]).astype(BF)
        j = own_block(jnp.int32(i), k)
        alt = jnp.logical_and(jnp.logical_not(is_long), lax.rem(j, 2) != y)
        c = jnp.where(alt, CA[i], CM[j]).astype(F32)
        cf[r, :] = c
        dg[r, :] = (m5 * c).astype(BF)
        block[r, :] = mid + bdown[...]
        ga[r, :] = jnp.zeros_like(mid)
        actsT[:, r] = acts2[r, :].T
    g_bdown[...] = jnp.sum(dg[...].astype(F32), axis=0, keepdims=True)

    @pl.loop(0, wup.shape[1] // CH)
    def _(f):
        cols = rows(f, CH)
        up = nn(acts2[...], wup[:, cols]) + bup[:, cols]
        half_erf = 0.5 * lax.erf(up * (2.0 ** -0.5)) + 0.5
        slope = half_erf + up * (jnp.exp(up * up * -0.5) * (1.0 / math.sqrt(2 * math.pi)))
        act = (up * half_erf).astype(BF)
        block[...] += nn(act, wdown[cols, :])
        upg = (nt(dg[...], wdown[cols, :]) * slope).astype(BF)
        g_bup[:, cols] = jnp.sum(upg.astype(F32), axis=0, keepdims=True)
        gdown[cols, :] = nn(act.T, dg[...]).astype(BF)
        gup[:, cols] = nn(actsT[...], upg).astype(BF)
        ga[...] += nt(upg, wup[:, cols])

    total = jnp.zeros((1, 768), F32)
    gg = jnp.zeros((1, 768), F32)
    gs = jnp.zeros((1, 768), F32)
    for i in range(4):
        r = slice(i * 128, (i + 1) * 128)
        n, inv = norm(middle[r, :])
        e = ga[r, :]
        gg += jnp.sum(e * n, axis=0, keepdims=True)
        gs += jnp.sum(e, axis=0, keepdims=True)
        gmid[r, :] = m5 * cf[r, :] + norm_grad(e, n, inv, gain[...])
        total += jnp.sum(cf[r, :] * block[r, :], axis=0, keepdims=True)
    g_gain[...] = gg
    g_shift[...] = gs
    mixsum[...] = total


def attn_bwd(flag, gmid, acts, Q, K, V, att, lse, wqkv, wout, COS, SIN,
             e, gqkv, gout, g_bqkv, g_bout, bias, KT, da, dQ, dK, dV, agrad, actsT, actsqT, KG, VG):
    z, y, x, k = where_am_i()
    is_long = flag[0] != 0
    fill_bias(bias, is_long, k)
    agrad[...] = gmid[...].astype(BF)
    g_bout[...] = jnp.sum(agrad[...].astype(F32), axis=0, keepdims=True)

    @pl.loop(0, 4)
    def _(i):
        da[rows(i), :] = nt(agrad[rows(i), :], wout[...]).astype(BF)

    for t in range(6):
        aT = att[:, t * 128:(t + 1) * 128].T.astype(BF)
        gout[t * 128:(t + 1) * 128, :] = nn(aT, agrad[...]).astype(BF)
    dK[...] = jnp.zeros_like(dK)
    dV[...] = jnp.zeros_like(dV)

    @pl.loop(0, 6)
    def _(h):
        lanes = rows(h)
        KT[...] = K[:, lanes].T
        at = 0
        for i in range(4):
            kk = 256 * (i + 1)
            r = slice(i * 128, (i + 1) * 128)
            d = da[r, lanes]
            qb, db = spread(Q[r, lanes]), spread(d)
            prod = (d.astype(F32) * att[r, lanes]).T
            delta = jnp.concatenate([jnp.sum(prod[:64], axis=0, keepdims=True), jnp.sum(prod[64:], axis=0, keepdims=True)], axis=1)
            st = nt(K[0:kk, lanes], qb) + bias[at:at + kk, :]
            p = jnp.exp(st - lse[h, i:i + 1, :])
            ds = (p * (nt(V[0:kk, lanes], db) - delta)).astype(BF)
            dV[0:kk, lanes] += nn(p.astype(BF), db)
            dK[0:kk, lanes] += nn(ds, qb)
            dQ[r, lanes] = pick(nn(KT[:, 0:kk], ds)) * 0.125
            at += kk

    def tables(j):
        off = jnp.where(is_long, j, lax.rem(j, 2))
        return COS[rows(off), :], SIN[rows(off), :]

    for j in range(8):
        actsT[:, j * 128:(j + 1) * 128] = acts[j * 128:(j + 1) * 128, :].T
    for i in range(4):
        j = own_block(jnp.int32(i), k)
        actsqT[:, i * 128:(i + 1) * 128] = acts[rows(j), :].T
        c, s = tables(j)
        for t in range(6):
            u = dQ[i * 128:(i + 1) * 128, t * 128:(t + 1) * 128]
            da[i * 128:(i + 1) * 128, t * 128:(t + 1) * 128] = (u * c - swap(u) * s).astype(BF)

    @pl.loop(0, 8)
    def _(j):
        c, s = tables(j)
        for t in range(6):
            u = dK[rows(j), t * 128:(t + 1) * 128]
            KG[rows(j), t * 128:(t + 1) * 128] = (u * c - swap(u) * s).astype(BF)
        VG[rows(j), :] = dV[rows(j), :].astype(BF)
        e[rows(j), :] = nt(KG[rows(j), :], wqkv[:, 768:1536]) + nt(VG[rows(j), :], wqkv[:, 1536:])

    @pl.loop(0, 4)
    def _(i):
        j = own_block(i, k)
        e[rows(j), :] += nt(da[rows(i), :], wqkv[:, :768])

    g_bqkv[:, :768] = jnp.sum(da[...].astype(F32), axis=0, keepdims=True)
    g_bqkv[:, 768:1536] = jnp.sum(KG[...].astype(F32), axis=0, keepdims=True)
    g_bqkv[:, 1536:] = jnp.sum(VG[...].astype(F32), axis=0, keepdims=True)

    @pl.loop(0, 6)
    def _(t):
        gqkv[rows(t), :768] = nn(actsqT[rows(t), :], da[...]).astype(BF)
        gqkv[rows(t), 768:1536] = nn(actsT[rows(t), :], KG[...]).astype(BF)
        gqkv[rows(t), 1536:] = nn(actsT[rows(t), :], VG[...]).astype(BF)


sd = jax.ShapeDtypeStruct
VM = pltpu.VMEM
vs = pl.BlockSpec(memory_space=pltpu.VMEM)
ss = pl.BlockSpec(memory_space=pltpu.SMEM)
CP = pltpu.CompilerParams(vmem_limit_bytes=60 * 2**20)


def attn_fwd_call(flag, *ins):
    return pl.pallas_call(attn_fwd,
        out_shape=[sd((1024, 768), BF), sd((512, 768), BF), sd((1024, 768), BF), sd((1024, 768), BF),
                   sd((512, 768), F32), sd((6, 4, 256), F32), sd((512, 768), F32)],
        in_specs=[ss] + [vs] * len(ins), out_specs=[vs] * 7,
        scratch_shapes=[VM((2560, 256), F32), VM((128, 1024), BF)],
        compiler_params=CP)(flag, *ins)


def mlp_call(flag, mix, *ins):
    r = sd((1, 768), F32)
    return pl.pallas_call(functools.partial(mlp, 512),
        out_shape=[sd((512, 768), F32), sd((512, 768), F32), sd((768, 3072), BF), sd((3072, 768), BF), r, r, sd((1, 3072), F32), r, r],
        in_specs=[ss, ss] + [vs] * len(ins), out_specs=[vs] * 9,
        scratch_shapes=[VM((512, 768), BF), VM((768, 512), BF), VM((512, 768), BF), VM((512, 768), F32), VM((512, 768), F32)],
        compiler_params=CP)(flag, mix, *ins)


def attn_bwd_call(flag, *ins):
    return pl.pallas_call(attn_bwd,
        out_shape=[sd((1024, 768), F32), sd((768, 2304), BF), sd((768, 768), BF), sd((1, 2304), F32), sd((1, 768), F32)],
        in_specs=[ss] + [vs] * len(ins), out_specs=[vs] * 5,
        scratch_shapes=[VM((2560, 256), F32), VM((128, 1024), BF), VM((512, 768), BF), VM((512, 768), F32), VM((1024, 768), F32),
                        VM((1024, 768), F32), VM((512, 768), BF), VM((768, 1024), BF), VM((768, 512), BF), VM((1024, 768), BF), VM((1024, 768), BF)],
        compiler_params=CP)(flag, *ins)


VROWS = (24, 24, 72, 24, 24, 24, 96, 24)


def widen(vecs, row, n):
    v = vecs[:, row, :].astype(BF)
    wide = 32 * n
    j = lax.broadcasted_iota(jnp.int32, (128, wide), 1)
    i = lax.broadcasted_iota(jnp.int32, (128, wide), 0)
    q = jnp.floor((j.astype(F32) + 0.5) * (1.0 / n)).astype(jnp.int32)
    hot = jnp.where(j - q * n == i, 1.0, 0.0).astype(BF)
    full = nn(v, hot)
    d = lax.broadcasted_iota(jnp.int32, (32, wide), 0)
    return jnp.sum(jnp.where(q[:32] == d, full, 0.0), axis=0, keepdims=True)


def lane(tile, row, at):
    r = lax.broadcasted_iota(jnp.int32, tile.shape, 0)
    c = lax.broadcasted_iota(jnp.int32, tile.shape, 1)
    v = jnp.sum(jnp.where((r == row) & (c == at), tile, 0.0), axis=1, keepdims=True)
    return jnp.sum(v, axis=0, keepdims=True)


def longer(length, shape):
    return jnp.broadcast_to(length, shape) > 512.0


def bias_rows(bias, length, k):
    at = 0
    for i in range(4):
        kk = 256 * (i + 1)
        key = lax.broadcasted_iota(jnp.int32, (kk, 128), 0)
        q = own_block(i, k) * 128 + lax.broadcasted_iota(jnp.int32, (kk, 128), 1)
        first = jnp.where(longer(length, (kk, 128)), 0, q - q % 256)
        bias[at:at + kk, :] = jnp.where((key <= q) & (key >= first), 0.0, -1e30)
        at += kk


def both_heads(bias, at, kk):
    b = bias[at:at + kk, :]
    return jnp.concatenate([b, b], axis=1)


def table_rows(COS, SIN, length, j):
    far = longer(length, (128, 128))
    near = lax.rem(j, 2)
    return (jnp.where(far, COS[rows(j), :], COS[rows(near), :]), jnp.where(far, SIN[rows(j), :], SIN[rows(near), :]))


def matrix(W, cols):
    w = W[:, :, :, :, cols]
    return w.reshape(768, w.shape[-1])


def forward_kernel(cols, qkv, out, up, down, xin, cin, COS, SIN, hist, v0, v1, v2, v3, v4, v5, v6, v7, mix, lens,
                   oX, oacts, oQ, oK, oV, oatt, olse, oWQ, oWO, ogmid, ogup, ogdown, ohome, opre, ogain, vgrad,
                   f_own, f_sib, block_w, WQ, WO, WU, WD, VEC, X, C, NB, SB,
                   Q, K, V, att, lse, middle, bias, VT, act, slope, block, ga, acts2, actsT, dg, gup, gdown, a1T, bl,
                   vq, vg, vu, vec, mixrow, cross, sel,
                   psend, precv, lsem, gsend, grecv, asend, arecv, nsend, nrecv, fsend, frecv, xsem, csem, hsem, osem, vsend, vrecv, *home_sems):
    pos = z, y, x, k = where_am_i()
    sib = dev(z, y, x, 1 - k)
    greet(z, y, x, k)
    s = 2 * z + y
    own_s = lax.rem(y + z, 2)
    def neighbour(a, src):
        cps = []
        for i in range(2):
            hi = src.at[i, pl.ds(pl.multiple_of((1 - y) * 128, 128), 128)]
            cp = remote(hi, NB.at[a, i], nsend.at[a, i], nrecv.at[a, i], dev(z, 1 - y, x, k))
            cp.start()
            cps.append(cp)
        return cps

    tokens = []
    def along_z(a, i, n, ref, dst, core):
        g = 2 * k + i
        me = (g == z) & (core == k)
        cp = remote(ref, dst, asend.at[a, i, n], arecv.at[a, z], dev(g, y, x, core))
        @pl.when(me)
        def _():
            pltpu.make_async_copy(ref, dst, arecv.at[a, z]).start()
        @pl.when(jnp.logical_not(me))
        def _():
            cp.start()
        tokens.append((cp, jnp.logical_not(me)))

    def straight(a, src, dst):
        for i in range(2):
            along_z(a, i, 0, src.at[i, pl.ds(pl.multiple_of(y * 128, 128), 128)], dst(s), own_s)

    def crossed(a, src, dst, cps):
        for i in range(2):
            cps[i].wait_recv()
            mine = src[i, pl.ds(pl.multiple_of((1 - y) * 128, 128), 128), :]
            far = jnp.broadcast_to(lens[i].astype(F32), (128, 768)) > 512.0
            SB[a, i] = jnp.where(far, NB[a, i].astype(F32), mine.astype(F32)).astype(BF)
            along_z(a, i, 1, SB.at[a, i], dst(s + 1 - 2 * y), 1 - own_s)

    def arrived(a, dst, i):
        remote(dst, dst, asend.at[a, 0, 0], arecv.at[a, i], sib).wait_recv()

    acts = gdown.at[pl.ds(0, 1024)]
    to_x = lambda j: X.at[j]
    to_c = lambda j: C.at[j // 2]
    vec[...] = jnp.zeros_like(vec)
    for r, v in enumerate((v0, v1, v2, v3, v4, v5, v6, v7)):
        vec[r:r + 1, 0:v.shape[1]] = v[...].astype(F32)
    place = lax.broadcasted_iota(jnp.int32, (1, 128), 1)
    first = vec[0:1, :]
    for i in range(2):
        first = jnp.where(place == 64 + i, lens[i].astype(F32), first)
    vec[0:1, :] = first
    at, offs = 0, []
    for n in cols:
        offs.append((at, n // 2))
        at += n // 2
    pres = []
    for i, ((at, half), ref) in enumerate(zip(offs, (qkv, out, up))):
        f_own[0, :, at:at + half] = ref[:, :half].astype(F32)
        f_own[1, :, at:at + half] = ref[:, half:].astype(F32)
        pre = remote(f_own.at[1 - k, :, pl.ds(at, half)], f_sib.at[:, pl.ds(at, half)], psend.at[i], precv.at[i], sib)
        pre.start()
        pres.append(pre)
    lvec = pltpu.make_async_copy(vec, VEC.at[z, y, x, k], lsem.at[4])
    ldown = pltpu.make_async_copy(down, WD.at[z, y, x, k], lsem.at[3])
    lvec.start(); ldown.start()

    def colpart(W, half):
        return lambda zz, yy, xx, kk: W.at[zz, yy, xx, :, pl.ds(pl.multiple_of(kk * half, 128), half)]
    def rowpart(W):
        return lambda zz, yy, xx, kk: W.at[zz, yy, xx, kk]
    gq, go, gu, gd = G = [Gather(p, gsend.at[i], grecv.at[i], pos, i in (1, 2), i > 1) for i, p in enumerate(
        [colpart(WQ, offs[0][1]), colpart(WO, offs[1][1]), colpart(WU, offs[2][1]), rowpart(WD)])]
    lvec.wait()
    vs_out = [remote(VEC.at[z, y, x, k], VEC.at[z, y, x, k], vsend.at[n], vrecv.at[15 - n], dev(*chip, k)) for n, chip in chips_of(z, y, x)]
    vs_in = [remote(VEC.at[chip[0], chip[1], chip[2], k], VEC.at[chip[0], chip[1], chip[2], k], vsend.at[n], vrecv.at[n - 1], dev(*chip, k)) for n, chip in chips_of(z, y, x)]
    v_sib = remote(VEC.at[:, :, :, k], VEC.at[:, :, :, k], vsend.at[0], vrecv.at[15], sib)
    for c in vs_out: c.start()

    def own_rows(i, W):
        at, half = offs[i]
        pres[i].wait_recv()
        mine = f_own[k, :, at:at + half]
        theirs = f_sib[:, at:at + half]
        block_w[:, at:at + half] = jnp.concatenate([jnp.where(k == 0, mine, theirs), jnp.where(k == 0, theirs, mine)], axis=0).astype(BF)
        c = pltpu.make_async_copy(block_w.at[:, pl.ds(at, half)], W.at[z, y, x, :, pl.ds(pl.multiple_of(k * half, 128), half)], lsem.at[i])
        c.start()
        return c

    own_rows(0, WQ).wait()
    gq.stage(0)
    gq.early()
    nx = neighbour(0, xin)
    lo, lu = own_rows(1, WO), own_rows(2, WU)
    hin = [[pltpu.make_async_copy(hist.at[j, g], gdown.at[pl.ds(512 * j + 256 * g, 256)], hsem.at[j, g]) for g in range(2)] for j in range(5)]
    for c in hin: c[0].start(); c[1].start()
    block[...] = jnp.zeros_like(block)
    mixrow[...] = jnp.zeros_like(mixrow)

    def mix_in(js):
        for j in js:
            for g in range(2):
                hin[j][g].wait()
                for t in range(2):
                    r = slice(512 * j + 256 * g + 128 * t, 512 * j + 256 * g + 128 * t + 128)
                    q = slice(256 * g + 128 * t, 256 * g + 128 * t + 128)
                    h = gdown[r, :].astype(F32)
                    c = cin[g, 128 * t:128 * t + 128, :].astype(F32)
                    mixrow[j:j + 1, :] += jnp.sum(h * c, axis=0, keepdims=True)
                    block[q, :] += mix[j] * h
    lo.wait(); lu.wait(); ldown.wait()
    go.early(); gu.early()
    mix_in((0, 1))
    for c in vs_in: c.wait_recv()
    v_sib.start()
    mix_in((2, 3))
    gq.early_on()
    gq.stage(2)
    gu.stage(0)
    go.stage(0)
    straight(0, xin, to_x)
    crossed(0, xin, to_x, nx)
    gd.early()
    go.early_on(); gu.early_on()
    mix_in((4,))
    opres = [pltpu.make_async_copy(block.at[pl.ds(256 * g, 256)], opre.at[g], osem.at[g]) for g in range(2)]
    for c in opres: c.start()
    v_sib.wait_recv()
    tiles = VEC[...].reshape(32, 8, 128)
    length = lane(VEC[0, 0, x, z // 2], 0, 64 + lax.rem(z, 2))
    vq[...] = widen(tiles, 2, 72)
    gq.stage(3)
    for n, r in enumerate((0, 1, 3, 4, 5, 7)):
        vg[n:n + 1, :] = widen(tiles, r, 24)
    a_gain, a_shift, bout, m_gain, m_shift, bdown = (vg[n:n + 1, :] for n in range(6))
    gu.stage(1)
    gd.early_on()
    gq.stage(4)
    vu[...] = widen(tiles, 6, 96)
    bias_rows(bias, length, k)
    fw = []
    def forward_x(i):
        j = own_block(jnp.int32(i), k)
        arrived(0, X.at[j], i)
        cp = remote(X.at[j], X.at[j], fsend.at[i], frecv.at[i], sib)
        cp.start(); fw.append(cp)
    def norm_block(j):
        n, _ = norm(X[j].astype(F32))
        acts[rows(j), :] = (n * a_gain + a_shift).astype(BF)
        a1T[:, rows(j)] = acts[rows(j), :].T
    gu.stage(2)
    gq.stage(5)
    go.stage(2)
    nc = neighbour(1, cin)
    gq.stage(6)
    for i in range(4):
        forward_x(i)
        norm_block(own_block(jnp.int32(i), k))
    gd.stage(0)
    gu.stage(3)
    go.stage(3)
    for i in range(4):
        fw[i].wait_recv()
        norm_block(own_block(jnp.int32(i), 1 - k))
    exports = []
    def export(ref, dst):
        c = pltpu.make_async_copy(ref, dst, xsem.at[len(exports)])
        c.start(); exports.append(c)

    def keys(j):
        a = acts[rows(j), :]
        c, sn = table_rows(COS, SIN, length, j)
        for t in range(3):
            u2 = nn(a, matrix(WQ, slice(768 + t * 256, 1024 + t * 256))) + vq[:, 768 + t * 256:1024 + t * 256]
            for h in range(2):
                u = u2[:, h * 128:(h + 1) * 128]
                K[rows(j), t * 256 + h * 128:t * 256 + (h + 1) * 128] = (u * c + swap(u) * sn).astype(BF)
        V[rows(j), :] = (nn(a, matrix(WQ, slice(1536, 2304))) + vq[:, 1536:]).astype(BF)

    pl.loop(0, 4)(keys)
    gd.stage(1)
    straight(1, cin, to_c)
    crossed(1, cin, to_c, nc)
    go.stage(4)
    pl.loop(4, 8)(keys)
    @pl.loop(0, 4)
    def _(i):
        j = own_block(i, k)
        a = acts[rows(j), :]
        c, sn = table_rows(COS, SIN, length, j)
        for t in range(3):
            u2 = nn(a, matrix(WQ, slice(t * 256, 256 + t * 256))) + vq[:, t * 256:256 + t * 256]
            for h in range(2):
                u = u2[:, h * 128:(h + 1) * 128]
                Q[rows(i), t * 256 + h * 128:t * 256 + (h + 1) * 128] = (u * c + swap(u) * sn).astype(BF) * jnp.asarray(0.125, BF)
    gu.stage(4)
    for i in range(4):
        j = own_block(jnp.int32(i), k)
        export(X.at[j], oX.at[i])
    export(a1T, oacts); export(Q, oQ); export(K, oK); export(V, oV)
    export(WQ, oWQ)

    def heads(h):
        lanes = rows(h)
        VT[...] = V[:, lanes].T
        at = 0
        for i in range(4):
            kk = 256 * (i + 1)
            qb = spread(Q[i * 128:(i + 1) * 128, lanes])
            st = nt(K[0:kk, lanes], qb) + both_heads(bias, at, kk)
            top = jnp.max(st, axis=0, keepdims=True)
            p = jnp.exp(st - top)
            den = jnp.sum(p, axis=0, keepdims=True)
            o = nn(VT[:, 0:kk], p.astype(BF)) * (1.0 / den)
            att[i * 128:(i + 1) * 128, lanes] = pick(o)
            lse[h, i:i + 1, :] = top + jnp.log(den)
            at += kk

    pl.loop(0, 2)(heads)
    gd.stage(2)
    go.stage(5)
    pl.loop(2, 4)(heads)
    gu.stage(5)
    pl.loop(4, 6)(heads)
    go.stage(6)
    export(WO, oWO)
    gd.stage(3)
    export(att, oatt); export(lse, olse)

    for c in opres: c.wait()

    @pl.loop(0, 4)
    def _(i):
        j = own_block(i, k)
        middle[rows(i), :] = X[j].astype(F32) + (nn(att[rows(i), :].astype(BF), WO[...].reshape(768, 768)) + bout)
    m5 = mix[5]
    for i in range(4):
        r = slice(i * 128, (i + 1) * 128)
        mid = middle[r, :]
        n, _ = norm(mid)
        a2 = (n * m_gain + m_shift).astype(BF)
        acts2[r, :] = a2
        actsT[:, r] = a2.T
        block[r, :] = mid + bdown
        ga[r, :] = jnp.zeros_like(mid)
    gu.stage(6)
    vgrad[...] = jnp.zeros_like(vgrad)

    def put_vec(row, v):
        for t in range(v.shape[1] // 128):
            vgrad[row + t:row + t + 1, :] = v[:, t * 128:(t + 1) * 128]

    def hidden(f):
        c = rows(f, 384)
        u = nn(acts2[...], matrix(WU, c)) + vu[:, c]
        half_erf = 0.5 * lax.erf(u * (2.0 ** -0.5)) + 0.5
        slope[:, c] = half_erf + u * (jnp.exp(u * u * -0.5) * (1.0 / math.sqrt(2 * math.pi)))
        act[:, c] = (u * half_erf).astype(BF)
    pl.loop(0, 4)(hidden)
    gd.stage(4)
    pl.loop(4, 8)(hidden)
    for i in range(4):
        arrived(1, C.at[i], i)
        dg[i * 128:(i + 1) * 128, :] = (m5 * C[i].astype(F32)).astype(BF)
    put_vec(72, jnp.sum(dg[...].astype(F32), axis=0, keepdims=True))
    gd.stage(5)
    gd.stage(6)

    @pl.loop(0, 4)
    def _(f):
        block[...] += nn(act[:, rows(f, 768)], WD[f].reshape(768, 768))

    total = jnp.zeros((1, 768), F32)
    for i in range(4):
        r = slice(i * 128, (i + 1) * 128)
        total += jnp.sum(C[i].astype(F32) * block[r, :], axis=0, keepdims=True)
        bl[i] = block[r, :].astype(BF)
    home = Home(bl, cross, sel, ohome, length, home_sems, pos)
    home.first()

    def chunk(f):
        c = rows(f, 768)
        wd = WD[f].reshape(768, 768)
        a = act[:, c]
        upg = (nt(dg[...], wd) * slope[:, c]).astype(BF)
        g = jnp.sum(upg.astype(F32), axis=0, keepdims=True)
        for t in range(6):
            vgrad[pl.ds(48 + f * 6 + t, 1), :] = g[:, t * 128:(t + 1) * 128]
        gdown[c, :] = nn(a.T, dg[...]).astype(BF)
        pltpu.make_async_copy(gdown.at[c, :], ogdown.at[c, :], csem.at[0, f]).start()
        gup[:, c] = nn(actsT[...], upg).astype(BF)
        pltpu.make_async_copy(gup.at[:, c], ogup.at[:, c], csem.at[1, f]).start()
        ga[...] += nt(upg, matrix(WU, c))

    pl.loop(0, 3)(chunk)
    home.second()
    pl.loop(3, 4)(chunk)
    gg = jnp.zeros((1, 768), F32)
    gs = jnp.zeros((1, 768), F32)
    for i in range(4):
        r = slice(i * 128, (i + 1) * 128)
        n, inv = norm(middle[r, :])
        e = ga[r, :]
        cf = C[i].astype(F32)
        gg += jnp.sum(e * n, axis=0, keepdims=True)
        gs += jnp.sum(e, axis=0, keepdims=True)
        ga[r, :] = m5 * cf + norm_grad(e, n, inv, m_gain)
    put_vec(36, gg); put_vec(42, gs)
    ogain[...] = jnp.broadcast_to(a_gain, (8, 768))
    whole = jnp.sum(total, axis=1, keepdims=True)
    row = jnp.where(place == 5, jnp.broadcast_to(whole, (1, 128)), 0.0)
    for j in range(5):
        row = jnp.where(place == j, jnp.broadcast_to(jnp.sum(mixrow[j:j + 1, :], axis=1, keepdims=True), (1, 128)), row)
    vgrad[78:79, :] = row
    vgrad[79:80, :] = jnp.broadcast_to(length, (1, 128))
    export(ga, ogmid)
    for f in range(4):
        c = slice(f * 768, (f + 1) * 768)
        pltpu.make_async_copy(gdown.at[c, :], ogdown.at[c, :], csem.at[0, f]).wait()
        pltpu.make_async_copy(gup.at[:, c], ogup.at[:, c], csem.at[1, f]).wait()
    for c in exports: c.wait()
    home.done()
    for c in fw + nx + nc: c.wait_send()
    for cp, cond in tokens:
        @pl.when(cond)
        def _():
            cp.wait_send()
    for c in pres: c.wait_send()
    for g in G: g.sent()
    for c in vs_out + [v_sib]: c.wait_send()


def forward_call(qkv, out, up, down, xin, cin, COS, SIN, hist, vectors, mix, lens):
    cols = (qkv.shape[1], out.shape[1], up.shape[1])
    H = sum(cols) // 2
    any_ = pl.BlockSpec(memory_space=pl.ANY)
    T = lambda n, t=BF: ((n, 768), t)
    shapes = [((4, 128, 768), BF), ((768, 1024), BF), T(512), T(1024), T(1024), T(512, F32), ((6, 4, 256), F32),
              ((4, 2, 2, 48, 2304), BF), ((4, 2, 2, 48, 768), BF), T(512, F32), ((768, 3072), BF), T(3072),
              (xin.shape, BF), (xin.shape, F32)]
    DS = pltpu.SemaphoreType.DMA
    return pl.pallas_call(functools.partial(forward_kernel, cols),
        out_shape=[sd(*t) for t in shapes] + [sd((8, 768), F32), sd((80, 128), F32)],
        in_specs=[vs] * 8 + [any_] + [vs] * 8 + [ss, ss], out_specs=[any_] * len(shapes) + [vs, vs],
        scratch_shapes=[VM((2, 24, H), F32), VM((24, H), F32), VM((48, H), BF),
                        VM((4, 2, 2, 48, 2304), BF), VM((4, 2, 2, 48, 768), BF), VM((4, 2, 2, 48, 3072), BF), VM((4, 2, 2, 2, 96, 768), BF),
                        VM((4, 2, 2, 2, 8, 128), F32), VM((8, 128, 768), BF), VM((4, 128, 768), BF), VM((2, 2, 128, 768), BF), VM((2, 2, 128, 768), BF),
                        VM((512, 768), BF), VM((1024, 768), BF), VM((1024, 768), BF), VM((512, 768), F32),
                        VM((6, 4, 256), F32), VM((512, 768), F32), VM((2560, 128), F32), VM((128, 1024), BF),
                        VM((512, 3072), BF), VM((512, 3072), F32), VM((512, 768), F32), VM((512, 768), F32), VM((512, 768), BF),
                        VM((768, 512), BF), VM((512, 768), BF), VM((768, 3072), BF), VM((3072, 768), BF), VM((768, 1024), BF), VM((4, 128, 768), BF),
                        VM((1, 2304), F32), VM((8, 768), F32), VM((1, 3072), F32), VM((8, 128), F32), VM((8, 768), F32), VM((2, 128, 768), BF), VM((2, 128, 768), BF),
                        DS((3,)), DS((3,)), DS((5,)), DS((4, 21)), DS((4, 20)), DS((2, 2, 2)), DS((2, 4)), DS((2, 2)), DS((2, 2)), DS((4,)), DS((4,)),
                        DS((16,)), DS((2, 4)), DS((5, 2)), DS((2,)), DS((16,)), DS((16,)), DS((2,)), DS((2,)), DS((4,)), DS((2,)), DS((2,))],
        compiler_params=pltpu.CompilerParams(collective_id=0, has_side_effects=True, vmem_limit_bytes=63 * 2**20),
    )(qkv, out, up, down, xin, cin, COS, SIN, hist, *[v.reshape(1, -1) for v in vectors], mix, lens)


class Scatter:
    STAGES = 7

    def __init__(self, mine, theirs, RA, RB, RC, RZ, put, finish, send, recv, pos, load=None):
        self.mine, self.RA, self.RB, self.RC, self.RZ, self.put, self.finish, self.pos, self.load = mine, RA, RB, RC, RZ, put, finish, pos, load
        z, y, x, k = pos
        self.own = (y, x)
        self.p2 = jnp.where(k == 0, 1 - y, y), jnp.where(k == 0, x, 1 - x)
        self.p3 = jnp.where(k == 0, y, 1 - y), jnp.where(k == 0, 1 - x, x)
        self.d4 = 1 - y, 1 - x
        blk = lambda yx: mine(slice(None), yx[0], yx[1])
        n3, n2 = dev(z, *self.p3, k), dev(z, *self.p2, k)
        self.pre = remote(theirs, RA, send.at[0], recv.at[0], dev(z, y, x, 1 - k))
        self.b1 = remote(blk(self.d4), RB.at[1], send.at[1], recv.at[1], n3)
        self.b0 = remote(blk(self.p3), RB.at[0], send.at[2], recv.at[2], n3)
        self.c = remote(blk(self.p2), RC, send.at[3], recv.at[3], n2)
        self.mid = (z == 1) | (z == 2)
        end, near = jnp.where(z < 2, 0, 3), jnp.where(z < 2, 1, 2)
        self.far = (3 - near, 3 - end)
        zdev = lambda zz: dev(zz, y, x, k)
        def zcp(n, block, slot, to):
            return remote(mine(block, y, x), RZ.at[slot], send.at[4 + n], recv.at[4 + slot], zdev(to))
        self.up = [zcp(0, near, 0, near), zcp(1, self.far[0], 2, near), zcp(2, self.far[1], 3, near)]
        self.down = zcp(0, end, 0, end)
        self.on = [zcp(1, self.far[0], 1, self.far[0]), zcp(2, self.far[1], 1, self.far[1])]
        self.sends = [self.pre, self.b1, self.b0, self.c]

    def add(self, yx, other):
        @pl.loop(0, 4)
        def _(i):
            ref = self.mine(i, yx[0], yx[1])
            ref[...] = (ref[...].astype(F32) + other[i].astype(F32)).astype(BF)

    def first(self, yx):
        self.add(yx, self.RA.at[:, yx[0], yx[1]])

    def stage(self, n):
        z, y, x, k = self.pos
        if n == 0:
            if self.load is not None: self.load.start()
            self.pre.start()
        elif n == 1:
            self.pre.wait_recv()
            if self.load is not None: self.load.wait()
            self.first(self.d4)
            self.b1.start()
            self.first(self.p3)
            self.b0.start()
            self.first(self.p2)
            self.first(self.own)
        elif n == 2:
            self.b1.wait_recv()
            self.add(self.p2, self.RB.at[1])
            self.c.start()
            self.b0.wait_recv()
            self.add(self.own, self.RB.at[0])
        elif n == 3:
            self.c.wait_recv()
            self.add(self.own, self.RC)
            @pl.when(self.mid)
            def _():
                self.down.start()
            @pl.when(jnp.logical_not(self.mid))
            def _():
                for c in self.up: c.start()
        elif n == 4:
            @pl.when(self.mid)
            def _():
                for i, c in enumerate(self.on):
                    self.up[1 + i].wait_recv()
                    ref = self.mine(self.far[i], y, x)
                    ref[...] = (ref[...].astype(F32) + self.RZ[2 + i].astype(F32)).astype(BF)
                    c.start()
        elif n == 5:
            self.up[0].wait_recv()
            self.on[0].wait_recv()
            self.put(self.mine(z, y, x)[...].astype(F32) + self.RZ[0].astype(F32) + self.RZ[1].astype(F32))
        elif n == 6:
            self.finish()
            for c in self.sends: c.wait_send()
            @pl.when(self.mid)
            def _():
                for c in [self.down] + self.on: c.wait_send()
            @pl.when(jnp.logical_not(self.mid))
            def _():
                for c in self.up: c.wait_send()


def backward_kernel(gup, gdown, gmid, X, actsT, Q, Kin, Vin, att, lse, WQ, WO, gain, COS, SIN, vin,
                    oq, oo, ou, od, vout, ox,
                    K, V, bias, KT, da, dQ, dK, dV, agrad, actsqT, GO, GQ, PU, PD,
                    AU, BU, CU, ZU, AD, BD, CD, ZD, AO, BO, CO, ZO, AQ, BQ, CQ, ZQ,
                    fin, fsib, finu, fsibu, es, er, gx, cross, sel, vbuf, vrec,
                    ssem, rsem, ldsem, fsend, frecv, esem_s, esem_r, vsend, vrecv, csem, *home_sems):
    pos = z, y, x, k = where_am_i()
    sib = dev(z, y, x, 1 - k)
    greet(z, y, x, k)
    length = vin[79:80, 0:1]
    ck = pltpu.make_async_copy(Kin, K, csem.at[0])
    cv = pltpu.make_async_copy(Vin, V, csem.at[1])
    ck.start(); cv.start()
    half_of = lambda kk, half: pl.ds(pl.multiple_of(kk * half, 128), half)

    def col_scatter(a, G, half, bufs, n, out, at, width, fi, fs, hbm=None):
        def put(t):
            fi[n, 0] = t[:24]
            fi[n, 1] = t[24:]
            last.start()
        last = remote(fi.at[n, 1 - k], fs.at[n], fsend.at[a], frecv.at[a], sib)
        def finish():
            last.wait_recv()
            mine, theirs = fi[n, k], fs[n]
            out[:, at:at + half] = jnp.where(k == 0, mine, theirs)
            out[:, at + half:at + 2 * half] = jnp.where(k == 0, theirs, mine)
            last.wait_send()
        if hbm is None:
            mine = lambda zz, yy, xx: G.at[zz, yy, xx, :, half_of(k, half)]
            theirs = G.at[:, :, :, :, half_of(1 - k, half)]
            load = None
        else:
            mine = lambda zz, yy, xx: G.at[zz, yy, xx]
            theirs = hbm.at[:, :, :, :, half_of(1 - k, half)]
            load = pltpu.make_async_copy(hbm.at[:, :, :, :, half_of(k, half)], G, ldsem.at[a])
        return Scatter(mine, theirs, *bufs, put, finish, ssem.at[a], rsem.at[a], pos, load)

    def put_down(t):
        od[...] = t
    sdn = Scatter(lambda zz, yy, xx: PD.at[zz, yy, xx], gdown.at[:, :, :, 1 - k], AD, BD, CD, ZD, put_down, lambda: None,
                  ssem.at[0], rsem.at[0], pos, pltpu.make_async_copy(gdown.at[:, :, :, k], PD, ldsem.at[0]))
    sup = col_scatter(1, PU, 1536, (AU, BU, CU, ZU), 0, ou, 0, 3072, finu, fsibu, gup)
    sout = col_scatter(2, GO, 384, (AO, BO, CO, ZO), 0, oo, 0, 768, fin, fsib)
    sq, sk, sv = (col_scatter(3 + n, GQ.at[n], 384, (AQ.at[n], BQ.at[n], CQ.at[n], ZQ.at[n]), 1 + n, oq, 768 * n, 768, fin, fsib)
                  for n in range(3))
    sdn.stage(0); sup.stage(0)

    home = Home(gx, cross, sel, ox, length, home_sems, pos)
    agrad[...] = gmid[...].astype(BF)
    vbuf[0] = vin[...]

    def put_vec(row, v):
        for t in range(v.shape[1] // 128):
            vbuf[0, row + t:row + t + 1, :] = v[:, t * 128:(t + 1) * 128]
    put_vec(30, jnp.sum(agrad[...].astype(F32), axis=0, keepdims=True))
    wo = lambda: WO[...].reshape(768, 768)

    da[...] = nt(agrad[...], wo()).astype(BF)
    for i in range(4):
        actsqT[:, i * 128:(i + 1) * 128] = actsT[:, rows(own_block(jnp.int32(i), k))]

    sdn.stage(1)

    def out_rows(t):
        aT = att[:, t * 384:(t + 1) * 384].T.astype(BF)
        g = nn(aT, agrad[...]).astype(BF)
        GO[2 * t:2 * t + 2] = g.reshape(2, 2, 2, 48, 768)
    sup.stage(1)
    for t in range(2): out_rows(t)
    sout.stage(0)
    bias_rows(bias, length, k)
    dK[...] = jnp.zeros_like(dK)
    dV[...] = jnp.zeros_like(dV)
    ck.wait(); cv.wait()

    def heads(h):
        lanes = rows(h)
        KT[...] = K[:, lanes].T
        at = 0
        for i in range(4):
            kk = 256 * (i + 1)
            r = slice(i * 128, (i + 1) * 128)
            d = da[r, lanes]
            qb, db = spread(Q[r, lanes]), spread(d)
            prod = (d.astype(F32) * att[r, lanes]).T
            delta = jnp.concatenate([jnp.sum(prod[:64], axis=0, keepdims=True), jnp.sum(prod[64:], axis=0, keepdims=True)], axis=1)
            st = nt(K[0:kk, lanes], qb) + both_heads(bias, at, kk)
            p = jnp.exp(st - lse[h, i:i + 1, :])
            ds = (p * (nt(V[0:kk, lanes], db) - delta)).astype(BF)
            dV[0:kk, lanes] += nn(p.astype(BF), db)
            dK[0:kk, lanes] += nn(ds, qb)
            dQ[r, lanes] = pick(nn(KT[:, 0:kk], ds)) * 0.125
            at += kk

    pl.loop(0, 2)(heads)
    sout.stage(1)
    pl.loop(2, 6)(heads)
    sdn.stage(2)
    V[...] = dV[...].astype(BF)
    put_vec(24, jnp.sum(V[...].astype(F32), axis=0, keepdims=True))

    def weight_rows(n, lhs, g):
        @pl.loop(0, 4)
        def _(t):
            GQ[n, t] = nn(lhs[rows(t, 192), :], g[...]).astype(BF).reshape(2, 2, 48, 768)
    weight_rows(2, actsT, V)
    sv.stage(0)
    sup.stage(2)

    @pl.loop(0, 8)
    def _(j):
        c, s = table_rows(COS, SIN, length, j)
        for t in range(6):
            u = dK[rows(j), t * 128:(t + 1) * 128]
            K[rows(j), t * 128:(t + 1) * 128] = (u * c - swap(u) * s).astype(BF)

    @pl.loop(0, 4)
    def _(i):
        j = own_block(i, k)
        c, s = table_rows(COS, SIN, length, j)
        for t in range(6):
            u = dQ[rows(i), t * 128:(t + 1) * 128]
            da[rows(i), t * 128:(t + 1) * 128] = (u * c - swap(u) * s).astype(BF)
    sdn.stage(3)
    sv.stage(1)
    weight_rows(1, actsT, K)
    sk.stage(0)

    @pl.loop(0, 2)
    def _(j):
        r = rows(j, 512)
        dK[r, :] = nt(K[r, :], matrix(WQ, slice(768, 1536))) + nt(V[r, :], matrix(WQ, slice(1536, 2304)))
    dQ[...] = nt(da[...], matrix(WQ, slice(0, 768)))
    for i in range(4):
        dK[rows(own_block(jnp.int32(i), k)), :] += dQ[i * 128:(i + 1) * 128, :]
        es[i] = dK[rows(own_block(jnp.int32(i), 1 - k)), :].astype(BF)
    ecp = remote(es, er, esem_s, esem_r, sib)
    ecp.start()
    sk.stage(1)
    sdn.stage(4)
    put_vec(18, jnp.sum(K[...].astype(F32), axis=0, keepdims=True))
    put_vec(12, jnp.sum(da[...].astype(F32), axis=0, keepdims=True))
    weight_rows(0, actsqT, da)
    sq.stage(0)
    ecp.wait_recv()
    gg = jnp.zeros((1, 768), F32)
    gsh = jnp.zeros((1, 768), F32)
    for i in range(4):
        n, inv = norm(X[i].astype(F32))
        ee = dK[rows(own_block(jnp.int32(i), k)), :] + er[i].astype(F32)
        gg += jnp.sum(ee * n, axis=0, keepdims=True)
        gsh += jnp.sum(ee, axis=0, keepdims=True)
        gx[i] = (gmid[i * 128:(i + 1) * 128, :] + norm_grad(ee, n, inv, gain[0:1, :])).astype(BF)
    home.first()
    put_vec(0, gg); put_vec(6, gsh)
    vec_steps = [[sib], [dev(z, *sq.p2, k)], [dev(z, *sq.p3, k)], [dev(lax.rem(z + d, 4), y, x, k) for d in (1, 2, 3)]]
    vcp = []
    def vec_stage(n):
        if n > 0:
            for c in vcp[-1]: c.wait_recv()
            t = vbuf[n - 1]
            for r in range(len(vcp[-1])):
                t = t + vrec[n - 1 + r]
            if n < 4: vbuf[n] = t
            else: vout[...] = t
        if n < 4:
            vcp.append([remote(vbuf.at[n], vrec.at[n + i], vsend.at[n + i], vrecv.at[n + i], d) for i, d in enumerate(vec_steps[n])])
            for c in vcp[-1]: c.start()

    sq.stage(1)
    vec_stage(0)
    sup.stage(3)
    sout.stage(2)
    vec_stage(1)
    home.second()
    sv.stage(2)
    sup.stage(4)
    sout.stage(3)
    sk.stage(2)
    sq.stage(2)
    sv.stage(3)
    sout.stage(4)
    sk.stage(3)
    sq.stage(3)
    sv.stage(4)
    vec_stage(2)
    sk.stage(4)
    sq.stage(4)
    vec_stage(3)
    sdn.stage(5); sup.stage(5); sout.stage(5)
    sdn.stage(6); sup.stage(6); sout.stage(6)
    sv.stage(5); sk.stage(5); sq.stage(5)
    vec_stage(4)
    sv.stage(6); sk.stage(6); sq.stage(6)
    home.done()
    ecp.wait_send()
    for cs in vcp:
        for c in cs: c.wait_send()


def backward_call(gup, gdown, *ins):
    n_up = gup.shape[1]
    gup = gup.reshape(4, 2, 2, 48, n_up)
    gdown = gdown.reshape(4, 2, 2, 2, 96, 768)
    any_ = pl.BlockSpec(memory_space=pl.ANY)
    def bufs(r, n, lead=()):
        return [VM(lead + s + (r, n), BF) for s in ((4, 2, 2), (2, 4), (4,), (4,))]
    DS = pltpu.SemaphoreType.DMA
    home = sd((2, 256, 768), BF)
    return pl.pallas_call(backward_kernel,
        out_shape=[sd((24, 2304), F32), sd((24, 768), F32), sd((24, 3072), F32), sd((96, 768), F32), sd((80, 128), F32), home],
        in_specs=[any_] * 2 + [vs] * 4 + [any_] * 2 + [vs] * 8, out_specs=[vs] * 5 + [any_],
        scratch_shapes=[VM((1024, 768), BF), VM((1024, 768), BF), VM((2560, 128), F32), VM((128, 1024), BF), VM((512, 768), BF), VM((512, 768), F32),
                        VM((1024, 768), F32), VM((1024, 768), F32), VM((512, 768), BF), VM((768, 512), BF),
                        VM((4, 2, 2, 48, 768), BF), VM((3, 4, 2, 2, 48, 768), BF), VM((4, 2, 2, 48, 1536), BF), VM((4, 2, 2, 96, 768), BF)]
        + bufs(48, 1536) + bufs(96, 768) + bufs(48, 384) + bufs(48, 384, (3,))
        + [VM((4, 2, 24, 384), F32), VM((4, 24, 384), F32), VM((1, 2, 24, 1536), F32), VM((1, 24, 1536), F32),
           VM((4, 128, 768), BF), VM((4, 128, 768), BF), VM((4, 128, 768), BF), VM((2, 128, 768), BF), VM((2, 128, 768), BF), VM((4, 80, 128), F32), VM((6, 80, 128), F32),
           DS((6, 7)), DS((6, 8)), DS((2,)), DS((6,)), DS((6,)), DS, DS, DS((6,)), DS((6,)), DS((2,)), DS((2,)), DS((2,)), DS((4,)), DS((2,)), DS((2,))],
        compiler_params=pltpu.CompilerParams(collective_id=1, has_side_effects=True, vmem_limit_bytes=63 * 2**20),
    )(gup, gdown, *ins)

def fast_shards(inputs, history, seq_lengths, attn_gain, attn_shift, qkv_weight, qkv_bias, out_weight, out_bias, mlp_gain,
                mlp_shift, up_weight, up_bias, down_weight, down_bias, mix_weights, cotangent):
    seq, batch = lax.axis_index("seq"), lax.axis_index("batch")
    z, y, x, k = seq // 2, seq % 2, batch // 2, batch % 2
    vectors = (attn_gain, attn_shift, qkv_bias, out_bias, mlp_gain, mlp_shift, up_bias, down_bias)
    COS, SIN = (jnp.asarray(t) for t in rope_tables())
    X, actsT, Q, K, V, att, lse, WQ, WO, gmid, gup, gdown, home, premix, gain, vin = forward_call(
        qkv_weight, out_weight, up_weight, down_weight, inputs, cotangent, COS, SIN, history, vectors, mix_weights, seq_lengths)
    oq, oo, ou, od, vout, grad_inputs = backward_call(gup, gdown, gmid, X, actsT, Q, K, V, att, lse, WQ, WO, gain, COS, SIN, vin)
    grad_history = (mix_weights[:-1, None, None, None] * cotangent.astype(F32)[None]).astype(BF)
    layer_out = (premix + mix_weights[-1] * home.astype(F32)).astype(BF)
    vflat = vout.reshape(-1)
    me = seq * 4 + batch
    gv, at = [], 0
    for v in vectors:
        n = v.shape[0]
        gv.append(lax.dynamic_slice_in_dim(vflat, at + me * n, n, 0))
        at += 32 * n
    grad_mix = vflat[at:at + 6]
    return (layer_out, grad_inputs, grad_history, gv[0], gv[1], oq, gv[2], oo, gv[3], gv[4], gv[5], ou, gv[6], od, gv[7], grad_mix)


def fits(mesh, inputs):
    shape = dict(mesh.shape)
    return shape == {"seq": 8, "batch": 4} and inputs.shape == (8, 2048, 768)


def solution(mesh):
    def run(*args):
        body = fast_shards if fits(mesh, args[0]) else shards
        return placed(mesh, body)(*args)
    return run
```

```python
import functools
import math

import jax
import jax.numpy as jnp
import numpy as np
from jax import lax
from jax.experimental import pallas as pl
from jax.experimental.pallas import tpu as pltpu
from jax.sharding import PartitionSpec as P

HEADS = 12
HEAD_DIM = 64
LONG_LEN = 1024
SHORT_LEN = 256


eps = 1e-05
masked = -1e30


def block_size(row_count):
    chosen = 1
    for candidate in range(1, min(row_count, 512) + 1):
        if row_count % candidate == 0:
            chosen = candidate
    return chosen


def exact_gelu(values):
    return jax.nn.gelu(values, approximate=False)


def layer_norm(values, norm_gain, norm_shift):
    average = jnp.mean(values, axis=-1, keepdims=True)
    centred = values - average
    inverse = lax.rsqrt(jnp.mean(centred * centred, axis=-1, keepdims=True) + eps)
    normed = centred * inverse
    return (normed * norm_gain + norm_shift, normed, inverse)


def norm_back(grad_out, normed, inverse, norm_gain):
    grad_normed = grad_out * norm_gain
    mean_grad = jnp.mean(grad_normed, axis=-1, keepdims=True)
    mean_cross = jnp.mean(grad_normed * normed, axis=-1, keepdims=True)
    grad_in = inverse * (grad_normed - mean_grad - normed * mean_cross)
    return (grad_in, jnp.sum(grad_out * normed, axis=0), jnp.sum(grad_out, axis=0))


def token_layout(index, info):
    seq_len, tok_count, slice_len = info
    is_long = seq_len == LONG_LEN
    offset = index % tok_count
    device = index // tok_count
    doc_ids = jnp.where(is_long, offset // slice_len, index // SHORT_LEN).astype(jnp.int32)
    relative = jnp.where(
        is_long, device * slice_len + offset % slice_len, index % SHORT_LEN
    ).astype(jnp.int32)
    return (doc_ids, relative)


def rotary_tables(relative):
    half_dim = HEAD_DIM // 2
    frequency = jnp.exp(
        -math.log(10000.0) * (2.0 * jnp.arange(half_dim, dtype=jnp.float32) / HEAD_DIM)
    )
    angles = relative.astype(jnp.float32)[:, None] * frequency[None, :]
    return (jnp.cos(angles)[:, None, :], jnp.sin(angles)[:, None, :])


def rotate(values, cosine, sine_table):
    half_dim = values.shape[-1] // 2
    lower_half = values[..., :half_dim]
    upper_half = values[..., half_dim:]
    return jnp.concatenate(
        [
            lower_half * cosine - upper_half * sine_table,
            upper_half * cosine + lower_half * sine_table,
        ],
        axis=-1,
    )


def allowed_mask(query_places, key_places, info):
    query_docs, query_rel = token_layout(query_places, info)
    key_docs, key_rel = token_layout(key_places, info)
    return (key_docs[None, :] == query_docs[:, None]) & (key_rel[None, :] <= query_rel[:, None])


def online_block(current, query_b, key_block, value_block, query_places, key_places, info):
    running, denominator, weighted = current
    key_count = key_block.shape[0]
    allowed = allowed_mask(query_places, key_places, info)
    key_heads = key_block.reshape(key_count, HEADS, HEAD_DIM)
    scores = jnp.einsum(
        "qhd,khd->hqk", query_b, key_heads, preferred_element_type=jnp.float32
    ) * HEAD_DIM ** (-0.5)
    scores = jnp.where(allowed[None], scores, masked)
    new_max = jnp.maximum(running, jnp.max(scores, axis=-1))
    exp_scores = jnp.where(allowed[None], jnp.exp(scores - new_max[..., None]), 0.0)
    rescale = jnp.exp(running - new_max)
    denominator = denominator * rescale + jnp.sum(exp_scores, axis=-1)
    value_heads = value_block.reshape(key_count, HEADS, HEAD_DIM)
    weighted = weighted * rescale[..., None] + jnp.einsum(
        "hqk,khd->hqd",
        exp_scores.astype(jnp.bfloat16),
        value_heads,
        preferred_element_type=jnp.float32,
    )
    return (new_max, denominator, weighted)


def attend_rows(current, query_b, key_rows, value_rows, first_row, query_places, info, last_place):
    key_count = key_rows.shape[0]
    block_rows = block_size(key_count)

    def one_block(carried, block_index):
        start_place = first_row + block_index * block_rows
        key_block = lax.dynamic_slice_in_dim(key_rows, block_index * block_rows, block_rows, 0)
        value_block = lax.dynamic_slice_in_dim(value_rows, block_index * block_rows, block_rows, 0)
        key_places = start_place + jnp.arange(block_rows, dtype=jnp.int32)

        def one_compute(state_in):
            return online_block(
                state_in, query_b, key_block, value_block, query_places, key_places, info
            )

        def unchanged(state_in):
            return state_in

        return (lax.cond(start_place > last_place, unchanged, one_compute, carried), None)

    result, unused = lax.scan(
        one_block, current, jnp.arange(key_count // block_rows, dtype=jnp.int32)
    )
    return result


def block_probs(query_b, key_b, query_places, key_places, info, lse_rows):
    allowed = allowed_mask(query_places, key_places, info)
    scores = jnp.einsum(
        "qhd,khd->hqk", query_b, key_b, preferred_element_type=jnp.float32
    ) * HEAD_DIM ** (-0.5)
    return jnp.exp(jnp.where(allowed[None], scores - lse_rows[..., None], masked))


def block_dscores(probabilities, grad_b, value_b, delta_rows):
    dprobs = jnp.einsum("qhd,khd->hqk", grad_b, value_b, preferred_element_type=jnp.float32)
    return (probabilities * (dprobs - delta_rows[..., None])).astype(jnp.bfloat16)


def shards(
    inputs,
    history,
    seq_lengths,
    attn_gain,
    attn_shift,
    qkv_weight,
    qkv_bias,
    out_weight,
    out_bias,
    mlp_gain,
    mlp_shift,
    up_weight,
    up_bias,
    down_weight,
    down_bias,
    mix_weights,
    cotangent,
):
    group_count = inputs.shape[0]
    tok_count = inputs.shape[1]
    model_width = inputs.shape[2]
    seq_count = lax.axis_size("seq")
    group_rows = tok_count * seq_count
    slice_len = LONG_LEN // seq_count
    factor = HEAD_DIM ** (-0.5)
    seq_index = lax.axis_index("seq")
    first_place = seq_index * tok_count
    last_place = first_place + tok_count - 1
    places = first_place + jnp.arange(tok_count, dtype=jnp.int32)
    gathered = (
        lax.all_gather(attn_gain, ("seq", "batch"), axis=0, tiled=True),
        lax.all_gather(attn_shift, ("seq", "batch"), axis=0, tiled=True),
        lax.all_gather(qkv_weight, ("seq", "batch"), axis=0, tiled=True),
        lax.all_gather(qkv_bias, ("seq", "batch"), axis=0, tiled=True),
        lax.all_gather(out_weight, ("seq", "batch"), axis=0, tiled=True),
        lax.all_gather(out_bias, ("seq", "batch"), axis=0, tiled=True),
        lax.all_gather(mlp_gain, ("seq", "batch"), axis=0, tiled=True),
        lax.all_gather(mlp_shift, ("seq", "batch"), axis=0, tiled=True),
        lax.all_gather(up_weight, ("seq", "batch"), axis=0, tiled=True),
        lax.all_gather(up_bias, ("seq", "batch"), axis=0, tiled=True),
        lax.all_gather(down_weight, ("seq", "batch"), axis=0, tiled=True),
        lax.all_gather(down_bias, ("seq", "batch"), axis=0, tiled=True),
    )
    (
        gain_one,
        shift_one,
        qkv_full,
        qkv_vec,
        out_full,
        out_vec,
        gain_two,
        shift_two,
        up_full,
        up_vec,
        down_full,
        down_vec,
    ) = gathered
    saved = []
    block_outs = []
    for group in range(group_count):
        info = (seq_lengths[group], tok_count, slice_len)
        doc_ids, relative = token_layout(places, info)
        cosine, sine_table = rotary_tables(relative)
        residual_in = inputs[group].astype(jnp.float32)
        normed_out, normed_one, inverse_one = layer_norm(
            residual_in, gain_one.astype(jnp.float32), shift_one.astype(jnp.float32)
        )
        acts_one = normed_out.astype(jnp.bfloat16)
        projected = jnp.dot(
            acts_one, qkv_full, preferred_element_type=jnp.float32
        ) + qkv_vec.astype(jnp.float32)
        queries = rotate(
            projected[:, :model_width].reshape(tok_count, HEADS, HEAD_DIM), cosine, sine_table
        ).astype(jnp.bfloat16)
        key_flat = (
            rotate(
                projected[:, model_width : 2 * model_width].reshape(tok_count, HEADS, HEAD_DIM),
                cosine,
                sine_table,
            )
            .reshape(tok_count, model_width)
            .astype(jnp.bfloat16)
        )
        value_flat = projected[:, 2 * model_width :].astype(jnp.bfloat16)
        start_state = (
            jnp.full((HEADS, tok_count), masked, jnp.float32),
            jnp.zeros((HEADS, tok_count), jnp.float32),
            jnp.zeros((HEADS, tok_count, HEAD_DIM), jnp.float32),
        )
        key_all = None
        value_all = None
        running, denominator, weighted = attend_rows(
            start_state,
            queries,
            lax.all_gather(key_flat, "seq", axis=0, tiled=True),
            lax.all_gather(value_flat, "seq", axis=0, tiled=True),
            jnp.int32(0),
            places,
            info,
            last_place,
        )
        attended = jnp.transpose(weighted / denominator[..., None], (1, 0, 2))
        lse_rows = running + jnp.log(denominator)
        attended_b = attended.reshape(tok_count, model_width).astype(jnp.bfloat16)
        middle = (
            residual_in
            + jnp.dot(attended_b, out_full, preferred_element_type=jnp.float32)
            + out_vec.astype(jnp.float32)
        )
        normed_out_two, normed_two, inverse_two = layer_norm(
            middle, gain_two.astype(jnp.float32), shift_two.astype(jnp.float32)
        )
        acts_two = normed_out_two.astype(jnp.bfloat16)
        upward = jnp.dot(acts_two, up_full, preferred_element_type=jnp.float32) + up_vec.astype(
            jnp.float32
        )
        activated, gelu_back = jax.vjp(exact_gelu, upward)
        activated_b = activated.astype(jnp.bfloat16)
        block_out = (
            middle
            + jnp.dot(activated_b, down_full, preferred_element_type=jnp.float32)
            + down_vec.astype(jnp.float32)
        )
        block_outs.append(block_out)
        saved.append(
            (
                info,
                cosine,
                sine_table,
                normed_one,
                inverse_one,
                acts_one,
                queries,
                key_flat,
                value_flat,
                key_all,
                value_all,
                attended,
                lse_rows,
                attended_b,
                normed_two,
                inverse_two,
                acts_two,
                gelu_back,
                activated_b,
            )
        )
    block_stack = jnp.stack(block_outs, axis=0)
    earlier = history.astype(jnp.float32)
    grad_out_all = cotangent.astype(jnp.float32)
    mixed_out = (
        jnp.sum(mix_weights[:-1, None, None, None] * earlier, axis=0)
        + mix_weights[-1] * block_stack
    )
    mix_terms = jnp.concatenate(
        [
            jnp.sum(earlier * grad_out_all[None], axis=(1, 2, 3)),
            jnp.sum(block_stack * grad_out_all)[None],
        ]
    )
    grad_history = (mix_weights[:-1, None, None, None] * grad_out_all[None]).astype(jnp.bfloat16)
    back_gain_one, back_qkv, back_out, back_gain_two, back_up, back_down = (
        lax.all_gather(attn_gain, ("seq", "batch"), axis=0, tiled=True),
        lax.all_gather(qkv_weight, ("seq", "batch"), axis=0, tiled=True),
        lax.all_gather(out_weight, ("seq", "batch"), axis=0, tiled=True),
        lax.all_gather(mlp_gain, ("seq", "batch"), axis=0, tiled=True),
        lax.all_gather(up_weight, ("seq", "batch"), axis=0, tiled=True),
        lax.all_gather(down_weight, ("seq", "batch"), axis=0, tiled=True),
    )
    totals = None
    grad_input_list = []
    for group in range(group_count):
        (
            info,
            cosine,
            sine_table,
            normed_one,
            inverse_one,
            acts_one,
            queries,
            key_flat,
            value_flat,
            key_all,
            value_all,
            attended,
            lse_rows,
            attended_b,
            normed_two,
            inverse_two,
            acts_two,
            gelu_back,
            activated_b,
        ) = saved[group]
        grad_block = mix_weights[-1] * grad_out_all[group]
        down_grad_b = grad_block.astype(jnp.bfloat16)
        grad_w_down = jnp.einsum(
            "tf,td->fd", activated_b, down_grad_b, preferred_element_type=jnp.float32
        )
        grad_b_down = jnp.sum(down_grad_b.astype(jnp.float32), axis=0)
        grad_act = jnp.einsum(
            "td,fd->tf", down_grad_b, back_down, preferred_element_type=jnp.float32
        )
        up_grad_b = gelu_back(grad_act)[0].astype(jnp.bfloat16)
        grad_w_up = jnp.einsum("td,tf->df", acts_two, up_grad_b, preferred_element_type=jnp.float32)
        grad_b_up = jnp.sum(up_grad_b.astype(jnp.float32), axis=0)
        grad_acts_two = jnp.einsum(
            "tf,df->td", up_grad_b, back_up, preferred_element_type=jnp.float32
        )
        grad_middle_norm, grad_gain_two, grad_shift_two = norm_back(
            grad_acts_two, normed_two, inverse_two, back_gain_two.astype(jnp.float32)
        )
        grad_middle = grad_block + grad_middle_norm
        attn_grad_b = grad_middle.astype(jnp.bfloat16)
        grad_w_out = jnp.einsum(
            "te,td->ed", attended_b, attn_grad_b, preferred_element_type=jnp.float32
        )
        grad_b_out = jnp.sum(attn_grad_b.astype(jnp.float32), axis=0)
        grad_heads = (
            jnp.einsum("td,ed->te", attn_grad_b, back_out, preferred_element_type=jnp.float32)
            .astype(jnp.bfloat16)
            .reshape(tok_count, HEADS, HEAD_DIM)
        )
        delta_rows = jnp.transpose(jnp.sum(grad_heads.astype(jnp.float32) * attended, axis=-1))
        key_all, value_all = (
            lax.all_gather(key_flat, "seq", axis=0, tiled=True),
            lax.all_gather(value_flat, "seq", axis=0, tiled=True),
        )
        key_block_rows = block_size(group_rows)

        def query_grad_block(carried, block_index):
            start_place = block_index * key_block_rows
            key_block = lax.dynamic_slice_in_dim(key_all, start_place, key_block_rows, 0).reshape(
                key_block_rows, HEADS, HEAD_DIM
            )
            value_block = lax.dynamic_slice_in_dim(
                value_all, start_place, key_block_rows, 0
            ).reshape(key_block_rows, HEADS, HEAD_DIM)
            key_places = start_place + jnp.arange(key_block_rows, dtype=jnp.int32)

            def query_compute(summed):
                probabilities = block_probs(queries, key_block, places, key_places, info, lse_rows)
                dscores = block_dscores(probabilities, grad_heads, value_block, delta_rows)
                return (
                    summed
                    + jnp.einsum(
                        "hqk,khd->qhd", dscores, key_block, preferred_element_type=jnp.float32
                    )
                    * factor
                )

            return (
                lax.cond(start_place > last_place, lambda summed: summed, query_compute, carried),
                None,
            )

        grad_queries, unused = lax.scan(
            query_grad_block,
            jnp.zeros((tok_count, HEADS, HEAD_DIM), jnp.float32),
            jnp.arange(group_rows // key_block_rows, dtype=jnp.int32),
        )
        key_first_row = jnp.int32(0)
        key_rows = key_all
        value_rows = value_all
        inner_rows = block_size(lax.axis_size("seq") * tok_count)

        def key_grad_block(carried, block_index):
            offset = block_index * inner_rows
            start_place = key_first_row + offset
            key_block = lax.dynamic_slice_in_dim(key_rows, offset, inner_rows, 0).reshape(
                inner_rows, HEADS, HEAD_DIM
            )
            value_block = lax.dynamic_slice_in_dim(value_rows, offset, inner_rows, 0).reshape(
                inner_rows, HEADS, HEAD_DIM
            )
            key_places = start_place + jnp.arange(inner_rows, dtype=jnp.int32)

            def key_compute(unused_in):
                probabilities = block_probs(queries, key_block, places, key_places, info, lse_rows)
                dscores = block_dscores(probabilities, grad_heads, value_block, delta_rows)
                grad_keys = (
                    jnp.einsum("hqk,qhd->khd", dscores, queries, preferred_element_type=jnp.float32)
                    * factor
                )
                grad_values = jnp.einsum(
                    "hqk,qhd->khd",
                    probabilities.astype(jnp.bfloat16),
                    grad_heads,
                    preferred_element_type=jnp.float32,
                )
                return jnp.concatenate(
                    [
                        grad_keys.reshape(inner_rows, model_width),
                        grad_values.reshape(inner_rows, model_width),
                    ],
                    axis=1,
                )

            def nothing(unused_in):
                return jnp.zeros((inner_rows, 2 * model_width), jnp.float32)

            return (carried, lax.cond(start_place > last_place, nothing, key_compute, carried))

        unused_out, blocks = lax.scan(
            key_grad_block,
            jnp.int32(0),
            jnp.arange(lax.axis_size("seq") * tok_count // inner_rows, dtype=jnp.int32),
        )
        key_grads = lax.psum_scatter(
            blocks.reshape(lax.axis_size("seq") * tok_count, 2 * model_width).astype(jnp.bfloat16),
            "seq",
            scatter_dimension=0,
            tiled=True,
        ).astype(jnp.float32)
        grad_keys_own = key_grads[:, :model_width]
        grad_values_own = key_grads[:, model_width:]
        grad_q_turned = rotate(grad_queries, cosine, -sine_table).reshape(tok_count, model_width)
        grad_k_turned = rotate(
            grad_keys_own.reshape(tok_count, HEADS, HEAD_DIM), cosine, -sine_table
        ).reshape(tok_count, model_width)
        qkv_grad_b = jnp.concatenate(
            [grad_q_turned, grad_k_turned, grad_values_own], axis=1
        ).astype(jnp.bfloat16)
        grad_w_qkv = jnp.einsum(
            "td,te->de", acts_one, qkv_grad_b, preferred_element_type=jnp.float32
        )
        grad_b_qkv = jnp.sum(qkv_grad_b.astype(jnp.float32), axis=0)
        grad_acts_one = jnp.einsum(
            "te,de->td", qkv_grad_b, back_qkv, preferred_element_type=jnp.float32
        )
        grad_in_norm, grad_gain_one, grad_shift_one = norm_back(
            grad_acts_one, normed_one, inverse_one, back_gain_one.astype(jnp.float32)
        )
        grad_input_list.append((grad_middle + grad_in_norm).astype(jnp.bfloat16))
        terms = [
            grad_gain_one,
            grad_shift_one,
            grad_w_qkv,
            grad_b_qkv,
            grad_w_out,
            grad_b_out,
            grad_gain_two,
            grad_shift_two,
            grad_w_up,
            grad_b_up,
            grad_w_down,
            grad_b_down,
        ]
        if totals is None:
            totals = terms
        else:
            totals = [older + newer for older, newer in zip(totals, terms)]
    shares = (
        lax.psum_scatter(totals[0], ("seq", "batch"), scatter_dimension=0, tiled=True),
        lax.psum_scatter(totals[1], ("seq", "batch"), scatter_dimension=0, tiled=True),
        lax.psum_scatter(totals[2], ("seq", "batch"), scatter_dimension=0, tiled=True),
        lax.psum_scatter(totals[3], ("seq", "batch"), scatter_dimension=0, tiled=True),
        lax.psum_scatter(totals[4], ("seq", "batch"), scatter_dimension=0, tiled=True),
        lax.psum_scatter(totals[5], ("seq", "batch"), scatter_dimension=0, tiled=True),
        lax.psum_scatter(totals[6], ("seq", "batch"), scatter_dimension=0, tiled=True),
        lax.psum_scatter(totals[7], ("seq", "batch"), scatter_dimension=0, tiled=True),
        lax.psum_scatter(totals[8], ("seq", "batch"), scatter_dimension=0, tiled=True),
        lax.psum_scatter(totals[9], ("seq", "batch"), scatter_dimension=0, tiled=True),
        lax.psum_scatter(totals[10], ("seq", "batch"), scatter_dimension=0, tiled=True),
        lax.psum_scatter(totals[11], ("seq", "batch"), scatter_dimension=0, tiled=True),
    )
    grad_mix = lax.psum(mix_terms, ("seq", "batch"))
    grad_inputs = jnp.stack(grad_input_list, axis=0)
    return (
        mixed_out.astype(jnp.bfloat16),
        grad_inputs,
        grad_history,
        shares[0],
        shares[1],
        shares[2],
        shares[3],
        shares[4],
        shares[5],
        shares[6],
        shares[7],
        shares[8],
        shares[9],
        shares[10],
        shares[11],
        grad_mix,
    )


def placed(mesh, body):
    return jax.shard_map(
        body,
        mesh=mesh,
        in_specs=(
            P("batch", "seq", None),
            P(None, "batch", "seq", None),
            P("batch"),
            P(("seq", "batch")),
            P(("seq", "batch")),
            P(("seq", "batch"), None),
            P(("seq", "batch")),
            P(("seq", "batch"), None),
            P(("seq", "batch")),
            P(("seq", "batch")),
            P(("seq", "batch")),
            P(("seq", "batch"), None),
            P(("seq", "batch")),
            P(("seq", "batch"), None),
            P(("seq", "batch")),
            P(),
            P("batch", "seq", None),
        ),
        out_specs=(
            P("batch", "seq", None),
            P("batch", "seq", None),
            P(None, "batch", "seq", None),
            P(("seq", "batch")),
            P(("seq", "batch")),
            P(("seq", "batch"), None),
            P(("seq", "batch")),
            P(("seq", "batch"), None),
            P(("seq", "batch")),
            P(("seq", "batch")),
            P(("seq", "batch")),
            P(("seq", "batch"), None),
            P(("seq", "batch")),
            P(("seq", "batch"), None),
            P(("seq", "batch")),
            P(),
        ),
        check_vma=False,
    )

MESH = pl.DeviceIdType.MESH
BF, F32 = jnp.bfloat16, jnp.float32


def where_am_i():
    seq, batch = lax.axis_index("seq"), lax.axis_index("batch")
    return seq // 2, seq % 2, batch // 2, batch % 2


def dev(z, y, x, k):
    return (z * 2 + y, x * 2 + k)


def remote(src, dst, ssem, rsem, device):
    return pltpu.make_async_remote_copy(src_ref=src, dst_ref=dst, send_sem=ssem, recv_sem=rsem,
                                        device_id=device, device_id_type=MESH)


def chips_of(z, y, x):
    mine = (z * 2 + y) * 2 + x
    for step in range(1, 16):
        other = lax.rem(mine + step, 16)
        yield step, (other // 4, (other // 2) % 2, other % 2)


def greet(z, y, x, k):
    barrier = pltpu.get_barrier_semaphore()
    for _, chip in chips_of(z, y, x):
        pl.semaphore_signal(barrier, inc=1, device_id=dev(*chip, k), device_id_type=MESH)
    for step in range(8):
        other = lax.rem(z * 2 + y + step, 8)
        pl.semaphore_signal(barrier, inc=1, device_id=dev(other // 2, other % 2, x, 1 - k), device_id_type=MESH)
    pl.semaphore_wait(barrier, 23)


class Gather:
    STAGES = 7

    def __init__(self, part, send, recv, pos, both, hops):
        z, y, x, k = pos
        self.hops = hops
        turn = (k == 0) | both
        p2 = jnp.where(turn, 1 - y, y), jnp.where(turn, x, 1 - x)
        p3 = jnp.where(turn, y, 1 - y), jnp.where(turn, 1 - x, x)
        d4 = 1 - y, 1 - x
        one = lambda zz: part(pl.ds(zz, 1), y, x, k)
        allz = lambda yx: part(slice(None), yx[0], yx[1], k)
        self.mid = (z == 1) | (z == 2)
        end = jnp.where(z == 1, 0, 3)
        def cp(n, ref, device, r=None):
            return remote(ref, ref, send.at[n], recv.at[n if r is None else r], device)
        others = [lax.rem(z + d, 4) for d in (1, 2, 3)]
        self.three = [cp(d, one(o), dev(o, y, x, k), o) for d, o in enumerate(others)]
        if hops:
            self.direct = [cp(0, one(z), dev(jnp.where(z == 1, 0, 1), y, x, k), z), cp(1, one(z), dev(jnp.where(z == 2, 3, 2), y, x, k), z)]
        else:
            self.direct = [cp(d, one(z), dev(o, y, x, k), z) for d, o in enumerate(others)]
        self.passed = [cp(3 + n, one(f), dev(end, y, x, k), f) for n, f in enumerate((3 - z, 3 - end))]
        self.near = cp(0, one(end), dev(end, y, x, k), end)
        n2, n3 = dev(z, *p2, k), dev(z, *p3, k)
        blocks = [z] + others
        self.a2 = [cp(5 + n, one(b), n2, 4 + b) for n, b in enumerate(blocks)]
        self.a3 = [cp(9 + n, one(b), n3, 8 + b) for n, b in enumerate(blocks)]
        self.b3 = [cp(13 + n, part(pl.ds(b, 1), *p2, k), n3, 12 + b) for n, b in enumerate(blocks)]
        sib = dev(z, y, x, 1 - k)
        self.s = [cp(17 + n, allz(p), sib, 16 + n) for n, p in enumerate(((y, x), p2, p3, d4))]

    def early(self):
        self.a2[0].start(); self.a3[0].start()

    def early_on(self):
        self.a2[0].wait_recv()
        self.b3[0].start()

    def stage(self, n):
        if n == 0:
            for c in self.direct: c.start()
        elif n == 1:
            if self.hops:
                @pl.when(self.mid)
                def _():
                    for c in self.passed:
                        c.wait_recv()
                        c.start()
        elif n == 2:
            if self.hops:
                @pl.when(self.mid)
                def _():
                    self.near.wait_recv()
                @pl.when(jnp.logical_not(self.mid))
                def _():
                    for c in self.three: c.wait_recv()
            else:
                for c in self.three: c.wait_recv()
            for c in self.a2[1:] + self.a3[1:]: c.start()
            self.s[0].start()
        elif n == 3:
            for c in self.a2[1:]: c.wait_recv()
            for c in self.b3[1:]: c.start()
            self.s[1].start()
        elif n == 4:
            for c in self.a3: c.wait_recv()
            self.s[2].start()
        elif n == 5:
            for c in self.b3: c.wait_recv()
            self.s[3].start()
        elif n == 6:
            for c in self.s: c.wait_recv()

    def sent(self):
        for c in self.direct + self.a2 + self.a3 + self.b3 + self.s: c.wait_send()
        if self.hops:
            @pl.when(self.mid)
            def _():
                for c in self.passed: c.wait_send()


class Home:
    def __init__(self, buf, cross, sel, out, length, sems, pos):
        self.__dict__.update(locals())
        z, y, x, k = pos
        self.esend, self.erecv, self.send, self.h0, self.hs = sems
        self.swap = [remote(buf.at[self.crossed(n)], cross.at[n], self.esend.at[n], self.erecv.at[n], dev(z, 1 - y, x, 1 - k)) for n in range(2)]
        self.sent = []

    def crossed(self, n):
        z, y, x, k = self.pos
        return lax.rem(1 - y + k, 2) + 2 * n

    def go(self, ref, i, h, sem, n):
        z, y, x, k = self.pos
        slot = lax.rem(z, 2)
        dst = self.out.at[slot, pl.ds(pl.multiple_of(h * 128, 128), 128)]
        me = (i == z) & (z // 2 == k)
        cp = remote(ref, dst, self.send.at[n], sem.at[slot], dev(i, y, x, z // 2))
        @pl.when(me)
        def _():
            pltpu.make_async_copy(ref, dst, sem.at[slot]).start()
        @pl.when(jnp.logical_not(me))
        def _():
            cp.start()
        self.sent.append((cp, jnp.logical_not(me)))

    def first(self):
        z, y, x, k = self.pos
        for c in self.swap: c.start()
        for n in range(2):
            i = lax.rem(y + k, 2) + 2 * n
            self.go(self.buf.at[i], i, y, self.h0, n)

    def second(self):
        z, y, x, k = self.pos
        for n in range(2):
            self.swap[n].wait_recv()
            i = self.crossed(n)
            far = jnp.broadcast_to(self.length, (128, 768)) > 512.0
            self.sel[n] = jnp.where(far, self.cross[n].astype(F32), self.buf[i].astype(F32)).astype(BF)
            self.go(self.sel.at[n], i, 1 - y, self.hs, 2 + n)

    def done(self):
        z, y, x, k = self.pos
        for g in range(2):
            for h, sem in ((y, self.h0), (1 - y, self.hs)):
                dst = self.out.at[g, pl.ds(pl.multiple_of(h * 128, 128), 128)]
                remote(dst, dst, self.send.at[0], sem.at[g], dev(z, y, x, 1 - k)).wait_recv()
        for c in self.swap: c.wait_send()
        for cp, cond in self.sent:
            @pl.when(cond)
            def _():
                cp.wait_send()

EPS = 1e-5
NT = (((1,), (1,)), ((), ()))


def nt(a, b):
    return lax.dot_general(a, b, NT, preferred_element_type=F32)


def nn(a, b):
    return jnp.dot(a, b, preferred_element_type=F32)


def rope_tables():
    freq = np.exp(-math.log(10000.0) * (2.0 * np.arange(32, dtype=np.float32) / 64)).astype(np.float32)
    ang = np.arange(1024, dtype=np.float32)[:, None] * freq[None, :]
    c, s = np.cos(ang.astype(np.float64)), np.sin(ang.astype(np.float64))
    return (np.concatenate([c, c, c, c], 1).astype(np.float32), np.concatenate([-s, s, -s, s], 1).astype(np.float32))


def swap(u):
    low = lax.broadcasted_iota(jnp.int32, u.shape, 1) % 64 < 32
    return jnp.where(low, pltpu.roll(u, 96, 1), pltpu.roll(u, 32, 1))


def norm(v):
    mean = jnp.mean(v, axis=-1, keepdims=True)
    cen = v - mean
    inv = lax.rsqrt(jnp.mean(cen * cen, axis=-1, keepdims=True) + EPS)
    return cen * inv, inv


def norm_grad(e, n, inv, gain):
    g = e * gain
    return inv * (g - jnp.mean(g, axis=-1, keepdims=True) - n * jnp.mean(g * n, axis=-1, keepdims=True))


def own_block(i, k):
    return 2 * i + lax.rem(i + k, 2)


def rows(i, n=128):
    return pl.ds(pl.multiple_of(i * n, n), n)


def spread(p):
    low = lax.broadcasted_iota(jnp.int32, p.shape, 1) < 64
    zero = jnp.zeros_like(p)
    return jnp.concatenate([jnp.where(low, p, zero), jnp.where(low, zero, p)], axis=0)


def pick(o):
    low = lax.broadcasted_iota(jnp.int32, (128, 128), 0) < 64
    return jnp.where(low, o[:, :128], o[:, 128:]).T


def fill_bias(bias, is_long, k):
    at = 0
    for i in range(4):
        kk = 256 * (i + 1)
        key = lax.broadcasted_iota(jnp.int32, (kk, 256), 0)
        q = own_block(i, k) * 128 + lax.broadcasted_iota(jnp.int32, (kk, 256), 1) % 128
        first = jnp.where(is_long, 0, q - q % 256)
        bias[at:at + kk, :] = jnp.where((key <= q) & (key >= first), 0.0, -1e30)
        at += kk


def attn_fwd(flag, XM, XA, wqkv, wout, gain, shift, bqkv, bout, COS, SIN,
             acts, Q, K, V, att, lse, middle, bias, VT):
    z, y, x, k = where_am_i()
    is_long = flag[0] != 0
    fill_bias(bias, is_long, k)
    for j in range(8):
        alt = jnp.logical_and(jnp.logical_not(is_long), lax.rem(jnp.int32(j), 2) != y)
        blk = jnp.where(alt, XA[j // 2], XM[j]).astype(F32)
        n, _ = norm(blk)
        acts[j * 128:(j + 1) * 128, :] = (n * gain[...] + shift[...]).astype(BF)

    def tables(j):
        off = jnp.where(is_long, j, lax.rem(j, 2))
        return COS[rows(off), :], SIN[rows(off), :]

    @pl.loop(0, 8)
    def _(j):
        a = acts[rows(j), :]
        c, s = tables(j)
        for t in range(6):
            u = nn(a, wqkv[:, 768 + t * 128:896 + t * 128]) + bqkv[:, 768 + t * 128:896 + t * 128]
            K[rows(j), t * 128:(t + 1) * 128] = (u * c + swap(u) * s).astype(BF)
        V[rows(j), :] = (nn(a, wqkv[:, 1536:]) + bqkv[:, 1536:]).astype(BF)

    @pl.loop(0, 4)
    def _(i):
        j = own_block(i, k)
        a = acts[rows(j), :]
        c, s = tables(j)
        for t in range(6):
            u = nn(a, wqkv[:, t * 128:(t + 1) * 128]) + bqkv[:, t * 128:(t + 1) * 128]
            Q[rows(i), t * 128:(t + 1) * 128] = (u * c + swap(u) * s).astype(BF) * jnp.asarray(0.125, BF)

    @pl.loop(0, 6)
    def _(h):
        lanes = rows(h)
        VT[...] = V[:, lanes].T
        at = 0
        for i in range(4):
            kk = 256 * (i + 1)
            qb = spread(Q[i * 128:(i + 1) * 128, lanes])
            st = nt(K[0:kk, lanes], qb) + bias[at:at + kk, :]
            top = jnp.max(st, axis=0, keepdims=True)
            p = jnp.exp(st - top)
            den = jnp.sum(p, axis=0, keepdims=True)
            o = nn(VT[:, 0:kk], p.astype(BF)) * (1.0 / den)
            att[i * 128:(i + 1) * 128, lanes] = pick(o)
            lse[h, i:i + 1, :] = top + jnp.log(den)
            at += kk

    @pl.loop(0, 4)
    def _(i):
        j = own_block(i, k)
        alt = jnp.logical_and(jnp.logical_not(is_long), lax.rem(j, 2) != y)
        xb = jnp.where(alt, XA[i], XM[j]).astype(F32)
        middle[rows(i), :] = xb + (nn(att[rows(i), :].astype(BF), wout[...]) + bout[...])


def mlp(CH, flag, mix, middle, CM, CA, wup, wdown, gain, shift, bup, bdown,
        block, gmid, gup, gdown, g_gain, g_shift, g_bup, g_bdown, mixsum, acts2, actsT, dg, ga, cf):
    z, y, x, k = where_am_i()
    is_long = flag[0] != 0
    m5 = mix[5]
    for i in range(4):
        r = slice(i * 128, (i + 1) * 128)
        mid = middle[r, :]
        n, _ = norm(mid)
        acts2[r, :] = (n * gain[...] + shift[...]).astype(BF)
        j = own_block(jnp.int32(i), k)
        alt = jnp.logical_and(jnp.logical_not(is_long), lax.rem(j, 2) != y)
        c = jnp.where(alt, CA[i], CM[j]).astype(F32)
        cf[r, :] = c
        dg[r, :] = (m5 * c).astype(BF)
        block[r, :] = mid + bdown[...]
        ga[r, :] = jnp.zeros_like(mid)
        actsT[:, r] = acts2[r, :].T
    g_bdown[...] = jnp.sum(dg[...].astype(F32), axis=0, keepdims=True)

    @pl.loop(0, wup.shape[1] // CH)
    def _(f):
        cols = rows(f, CH)
        up = nn(acts2[...], wup[:, cols]) + bup[:, cols]
        half_erf = 0.5 * lax.erf(up * (2.0 ** -0.5)) + 0.5
        slope = half_erf + up * (jnp.exp(up * up * -0.5) * (1.0 / math.sqrt(2 * math.pi)))
        act = (up * half_erf).astype(BF)
        block[...] += nn(act, wdown[cols, :])
        upg = (nt(dg[...], wdown[cols, :]) * slope).astype(BF)
        g_bup[:, cols] = jnp.sum(upg.astype(F32), axis=0, keepdims=True)
        gdown[cols, :] = nn(act.T, dg[...]).astype(BF)
        gup[:, cols] = nn(actsT[...], upg).astype(BF)
        ga[...] += nt(upg, wup[:, cols])

    total = jnp.zeros((1, 768), F32)
    gg = jnp.zeros((1, 768), F32)
    gs = jnp.zeros((1, 768), F32)
    for i in range(4):
        r = slice(i * 128, (i + 1) * 128)
        n, inv = norm(middle[r, :])
        e = ga[r, :]
        gg += jnp.sum(e * n, axis=0, keepdims=True)
        gs += jnp.sum(e, axis=0, keepdims=True)
        gmid[r, :] = m5 * cf[r, :] + norm_grad(e, n, inv, gain[...])
        total += jnp.sum(cf[r, :] * block[r, :], axis=0, keepdims=True)
    g_gain[...] = gg
    g_shift[...] = gs
    mixsum[...] = total


def attn_bwd(flag, gmid, acts, Q, K, V, att, lse, wqkv, wout, COS, SIN,
             e, gqkv, gout, g_bqkv, g_bout, bias, KT, da, dQ, dK, dV, agrad, actsT, actsqT, KG, VG):
    z, y, x, k = where_am_i()
    is_long = flag[0] != 0
    fill_bias(bias, is_long, k)
    agrad[...] = gmid[...].astype(BF)
    g_bout[...] = jnp.sum(agrad[...].astype(F32), axis=0, keepdims=True)

    @pl.loop(0, 4)
    def _(i):
        da[rows(i), :] = nt(agrad[rows(i), :], wout[...]).astype(BF)

    for t in range(6):
        aT = att[:, t * 128:(t + 1) * 128].T.astype(BF)
        gout[t * 128:(t + 1) * 128, :] = nn(aT, agrad[...]).astype(BF)
    dK[...] = jnp.zeros_like(dK)
    dV[...] = jnp.zeros_like(dV)

    @pl.loop(0, 6)
    def _(h):
        lanes = rows(h)
        KT[...] = K[:, lanes].T
        at = 0
        for i in range(4):
            kk = 256 * (i + 1)
            r = slice(i * 128, (i + 1) * 128)
            d = da[r, lanes]
            qb, db = spread(Q[r, lanes]), spread(d)
            prod = (d.astype(F32) * att[r, lanes]).T
            delta = jnp.concatenate([jnp.sum(prod[:64], axis=0, keepdims=True), jnp.sum(prod[64:], axis=0, keepdims=True)], axis=1)
            st = nt(K[0:kk, lanes], qb) + bias[at:at + kk, :]
            p = jnp.exp(st - lse[h, i:i + 1, :])
            ds = (p * (nt(V[0:kk, lanes], db) - delta)).astype(BF)
            dV[0:kk, lanes] += nn(p.astype(BF), db)
            dK[0:kk, lanes] += nn(ds, qb)
            dQ[r, lanes] = pick(nn(KT[:, 0:kk], ds)) * 0.125
            at += kk

    def tables(j):
        off = jnp.where(is_long, j, lax.rem(j, 2))
        return COS[rows(off), :], SIN[rows(off), :]

    for j in range(8):
        actsT[:, j * 128:(j + 1) * 128] = acts[j * 128:(j + 1) * 128, :].T
    for i in range(4):
        j = own_block(jnp.int32(i), k)
        actsqT[:, i * 128:(i + 1) * 128] = acts[rows(j), :].T
        c, s = tables(j)
        for t in range(6):
            u = dQ[i * 128:(i + 1) * 128, t * 128:(t + 1) * 128]
            da[i * 128:(i + 1) * 128, t * 128:(t + 1) * 128] = (u * c - swap(u) * s).astype(BF)

    @pl.loop(0, 8)
    def _(j):
        c, s = tables(j)
        for t in range(6):
            u = dK[rows(j), t * 128:(t + 1) * 128]
            KG[rows(j), t * 128:(t + 1) * 128] = (u * c - swap(u) * s).astype(BF)
        VG[rows(j), :] = dV[rows(j), :].astype(BF)
        e[rows(j), :] = nt(KG[rows(j), :], wqkv[:, 768:1536]) + nt(VG[rows(j), :], wqkv[:, 1536:])

    @pl.loop(0, 4)
    def _(i):
        j = own_block(i, k)
        e[rows(j), :] += nt(da[rows(i), :], wqkv[:, :768])

    g_bqkv[:, :768] = jnp.sum(da[...].astype(F32), axis=0, keepdims=True)
    g_bqkv[:, 768:1536] = jnp.sum(KG[...].astype(F32), axis=0, keepdims=True)
    g_bqkv[:, 1536:] = jnp.sum(VG[...].astype(F32), axis=0, keepdims=True)

    @pl.loop(0, 6)
    def _(t):
        gqkv[rows(t), :768] = nn(actsqT[rows(t), :], da[...]).astype(BF)
        gqkv[rows(t), 768:1536] = nn(actsT[rows(t), :], KG[...]).astype(BF)
        gqkv[rows(t), 1536:] = nn(actsT[rows(t), :], VG[...]).astype(BF)


sd = jax.ShapeDtypeStruct
VM = pltpu.VMEM
vs = pl.BlockSpec(memory_space=pltpu.VMEM)
ss = pl.BlockSpec(memory_space=pltpu.SMEM)
CP = pltpu.CompilerParams(vmem_limit_bytes=60 * 2**20)


def attn_fwd_call(flag, *ins):
    return pl.pallas_call(attn_fwd,
        out_shape=[sd((1024, 768), BF), sd((512, 768), BF), sd((1024, 768), BF), sd((1024, 768), BF),
                   sd((512, 768), F32), sd((6, 4, 256), F32), sd((512, 768), F32)],
        in_specs=[ss] + [vs] * len(ins), out_specs=[vs] * 7,
        scratch_shapes=[VM((2560, 256), F32), VM((128, 1024), BF)],
        compiler_params=CP)(flag, *ins)


def mlp_call(flag, mix, *ins):
    r = sd((1, 768), F32)
    return pl.pallas_call(functools.partial(mlp, 512),
        out_shape=[sd((512, 768), F32), sd((512, 768), F32), sd((768, 3072), BF), sd((3072, 768), BF), r, r, sd((1, 3072), F32), r, r],
        in_specs=[ss, ss] + [vs] * len(ins), out_specs=[vs] * 9,
        scratch_shapes=[VM((512, 768), BF), VM((768, 512), BF), VM((512, 768), BF), VM((512, 768), F32), VM((512, 768), F32)],
        compiler_params=CP)(flag, mix, *ins)


def attn_bwd_call(flag, *ins):
    return pl.pallas_call(attn_bwd,
        out_shape=[sd((1024, 768), F32), sd((768, 2304), BF), sd((768, 768), BF), sd((1, 2304), F32), sd((1, 768), F32)],
        in_specs=[ss] + [vs] * len(ins), out_specs=[vs] * 5,
        scratch_shapes=[VM((2560, 256), F32), VM((128, 1024), BF), VM((512, 768), BF), VM((512, 768), F32), VM((1024, 768), F32),
                        VM((1024, 768), F32), VM((512, 768), BF), VM((768, 1024), BF), VM((768, 512), BF), VM((1024, 768), BF), VM((1024, 768), BF)],
        compiler_params=CP)(flag, *ins)


VROWS = (24, 24, 72, 24, 24, 24, 96, 24)


def widen(vecs, row, n):
    v = vecs[:, row, :].astype(BF)
    wide = 32 * n
    j = lax.broadcasted_iota(jnp.int32, (128, wide), 1)
    i = lax.broadcasted_iota(jnp.int32, (128, wide), 0)
    q = jnp.floor((j.astype(F32) + 0.5) * (1.0 / n)).astype(jnp.int32)
    hot = jnp.where(j - q * n == i, 1.0, 0.0).astype(BF)
    full = nn(v, hot)
    d = lax.broadcasted_iota(jnp.int32, (32, wide), 0)
    return jnp.sum(jnp.where(q[:32] == d, full, 0.0), axis=0, keepdims=True)


def lane(tile, row, at):
    r = lax.broadcasted_iota(jnp.int32, tile.shape, 0)
    c = lax.broadcasted_iota(jnp.int32, tile.shape, 1)
    v = jnp.sum(jnp.where((r == row) & (c == at), tile, 0.0), axis=1, keepdims=True)
    return jnp.sum(v, axis=0, keepdims=True)


def longer(length, shape):
    return jnp.broadcast_to(length, shape) > 512.0


def bias_rows(bias, length, k):
    at = 0
    for i in range(4):
        kk = 256 * (i + 1)
        key = lax.broadcasted_iota(jnp.int32, (kk, 128), 0)
        q = own_block(i, k) * 128 + lax.broadcasted_iota(jnp.int32, (kk, 128), 1)
        first = jnp.where(longer(length, (kk, 128)), 0, q - q % 256)
        bias[at:at + kk, :] = jnp.where((key <= q) & (key >= first), 0.0, -1e30)
        at += kk


def both_heads(bias, at, kk):
    b = bias[at:at + kk, :]
    return jnp.concatenate([b, b], axis=1)


def table_rows(COS, SIN, length, j):
    far = longer(length, (128, 128))
    near = lax.rem(j, 2)
    return (jnp.where(far, COS[rows(j), :], COS[rows(near), :]), jnp.where(far, SIN[rows(j), :], SIN[rows(near), :]))


def matrix(W, cols):
    w = W[:, :, :, :, cols]
    return w.reshape(768, w.shape[-1])


def forward_kernel(cols, qkv, out, up, down, xin, cin, COS, SIN, hist, v0, v1, v2, v3, v4, v5, v6, v7, mix, lens,
                   oX, oacts, oQ, oK, oV, oatt, olse, oWQ, oWO, ogmid, ogup, ogdown, ohome, opre, ogain, vgrad,
                   f_own, f_sib, block_w, WQ, WO, WU, WD, VEC, X, C, NB, SB,
                   Q, K, V, att, lse, middle, bias, VT, act, slope, block, ga, acts2, actsT, dg, gup, gdown, a1T, bl,
                   vq, vg, vu, vec, mixrow, cross, sel,
                   psend, precv, lsem, gsend, grecv, asend, arecv, nsend, nrecv, fsend, frecv, xsem, csem, hsem, osem, vsend, vrecv, *home_sems):
    pos = z, y, x, k = where_am_i()
    sib = dev(z, y, x, 1 - k)
    greet(z, y, x, k)
    s = 2 * z + y
    own_s = lax.rem(y + z, 2)
    def neighbour(a, src):
        cps = []
        for i in range(2):
            hi = src.at[i, pl.ds(pl.multiple_of((1 - y) * 128, 128), 128)]
            cp = remote(hi, NB.at[a, i], nsend.at[a, i], nrecv.at[a, i], dev(z, 1 - y, x, k))
            cp.start()
            cps.append(cp)
        return cps

    tokens = []
    def along_z(a, i, n, ref, dst, core):
        g = 2 * k + i
        me = (g == z) & (core == k)
        cp = remote(ref, dst, asend.at[a, i, n], arecv.at[a, z], dev(g, y, x, core))
        @pl.when(me)
        def _():
            pltpu.make_async_copy(ref, dst, arecv.at[a, z]).start()
        @pl.when(jnp.logical_not(me))
        def _():
            cp.start()
        tokens.append((cp, jnp.logical_not(me)))

    def straight(a, src, dst):
        for i in range(2):
            along_z(a, i, 0, src.at[i, pl.ds(pl.multiple_of(y * 128, 128), 128)], dst(s), own_s)

    def crossed(a, src, dst, cps):
        for i in range(2):
            cps[i].wait_recv()
            mine = src[i, pl.ds(pl.multiple_of((1 - y) * 128, 128), 128), :]
            far = jnp.broadcast_to(lens[i].astype(F32), (128, 768)) > 512.0
            SB[a, i] = jnp.where(far, NB[a, i].astype(F32), mine.astype(F32)).astype(BF)
            along_z(a, i, 1, SB.at[a, i], dst(s + 1 - 2 * y), 1 - own_s)

    def arrived(a, dst, i):
        remote(dst, dst, asend.at[a, 0, 0], arecv.at[a, i], sib).wait_recv()

    acts = gdown.at[pl.ds(0, 1024)]
    to_x = lambda j: X.at[j]
    to_c = lambda j: C.at[j // 2]
    vec[...] = jnp.zeros_like(vec)
    for r, v in enumerate((v0, v1, v2, v3, v4, v5, v6, v7)):
        vec[r:r + 1, 0:v.shape[1]] = v[...].astype(F32)
    place = lax.broadcasted_iota(jnp.int32, (1, 128), 1)
    first = vec[0:1, :]
    for i in range(2):
        first = jnp.where(place == 64 + i, lens[i].astype(F32), first)
    vec[0:1, :] = first
    at, offs = 0, []
    for n in cols:
        offs.append((at, n // 2))
        at += n // 2
    pres = []
    for i, ((at, half), ref) in enumerate(zip(offs, (qkv, out, up))):
        f_own[0, :, at:at + half] = ref[:, :half].astype(F32)
        f_own[1, :, at:at + half] = ref[:, half:].astype(F32)
        pre = remote(f_own.at[1 - k, :, pl.ds(at, half)], f_sib.at[:, pl.ds(at, half)], psend.at[i], precv.at[i], sib)
        pre.start()
        pres.append(pre)
    lvec = pltpu.make_async_copy(vec, VEC.at[z, y, x, k], lsem.at[4])
    ldown = pltpu.make_async_copy(down, WD.at[z, y, x, k], lsem.at[3])
    lvec.start(); ldown.start()

    def colpart(W, half):
        return lambda zz, yy, xx, kk: W.at[zz, yy, xx, :, pl.ds(pl.multiple_of(kk * half, 128), half)]
    def rowpart(W):
        return lambda zz, yy, xx, kk: W.at[zz, yy, xx, kk]
    gq, go, gu, gd = G = [Gather(p, gsend.at[i], grecv.at[i], pos, i in (1, 2), i > 1) for i, p in enumerate(
        [colpart(WQ, offs[0][1]), colpart(WO, offs[1][1]), colpart(WU, offs[2][1]), rowpart(WD)])]
    lvec.wait()
    vs_out = [remote(VEC.at[z, y, x, k], VEC.at[z, y, x, k], vsend.at[n], vrecv.at[15 - n], dev(*chip, k)) for n, chip in chips_of(z, y, x)]
    vs_in = [remote(VEC.at[chip[0], chip[1], chip[2], k], VEC.at[chip[0], chip[1], chip[2], k], vsend.at[n], vrecv.at[n - 1], dev(*chip, k)) for n, chip in chips_of(z, y, x)]
    v_sib = remote(VEC.at[:, :, :, k], VEC.at[:, :, :, k], vsend.at[0], vrecv.at[15], sib)
    for c in vs_out: c.start()

    def own_rows(i, W):
        at, half = offs[i]
        pres[i].wait_recv()
        mine = f_own[k, :, at:at + half]
        theirs = f_sib[:, at:at + half]
        block_w[:, at:at + half] = jnp.concatenate([jnp.where(k == 0, mine, theirs), jnp.where(k == 0, theirs, mine)], axis=0).astype(BF)
        c = pltpu.make_async_copy(block_w.at[:, pl.ds(at, half)], W.at[z, y, x, :, pl.ds(pl.multiple_of(k * half, 128), half)], lsem.at[i])
        c.start()
        return c

    own_rows(0, WQ).wait()
    gq.stage(0)
    gq.early()
    nx = neighbour(0, xin)
    lo, lu = own_rows(1, WO), own_rows(2, WU)
    hin = [[pltpu.make_async_copy(hist.at[j, g], gdown.at[pl.ds(512 * j + 256 * g, 256)], hsem.at[j, g]) for g in range(2)] for j in range(5)]
    for c in hin: c[0].start(); c[1].start()
    block[...] = jnp.zeros_like(block)
    mixrow[...] = jnp.zeros_like(mixrow)

    def mix_in(js):
        for j in js:
            for g in range(2):
                hin[j][g].wait()
                for t in range(2):
                    r = slice(512 * j + 256 * g + 128 * t, 512 * j + 256 * g + 128 * t + 128)
                    q = slice(256 * g + 128 * t, 256 * g + 128 * t + 128)
                    h = gdown[r, :].astype(F32)
                    c = cin[g, 128 * t:128 * t + 128, :].astype(F32)
                    mixrow[j:j + 1, :] += jnp.sum(h * c, axis=0, keepdims=True)
                    block[q, :] += mix[j] * h
    lo.wait(); lu.wait(); ldown.wait()
    go.early(); gu.early()
    mix_in((0, 1))
    for c in vs_in: c.wait_recv()
    v_sib.start()
    mix_in((2, 3))
    gq.early_on()
    gq.stage(2)
    gu.stage(0)
    go.stage(0)
    straight(0, xin, to_x)
    crossed(0, xin, to_x, nx)
    gd.early()
    go.early_on(); gu.early_on()
    mix_in((4,))
    opres = [pltpu.make_async_copy(block.at[pl.ds(256 * g, 256)], opre.at[g], osem.at[g]) for g in range(2)]
    for c in opres: c.start()
    v_sib.wait_recv()
    tiles = VEC[...].reshape(32, 8, 128)
    length = lane(VEC[0, 0, x, z // 2], 0, 64 + lax.rem(z, 2))
    vq[...] = widen(tiles, 2, 72)
    gq.stage(3)
    for n, r in enumerate((0, 1, 3, 4, 5, 7)):
        vg[n:n + 1, :] = widen(tiles, r, 24)
    a_gain, a_shift, bout, m_gain, m_shift, bdown = (vg[n:n + 1, :] for n in range(6))
    gu.stage(1)
    gd.early_on()
    gq.stage(4)
    vu[...] = widen(tiles, 6, 96)
    bias_rows(bias, length, k)
    fw = []
    def forward_x(i):
        j = own_block(jnp.int32(i), k)
        arrived(0, X.at[j], i)
        cp = remote(X.at[j], X.at[j], fsend.at[i], frecv.at[i], sib)
        cp.start(); fw.append(cp)
    def norm_block(j):
        n, _ = norm(X[j].astype(F32))
        acts[rows(j), :] = (n * a_gain + a_shift).astype(BF)
        a1T[:, rows(j)] = acts[rows(j), :].T
    gq.stage(5)
    gu.stage(2)
    go.stage(2)
    nc = neighbour(1, cin)
    for i in range(4):
        forward_x(i)
        norm_block(own_block(jnp.int32(i), k))
    gd.stage(0)
    gq.stage(6)
    for i in range(4):
        fw[i].wait_recv()
        norm_block(own_block(jnp.int32(i), 1 - k))
    exports = []
    def export(ref, dst):
        c = pltpu.make_async_copy(ref, dst, xsem.at[len(exports)])
        c.start(); exports.append(c)

    def keys(j):
        a = acts[rows(j), :]
        c, sn = table_rows(COS, SIN, length, j)
        for t in range(3):
            u2 = nn(a, matrix(WQ, slice(768 + t * 256, 1024 + t * 256))) + vq[:, 768 + t * 256:1024 + t * 256]
            for h in range(2):
                u = u2[:, h * 128:(h + 1) * 128]
                K[rows(j), t * 256 + h * 128:t * 256 + (h + 1) * 128] = (u * c + swap(u) * sn).astype(BF)
        V[rows(j), :] = (nn(a, matrix(WQ, slice(1536, 2304))) + vq[:, 1536:]).astype(BF)

    pl.loop(0, 4)(keys)
    gu.stage(3)
    go.stage(3)
    gd.stage(1)
    pl.loop(4, 8)(keys)
    @pl.loop(0, 4)
    def _(i):
        j = own_block(i, k)
        a = acts[rows(j), :]
        c, sn = table_rows(COS, SIN, length, j)
        for t in range(3):
            u2 = nn(a, matrix(WQ, slice(t * 256, 256 + t * 256))) + vq[:, t * 256:256 + t * 256]
            for h in range(2):
                u = u2[:, h * 128:(h + 1) * 128]
                Q[rows(i), t * 256 + h * 128:t * 256 + (h + 1) * 128] = (u * c + swap(u) * sn).astype(BF) * jnp.asarray(0.125, BF)
    straight(1, cin, to_c)
    crossed(1, cin, to_c, nc)
    go.stage(4)
    gu.stage(4)
    for i in range(4):
        j = own_block(jnp.int32(i), k)
        export(X.at[j], oX.at[i])
    export(a1T, oacts); export(Q, oQ); export(K, oK); export(V, oV)
    export(WQ, oWQ)

    def heads(h):
        lanes = rows(h)
        VT[...] = V[:, lanes].T
        at = 0
        for i in range(4):
            kk = 256 * (i + 1)
            qb = spread(Q[i * 128:(i + 1) * 128, lanes])
            st = nt(K[0:kk, lanes], qb) + both_heads(bias, at, kk)
            top = jnp.max(st, axis=0, keepdims=True)
            p = jnp.exp(st - top)
            den = jnp.sum(p, axis=0, keepdims=True)
            o = nn(VT[:, 0:kk], p.astype(BF)) * (1.0 / den)
            att[i * 128:(i + 1) * 128, lanes] = pick(o)
            lse[h, i:i + 1, :] = top + jnp.log(den)
            at += kk

    pl.loop(0, 2)(heads)
    gd.stage(2)
    go.stage(5)
    pl.loop(2, 4)(heads)
    gu.stage(5)
    pl.loop(4, 6)(heads)
    go.stage(6)
    export(WO, oWO)
    gd.stage(3)
    export(att, oatt); export(lse, olse)

    for c in opres: c.wait()

    @pl.loop(0, 4)
    def _(i):
        j = own_block(i, k)
        middle[rows(i), :] = X[j].astype(F32) + (nn(att[rows(i), :].astype(BF), WO[...].reshape(768, 768)) + bout)
    m5 = mix[5]
    for i in range(4):
        r = slice(i * 128, (i + 1) * 128)
        mid = middle[r, :]
        n, _ = norm(mid)
        a2 = (n * m_gain + m_shift).astype(BF)
        acts2[r, :] = a2
        actsT[:, r] = a2.T
        block[r, :] = mid + bdown
        ga[r, :] = jnp.zeros_like(mid)
    gu.stage(6)
    vgrad[...] = jnp.zeros_like(vgrad)

    def put_vec(row, v):
        for t in range(v.shape[1] // 128):
            vgrad[row + t:row + t + 1, :] = v[:, t * 128:(t + 1) * 128]

    def hidden(f):
        c = rows(f, 384)
        u = nn(acts2[...], matrix(WU, c)) + vu[:, c]
        half_erf = 0.5 * lax.erf(u * (2.0 ** -0.5)) + 0.5
        slope[:, c] = half_erf + u * (jnp.exp(u * u * -0.5) * (1.0 / math.sqrt(2 * math.pi)))
        act[:, c] = (u * half_erf).astype(BF)
    pl.loop(0, 4)(hidden)
    gd.stage(4)
    pl.loop(4, 8)(hidden)
    for i in range(4):
        arrived(1, C.at[i], i)
        dg[i * 128:(i + 1) * 128, :] = (m5 * C[i].astype(F32)).astype(BF)
    put_vec(72, jnp.sum(dg[...].astype(F32), axis=0, keepdims=True))
    gd.stage(5)
    gd.stage(6)

    @pl.loop(0, 4)
    def _(f):
        block[...] += nn(act[:, rows(f, 768)], WD[f].reshape(768, 768))

    total = jnp.zeros((1, 768), F32)
    for i in range(4):
        r = slice(i * 128, (i + 1) * 128)
        total += jnp.sum(C[i].astype(F32) * block[r, :], axis=0, keepdims=True)
        bl[i] = block[r, :].astype(BF)
    home = Home(bl, cross, sel, ohome, length, home_sems, pos)
    home.first()

    def chunk(f):
        c = rows(f, 768)
        wd = WD[f].reshape(768, 768)
        a = act[:, c]
        upg = (nt(dg[...], wd) * slope[:, c]).astype(BF)
        g = jnp.sum(upg.astype(F32), axis=0, keepdims=True)
        for t in range(6):
            vgrad[pl.ds(48 + f * 6 + t, 1), :] = g[:, t * 128:(t + 1) * 128]
        gdown[c, :] = nn(a.T, dg[...]).astype(BF)
        pltpu.make_async_copy(gdown.at[c, :], ogdown.at[c, :], csem.at[0, f]).start()
        gup[:, c] = nn(actsT[...], upg).astype(BF)
        pltpu.make_async_copy(gup.at[:, c], ogup.at[:, c], csem.at[1, f]).start()
        ga[...] += nt(upg, matrix(WU, c))

    pl.loop(0, 3)(chunk)
    home.second()
    pl.loop(3, 4)(chunk)
    gg = jnp.zeros((1, 768), F32)
    gs = jnp.zeros((1, 768), F32)
    for i in range(4):
        r = slice(i * 128, (i + 1) * 128)
        n, inv = norm(middle[r, :])
        e = ga[r, :]
        cf = C[i].astype(F32)
        gg += jnp.sum(e * n, axis=0, keepdims=True)
        gs += jnp.sum(e, axis=0, keepdims=True)
        ga[r, :] = m5 * cf + norm_grad(e, n, inv, m_gain)
    put_vec(36, gg); put_vec(42, gs)
    ogain[...] = jnp.broadcast_to(a_gain, (8, 768))
    whole = jnp.sum(total, axis=1, keepdims=True)
    row = jnp.where(place == 5, jnp.broadcast_to(whole, (1, 128)), 0.0)
    for j in range(5):
        row = jnp.where(place == j, jnp.broadcast_to(jnp.sum(mixrow[j:j + 1, :], axis=1, keepdims=True), (1, 128)), row)
    vgrad[78:79, :] = row
    vgrad[79:80, :] = jnp.broadcast_to(length, (1, 128))
    export(ga, ogmid)
    for f in range(4):
        c = slice(f * 768, (f + 1) * 768)
        pltpu.make_async_copy(gdown.at[c, :], ogdown.at[c, :], csem.at[0, f]).wait()
        pltpu.make_async_copy(gup.at[:, c], ogup.at[:, c], csem.at[1, f]).wait()
    for c in exports: c.wait()
    home.done()
    for c in fw + nx + nc: c.wait_send()
    for cp, cond in tokens:
        @pl.when(cond)
        def _():
            cp.wait_send()
    for c in pres: c.wait_send()
    for g in G: g.sent()
    for c in vs_out + [v_sib]: c.wait_send()


def forward_call(qkv, out, up, down, xin, cin, COS, SIN, hist, vectors, mix, lens):
    cols = (qkv.shape[1], out.shape[1], up.shape[1])
    H = sum(cols) // 2
    any_ = pl.BlockSpec(memory_space=pl.ANY)
    T = lambda n, t=BF: ((n, 768), t)
    shapes = [((4, 128, 768), BF), ((768, 1024), BF), T(512), T(1024), T(1024), T(512, F32), ((6, 4, 256), F32),
              ((4, 2, 2, 48, 2304), BF), ((4, 2, 2, 48, 768), BF), T(512, F32), ((768, 3072), BF), T(3072),
              (xin.shape, BF), (xin.shape, F32)]
    DS = pltpu.SemaphoreType.DMA
    return pl.pallas_call(functools.partial(forward_kernel, cols),
        out_shape=[sd(*t) for t in shapes] + [sd((8, 768), F32), sd((80, 128), F32)],
        in_specs=[vs] * 8 + [any_] + [vs] * 8 + [ss, ss], out_specs=[any_] * len(shapes) + [vs, vs],
        scratch_shapes=[VM((2, 24, H), F32), VM((24, H), F32), VM((48, H), BF),
                        VM((4, 2, 2, 48, 2304), BF), VM((4, 2, 2, 48, 768), BF), VM((4, 2, 2, 48, 3072), BF), VM((4, 2, 2, 2, 96, 768), BF),
                        VM((4, 2, 2, 2, 8, 128), F32), VM((8, 128, 768), BF), VM((4, 128, 768), BF), VM((2, 2, 128, 768), BF), VM((2, 2, 128, 768), BF),
                        VM((512, 768), BF), VM((1024, 768), BF), VM((1024, 768), BF), VM((512, 768), F32),
                        VM((6, 4, 256), F32), VM((512, 768), F32), VM((2560, 128), F32), VM((128, 1024), BF),
                        VM((512, 3072), BF), VM((512, 3072), F32), VM((512, 768), F32), VM((512, 768), F32), VM((512, 768), BF),
                        VM((768, 512), BF), VM((512, 768), BF), VM((768, 3072), BF), VM((3072, 768), BF), VM((768, 1024), BF), VM((4, 128, 768), BF),
                        VM((1, 2304), F32), VM((8, 768), F32), VM((1, 3072), F32), VM((8, 128), F32), VM((8, 768), F32), VM((2, 128, 768), BF), VM((2, 128, 768), BF),
                        DS((3,)), DS((3,)), DS((5,)), DS((4, 21)), DS((4, 20)), DS((2, 2, 2)), DS((2, 4)), DS((2, 2)), DS((2, 2)), DS((4,)), DS((4,)),
                        DS((16,)), DS((2, 4)), DS((5, 2)), DS((2,)), DS((16,)), DS((16,)), DS((2,)), DS((2,)), DS((4,)), DS((2,)), DS((2,))],
        compiler_params=pltpu.CompilerParams(collective_id=0, has_side_effects=True, vmem_limit_bytes=63 * 2**20),
    )(qkv, out, up, down, xin, cin, COS, SIN, hist, *[v.reshape(1, -1) for v in vectors], mix, lens)


class Scatter:
    STAGES = 7

    def __init__(self, mine, theirs, RA, RB, RC, RZ, put, finish, send, recv, pos, load=None, both=False):
        self.mine, self.RA, self.RB, self.RC, self.RZ, self.put, self.finish, self.pos, self.load = mine, RA, RB, RC, RZ, put, finish, pos, load
        z, y, x, k = pos
        self.own = (y, x)
        turn = (k == 0) | both
        self.p2 = jnp.where(turn, 1 - y, y), jnp.where(turn, x, 1 - x)
        self.p3 = jnp.where(turn, y, 1 - y), jnp.where(turn, 1 - x, x)
        self.d4 = 1 - y, 1 - x
        blk = lambda yx: mine(slice(None), yx[0], yx[1])
        n3, n2 = dev(z, *self.p3, k), dev(z, *self.p2, k)
        self.pre = remote(theirs, RA, send.at[0], recv.at[0], dev(z, y, x, 1 - k))
        self.b1 = remote(blk(self.d4), RB.at[1], send.at[1], recv.at[1], n3)
        self.b0 = remote(blk(self.p3), RB.at[0], send.at[2], recv.at[2], n3)
        self.c = remote(blk(self.p2), RC, send.at[3], recv.at[3], n2)
        self.mid = (z == 1) | (z == 2)
        end, near = jnp.where(z < 2, 0, 3), jnp.where(z < 2, 1, 2)
        self.far = (3 - near, 3 - end)
        zdev = lambda zz: dev(zz, y, x, k)
        def zcp(n, block, slot, to):
            return remote(mine(block, y, x), RZ.at[slot], send.at[4 + n], recv.at[4 + slot], zdev(to))
        self.up = [zcp(0, near, 0, near), zcp(1, self.far[0], 2, near), zcp(2, self.far[1], 3, near)]
        self.down = zcp(0, end, 0, end)
        self.on = [zcp(1, self.far[0], 1, self.far[0]), zcp(2, self.far[1], 1, self.far[1])]
        self.sends = [self.pre, self.b1, self.b0, self.c]

    def add(self, yx, other):
        @pl.loop(0, 4)
        def _(i):
            ref = self.mine(i, yx[0], yx[1])
            ref[...] = (ref[...].astype(F32) + other[i].astype(F32)).astype(BF)

    def first(self, yx):
        self.add(yx, self.RA.at[:, yx[0], yx[1]])

    def stage(self, n):
        z, y, x, k = self.pos
        if n == 0:
            if self.load is not None: self.load.start()
            self.pre.start()
        elif n == 1:
            self.pre.wait_recv()
            if self.load is not None: self.load.wait()
            self.first(self.d4)
            self.b1.start()
            self.first(self.p3)
            self.b0.start()
            self.first(self.p2)
            self.first(self.own)
        elif n == 2:
            self.b1.wait_recv()
            self.add(self.p2, self.RB.at[1])
            self.c.start()
            self.b0.wait_recv()
            self.add(self.own, self.RB.at[0])
        elif n == 3:
            self.c.wait_recv()
            self.add(self.own, self.RC)
            @pl.when(self.mid)
            def _():
                self.down.start()
            @pl.when(jnp.logical_not(self.mid))
            def _():
                for c in self.up: c.start()
        elif n == 4:
            @pl.when(self.mid)
            def _():
                for i, c in enumerate(self.on):
                    self.up[1 + i].wait_recv()
                    ref = self.mine(self.far[i], y, x)
                    ref[...] = (ref[...].astype(F32) + self.RZ[2 + i].astype(F32)).astype(BF)
                    c.start()
        elif n == 5:
            self.up[0].wait_recv()
            self.on[0].wait_recv()
            self.put(self.mine(z, y, x)[...].astype(F32) + self.RZ[0].astype(F32) + self.RZ[1].astype(F32))
        elif n == 6:
            self.finish()
            for c in self.sends: c.wait_send()
            @pl.when(self.mid)
            def _():
                for c in [self.down] + self.on: c.wait_send()
            @pl.when(jnp.logical_not(self.mid))
            def _():
                for c in self.up: c.wait_send()


def backward_kernel(gup, gdown, gmid, X, actsT, Q, Kin, Vin, att, lse, WQ, WO, gain, COS, SIN, vin,
                    oq, oo, ou, od, vout, ox,
                    K, V, bias, KT, da, dQ, dK, dV, agrad, actsqT, GO, GQ, PU, PD,
                    AU, BU, CU, ZU, AD, BD, CD, ZD, AO, BO, CO, ZO, AQ, BQ, CQ, ZQ,
                    fin, fsib, finu, fsibu, es, er, gx, cross, sel, vbuf, vrec,
                    ssem, rsem, ldsem, fsend, frecv, esem_s, esem_r, vsend, vrecv, csem, *home_sems):
    pos = z, y, x, k = where_am_i()
    sib = dev(z, y, x, 1 - k)
    greet(z, y, x, k)
    length = vin[79:80, 0:1]
    ck = pltpu.make_async_copy(Kin, K, csem.at[0])
    cv = pltpu.make_async_copy(Vin, V, csem.at[1])
    ck.start(); cv.start()
    half_of = lambda kk, half: pl.ds(pl.multiple_of(kk * half, 128), half)

    def col_scatter(a, G, half, bufs, n, out, at, width, fi, fs, hbm=None, both=False):
        def put(t):
            fi[n, 0] = t[:24]
            fi[n, 1] = t[24:]
            last.start()
        last = remote(fi.at[n, 1 - k], fs.at[n], fsend.at[a], frecv.at[a], sib)
        def finish():
            last.wait_recv()
            mine, theirs = fi[n, k], fs[n]
            out[:, at:at + half] = jnp.where(k == 0, mine, theirs)
            out[:, at + half:at + 2 * half] = jnp.where(k == 0, theirs, mine)
            last.wait_send()
        if hbm is None:
            mine = lambda zz, yy, xx: G.at[zz, yy, xx, :, half_of(k, half)]
            theirs = G.at[:, :, :, :, half_of(1 - k, half)]
            load = None
        else:
            mine = lambda zz, yy, xx: G.at[zz, yy, xx]
            theirs = hbm.at[:, :, :, :, half_of(1 - k, half)]
            load = pltpu.make_async_copy(hbm.at[:, :, :, :, half_of(k, half)], G, ldsem.at[a])
        return Scatter(mine, theirs, *bufs, put, finish, ssem.at[a], rsem.at[a], pos, load, both)

    def put_down(t):
        od[...] = t
    sdn = Scatter(lambda zz, yy, xx: PD.at[zz, yy, xx], gdown.at[:, :, :, 1 - k], AD, BD, CD, ZD, put_down, lambda: None,
                  ssem.at[0], rsem.at[0], pos, pltpu.make_async_copy(gdown.at[:, :, :, k], PD, ldsem.at[0]))
    sup = col_scatter(1, PU, 1536, (AU, BU, CU, ZU), 0, ou, 0, 3072, finu, fsibu, gup)
    sout = col_scatter(2, GO, 384, (AO, BO, CO, ZO), 0, oo, 0, 768, fin, fsib, both=True)
    sq, sk, sv = (col_scatter(3 + n, GQ.at[n], 384, (AQ.at[n], BQ.at[n], CQ.at[n], ZQ.at[n]), 1 + n, oq, 768 * n, 768, fin, fsib, both=n == 2)
                  for n in range(3))
    sdn.stage(0); sup.stage(0)

    home = Home(gx, cross, sel, ox, length, home_sems, pos)
    agrad[...] = gmid[...].astype(BF)
    vbuf[0] = vin[...]

    def put_vec(row, v):
        for t in range(v.shape[1] // 128):
            vbuf[0, row + t:row + t + 1, :] = v[:, t * 128:(t + 1) * 128]
    put_vec(30, jnp.sum(agrad[...].astype(F32), axis=0, keepdims=True))
    wo = lambda: WO[...].reshape(768, 768)

    da[...] = nt(agrad[...], wo()).astype(BF)
    for i in range(4):
        actsqT[:, i * 128:(i + 1) * 128] = actsT[:, rows(own_block(jnp.int32(i), k))]

    sdn.stage(1)

    def out_rows(t):
        aT = att[:, t * 384:(t + 1) * 384].T.astype(BF)
        g = nn(aT, agrad[...]).astype(BF)
        GO[2 * t:2 * t + 2] = g.reshape(2, 2, 2, 48, 768)
    sup.stage(1)
    for t in range(2): out_rows(t)
    sout.stage(0)
    bias_rows(bias, length, k)
    dK[...] = jnp.zeros_like(dK)
    dV[...] = jnp.zeros_like(dV)
    ck.wait(); cv.wait()

    def heads(h):
        lanes = rows(h)
        KT[...] = K[:, lanes].T
        at = 0
        for i in range(4):
            kk = 256 * (i + 1)
            r = slice(i * 128, (i + 1) * 128)
            d = da[r, lanes]
            qb, db = spread(Q[r, lanes]), spread(d)
            prod = (d.astype(F32) * att[r, lanes]).T
            delta = jnp.concatenate([jnp.sum(prod[:64], axis=0, keepdims=True), jnp.sum(prod[64:], axis=0, keepdims=True)], axis=1)
            st = nt(K[0:kk, lanes], qb) + both_heads(bias, at, kk)
            p = jnp.exp(st - lse[h, i:i + 1, :])
            ds = (p * (nt(V[0:kk, lanes], db) - delta)).astype(BF)
            dV[0:kk, lanes] += nn(p.astype(BF), db)
            dK[0:kk, lanes] += nn(ds, qb)
            dQ[r, lanes] = pick(nn(KT[:, 0:kk], ds)) * 0.125
            at += kk

    pl.loop(0, 2)(heads)
    sout.stage(1)
    pl.loop(2, 6)(heads)
    sdn.stage(2)
    V[...] = dV[...].astype(BF)
    put_vec(24, jnp.sum(V[...].astype(F32), axis=0, keepdims=True))

    def weight_rows(n, lhs, g):
        @pl.loop(0, 4)
        def _(t):
            GQ[n, t] = nn(lhs[rows(t, 192), :], g[...]).astype(BF).reshape(2, 2, 48, 768)
    weight_rows(2, actsT, V)
    sv.stage(0)

    @pl.loop(0, 8)
    def _(j):
        c, s = table_rows(COS, SIN, length, j)
        for t in range(6):
            u = dK[rows(j), t * 128:(t + 1) * 128]
            K[rows(j), t * 128:(t + 1) * 128] = (u * c - swap(u) * s).astype(BF)

    @pl.loop(0, 4)
    def _(i):
        j = own_block(i, k)
        c, s = table_rows(COS, SIN, length, j)
        for t in range(6):
            u = dQ[rows(i), t * 128:(t + 1) * 128]
            da[rows(i), t * 128:(t + 1) * 128] = (u * c - swap(u) * s).astype(BF)
    sv.stage(1)
    weight_rows(1, actsT, K)
    sk.stage(0)

    @pl.loop(0, 2)
    def _(j):
        r = rows(j, 512)
        dK[r, :] = nt(K[r, :], matrix(WQ, slice(768, 1536))) + nt(V[r, :], matrix(WQ, slice(1536, 2304)))
    dQ[...] = nt(da[...], matrix(WQ, slice(0, 768)))
    for i in range(4):
        dK[rows(own_block(jnp.int32(i), k)), :] += dQ[i * 128:(i + 1) * 128, :]
        es[i] = dK[rows(own_block(jnp.int32(i), 1 - k)), :].astype(BF)
    ecp = remote(es, er, esem_s, esem_r, sib)
    ecp.start()
    sdn.stage(3)
    sk.stage(1)
    sup.stage(2)
    put_vec(18, jnp.sum(K[...].astype(F32), axis=0, keepdims=True))
    put_vec(12, jnp.sum(da[...].astype(F32), axis=0, keepdims=True))
    weight_rows(0, actsqT, da)
    sq.stage(0)
    ecp.wait_recv()
    gg = jnp.zeros((1, 768), F32)
    gsh = jnp.zeros((1, 768), F32)
    for i in range(4):
        n, inv = norm(X[i].astype(F32))
        ee = dK[rows(own_block(jnp.int32(i), k)), :] + er[i].astype(F32)
        gg += jnp.sum(ee * n, axis=0, keepdims=True)
        gsh += jnp.sum(ee, axis=0, keepdims=True)
        gx[i] = (gmid[i * 128:(i + 1) * 128, :] + norm_grad(ee, n, inv, gain[0:1, :])).astype(BF)
    home.first()
    put_vec(0, gg); put_vec(6, gsh)
    vec_steps = [[sib], [dev(z, *sdn.p2, k)], [dev(z, *sdn.p3, k)], [dev(lax.rem(z + d, 4), y, x, k) for d in (1, 2, 3)]]
    vcp = []
    def vec_stage(n):
        if n > 0:
            for c in vcp[-1]: c.wait_recv()
            t = vbuf[n - 1]
            for r in range(len(vcp[-1])):
                t = t + vrec[n - 1 + r]
            if n < 4: vbuf[n] = t
            else: vout[...] = t
        if n < 4:
            vcp.append([remote(vbuf.at[n], vrec.at[n + i], vsend.at[n + i], vrecv.at[n + i], d) for i, d in enumerate(vec_steps[n])])
            for c in vcp[-1]: c.start()

    sq.stage(1)
    vec_stage(0)
    sdn.stage(4)
    sout.stage(2)
    sup.stage(3)
    home.second()
    vec_stage(1)
    sv.stage(2)
    sout.stage(3)
    sup.stage(4)
    sk.stage(2)
    sq.stage(2)
    sv.stage(3)
    sout.stage(4)
    sdn.stage(5); sdn.stage(6)
    sk.stage(3)
    sv.stage(4)
    sq.stage(3)
    vec_stage(2)
    sk.stage(4)
    sq.stage(4)
    vec_stage(3)
    sup.stage(5); sout.stage(5)
    sv.stage(5); sk.stage(5); sq.stage(5)
    sup.stage(6); sout.stage(6)
    vec_stage(4)
    sv.stage(6); sk.stage(6); sq.stage(6)
    home.done()
    ecp.wait_send()
    for cs in vcp:
        for c in cs: c.wait_send()


def backward_call(gup, gdown, *ins):
    n_up = gup.shape[1]
    gup = gup.reshape(4, 2, 2, 48, n_up)
    gdown = gdown.reshape(4, 2, 2, 2, 96, 768)
    any_ = pl.BlockSpec(memory_space=pl.ANY)
    def bufs(r, n, lead=()):
        return [VM(lead + s + (r, n), BF) for s in ((4, 2, 2), (2, 4), (4,), (4,))]
    DS = pltpu.SemaphoreType.DMA
    home = sd((2, 256, 768), BF)
    return pl.pallas_call(backward_kernel,
        out_shape=[sd((24, 2304), F32), sd((24, 768), F32), sd((24, 3072), F32), sd((96, 768), F32), sd((80, 128), F32), home],
        in_specs=[any_] * 2 + [vs] * 4 + [any_] * 2 + [vs] * 8, out_specs=[vs] * 5 + [any_],
        scratch_shapes=[VM((1024, 768), BF), VM((1024, 768), BF), VM((2560, 128), F32), VM((128, 1024), BF), VM((512, 768), BF), VM((512, 768), F32),
                        VM((1024, 768), F32), VM((1024, 768), F32), VM((512, 768), BF), VM((768, 512), BF),
                        VM((4, 2, 2, 48, 768), BF), VM((3, 4, 2, 2, 48, 768), BF), VM((4, 2, 2, 48, 1536), BF), VM((4, 2, 2, 96, 768), BF)]
        + bufs(48, 1536) + bufs(96, 768) + bufs(48, 384) + bufs(48, 384, (3,))
        + [VM((4, 2, 24, 384), F32), VM((4, 24, 384), F32), VM((1, 2, 24, 1536), F32), VM((1, 24, 1536), F32),
           VM((4, 128, 768), BF), VM((4, 128, 768), BF), VM((4, 128, 768), BF), VM((2, 128, 768), BF), VM((2, 128, 768), BF), VM((4, 80, 128), F32), VM((6, 80, 128), F32),
           DS((6, 7)), DS((6, 8)), DS((2,)), DS((6,)), DS((6,)), DS, DS, DS((6,)), DS((6,)), DS((2,)), DS((2,)), DS((2,)), DS((4,)), DS((2,)), DS((2,))],
        compiler_params=pltpu.CompilerParams(collective_id=1, has_side_effects=True, vmem_limit_bytes=63 * 2**20),
    )(gup, gdown, *ins)


def finish_kernel(vout, cin, premix, home, gx, gq, go, gu, gd, mix,
                  lo, ox, gh, oq, oo, ou, od, v0, v1, v2, v3, v4, v5, v6, v7, gm, stage, sems):
    z, y, x, k = where_am_i()
    copies = []
    for j in range(5):
        stage[j] = (mix[j] * cin[...].astype(F32)).astype(BF)
        c = pltpu.make_async_copy(stage.at[j], gh.at[j], sems.at[j])
        c.start(); copies.append(c)
    lo[...] = (premix[...] + mix[5] * home[...].astype(F32)).astype(BF)
    me = ((z * 2 + y) * 2 + x) * 2 + k
    spot = lax.broadcasted_iota(jnp.int32, (8, 128), 1)
    base = 0
    for v in (v0, v1, v2, v3, v4, v5, v6, v7):
        n = v.shape[0]
        first = me * n
        row, shift = first // 128, lax.rem(first, 128)
        a = jnp.broadcast_to(vout[pl.ds(base + row, 1), :], (8, 128))
        b = jnp.broadcast_to(vout[pl.ds(base + row + 1, 1), :], (8, 128))
        back = lax.rem(128 - shift, 128)
        both = jnp.where(spot < 128 - shift, pltpu.roll(a, back, 1), pltpu.roll(b, back, 1))
        v[...] = both[0, :n]
        base += n // 4
    gm[...] = vout[78, :6]
    for a, b in ((gx, ox), (gq, oq), (go, oo), (gu, ou), (gd, od)):
        b[...] = a[...]
    for c in copies: c.wait()


def finish_call(vectors, vout, cin, premix, home, gx, gq, go, gu, gd, mix):
    any_ = pl.BlockSpec(memory_space=pl.ANY)
    like = lambda a: sd(a.shape, a.dtype)
    return pl.pallas_call(finish_kernel,
        out_shape=[sd(cin.shape, BF), like(gx), sd((5,) + cin.shape, BF), like(gq), like(go), like(gu), like(gd)]
        + [sd(v.shape, F32) for v in vectors] + [sd((6,), F32)],
        in_specs=[vs] * 9 + [ss], out_specs=[vs, vs, any_] + [vs] * 13,
        scratch_shapes=[VM((5,) + cin.shape, BF), pltpu.SemaphoreType.DMA((5,))],
        compiler_params=pltpu.CompilerParams(vmem_limit_bytes=62 * 2**20),
    )(vout, cin, premix, home, gx, gq, go, gu, gd, mix)

def fast_shards(inputs, history, seq_lengths, attn_gain, attn_shift, qkv_weight, qkv_bias, out_weight, out_bias, mlp_gain,
                mlp_shift, up_weight, up_bias, down_weight, down_bias, mix_weights, cotangent):
    seq, batch = lax.axis_index("seq"), lax.axis_index("batch")
    z, y, x, k = seq // 2, seq % 2, batch // 2, batch % 2
    vectors = (attn_gain, attn_shift, qkv_bias, out_bias, mlp_gain, mlp_shift, up_bias, down_bias)
    COS, SIN = (jnp.asarray(t) for t in rope_tables())
    X, actsT, Q, K, V, att, lse, WQ, WO, gmid, gup, gdown, home, premix, gain, vin = forward_call(
        qkv_weight, out_weight, up_weight, down_weight, inputs, cotangent, COS, SIN, history, vectors, mix_weights, seq_lengths)
    oq, oo, ou, od, vout, grad_inputs = backward_call(gup, gdown, gmid, X, actsT, Q, K, V, att, lse, WQ, WO, gain, COS, SIN, vin)
    layer_out, grad_inputs, grad_history, oq, oo, ou, od, *gv, grad_mix = finish_call(
        vectors, vout, cotangent, premix, home, grad_inputs, oq, oo, ou, od, mix_weights)
    return (layer_out, grad_inputs, grad_history, gv[0], gv[1], oq, gv[2], oo, gv[3], gv[4], gv[5], ou, gv[6], od, gv[7], grad_mix)


def fits(mesh, inputs):
    shape = dict(mesh.shape)
    return shape == {"seq": 8, "batch": 4} and inputs.shape == (8, 2048, 768)


def solution(mesh):
    def run(*args):
        body = fast_shards if fits(mesh, args[0]) else shards
        return placed(mesh, body)(*args)
    return run
```

```python
import functools
import math

import jax
import jax.numpy as jnp
import numpy as np
from jax import lax
from jax.experimental import pallas as pl
from jax.experimental.pallas import tpu as pltpu
from jax.sharding import PartitionSpec as P

HEADS = 12
HEAD_DIM = 64
LONG_LEN = 1024
SHORT_LEN = 256


eps = 1e-05
masked = -1e30


def block_size(row_count):
    chosen = 1
    for candidate in range(1, min(row_count, 512) + 1):
        if row_count % candidate == 0:
            chosen = candidate
    return chosen


def exact_gelu(values):
    return jax.nn.gelu(values, approximate=False)


def layer_norm(values, norm_gain, norm_shift):
    average = jnp.mean(values, axis=-1, keepdims=True)
    centred = values - average
    inverse = lax.rsqrt(jnp.mean(centred * centred, axis=-1, keepdims=True) + eps)
    normed = centred * inverse
    return (normed * norm_gain + norm_shift, normed, inverse)


def norm_back(grad_out, normed, inverse, norm_gain):
    grad_normed = grad_out * norm_gain
    mean_grad = jnp.mean(grad_normed, axis=-1, keepdims=True)
    mean_cross = jnp.mean(grad_normed * normed, axis=-1, keepdims=True)
    grad_in = inverse * (grad_normed - mean_grad - normed * mean_cross)
    return (grad_in, jnp.sum(grad_out * normed, axis=0), jnp.sum(grad_out, axis=0))


def token_layout(index, info):
    seq_len, tok_count, slice_len = info
    is_long = seq_len == LONG_LEN
    offset = index % tok_count
    device = index // tok_count
    doc_ids = jnp.where(is_long, offset // slice_len, index // SHORT_LEN).astype(jnp.int32)
    relative = jnp.where(
        is_long, device * slice_len + offset % slice_len, index % SHORT_LEN
    ).astype(jnp.int32)
    return (doc_ids, relative)


def rotary_tables(relative):
    half_dim = HEAD_DIM // 2
    frequency = jnp.exp(
        -math.log(10000.0) * (2.0 * jnp.arange(half_dim, dtype=jnp.float32) / HEAD_DIM)
    )
    angles = relative.astype(jnp.float32)[:, None] * frequency[None, :]
    return (jnp.cos(angles)[:, None, :], jnp.sin(angles)[:, None, :])


def rotate(values, cosine, sine_table):
    half_dim = values.shape[-1] // 2
    lower_half = values[..., :half_dim]
    upper_half = values[..., half_dim:]
    return jnp.concatenate(
        [
            lower_half * cosine - upper_half * sine_table,
            upper_half * cosine + lower_half * sine_table,
        ],
        axis=-1,
    )


def allowed_mask(query_places, key_places, info):
    query_docs, query_rel = token_layout(query_places, info)
    key_docs, key_rel = token_layout(key_places, info)
    return (key_docs[None, :] == query_docs[:, None]) & (key_rel[None, :] <= query_rel[:, None])


def online_block(current, query_b, key_block, value_block, query_places, key_places, info):
    running, denominator, weighted = current
    key_count = key_block.shape[0]
    allowed = allowed_mask(query_places, key_places, info)
    key_heads = key_block.reshape(key_count, HEADS, HEAD_DIM)
    scores = jnp.einsum(
        "qhd,khd->hqk", query_b, key_heads, preferred_element_type=jnp.float32
    ) * HEAD_DIM ** (-0.5)
    scores = jnp.where(allowed[None], scores, masked)
    new_max = jnp.maximum(running, jnp.max(scores, axis=-1))
    exp_scores = jnp.where(allowed[None], jnp.exp(scores - new_max[..., None]), 0.0)
    rescale = jnp.exp(running - new_max)
    denominator = denominator * rescale + jnp.sum(exp_scores, axis=-1)
    value_heads = value_block.reshape(key_count, HEADS, HEAD_DIM)
    weighted = weighted * rescale[..., None] + jnp.einsum(
        "hqk,khd->hqd",
        exp_scores.astype(jnp.bfloat16),
        value_heads,
        preferred_element_type=jnp.float32,
    )
    return (new_max, denominator, weighted)


def attend_rows(current, query_b, key_rows, value_rows, first_row, query_places, info, last_place):
    key_count = key_rows.shape[0]
    block_rows = block_size(key_count)

    def one_block(carried, block_index):
        start_place = first_row + block_index * block_rows
        key_block = lax.dynamic_slice_in_dim(key_rows, block_index * block_rows, block_rows, 0)
        value_block = lax.dynamic_slice_in_dim(value_rows, block_index * block_rows, block_rows, 0)
        key_places = start_place + jnp.arange(block_rows, dtype=jnp.int32)

        def one_compute(state_in):
            return online_block(
                state_in, query_b, key_block, value_block, query_places, key_places, info
            )

        def unchanged(state_in):
            return state_in

        return (lax.cond(start_place > last_place, unchanged, one_compute, carried), None)

    result, unused = lax.scan(
        one_block, current, jnp.arange(key_count // block_rows, dtype=jnp.int32)
    )
    return result


def block_probs(query_b, key_b, query_places, key_places, info, lse_rows):
    allowed = allowed_mask(query_places, key_places, info)
    scores = jnp.einsum(
        "qhd,khd->hqk", query_b, key_b, preferred_element_type=jnp.float32
    ) * HEAD_DIM ** (-0.5)
    return jnp.exp(jnp.where(allowed[None], scores - lse_rows[..., None], masked))


def block_dscores(probabilities, grad_b, value_b, delta_rows):
    dprobs = jnp.einsum("qhd,khd->hqk", grad_b, value_b, preferred_element_type=jnp.float32)
    return (probabilities * (dprobs - delta_rows[..., None])).astype(jnp.bfloat16)


def shards(
    inputs,
    history,
    seq_lengths,
    attn_gain,
    attn_shift,
    qkv_weight,
    qkv_bias,
    out_weight,
    out_bias,
    mlp_gain,
    mlp_shift,
    up_weight,
    up_bias,
    down_weight,
    down_bias,
    mix_weights,
    cotangent,
):
    group_count = inputs.shape[0]
    tok_count = inputs.shape[1]
    model_width = inputs.shape[2]
    seq_count = lax.axis_size("seq")
    group_rows = tok_count * seq_count
    slice_len = LONG_LEN // seq_count
    factor = HEAD_DIM ** (-0.5)
    seq_index = lax.axis_index("seq")
    first_place = seq_index * tok_count
    last_place = first_place + tok_count - 1
    places = first_place + jnp.arange(tok_count, dtype=jnp.int32)
    gathered = (
        lax.all_gather(attn_gain, ("seq", "batch"), axis=0, tiled=True),
        lax.all_gather(attn_shift, ("seq", "batch"), axis=0, tiled=True),
        lax.all_gather(qkv_weight, ("seq", "batch"), axis=0, tiled=True),
        lax.all_gather(qkv_bias, ("seq", "batch"), axis=0, tiled=True),
        lax.all_gather(out_weight, ("seq", "batch"), axis=0, tiled=True),
        lax.all_gather(out_bias, ("seq", "batch"), axis=0, tiled=True),
        lax.all_gather(mlp_gain, ("seq", "batch"), axis=0, tiled=True),
        lax.all_gather(mlp_shift, ("seq", "batch"), axis=0, tiled=True),
        lax.all_gather(up_weight, ("seq", "batch"), axis=0, tiled=True),
        lax.all_gather(up_bias, ("seq", "batch"), axis=0, tiled=True),
        lax.all_gather(down_weight, ("seq", "batch"), axis=0, tiled=True),
        lax.all_gather(down_bias, ("seq", "batch"), axis=0, tiled=True),
    )
    (
        gain_one,
        shift_one,
        qkv_full,
        qkv_vec,
        out_full,
        out_vec,
        gain_two,
        shift_two,
        up_full,
        up_vec,
        down_full,
        down_vec,
    ) = gathered
    saved = []
    block_outs = []
    for group in range(group_count):
        info = (seq_lengths[group], tok_count, slice_len)
        doc_ids, relative = token_layout(places, info)
        cosine, sine_table = rotary_tables(relative)
        residual_in = inputs[group].astype(jnp.float32)
        normed_out, normed_one, inverse_one = layer_norm(
            residual_in, gain_one.astype(jnp.float32), shift_one.astype(jnp.float32)
        )
        acts_one = normed_out.astype(jnp.bfloat16)
        projected = jnp.dot(
            acts_one, qkv_full, preferred_element_type=jnp.float32
        ) + qkv_vec.astype(jnp.float32)
        queries = rotate(
            projected[:, :model_width].reshape(tok_count, HEADS, HEAD_DIM), cosine, sine_table
        ).astype(jnp.bfloat16)
        key_flat = (
            rotate(
                projected[:, model_width : 2 * model_width].reshape(tok_count, HEADS, HEAD_DIM),
                cosine,
                sine_table,
            )
            .reshape(tok_count, model_width)
            .astype(jnp.bfloat16)
        )
        value_flat = projected[:, 2 * model_width :].astype(jnp.bfloat16)
        start_state = (
            jnp.full((HEADS, tok_count), masked, jnp.float32),
            jnp.zeros((HEADS, tok_count), jnp.float32),
            jnp.zeros((HEADS, tok_count, HEAD_DIM), jnp.float32),
        )
        key_all = None
        value_all = None
        running, denominator, weighted = attend_rows(
            start_state,
            queries,
            lax.all_gather(key_flat, "seq", axis=0, tiled=True),
            lax.all_gather(value_flat, "seq", axis=0, tiled=True),
            jnp.int32(0),
            places,
            info,
            last_place,
        )
        attended = jnp.transpose(weighted / denominator[..., None], (1, 0, 2))
        lse_rows = running + jnp.log(denominator)
        attended_b = attended.reshape(tok_count, model_width).astype(jnp.bfloat16)
        middle = (
            residual_in
            + jnp.dot(attended_b, out_full, preferred_element_type=jnp.float32)
            + out_vec.astype(jnp.float32)
        )
        normed_out_two, normed_two, inverse_two = layer_norm(
            middle, gain_two.astype(jnp.float32), shift_two.astype(jnp.float32)
        )
        acts_two = normed_out_two.astype(jnp.bfloat16)
        upward = jnp.dot(acts_two, up_full, preferred_element_type=jnp.float32) + up_vec.astype(
            jnp.float32
        )
        activated, gelu_back = jax.vjp(exact_gelu, upward)
        activated_b = activated.astype(jnp.bfloat16)
        block_out = (
            middle
            + jnp.dot(activated_b, down_full, preferred_element_type=jnp.float32)
            + down_vec.astype(jnp.float32)
        )
        block_outs.append(block_out)
        saved.append(
            (
                info,
                cosine,
                sine_table,
                normed_one,
                inverse_one,
                acts_one,
                queries,
                key_flat,
                value_flat,
                key_all,
                value_all,
                attended,
                lse_rows,
                attended_b,
                normed_two,
                inverse_two,
                acts_two,
                gelu_back,
                activated_b,
            )
        )
    block_stack = jnp.stack(block_outs, axis=0)
    earlier = history.astype(jnp.float32)
    grad_out_all = cotangent.astype(jnp.float32)
    mixed_out = (
        jnp.sum(mix_weights[:-1, None, None, None] * earlier, axis=0)
        + mix_weights[-1] * block_stack
    )
    mix_terms = jnp.concatenate(
        [
            jnp.sum(earlier * grad_out_all[None], axis=(1, 2, 3)),
            jnp.sum(block_stack * grad_out_all)[None],
        ]
    )
    grad_history = (mix_weights[:-1, None, None, None] * grad_out_all[None]).astype(jnp.bfloat16)
    back_gain_one, back_qkv, back_out, back_gain_two, back_up, back_down = (
        lax.all_gather(attn_gain, ("seq", "batch"), axis=0, tiled=True),
        lax.all_gather(qkv_weight, ("seq", "batch"), axis=0, tiled=True),
        lax.all_gather(out_weight, ("seq", "batch"), axis=0, tiled=True),
        lax.all_gather(mlp_gain, ("seq", "batch"), axis=0, tiled=True),
        lax.all_gather(up_weight, ("seq", "batch"), axis=0, tiled=True),
        lax.all_gather(down_weight, ("seq", "batch"), axis=0, tiled=True),
    )
    totals = None
    grad_input_list = []
    for group in range(group_count):
        (
            info,
            cosine,
            sine_table,
            normed_one,
            inverse_one,
            acts_one,
            queries,
            key_flat,
            value_flat,
            key_all,
            value_all,
            attended,
            lse_rows,
            attended_b,
            normed_two,
            inverse_two,
            acts_two,
            gelu_back,
            activated_b,
        ) = saved[group]
        grad_block = mix_weights[-1] * grad_out_all[group]
        down_grad_b = grad_block.astype(jnp.bfloat16)
        grad_w_down = jnp.einsum(
            "tf,td->fd", activated_b, down_grad_b, preferred_element_type=jnp.float32
        )
        grad_b_down = jnp.sum(down_grad_b.astype(jnp.float32), axis=0)
        grad_act = jnp.einsum(
            "td,fd->tf", down_grad_b, back_down, preferred_element_type=jnp.float32
        )
        up_grad_b = gelu_back(grad_act)[0].astype(jnp.bfloat16)
        grad_w_up = jnp.einsum("td,tf->df", acts_two, up_grad_b, preferred_element_type=jnp.float32)
        grad_b_up = jnp.sum(up_grad_b.astype(jnp.float32), axis=0)
        grad_acts_two = jnp.einsum(
            "tf,df->td", up_grad_b, back_up, preferred_element_type=jnp.float32
        )
        grad_middle_norm, grad_gain_two, grad_shift_two = norm_back(
            grad_acts_two, normed_two, inverse_two, back_gain_two.astype(jnp.float32)
        )
        grad_middle = grad_block + grad_middle_norm
        attn_grad_b = grad_middle.astype(jnp.bfloat16)
        grad_w_out = jnp.einsum(
            "te,td->ed", attended_b, attn_grad_b, preferred_element_type=jnp.float32
        )
        grad_b_out = jnp.sum(attn_grad_b.astype(jnp.float32), axis=0)
        grad_heads = (
            jnp.einsum("td,ed->te", attn_grad_b, back_out, preferred_element_type=jnp.float32)
            .astype(jnp.bfloat16)
            .reshape(tok_count, HEADS, HEAD_DIM)
        )
        delta_rows = jnp.transpose(jnp.sum(grad_heads.astype(jnp.float32) * attended, axis=-1))
        key_all, value_all = (
            lax.all_gather(key_flat, "seq", axis=0, tiled=True),
            lax.all_gather(value_flat, "seq", axis=0, tiled=True),
        )
        key_block_rows = block_size(group_rows)

        def query_grad_block(carried, block_index):
            start_place = block_index * key_block_rows
            key_block = lax.dynamic_slice_in_dim(key_all, start_place, key_block_rows, 0).reshape(
                key_block_rows, HEADS, HEAD_DIM
            )
            value_block = lax.dynamic_slice_in_dim(
                value_all, start_place, key_block_rows, 0
            ).reshape(key_block_rows, HEADS, HEAD_DIM)
            key_places = start_place + jnp.arange(key_block_rows, dtype=jnp.int32)

            def query_compute(summed):
                probabilities = block_probs(queries, key_block, places, key_places, info, lse_rows)
                dscores = block_dscores(probabilities, grad_heads, value_block, delta_rows)
                return (
                    summed
                    + jnp.einsum(
                        "hqk,khd->qhd", dscores, key_block, preferred_element_type=jnp.float32
                    )
                    * factor
                )

            return (
                lax.cond(start_place > last_place, lambda summed: summed, query_compute, carried),
                None,
            )

        grad_queries, unused = lax.scan(
            query_grad_block,
            jnp.zeros((tok_count, HEADS, HEAD_DIM), jnp.float32),
            jnp.arange(group_rows // key_block_rows, dtype=jnp.int32),
        )
        key_first_row = jnp.int32(0)
        key_rows = key_all
        value_rows = value_all
        inner_rows = block_size(lax.axis_size("seq") * tok_count)

        def key_grad_block(carried, block_index):
            offset = block_index * inner_rows
            start_place = key_first_row + offset
            key_block = lax.dynamic_slice_in_dim(key_rows, offset, inner_rows, 0).reshape(
                inner_rows, HEADS, HEAD_DIM
            )
            value_block = lax.dynamic_slice_in_dim(value_rows, offset, inner_rows, 0).reshape(
                inner_rows, HEADS, HEAD_DIM
            )
            key_places = start_place + jnp.arange(inner_rows, dtype=jnp.int32)

            def key_compute(unused_in):
                probabilities = block_probs(queries, key_block, places, key_places, info, lse_rows)
                dscores = block_dscores(probabilities, grad_heads, value_block, delta_rows)
                grad_keys = (
                    jnp.einsum("hqk,qhd->khd", dscores, queries, preferred_element_type=jnp.float32)
                    * factor
                )
                grad_values = jnp.einsum(
                    "hqk,qhd->khd",
                    probabilities.astype(jnp.bfloat16),
                    grad_heads,
                    preferred_element_type=jnp.float32,
                )
                return jnp.concatenate(
                    [
                        grad_keys.reshape(inner_rows, model_width),
                        grad_values.reshape(inner_rows, model_width),
                    ],
                    axis=1,
                )

            def nothing(unused_in):
                return jnp.zeros((inner_rows, 2 * model_width), jnp.float32)

            return (carried, lax.cond(start_place > last_place, nothing, key_compute, carried))

        unused_out, blocks = lax.scan(
            key_grad_block,
            jnp.int32(0),
            jnp.arange(lax.axis_size("seq") * tok_count // inner_rows, dtype=jnp.int32),
        )
        key_grads = lax.psum_scatter(
            blocks.reshape(lax.axis_size("seq") * tok_count, 2 * model_width).astype(jnp.bfloat16),
            "seq",
            scatter_dimension=0,
            tiled=True,
        ).astype(jnp.float32)
        grad_keys_own = key_grads[:, :model_width]
        grad_values_own = key_grads[:, model_width:]
        grad_q_turned = rotate(grad_queries, cosine, -sine_table).reshape(tok_count, model_width)
        grad_k_turned = rotate(
            grad_keys_own.reshape(tok_count, HEADS, HEAD_DIM), cosine, -sine_table
        ).reshape(tok_count, model_width)
        qkv_grad_b = jnp.concatenate(
            [grad_q_turned, grad_k_turned, grad_values_own], axis=1
        ).astype(jnp.bfloat16)
        grad_w_qkv = jnp.einsum(
            "td,te->de", acts_one, qkv_grad_b, preferred_element_type=jnp.float32
        )
        grad_b_qkv = jnp.sum(qkv_grad_b.astype(jnp.float32), axis=0)
        grad_acts_one = jnp.einsum(
            "te,de->td", qkv_grad_b, back_qkv, preferred_element_type=jnp.float32
        )
        grad_in_norm, grad_gain_one, grad_shift_one = norm_back(
            grad_acts_one, normed_one, inverse_one, back_gain_one.astype(jnp.float32)
        )
        grad_input_list.append((grad_middle + grad_in_norm).astype(jnp.bfloat16))
        terms = [
            grad_gain_one,
            grad_shift_one,
            grad_w_qkv,
            grad_b_qkv,
            grad_w_out,
            grad_b_out,
            grad_gain_two,
            grad_shift_two,
            grad_w_up,
            grad_b_up,
            grad_w_down,
            grad_b_down,
        ]
        if totals is None:
            totals = terms
        else:
            totals = [older + newer for older, newer in zip(totals, terms)]
    shares = (
        lax.psum_scatter(totals[0], ("seq", "batch"), scatter_dimension=0, tiled=True),
        lax.psum_scatter(totals[1], ("seq", "batch"), scatter_dimension=0, tiled=True),
        lax.psum_scatter(totals[2], ("seq", "batch"), scatter_dimension=0, tiled=True),
        lax.psum_scatter(totals[3], ("seq", "batch"), scatter_dimension=0, tiled=True),
        lax.psum_scatter(totals[4], ("seq", "batch"), scatter_dimension=0, tiled=True),
        lax.psum_scatter(totals[5], ("seq", "batch"), scatter_dimension=0, tiled=True),
        lax.psum_scatter(totals[6], ("seq", "batch"), scatter_dimension=0, tiled=True),
        lax.psum_scatter(totals[7], ("seq", "batch"), scatter_dimension=0, tiled=True),
        lax.psum_scatter(totals[8], ("seq", "batch"), scatter_dimension=0, tiled=True),
        lax.psum_scatter(totals[9], ("seq", "batch"), scatter_dimension=0, tiled=True),
        lax.psum_scatter(totals[10], ("seq", "batch"), scatter_dimension=0, tiled=True),
        lax.psum_scatter(totals[11], ("seq", "batch"), scatter_dimension=0, tiled=True),
    )
    grad_mix = lax.psum(mix_terms, ("seq", "batch"))
    grad_inputs = jnp.stack(grad_input_list, axis=0)
    return (
        mixed_out.astype(jnp.bfloat16),
        grad_inputs,
        grad_history,
        shares[0],
        shares[1],
        shares[2],
        shares[3],
        shares[4],
        shares[5],
        shares[6],
        shares[7],
        shares[8],
        shares[9],
        shares[10],
        shares[11],
        grad_mix,
    )


def placed(mesh, body):
    return jax.shard_map(
        body,
        mesh=mesh,
        in_specs=(
            P("batch", "seq", None),
            P(None, "batch", "seq", None),
            P("batch"),
            P(("seq", "batch")),
            P(("seq", "batch")),
            P(("seq", "batch"), None),
            P(("seq", "batch")),
            P(("seq", "batch"), None),
            P(("seq", "batch")),
            P(("seq", "batch")),
            P(("seq", "batch")),
            P(("seq", "batch"), None),
            P(("seq", "batch")),
            P(("seq", "batch"), None),
            P(("seq", "batch")),
            P(),
            P("batch", "seq", None),
        ),
        out_specs=(
            P("batch", "seq", None),
            P("batch", "seq", None),
            P(None, "batch", "seq", None),
            P(("seq", "batch")),
            P(("seq", "batch")),
            P(("seq", "batch"), None),
            P(("seq", "batch")),
            P(("seq", "batch"), None),
            P(("seq", "batch")),
            P(("seq", "batch")),
            P(("seq", "batch")),
            P(("seq", "batch"), None),
            P(("seq", "batch")),
            P(("seq", "batch"), None),
            P(("seq", "batch")),
            P(),
        ),
        check_vma=False,
    )

MESH = pl.DeviceIdType.MESH
BF, F32 = jnp.bfloat16, jnp.float32


def where_am_i():
    seq, batch = lax.axis_index("seq"), lax.axis_index("batch")
    return seq // 2, seq % 2, batch // 2, batch % 2


def dev(z, y, x, k):
    return (z * 2 + y, x * 2 + k)


def remote(src, dst, ssem, rsem, device):
    return pltpu.make_async_remote_copy(src_ref=src, dst_ref=dst, send_sem=ssem, recv_sem=rsem,
                                        device_id=device, device_id_type=MESH)


def chips_of(z, y, x):
    mine = (z * 2 + y) * 2 + x
    for step in range(1, 16):
        other = lax.rem(mine + step, 16)
        yield step, (other // 4, (other // 2) % 2, other % 2)


def greet(z, y, x, k):
    barrier = pltpu.get_barrier_semaphore()
    for _, chip in chips_of(z, y, x):
        pl.semaphore_signal(barrier, inc=1, device_id=dev(*chip, k), device_id_type=MESH)
    for step in range(8):
        other = lax.rem(z * 2 + y + step, 8)
        pl.semaphore_signal(barrier, inc=1, device_id=dev(other // 2, other % 2, x, 1 - k), device_id_type=MESH)
    pl.semaphore_wait(barrier, 23)


class Gather:
    STAGES = 7

    def __init__(self, part, send, recv, pos, both, hops):
        z, y, x, k = pos
        self.hops = hops
        turn = (k == 0) | both
        p2 = jnp.where(turn, 1 - y, y), jnp.where(turn, x, 1 - x)
        p3 = jnp.where(turn, y, 1 - y), jnp.where(turn, 1 - x, x)
        d4 = 1 - y, 1 - x
        one = lambda zz: part(pl.ds(zz, 1), y, x, k)
        allz = lambda yx: part(slice(None), yx[0], yx[1], k)
        self.mid = (z == 1) | (z == 2)
        end = jnp.where(z == 1, 0, 3)
        def cp(n, ref, device, r=None):
            return remote(ref, ref, send.at[n], recv.at[n if r is None else r], device)
        others = [lax.rem(z + d, 4) for d in (1, 2, 3)]
        self.three = [cp(d, one(o), dev(o, y, x, k), o) for d, o in enumerate(others)]
        if hops:
            self.direct = [cp(0, one(z), dev(jnp.where(z == 1, 0, 1), y, x, k), z), cp(1, one(z), dev(jnp.where(z == 2, 3, 2), y, x, k), z)]
        else:
            self.direct = [cp(d, one(z), dev(o, y, x, k), z) for d, o in enumerate(others)]
        self.passed = [cp(3 + n, one(f), dev(end, y, x, k), f) for n, f in enumerate((3 - z, 3 - end))]
        self.near = cp(0, one(end), dev(end, y, x, k), end)
        n2, n3 = dev(z, *p2, k), dev(z, *p3, k)
        blocks = [z] + others
        self.a2 = [cp(5 + n, one(b), n2, 4 + b) for n, b in enumerate(blocks)]
        self.a3 = [cp(9 + n, one(b), n3, 8 + b) for n, b in enumerate(blocks)]
        self.b3 = [cp(13 + n, part(pl.ds(b, 1), *p2, k), n3, 12 + b) for n, b in enumerate(blocks)]
        sib = dev(z, y, x, 1 - k)
        self.s = [cp(17 + n, allz(p), sib, 16 + n) for n, p in enumerate(((y, x), p2, p3, d4))]

    def early(self):
        self.a2[0].start(); self.a3[0].start()

    def early_on(self):
        self.a2[0].wait_recv()
        self.b3[0].start()

    def stage(self, n):
        if n == 0:
            for c in self.direct: c.start()
        elif n == 1:
            if self.hops:
                @pl.when(self.mid)
                def _():
                    for c in self.passed:
                        c.wait_recv()
                        c.start()
        elif n == 2:
            if self.hops:
                @pl.when(self.mid)
                def _():
                    self.near.wait_recv()
                @pl.when(jnp.logical_not(self.mid))
                def _():
                    for c in self.three: c.wait_recv()
            else:
                for c in self.three: c.wait_recv()
            for c in self.a2[1:] + self.a3[1:]: c.start()
            self.s[0].start()
        elif n == 3:
            for c in self.a2[1:]: c.wait_recv()
            for c in self.b3[1:]: c.start()
            self.s[1].start()
        elif n == 4:
            for c in self.a3: c.wait_recv()
            self.s[2].start()
        elif n == 5:
            for c in self.b3: c.wait_recv()
            self.s[3].start()
        elif n == 6:
            for c in self.s: c.wait_recv()

    def sent(self):
        for c in self.direct + self.a2 + self.a3 + self.b3 + self.s: c.wait_send()
        if self.hops:
            @pl.when(self.mid)
            def _():
                for c in self.passed: c.wait_send()


class Home:
    def __init__(self, buf, cross, sel, out_straight, out_crossed, length, sems, pos):
        self.__dict__.update(locals())
        z, y, x, k = pos
        self.esend, self.erecv, self.send, self.h0, self.hs = sems
        self.swap = [remote(buf.at[self.crossed(n)], cross.at[n], self.esend.at[n], self.erecv.at[n], dev(z, 1 - y, x, 1 - k))
                     for n in range(2)] if cross is not None else []
        self.sent = []

    def crossed(self, n):
        z, y, x, k = self.pos
        return lax.rem(1 - y + k, 2) + 2 * n

    def go(self, ref, i, out, sem, n):
        z, y, x, k = self.pos
        slot = lax.rem(z, 2)
        dst = out(slot)
        me = (i == z) & (z // 2 == k)
        cp = remote(ref, dst, self.send.at[n], sem.at[slot], dev(i, y, x, z // 2))
        @pl.when(me)
        def _():
            pltpu.make_async_copy(ref, dst, sem.at[slot]).start()
        @pl.when(jnp.logical_not(me))
        def _():
            cp.start()
        self.sent.append((cp, jnp.logical_not(me)))

    def first(self):
        for c in self.swap: c.start()

    def straight(self):
        z, y, x, k = self.pos
        for n in range(2):
            i = lax.rem(y + k, 2) + 2 * n
            self.go(self.buf.at[i], i, self.out_straight, self.h0, n)

    def second(self):
        for n in range(2):
            self.swap[n].wait_recv()
            i = self.crossed(n)
            far = jnp.broadcast_to(self.length, (128, 768)) > 512.0
            self.sel[n] = jnp.where(far, self.cross[n].astype(F32), self.buf[i].astype(F32)).astype(BF)
            self.go(self.sel.at[n], i, self.out_crossed, self.hs, 2 + n)

    def done(self):
        z, y, x, k = self.pos
        for g in range(2):
            for out, sem in ((self.out_straight, self.h0), (self.out_crossed, self.hs)):
                if out is not None:
                    remote(out(g), out(g), self.send.at[0], sem.at[g], dev(z, y, x, 1 - k)).wait_recv()
        for c in self.swap: c.wait_send()
        for cp, cond in self.sent:
            @pl.when(cond)
            def _():
                cp.wait_send()


class Scatter:
    STAGES = 7

    def __init__(self, mine, theirs, RA, RB, RC, RZ, put, finish, send, recv, pos, load=None, both=False, begun=False):
        self.mine, self.RA, self.RB, self.RC, self.RZ, self.put, self.finish, self.pos, self.load = mine, RA, RB, RC, RZ, put, finish, pos, load
        self.begun = begun
        z, y, x, k = pos
        self.own = (y, x)
        turn = (k == 0) | both
        self.p2 = jnp.where(turn, 1 - y, y), jnp.where(turn, x, 1 - x)
        self.p3 = jnp.where(turn, y, 1 - y), jnp.where(turn, 1 - x, x)
        self.d4 = 1 - y, 1 - x
        blk = lambda yx: mine(slice(None), yx[0], yx[1])
        n3, n2 = dev(z, *self.p3, k), dev(z, *self.p2, k)
        if not begun:
            self.pre = [remote(a, b, send.at[8 * n], recv.at[8 * n], dev(z, y, x, 1 - k)) for n, (a, b) in enumerate(theirs)]
            self.b1 = remote(blk(self.d4), RB.at[1], send.at[1], recv.at[1], n3)
            self.b0 = remote(blk(self.p3), RB.at[0], send.at[2], recv.at[2], n3)
        if RC is None: return
        self.c = remote(blk(self.p2), RC, send.at[3], recv.at[3], n2)
        self.mid = (z == 1) | (z == 2)
        end, near = jnp.where(z < 2, 0, 3), jnp.where(z < 2, 1, 2)
        self.far = (3 - near, 3 - end)
        zdev = lambda zz: dev(zz, y, x, k)
        def zcp(n, block, slot, to):
            return remote(mine(block, y, x), RZ.at[slot], send.at[4 + n], recv.at[4 + slot], zdev(to))
        self.up = [zcp(0, near, 0, near), zcp(1, self.far[0], 2, near), zcp(2, self.far[1], 3, near)]
        self.down = zcp(0, end, 0, end)
        self.on = [zcp(1, self.far[0], 1, self.far[0]), zcp(2, self.far[1], 1, self.far[1])]
        self.sends = [self.c] if begun else self.pre + [self.b1, self.b0, self.c]

    def add(self, yx, other):
        @pl.loop(0, 4)
        def _(i):
            ref = self.mine(i, yx[0], yx[1])
            ref[...] = (ref[...].astype(F32) + other[i].astype(F32)).astype(BF)

    def first(self, yx):
        for rows_of, part in self.RA:
            @pl.loop(0, 4)
            def _(i):
                ref = rows_of(self.mine(i, yx[0], yx[1]))
                ref[...] = (ref[...].astype(F32) + part.at[:, yx[0], yx[1]][i].astype(F32)).astype(BF)

    def stage(self, n):
        z, y, x, k = self.pos
        if n == 0:
            for c in self.load or (): c.start()
            for c in self.pre: c.start()
        elif n == 1:
            for c in self.pre: c.wait_recv()
            for c in self.load or (): c.wait()
            self.first(self.d4)
            self.b1.start()
            self.first(self.p3)
            self.b0.start()
            self.first(self.p2)
            self.first(self.own)
        elif n == 2:
            if self.begun:
                for c in self.load: c.wait()
            else:
                self.b1.wait_recv()
            self.add(self.p2, self.RB.at[1])
            self.c.start()
            if not self.begun: self.b0.wait_recv()
            self.add(self.own, self.RB.at[0])
        elif n == 3:
            self.c.wait_recv()
            self.add(self.own, self.RC)
            @pl.when(self.mid)
            def _():
                self.down.start()
            @pl.when(jnp.logical_not(self.mid))
            def _():
                for c in self.up: c.start()
        elif n == 4:
            @pl.when(self.mid)
            def _():
                for i, c in enumerate(self.on):
                    self.up[1 + i].wait_recv()
                    ref = self.mine(self.far[i], y, x)
                    ref[...] = (ref[...].astype(F32) + self.RZ[2 + i].astype(F32)).astype(BF)
                    c.start()
        elif n == 5:
            self.up[0].wait_recv()
            self.on[0].wait_recv()
            self.put(self.mine(z, y, x)[...].astype(F32) + self.RZ[0].astype(F32) + self.RZ[1].astype(F32))
        elif n == 6:
            self.finish()
            for c in self.sends: c.wait_send()
            @pl.when(self.mid)
            def _():
                for c in [self.down] + self.on: c.wait_send()
            @pl.when(jnp.logical_not(self.mid))
            def _():
                for c in self.up: c.wait_send()

EPS = 1e-5
NT = (((1,), (1,)), ((), ()))


def nt(a, b):
    return lax.dot_general(a, b, NT, preferred_element_type=F32)


def nn(a, b):
    return jnp.dot(a, b, preferred_element_type=F32)


def rope_tables():
    freq = np.exp(-math.log(10000.0) * (2.0 * np.arange(32, dtype=np.float32) / 64)).astype(np.float32)
    ang = np.arange(1024, dtype=np.float32)[:, None] * freq[None, :]
    c, s = np.cos(ang.astype(np.float64)), np.sin(ang.astype(np.float64))
    return (np.concatenate([c, c, c, c], 1).astype(np.float32), np.concatenate([-s, s, -s, s], 1).astype(np.float32))


def swap(u):
    low = lax.broadcasted_iota(jnp.int32, u.shape, 1) % 64 < 32
    return jnp.where(low, pltpu.roll(u, 96, 1), pltpu.roll(u, 32, 1))


def norm(v):
    mean = jnp.mean(v, axis=-1, keepdims=True)
    cen = v - mean
    inv = lax.rsqrt(jnp.mean(cen * cen, axis=-1, keepdims=True) + EPS)
    return cen * inv, inv


def norm_grad(e, n, inv, gain):
    g = e * gain
    return inv * (g - jnp.mean(g, axis=-1, keepdims=True) - n * jnp.mean(g * n, axis=-1, keepdims=True))


def own_block(i, k):
    return 2 * i + lax.rem(i + k, 2)


def rows(i, n=128):
    return pl.ds(pl.multiple_of(i * n, n), n)


def spread(p):
    low = lax.broadcasted_iota(jnp.int32, p.shape, 1) < 64
    zero = jnp.zeros_like(p)
    return jnp.concatenate([jnp.where(low, p, zero), jnp.where(low, zero, p)], axis=0)


def pick(o):
    low = lax.broadcasted_iota(jnp.int32, (128, 128), 0) < 64
    return jnp.where(low, o[:, :128], o[:, 128:]).T


def fill_bias(bias, is_long, k):
    at = 0
    for i in range(4):
        kk = 256 * (i + 1)
        key = lax.broadcasted_iota(jnp.int32, (kk, 256), 0)
        q = own_block(i, k) * 128 + lax.broadcasted_iota(jnp.int32, (kk, 256), 1) % 128
        first = jnp.where(is_long, 0, q - q % 256)
        bias[at:at + kk, :] = jnp.where((key <= q) & (key >= first), 0.0, -1e30)
        at += kk


def attn_fwd(flag, XM, XA, wqkv, wout, gain, shift, bqkv, bout, COS, SIN,
             acts, Q, K, V, att, lse, middle, bias, VT):
    z, y, x, k = where_am_i()
    is_long = flag[0] != 0
    fill_bias(bias, is_long, k)
    for j in range(8):
        alt = jnp.logical_and(jnp.logical_not(is_long), lax.rem(jnp.int32(j), 2) != y)
        blk = jnp.where(alt, XA[j // 2], XM[j]).astype(F32)
        n, _ = norm(blk)
        acts[j * 128:(j + 1) * 128, :] = (n * gain[...] + shift[...]).astype(BF)

    def tables(j):
        off = jnp.where(is_long, j, lax.rem(j, 2))
        return COS[rows(off), :], SIN[rows(off), :]

    @pl.loop(0, 8)
    def _(j):
        a = acts[rows(j), :]
        c, s = tables(j)
        for t in range(6):
            u = nn(a, wqkv[:, 768 + t * 128:896 + t * 128]) + bqkv[:, 768 + t * 128:896 + t * 128]
            K[rows(j), t * 128:(t + 1) * 128] = (u * c + swap(u) * s).astype(BF)
        V[rows(j), :] = (nn(a, wqkv[:, 1536:]) + bqkv[:, 1536:]).astype(BF)

    @pl.loop(0, 4)
    def _(i):
        j = own_block(i, k)
        a = acts[rows(j), :]
        c, s = tables(j)
        for t in range(6):
            u = nn(a, wqkv[:, t * 128:(t + 1) * 128]) + bqkv[:, t * 128:(t + 1) * 128]
            Q[rows(i), t * 128:(t + 1) * 128] = (u * c + swap(u) * s).astype(BF) * jnp.asarray(0.125, BF)

    @pl.loop(0, 6)
    def _(h):
        lanes = rows(h)
        VT[...] = V[:, lanes].T
        at = 0
        for i in range(4):
            kk = 256 * (i + 1)
            qb = spread(Q[i * 128:(i + 1) * 128, lanes])
            st = nt(K[0:kk, lanes], qb) + bias[at:at + kk, :]
            top = jnp.max(st, axis=0, keepdims=True)
            p = jnp.exp(st - top)
            den = jnp.sum(p, axis=0, keepdims=True)
            o = nn(VT[:, 0:kk], p.astype(BF)) * (1.0 / den)
            att[i * 128:(i + 1) * 128, lanes] = pick(o)
            lse[h, i:i + 1, :] = top + jnp.log(den)
            at += kk

    @pl.loop(0, 4)
    def _(i):
        j = own_block(i, k)
        alt = jnp.logical_and(jnp.logical_not(is_long), lax.rem(j, 2) != y)
        xb = jnp.where(alt, XA[i], XM[j]).astype(F32)
        middle[rows(i), :] = xb + (nn(att[rows(i), :].astype(BF), wout[...]) + bout[...])


def mlp(CH, flag, mix, middle, CM, CA, wup, wdown, gain, shift, bup, bdown,
        block, gmid, gup, gdown, g_gain, g_shift, g_bup, g_bdown, mixsum, acts2, actsT, dg, ga, cf):
    z, y, x, k = where_am_i()
    is_long = flag[0] != 0
    m5 = mix[5]
    for i in range(4):
        r = slice(i * 128, (i + 1) * 128)
        mid = middle[r, :]
        n, _ = norm(mid)
        acts2[r, :] = (n * gain[...] + shift[...]).astype(BF)
        j = own_block(jnp.int32(i), k)
        alt = jnp.logical_and(jnp.logical_not(is_long), lax.rem(j, 2) != y)
        c = jnp.where(alt, CA[i], CM[j]).astype(F32)
        cf[r, :] = c
        dg[r, :] = (m5 * c).astype(BF)
        block[r, :] = mid + bdown[...]
        ga[r, :] = jnp.zeros_like(mid)
        actsT[:, r] = acts2[r, :].T
    g_bdown[...] = jnp.sum(dg[...].astype(F32), axis=0, keepdims=True)

    @pl.loop(0, wup.shape[1] // CH)
    def _(f):
        cols = rows(f, CH)
        up = nn(acts2[...], wup[:, cols]) + bup[:, cols]
        half_erf = 0.5 * lax.erf(up * (2.0 ** -0.5)) + 0.5
        slope = half_erf + up * (jnp.exp(up * up * -0.5) * (1.0 / math.sqrt(2 * math.pi)))
        act = (up * half_erf).astype(BF)
        block[...] += nn(act, wdown[cols, :])
        upg = (nt(dg[...], wdown[cols, :]) * slope).astype(BF)
        g_bup[:, cols] = jnp.sum(upg.astype(F32), axis=0, keepdims=True)
        gdown[cols, :] = nn(act.T, dg[...]).astype(BF)
        gup[:, cols] = nn(actsT[...], upg).astype(BF)
        ga[...] += nt(upg, wup[:, cols])

    total = jnp.zeros((1, 768), F32)
    gg = jnp.zeros((1, 768), F32)
    gs = jnp.zeros((1, 768), F32)
    for i in range(4):
        r = slice(i * 128, (i + 1) * 128)
        n, inv = norm(middle[r, :])
        e = ga[r, :]
        gg += jnp.sum(e * n, axis=0, keepdims=True)
        gs += jnp.sum(e, axis=0, keepdims=True)
        gmid[r, :] = m5 * cf[r, :] + norm_grad(e, n, inv, gain[...])
        total += jnp.sum(cf[r, :] * block[r, :], axis=0, keepdims=True)
    g_gain[...] = gg
    g_shift[...] = gs
    mixsum[...] = total


def attn_bwd(flag, gmid, acts, Q, K, V, att, lse, wqkv, wout, COS, SIN,
             e, gqkv, gout, g_bqkv, g_bout, bias, KT, da, dQ, dK, dV, agrad, actsT, actsqT, KG, VG):
    z, y, x, k = where_am_i()
    is_long = flag[0] != 0
    fill_bias(bias, is_long, k)
    agrad[...] = gmid[...].astype(BF)
    g_bout[...] = jnp.sum(agrad[...].astype(F32), axis=0, keepdims=True)

    @pl.loop(0, 4)
    def _(i):
        da[rows(i), :] = nt(agrad[rows(i), :], wout[...]).astype(BF)

    for t in range(6):
        aT = att[:, t * 128:(t + 1) * 128].T.astype(BF)
        gout[t * 128:(t + 1) * 128, :] = nn(aT, agrad[...]).astype(BF)
    dK[...] = jnp.zeros_like(dK)
    dV[...] = jnp.zeros_like(dV)

    @pl.loop(0, 6)
    def _(h):
        lanes = rows(h)
        KT[...] = K[:, lanes].T
        at = 0
        for i in range(4):
            kk = 256 * (i + 1)
            r = slice(i * 128, (i + 1) * 128)
            d = da[r, lanes]
            qb, db = spread(Q[r, lanes]), spread(d)
            prod = (d.astype(F32) * att[r, lanes]).T
            delta = jnp.concatenate([jnp.sum(prod[:64], axis=0, keepdims=True), jnp.sum(prod[64:], axis=0, keepdims=True)], axis=1)
            st = nt(K[0:kk, lanes], qb) + bias[at:at + kk, :]
            p = jnp.exp(st - lse[h, i:i + 1, :])
            ds = (p * (nt(V[0:kk, lanes], db) - delta)).astype(BF)
            dV[0:kk, lanes] += nn(p.astype(BF), db)
            dK[0:kk, lanes] += nn(ds, qb)
            dQ[r, lanes] = pick(nn(KT[:, 0:kk], ds)) * 0.125
            at += kk

    def tables(j):
        off = jnp.where(is_long, j, lax.rem(j, 2))
        return COS[rows(off), :], SIN[rows(off), :]

    for j in range(8):
        actsT[:, j * 128:(j + 1) * 128] = acts[j * 128:(j + 1) * 128, :].T
    for i in range(4):
        j = own_block(jnp.int32(i), k)
        actsqT[:, i * 128:(i + 1) * 128] = acts[rows(j), :].T
        c, s = tables(j)
        for t in range(6):
            u = dQ[i * 128:(i + 1) * 128, t * 128:(t + 1) * 128]
            da[i * 128:(i + 1) * 128, t * 128:(t + 1) * 128] = (u * c - swap(u) * s).astype(BF)

    @pl.loop(0, 8)
    def _(j):
        c, s = tables(j)
        for t in range(6):
            u = dK[rows(j), t * 128:(t + 1) * 128]
            KG[rows(j), t * 128:(t + 1) * 128] = (u * c - swap(u) * s).astype(BF)
        VG[rows(j), :] = dV[rows(j), :].astype(BF)
        e[rows(j), :] = nt(KG[rows(j), :], wqkv[:, 768:1536]) + nt(VG[rows(j), :], wqkv[:, 1536:])

    @pl.loop(0, 4)
    def _(i):
        j = own_block(i, k)
        e[rows(j), :] += nt(da[rows(i), :], wqkv[:, :768])

    g_bqkv[:, :768] = jnp.sum(da[...].astype(F32), axis=0, keepdims=True)
    g_bqkv[:, 768:1536] = jnp.sum(KG[...].astype(F32), axis=0, keepdims=True)
    g_bqkv[:, 1536:] = jnp.sum(VG[...].astype(F32), axis=0, keepdims=True)

    @pl.loop(0, 6)
    def _(t):
        gqkv[rows(t), :768] = nn(actsqT[rows(t), :], da[...]).astype(BF)
        gqkv[rows(t), 768:1536] = nn(actsT[rows(t), :], KG[...]).astype(BF)
        gqkv[rows(t), 1536:] = nn(actsT[rows(t), :], VG[...]).astype(BF)


sd = jax.ShapeDtypeStruct
VM = pltpu.VMEM
vs = pl.BlockSpec(memory_space=pltpu.VMEM)
ss = pl.BlockSpec(memory_space=pltpu.SMEM)
CP = pltpu.CompilerParams(vmem_limit_bytes=60 * 2**20)


def attn_fwd_call(flag, *ins):
    return pl.pallas_call(attn_fwd,
        out_shape=[sd((1024, 768), BF), sd((512, 768), BF), sd((1024, 768), BF), sd((1024, 768), BF),
                   sd((512, 768), F32), sd((6, 4, 256), F32), sd((512, 768), F32)],
        in_specs=[ss] + [vs] * len(ins), out_specs=[vs] * 7,
        scratch_shapes=[VM((2560, 256), F32), VM((128, 1024), BF)],
        compiler_params=CP)(flag, *ins)


def mlp_call(flag, mix, *ins):
    r = sd((1, 768), F32)
    return pl.pallas_call(functools.partial(mlp, 512),
        out_shape=[sd((512, 768), F32), sd((512, 768), F32), sd((768, 3072), BF), sd((3072, 768), BF), r, r, sd((1, 3072), F32), r, r],
        in_specs=[ss, ss] + [vs] * len(ins), out_specs=[vs] * 9,
        scratch_shapes=[VM((512, 768), BF), VM((768, 512), BF), VM((512, 768), BF), VM((512, 768), F32), VM((512, 768), F32)],
        compiler_params=CP)(flag, mix, *ins)


def attn_bwd_call(flag, *ins):
    return pl.pallas_call(attn_bwd,
        out_shape=[sd((1024, 768), F32), sd((768, 2304), BF), sd((768, 768), BF), sd((1, 2304), F32), sd((1, 768), F32)],
        in_specs=[ss] + [vs] * len(ins), out_specs=[vs] * 5,
        scratch_shapes=[VM((2560, 256), F32), VM((128, 1024), BF), VM((512, 768), BF), VM((512, 768), F32), VM((1024, 768), F32),
                        VM((1024, 768), F32), VM((512, 768), BF), VM((768, 1024), BF), VM((768, 512), BF), VM((1024, 768), BF), VM((1024, 768), BF)],
        compiler_params=CP)(flag, *ins)


VROWS = (24, 24, 72, 24, 24, 24, 96, 24)


def widen(vecs, row, n):
    v = vecs[:, row, :].astype(BF)
    wide = 32 * n
    j = lax.broadcasted_iota(jnp.int32, (128, wide), 1)
    i = lax.broadcasted_iota(jnp.int32, (128, wide), 0)
    q = jnp.floor((j.astype(F32) + 0.5) * (1.0 / n)).astype(jnp.int32)
    hot = jnp.where(j - q * n == i, 1.0, 0.0).astype(BF)
    full = nn(v, hot)
    d = lax.broadcasted_iota(jnp.int32, (32, wide), 0)
    return jnp.sum(jnp.where(q[:32] == d, full, 0.0), axis=0, keepdims=True)


def lane(tile, row, at):
    r = lax.broadcasted_iota(jnp.int32, tile.shape, 0)
    c = lax.broadcasted_iota(jnp.int32, tile.shape, 1)
    v = jnp.sum(jnp.where((r == row) & (c == at), tile, 0.0), axis=1, keepdims=True)
    return jnp.sum(v, axis=0, keepdims=True)


def longer(length, shape):
    return jnp.broadcast_to(length, shape) > 512.0


def bias_rows(bias, length, k):
    at = 0
    for i in range(4):
        kk = 256 * (i + 1)
        key = lax.broadcasted_iota(jnp.int32, (kk, 128), 0)
        q = own_block(i, k) * 128 + lax.broadcasted_iota(jnp.int32, (kk, 128), 1)
        first = jnp.where(longer(length, (kk, 128)), 0, q - q % 256)
        bias[at:at + kk, :] = jnp.where((key <= q) & (key >= first), 0.0, -1e30)
        at += kk


def both_heads(bias, at, kk):
    b = bias[at:at + kk, :]
    return jnp.concatenate([b, b], axis=1)


def table_rows(COS, SIN, length, j):
    far = longer(length, (128, 128))
    near = lax.rem(j, 2)
    return (jnp.where(far, COS[rows(j), :], COS[rows(near), :]), jnp.where(far, SIN[rows(j), :], SIN[rows(near), :]))


def matrix(W, cols):
    w = W[:, :, :, :, cols]
    return w.reshape(768, w.shape[-1])


def forward_kernel(cols, qkv, out, up, down, xin, cin, COS, SIN, hist, v0, v1, v2, v3, v4, v5, v6, v7, mix, lens,
                   oX, oacts, oQ, oK, oV, oatt, olse, oWQ, oWO, ogmid, ogup, opd, orb, obl, ohome, opre, ogain, vgrad,
                   f_own, f_sib, block_w, WQ, WO, WU, WD, VEC, X, C, NB, SB,
                   Q, K, V, att, lse, middle, bias, VT, act, slope, block, ga, acts2, actsT, dg, gup, GD, a1T, bl,
                   vq, vg, vu, vec, mixrow,
                   psend, precv, lsem, gsend, grecv, asend, arecv, nsend, nrecv, fsend, frecv, xsem, csem, hsem, osem, vsend, vrecv, dsend, drecv, free, *home_sems):
    pos = z, y, x, k = where_am_i()
    sib = dev(z, y, x, 1 - k)
    greet(z, y, x, k)
    s = 2 * z + y
    own_s = lax.rem(y + z, 2)
    def neighbour(a, src):
        cps = []
        for i in range(2):
            hi = src.at[i, pl.ds(pl.multiple_of((1 - y) * 128, 128), 128)]
            cp = remote(hi, NB.at[a, i], nsend.at[a, i], nrecv.at[a, i], dev(z, 1 - y, x, k))
            cp.start()
            cps.append(cp)
        return cps

    tokens = []
    def along_z(a, i, n, ref, dst, core):
        g = 2 * k + i
        me = (g == z) & (core == k)
        cp = remote(ref, dst, asend.at[a, i, n], arecv.at[a, z], dev(g, y, x, core))
        @pl.when(me)
        def _():
            pltpu.make_async_copy(ref, dst, arecv.at[a, z]).start()
        @pl.when(jnp.logical_not(me))
        def _():
            cp.start()
        tokens.append((cp, jnp.logical_not(me)))

    def straight(a, src, dst):
        for i in range(2):
            along_z(a, i, 0, src.at[i, pl.ds(pl.multiple_of(y * 128, 128), 128)], dst(s), own_s)

    def crossed(a, src, dst, cps):
        for i in range(2):
            cps[i].wait_recv()
            mine = src[i, pl.ds(pl.multiple_of((1 - y) * 128, 128), 128), :]
            far = jnp.broadcast_to(lens[i].astype(F32), (128, 768)) > 512.0
            SB[a, i] = jnp.where(far, NB[a, i].astype(F32), mine.astype(F32)).astype(BF)
            along_z(a, i, 1, SB.at[a, i], dst(s + 1 - 2 * y), 1 - own_s)

    def arrived(a, dst, i):
        remote(dst, dst, asend.at[a, 0, 0], arecv.at[a, i], sib).wait_recv()

    def acts(j, low):
        return (acts2 if low else dg).at[rows(j if low else j - 4)]
    slots = [act.at[:, pl.ds(768 * n, 768)] for n in range(4)] + [dg]
    to_x = lambda j: X.at[j]
    to_c = lambda j: C.at[j // 2]
    vec[...] = jnp.zeros_like(vec)
    for r, v in enumerate((v0, v1, v2, v3, v4, v5, v6, v7)):
        vec[r:r + 1, 0:v.shape[1]] = v[...].astype(F32)
    place = lax.broadcasted_iota(jnp.int32, (1, 128), 1)
    first = vec[0:1, :]
    for i in range(2):
        first = jnp.where(place == 64 + i, lens[i].astype(F32), first)
    vec[0:1, :] = first
    at, offs = 0, []
    for n in cols:
        offs.append((at, n // 2))
        at += n // 2
    pres = []
    for i, ((at, half), ref) in enumerate(zip(offs, (qkv, out, up))):
        f_own[0, :, at:at + half] = ref[:, :half].astype(F32)
        f_own[1, :, at:at + half] = ref[:, half:].astype(F32)
        pre = remote(f_own.at[1 - k, :, pl.ds(at, half)], f_sib.at[:, pl.ds(at, half)], psend.at[i], precv.at[i], sib)
        pre.start()
        pres.append(pre)
    lvec = pltpu.make_async_copy(vec, VEC.at[z, y, x, k], lsem.at[4])
    ldown = pltpu.make_async_copy(down, WD.at[z, y, x, k], lsem.at[3])
    lvec.start(); ldown.start()

    def colpart(W, half):
        return lambda zz, yy, xx, kk: W.at[zz, yy, xx, :, pl.ds(pl.multiple_of(kk * half, 128), half)]
    def rowpart(W):
        return lambda zz, yy, xx, kk: W.at[zz, yy, xx, kk]
    gq, go, gu, gd = G = [Gather(p, gsend.at[i], grecv.at[i], pos, i in (1, 2), i > 1) for i, p in enumerate(
        [colpart(WQ, offs[0][1]), colpart(WO, offs[1][1]), colpart(WU, offs[2][1]), rowpart(WD)])]
    lvec.wait()
    vs_out = [remote(VEC.at[z, y, x, k], VEC.at[z, y, x, k], vsend.at[n], vrecv.at[15 - n], dev(*chip, k)) for n, chip in chips_of(z, y, x)]
    vs_in = [remote(VEC.at[chip[0], chip[1], chip[2], k], VEC.at[chip[0], chip[1], chip[2], k], vsend.at[n], vrecv.at[n - 1], dev(*chip, k)) for n, chip in chips_of(z, y, x)]
    v_sib = remote(VEC.at[:, :, :, k], VEC.at[:, :, :, k], vsend.at[0], vrecv.at[15], sib)
    for c in vs_out: c.start()

    def own_rows(i, W):
        at, half = offs[i]
        pres[i].wait_recv()
        mine = f_own[k, :, at:at + half]
        theirs = f_sib[:, at:at + half]
        block_w[:, at:at + half] = jnp.concatenate([jnp.where(k == 0, mine, theirs), jnp.where(k == 0, theirs, mine)], axis=0).astype(BF)
        c = pltpu.make_async_copy(block_w.at[:, pl.ds(at, half)], W.at[z, y, x, :, pl.ds(pl.multiple_of(k * half, 128), half)], lsem.at[i])
        c.start()
        return c

    own_rows(0, WQ).wait()
    gq.stage(0)
    gq.early()
    nx = neighbour(0, xin)
    lo, lu = own_rows(1, WO), own_rows(2, WU)
    hin = [[pltpu.make_async_copy(hist.at[j, g], slots[j].at[pl.ds(256 * g, 256)], hsem.at[j, g]) for g in range(2)] for j in range(5)]
    for c in hin: c[0].start(); c[1].start()
    block[...] = jnp.zeros_like(block)
    mixrow[...] = jnp.zeros_like(mixrow)

    def mix_in(js):
        for j in js:
            for g in range(2):
                hin[j][g].wait()
                for t in range(2):
                    q = slice(256 * g + 128 * t, 256 * g + 128 * t + 128)
                    h = slots[j][q, :].astype(F32)
                    c = cin[g, 128 * t:128 * t + 128, :].astype(F32)
                    mixrow[j:j + 1, :] += jnp.sum(h * c, axis=0, keepdims=True)
                    block[q, :] += mix[j] * h
    lo.wait(); lu.wait(); ldown.wait()
    go.early(); gu.early()
    mix_in((0, 1))
    for c in vs_in: c.wait_recv()
    v_sib.start()
    mix_in((2, 3))
    gq.early_on()
    gq.stage(2)
    gu.stage(0)
    go.stage(0)
    straight(0, xin, to_x)
    crossed(0, xin, to_x, nx)
    gd.early()
    go.early_on(); gu.early_on()
    mix_in((4,))
    opres = [pltpu.make_async_copy(block.at[pl.ds(256 * g, 256)], opre.at[g], osem.at[g]) for g in range(2)]
    for c in opres: c.start()
    v_sib.wait_recv()
    tiles = VEC[...].reshape(32, 8, 128)
    length = lane(VEC[0, 0, x, z // 2], 0, 64 + lax.rem(z, 2))
    vq[...] = widen(tiles, 2, 72)
    gq.stage(3)
    for n, r in enumerate((0, 1, 3, 4, 5, 7)):
        vg[n:n + 1, :] = widen(tiles, r, 24)
    a_gain, a_shift, bout, m_gain, m_shift, bdown = (vg[n:n + 1, :] for n in range(6))
    gu.stage(1)
    gd.early_on()
    gq.stage(4)
    vu[...] = widen(tiles, 6, 96)
    bias_rows(bias, length, k)
    fw = []
    def forward_x(i):
        j = own_block(jnp.int32(i), k)
        arrived(0, X.at[j], i)
        cp = remote(X.at[j], X.at[j], fsend.at[i], frecv.at[i], sib)
        cp.start(); fw.append(cp)
    def norm_block(i, core):
        j = own_block(jnp.int32(i), core)
        n, _ = norm(X[j].astype(F32))
        a = (n * a_gain + a_shift).astype(BF)
        acts(j, i < 2)[...] = a
        a1T[:, rows(j)] = a.T
    gq.stage(5)
    gu.stage(2)
    go.stage(2)
    nc = neighbour(1, cin)
    for i in range(4):
        forward_x(i)
        norm_block(i, k)
    gd.stage(0)
    gq.stage(6)
    for i in range(4):
        fw[i].wait_recv()
        norm_block(i, 1 - k)
    exports, turn = [], iter(range(16))
    def export(ref, dst):
        c = pltpu.make_async_copy(ref, dst, xsem.at[next(turn)])
        c.start(); exports.append(c)

    def keys(low, j):
        a = acts(j, low)[...]
        c, sn = table_rows(COS, SIN, length, j)
        for t in range(3):
            u2 = nn(a, matrix(WQ, slice(768 + t * 256, 1024 + t * 256))) + vq[:, 768 + t * 256:1024 + t * 256]
            for h in range(2):
                u = u2[:, h * 128:(h + 1) * 128]
                K[rows(j), t * 256 + h * 128:t * 256 + (h + 1) * 128] = (u * c + swap(u) * sn).astype(BF)
        V[rows(j), :] = (nn(a, matrix(WQ, slice(1536, 2304))) + vq[:, 1536:]).astype(BF)

    pl.loop(0, 4)(functools.partial(keys, True))
    gu.stage(3)
    go.stage(3)
    gd.stage(1)
    pl.loop(4, 8)(functools.partial(keys, False))
    def ask(low, i):
        j = own_block(i, k)
        a = acts(j, low)[...]
        c, sn = table_rows(COS, SIN, length, j)
        for t in range(3):
            u2 = nn(a, matrix(WQ, slice(t * 256, 256 + t * 256))) + vq[:, t * 256:256 + t * 256]
            for h in range(2):
                u = u2[:, h * 128:(h + 1) * 128]
                Q[rows(i), t * 256 + h * 128:t * 256 + (h + 1) * 128] = (u * c + swap(u) * sn).astype(BF) * jnp.asarray(0.125, BF)
    pl.loop(0, 2)(functools.partial(ask, True))
    pl.loop(2, 4)(functools.partial(ask, False))
    straight(1, cin, to_c)
    crossed(1, cin, to_c, nc)
    go.stage(4)
    gu.stage(4)
    for i in range(4):
        j = own_block(jnp.int32(i), k)
        export(X.at[j], oX.at[i])
    export(a1T, oacts); export(Q, oQ); export(K, oK); export(V, oV)
    export(WQ, oWQ)
    free_wq = exports.pop()

    def heads(h):
        lanes = rows(h)
        VT[...] = V[:, lanes].T
        at = 0
        for i in range(4):
            kk = 256 * (i + 1)
            qb = spread(Q[i * 128:(i + 1) * 128, lanes])
            st = nt(K[0:kk, lanes], qb) + both_heads(bias, at, kk)
            top = jnp.max(st, axis=0, keepdims=True)
            p = jnp.exp(st - top)
            den = jnp.sum(p, axis=0, keepdims=True)
            o = nn(VT[:, 0:kk], p.astype(BF)) * (1.0 / den)
            att[i * 128:(i + 1) * 128, lanes] = pick(o)
            lse[h, i:i + 1, :] = top + jnp.log(den)
            at += kk

    pl.loop(0, 2)(heads)
    gd.stage(2)
    go.stage(5)
    pl.loop(2, 4)(heads)
    gu.stage(5)
    pl.loop(4, 6)(heads)
    go.stage(6)
    export(WO, oWO)
    gd.stage(3)
    export(att, oatt); export(lse, olse)

    for c in opres: c.wait()

    @pl.loop(0, 4)
    def _(i):
        j = own_block(i, k)
        middle[rows(i), :] = X[j].astype(F32) + (nn(att[rows(i), :].astype(BF), WO[...].reshape(768, 768)) + bout)
    m5 = mix[5]
    free_wq.wait()
    gq.sent()
    pl.semaphore_signal(free, inc=1, device_id=sib, device_id_type=MESH)
    for i in range(4):
        r = slice(i * 128, (i + 1) * 128)
        mid = middle[r, :]
        n, _ = norm(mid)
        a2 = (n * m_gain + m_shift).astype(BF)
        acts2[r, :] = a2
        actsT[:, r] = a2.T
        block[r, :] = mid + bdown
        ga[r, :] = jnp.zeros_like(mid)
    gu.stage(6)
    vgrad[...] = jnp.zeros_like(vgrad)

    def put_vec(row, v):
        for t in range(v.shape[1] // 128):
            vgrad[row + t:row + t + 1, :] = v[:, t * 128:(t + 1) * 128]

    def hidden(f):
        c = rows(f, 384)
        u = nn(acts2[...], matrix(WU, c)) + vu[:, c]
        half_erf = 0.5 * lax.erf(u * (2.0 ** -0.5)) + 0.5
        slope[:, c] = half_erf + u * (jnp.exp(u * u * -0.5) * (1.0 / math.sqrt(2 * math.pi)))
        act[:, c] = (u * half_erf).astype(BF)
    pl.loop(0, 4)(hidden)
    gd.stage(4)
    pl.loop(4, 8)(hidden)
    for i in range(4):
        arrived(1, C.at[i], i)
        dg[i * 128:(i + 1) * 128, :] = (m5 * C[i].astype(F32)).astype(BF)
    put_vec(72, jnp.sum(dg[...].astype(F32), axis=0, keepdims=True))
    sdn = Scatter(lambda zz, yy, xx: GD.at[zz, yy, xx, k],
                  [(GD.at[:, :, :, 1 - k, pl.ds(48 * n, 48)], WQ.at[:, :, :, :, pl.ds(768 * n, 768)]) for n in range(2)],
                  [(lambda r, n=n: r.at[pl.ds(48 * n, 48)], WQ.at[:, :, :, :, pl.ds(768 * n, 768)]) for n in range(2)],
                  orb, None, None, None, None, dsend, drecv, pos)

    gd.stage(5)

    @pl.loop(0, 4)
    def _(f):
        GD[f] = nn(act[:, rows(f, 768)].T, dg[...]).astype(BF).reshape(2, 2, 2, 96, 768)
    pl.semaphore_wait(free, 1)
    gd.stage(6)
    sdn.stage(0)

    @pl.loop(0, 4)
    def _(f):
        block[...] += nn(act[:, rows(f, 768)], WD[f].reshape(768, 768))

    total = jnp.zeros((1, 768), F32)
    for i in range(4):
        r = slice(i * 128, (i + 1) * 128)
        total += jnp.sum(C[i].astype(F32) * block[r, :], axis=0, keepdims=True)
        bl[i] = block[r, :].astype(BF)
    home = Home(bl, None, None, lambda slot: ohome.at[slot], None, length, home_sems, pos)
    home.straight()
    export(bl, obl)
    sdn.stage(1)
    export(GD.at[:, :, :, k], opd)

    def chunk(f):
        c = rows(f, 768)
        wd = WD[f].reshape(768, 768)
        upg = (nt(dg[...], wd) * slope[:, c]).astype(BF)
        g = jnp.sum(upg.astype(F32), axis=0, keepdims=True)
        for t in range(6):
            vgrad[pl.ds(48 + f * 6 + t, 1), :] = g[:, t * 128:(t + 1) * 128]
        gup[:, c] = nn(actsT[...], upg).astype(BF)
        pltpu.make_async_copy(gup.at[:, c], ogup.at[:, c], csem.at[1, f]).start()
        ga[...] += nt(upg, matrix(WU, c))

    pl.loop(0, 4)(chunk)
    gg = jnp.zeros((1, 768), F32)
    gs = jnp.zeros((1, 768), F32)
    for i in range(4):
        r = slice(i * 128, (i + 1) * 128)
        n, inv = norm(middle[r, :])
        e = ga[r, :]
        cf = C[i].astype(F32)
        gg += jnp.sum(e * n, axis=0, keepdims=True)
        gs += jnp.sum(e, axis=0, keepdims=True)
        ga[r, :] = m5 * cf + norm_grad(e, n, inv, m_gain)
    put_vec(36, gg); put_vec(42, gs)
    ogain[...] = jnp.broadcast_to(a_gain, (8, 768))
    whole = jnp.sum(total, axis=1, keepdims=True)
    row = jnp.where(place == 5, jnp.broadcast_to(whole, (1, 128)), 0.0)
    for j in range(5):
        row = jnp.where(place == j, jnp.broadcast_to(jnp.sum(mixrow[j:j + 1, :], axis=1, keepdims=True), (1, 128)), row)
    vgrad[78:79, :] = row
    vgrad[79:80, :] = jnp.broadcast_to(length, (1, 128))
    export(ga, ogmid)
    for f in range(4):
        c = slice(f * 768, (f + 1) * 768)
        pltpu.make_async_copy(gup.at[:, c], ogup.at[:, c], csem.at[1, f]).wait()
    for c in exports: c.wait()
    sdn.b1.wait_recv(); sdn.b0.wait_recv()
    for c in sdn.pre + [sdn.b1, sdn.b0]: c.wait_send()
    home.done()
    for c in fw + nx + nc: c.wait_send()
    for cp, cond in tokens:
        @pl.when(cond)
        def _():
            cp.wait_send()
    for c in pres: c.wait_send()
    for g in G[1:]: g.sent()
    for c in vs_out + [v_sib]: c.wait_send()


def forward_call(qkv, out, up, down, xin, cin, COS, SIN, hist, vectors, mix, lens):
    cols = (qkv.shape[1], out.shape[1], up.shape[1])
    H = sum(cols) // 2
    any_ = pl.BlockSpec(memory_space=pl.ANY)
    T = lambda n, t=BF: ((n, 768), t)
    shapes = [((4, 128, 768), BF), ((768, 1024), BF), T(512), T(1024), T(1024), T(512, F32), ((6, 4, 256), F32),
              ((4, 2, 2, 48, 2304), BF), ((4, 2, 2, 48, 768), BF), T(512, F32), ((768, 3072), BF), ((4, 2, 2, 96, 768), BF), ((2, 4, 96, 768), BF), ((4, 128, 768), BF),
              ((2, 128, 768), BF), (xin.shape, F32)]
    DS = pltpu.SemaphoreType.DMA
    return pl.pallas_call(functools.partial(forward_kernel, cols),
        out_shape=[sd(*t) for t in shapes] + [sd((8, 768), F32), sd((80, 128), F32)],
        in_specs=[vs] * 8 + [any_] + [vs] * 8 + [ss, ss], out_specs=[any_] * len(shapes) + [vs, vs],
        scratch_shapes=[VM((2, 24, H), F32), VM((24, H), F32), VM((48, H), BF),
                        VM((4, 2, 2, 48, 2304), BF), VM((4, 2, 2, 48, 768), BF), VM((4, 2, 2, 48, 3072), BF), VM((4, 2, 2, 2, 96, 768), BF),
                        VM((4, 2, 2, 2, 8, 128), F32), VM((8, 128, 768), BF), VM((4, 128, 768), BF), VM((2, 2, 128, 768), BF), VM((2, 2, 128, 768), BF),
                        VM((512, 768), BF), VM((1024, 768), BF), VM((1024, 768), BF), VM((512, 768), F32),
                        VM((6, 4, 256), F32), VM((512, 768), F32), VM((2560, 128), F32), VM((128, 1024), BF),
                        VM((512, 3072), BF), VM((512, 3072), F32), VM((512, 768), F32), VM((512, 768), F32), VM((512, 768), BF),
                        VM((768, 512), BF), VM((512, 768), BF), VM((768, 3072), BF), VM((4, 2, 2, 2, 96, 768), BF), VM((768, 1024), BF), VM((4, 128, 768), BF),
                        VM((1, 2304), F32), VM((8, 768), F32), VM((1, 3072), F32), VM((8, 128), F32), VM((8, 768), F32),
                        DS((3,)), DS((3,)), DS((5,)), DS((4, 21)), DS((4, 20)), DS((2, 2, 2)), DS((2, 4)), DS((2, 2)), DS((2, 2)), DS((4,)), DS((4,)),
                        DS((16,)), DS((2, 4)), DS((5, 2)), DS((2,)), DS((16,)), DS((16,)), DS((9,)), DS((9,)), pltpu.SemaphoreType.REGULAR, DS((2,)), DS((2,)), DS((4,)), DS((2,)), DS((2,))],
        compiler_params=pltpu.CompilerParams(collective_id=0, has_side_effects=True, vmem_limit_bytes=63 * 2**20),
    )(qkv, out, up, down, xin, cin, COS, SIN, hist, *[v.reshape(1, -1) for v in vectors], mix, lens)


def backward_kernel(gup, pdown, bdown, bl, gmid, X, actsT, Q, Kin, Vin, att, lse, WQ, WO, gain, COS, SIN, vin,
                    oq, oo, ou, od, vout, ox, ocross,
                    K, V, bias, KT, da, dQ, dK, dV, agrad, actsqT, GO, GQ, PU, PD,
                    AU, BU, CU, ZU, BD, CD, ZD, AO, BO, CO, ZO, AQ, BQ, CQ, ZQ,
                    fin, fsib, finu, fsibu, es, er, gx, cross, sel, cross_b, sel_b, vbuf, vrec,
                    ssem, rsem, ldsem, fsend, frecv, esem_s, esem_r, vsend, vrecv, csem, *home_sems):
    pos = z, y, x, k = where_am_i()
    sib = dev(z, y, x, 1 - k)
    greet(z, y, x, k)
    length = vin[79:80, 0:1]
    ck = pltpu.make_async_copy(Kin, K, csem.at[0])
    cv = pltpu.make_async_copy(Vin, V, csem.at[1])
    ck.start(); cv.start()
    half_of = lambda kk, half: pl.ds(pl.multiple_of(kk * half, 128), half)

    def col_scatter(a, G, half, bufs, n, out, at, width, fi, fs, hbm=None, both=False):
        def put(t):
            fi[n, 0] = t[:24]
            fi[n, 1] = t[24:]
            last.start()
        last = remote(fi.at[n, 1 - k], fs.at[n], fsend.at[a], frecv.at[a], sib)
        def finish():
            last.wait_recv()
            mine, theirs = fi[n, k], fs[n]
            out[:, at:at + half] = jnp.where(k == 0, mine, theirs)
            out[:, at + half:at + 2 * half] = jnp.where(k == 0, theirs, mine)
            last.wait_send()
        if hbm is None:
            mine = lambda zz, yy, xx: G.at[zz, yy, xx, :, half_of(k, half)]
            theirs = G.at[:, :, :, :, half_of(1 - k, half)]
            load = None
        else:
            mine = lambda zz, yy, xx: G.at[zz, yy, xx]
            theirs = hbm.at[:, :, :, :, half_of(1 - k, half)]
            load = [pltpu.make_async_copy(hbm.at[:, :, :, :, half_of(k, half)], G, ldsem.at[a])]
        RA, RB, RC, RZ = bufs
        return Scatter(mine, [(theirs, RA)], [(lambda r: r, RA)], RB, RC, RZ, put, finish, ssem.at[a], rsem.at[a], pos, load, both)

    def put_down(t):
        od[...] = t
    loads = [pltpu.make_async_copy(pdown, PD, ldsem.at[0]), pltpu.make_async_copy(bdown, BD, ldsem.at[2])]
    for c in loads: c.start()
    sdn = Scatter(lambda zz, yy, xx: PD.at[zz, yy, xx], None, None, BD, CD, ZD, put_down, lambda: None,
                  ssem.at[0], rsem.at[0], pos, loads, begun=True)
    sup = col_scatter(1, PU, 1536, (AU, BU, CU, ZU), 0, ou, 0, 3072, finu, fsibu, gup)
    sout = col_scatter(2, GO, 384, (AO, BO, CO, ZO), 0, oo, 0, 768, fin, fsib, both=True)
    sq, sk, sv = (col_scatter(3 + n, GQ.at[n], 384, (AQ.at[n], BQ.at[n], CQ.at[n], ZQ.at[n]), 1 + n, oq, 768 * n, 768, fin, fsib, both=n == 2)
                  for n in range(3))
    sup.stage(0)

    part_of = lambda half: lambda slot: ox.at[slot, pl.ds(pl.multiple_of(half * 128, 128), 128)]
    home = Home(gx, cross, sel, part_of(y), part_of(1 - y), length, home_sems[:5], pos)
    outs = Home(bl, cross_b, sel_b, None, lambda slot: ocross.at[slot], length, home_sems[5:], pos)
    outs.first()
    agrad[...] = gmid[...].astype(BF)
    vbuf[0] = vin[...]

    def put_vec(row, v):
        for t in range(v.shape[1] // 128):
            vbuf[0, row + t:row + t + 1, :] = v[:, t * 128:(t + 1) * 128]
    put_vec(30, jnp.sum(agrad[...].astype(F32), axis=0, keepdims=True))
    wo = lambda: WO[...].reshape(768, 768)

    da[...] = nt(agrad[...], wo()).astype(BF)
    for i in range(4):
        actsqT[:, i * 128:(i + 1) * 128] = actsT[:, rows(own_block(jnp.int32(i), k))]

    sdn.stage(2)

    def out_rows(t):
        aT = att[:, t * 384:(t + 1) * 384].T.astype(BF)
        g = nn(aT, agrad[...]).astype(BF)
        GO[2 * t:2 * t + 2] = g.reshape(2, 2, 2, 48, 768)
    sup.stage(1)
    for t in range(2): out_rows(t)
    sout.stage(0)
    outs.second()
    bias_rows(bias, length, k)
    dK[...] = jnp.zeros_like(dK)
    dV[...] = jnp.zeros_like(dV)
    ck.wait(); cv.wait()

    def heads(h):
        lanes = rows(h)
        KT[...] = K[:, lanes].T
        at = 0
        for i in range(4):
            kk = 256 * (i + 1)
            r = slice(i * 128, (i + 1) * 128)
            d = da[r, lanes]
            qb, db = spread(Q[r, lanes]), spread(d)
            prod = (d.astype(F32) * att[r, lanes]).T
            delta = jnp.concatenate([jnp.sum(prod[:64], axis=0, keepdims=True), jnp.sum(prod[64:], axis=0, keepdims=True)], axis=1)
            st = nt(K[0:kk, lanes], qb) + both_heads(bias, at, kk)
            p = jnp.exp(st - lse[h, i:i + 1, :])
            ds = (p * (nt(V[0:kk, lanes], db) - delta)).astype(BF)
            dV[0:kk, lanes] += nn(p.astype(BF), db)
            dK[0:kk, lanes] += nn(ds, qb)
            dQ[r, lanes] = pick(nn(KT[:, 0:kk], ds)) * 0.125
            at += kk

    pl.loop(0, 2)(heads)
    sout.stage(1)
    pl.loop(2, 4)(heads)
    sdn.stage(3)
    pl.loop(4, 6)(heads)
    V[...] = dV[...].astype(BF)
    put_vec(24, jnp.sum(V[...].astype(F32), axis=0, keepdims=True))

    def weight_rows(n, lhs, g):
        @pl.loop(0, 4)
        def _(t):
            GQ[n, t] = nn(lhs[rows(t, 192), :], g[...]).astype(BF).reshape(2, 2, 48, 768)
    @pl.loop(0, 8)
    def _(j):
        c, s = table_rows(COS, SIN, length, j)
        for t in range(6):
            u = dK[rows(j), t * 128:(t + 1) * 128]
            K[rows(j), t * 128:(t + 1) * 128] = (u * c - swap(u) * s).astype(BF)

    @pl.loop(0, 4)
    def _(i):
        j = own_block(i, k)
        c, s = table_rows(COS, SIN, length, j)
        for t in range(6):
            u = dQ[rows(i), t * 128:(t + 1) * 128]
            da[rows(i), t * 128:(t + 1) * 128] = (u * c - swap(u) * s).astype(BF)
    @pl.loop(0, 2)
    def _(j):
        r = rows(j, 512)
        dK[r, :] = nt(K[r, :], matrix(WQ, slice(768, 1536))) + nt(V[r, :], matrix(WQ, slice(1536, 2304)))
    dQ[...] = nt(da[...], matrix(WQ, slice(0, 768)))
    for i in range(4):
        dK[rows(own_block(jnp.int32(i), k)), :] += dQ[i * 128:(i + 1) * 128, :]
        es[i] = dK[rows(own_block(jnp.int32(i), 1 - k)), :].astype(BF)
    ecp = remote(es, er, esem_s, esem_r, sib)
    ecp.start()
    sup.stage(2)
    sout.stage(2)
    weight_rows(2, actsT, V)
    sv.stage(0)
    put_vec(18, jnp.sum(K[...].astype(F32), axis=0, keepdims=True))
    put_vec(12, jnp.sum(da[...].astype(F32), axis=0, keepdims=True))
    ecp.wait_recv()
    gg = jnp.zeros((1, 768), F32)
    gsh = jnp.zeros((1, 768), F32)
    for i in range(4):
        n, inv = norm(X[i].astype(F32))
        ee = dK[rows(own_block(jnp.int32(i), k)), :] + er[i].astype(F32)
        gg += jnp.sum(ee * n, axis=0, keepdims=True)
        gsh += jnp.sum(ee, axis=0, keepdims=True)
        gx[i] = (gmid[i * 128:(i + 1) * 128, :] + norm_grad(ee, n, inv, gain[0:1, :])).astype(BF)
    home.first(); home.straight()
    put_vec(0, gg); put_vec(6, gsh)
    vec_steps = [[sib], [dev(z, *sdn.p2, k)], [dev(z, *sdn.p3, k)], [dev(lax.rem(z + d, 4), y, x, k) for d in (1, 2, 3)]]
    vcp = []
    def vec_stage(n):
        if n > 0:
            for c in vcp[-1]: c.wait_recv()
            t = vbuf[n - 1]
            for r in range(len(vcp[-1])):
                t = t + vrec[n - 1 + r]
            if n < 4: vbuf[n] = t
            else: vout[...] = t
        if n < 4:
            vcp.append([remote(vbuf.at[n], vrec.at[n + i], vsend.at[n + i], vrecv.at[n + i], d) for i, d in enumerate(vec_steps[n])])
            for c in vcp[-1]: c.start()

    weight_rows(1, actsT, K)
    sk.stage(0)
    sv.stage(1)
    sdn.stage(4)
    weight_rows(0, actsqT, da)
    sq.stage(0)
    sk.stage(1)
    sq.stage(1)
    vec_stage(0)
    sout.stage(3)
    sup.stage(3)
    home.second()
    vec_stage(1)
    sv.stage(2)
    sk.stage(2)
    sq.stage(2)
    sup.stage(4)
    sv.stage(3)
    sout.stage(4)
    sk.stage(3)
    sdn.stage(5); sdn.stage(6)
    sv.stage(4)
    sq.stage(3)
    vec_stage(2)
    sk.stage(4)
    sq.stage(4)
    vec_stage(3)
    sup.stage(5); sout.stage(5)
    sv.stage(5); sk.stage(5); sq.stage(5)
    sup.stage(6); sout.stage(6)
    vec_stage(4)
    sv.stage(6); sk.stage(6); sq.stage(6)
    outs.done()
    home.done()
    ecp.wait_send()
    for cs in vcp:
        for c in cs: c.wait_send()


def backward_call(gup, pdown, bdown, *ins):
    n_up = gup.shape[1]
    gup = gup.reshape(4, 2, 2, 48, n_up)
    any_ = pl.BlockSpec(memory_space=pl.ANY)
    def bufs(r, n, lead=()):
        return [VM(lead + s + (r, n), BF) for s in ((4, 2, 2), (2, 4), (4,), (4,))]
    DS = pltpu.SemaphoreType.DMA
    home = sd((2, 256, 768), BF)
    return pl.pallas_call(backward_kernel,
        out_shape=[sd((24, 2304), F32), sd((24, 768), F32), sd((24, 3072), F32), sd((96, 768), F32), sd((80, 128), F32), home, sd((2, 128, 768), BF)],
        in_specs=[any_] * 3 + [vs] * 5 + [any_] * 2 + [vs] * 8, out_specs=[vs] * 5 + [any_] * 2,
        scratch_shapes=[VM((1024, 768), BF), VM((1024, 768), BF), VM((2560, 128), F32), VM((128, 1024), BF), VM((512, 768), BF), VM((512, 768), F32),
                        VM((1024, 768), F32), VM((1024, 768), F32), VM((512, 768), BF), VM((768, 512), BF),
                        VM((4, 2, 2, 48, 768), BF), VM((3, 4, 2, 2, 48, 768), BF), VM((4, 2, 2, 48, 1536), BF), VM((4, 2, 2, 96, 768), BF)]
        + bufs(48, 1536) + bufs(96, 768)[1:] + bufs(48, 384) + bufs(48, 384, (3,))
        + [VM((4, 2, 24, 384), F32), VM((4, 24, 384), F32), VM((1, 2, 24, 1536), F32), VM((1, 24, 1536), F32),
           VM((4, 128, 768), BF), VM((4, 128, 768), BF), VM((4, 128, 768), BF), VM((2, 128, 768), BF), VM((2, 128, 768), BF), VM((2, 128, 768), BF), VM((2, 128, 768), BF), VM((4, 80, 128), F32), VM((6, 80, 128), F32),
           DS((6, 9)), DS((6, 9)), DS((3,)), DS((6,)), DS((6,)), DS, DS, DS((6,)), DS((6,)), DS((2,)), DS((2,)), DS((2,)), DS((4,)), DS((2,)), DS((2,)), DS((2,)), DS((2,)), DS((4,)), DS((2,)), DS((2,))],
        compiler_params=pltpu.CompilerParams(collective_id=1, has_side_effects=True, vmem_limit_bytes=63 * 2**20),
    )(gup, pdown, bdown, *ins)


def finish_kernel(vout, cin, premix, home, across, gx, gq, go, gu, gd, mix,
                  lo, ox, gh, oq, oo, ou, od, v0, v1, v2, v3, v4, v5, v6, v7, gm, stage, sems):
    z, y, x, k = where_am_i()
    copies = []
    for j in range(5):
        stage[j] = (mix[j] * cin[...].astype(F32)).astype(BF)
        c = pltpu.make_async_copy(stage.at[j], gh.at[j], sems.at[j])
        c.start(); copies.append(c)
    for src, half in ((home, y), (across, 1 - y)):
        r = pl.ds(pl.multiple_of(half * 128, 128), 128)
        lo[:, r, :] = (premix[:, r, :] + mix[5] * src[...].astype(F32)).astype(BF)
    me = ((z * 2 + y) * 2 + x) * 2 + k
    spot = lax.broadcasted_iota(jnp.int32, (8, 128), 1)
    base = 0
    for v in (v0, v1, v2, v3, v4, v5, v6, v7):
        n = v.shape[0]
        first = me * n
        row, shift = first // 128, lax.rem(first, 128)
        a = jnp.broadcast_to(vout[pl.ds(base + row, 1), :], (8, 128))
        b = jnp.broadcast_to(vout[pl.ds(base + row + 1, 1), :], (8, 128))
        back = lax.rem(128 - shift, 128)
        both = jnp.where(spot < 128 - shift, pltpu.roll(a, back, 1), pltpu.roll(b, back, 1))
        v[...] = both[0, :n]
        base += n // 4
    gm[...] = vout[78, :6]
    for a, b in ((gx, ox), (gq, oq), (go, oo), (gu, ou), (gd, od)):
        b[...] = a[...]
    for c in copies: c.wait()


def finish_call(vectors, vout, cin, premix, home, across, gx, gq, go, gu, gd, mix):
    any_ = pl.BlockSpec(memory_space=pl.ANY)
    like = lambda a: sd(a.shape, a.dtype)
    return pl.pallas_call(finish_kernel,
        out_shape=[sd(cin.shape, BF), like(gx), sd((5,) + cin.shape, BF), like(gq), like(go), like(gu), like(gd)]
        + [sd(v.shape, F32) for v in vectors] + [sd((6,), F32)],
        in_specs=[vs] * 10 + [ss], out_specs=[vs, vs, any_] + [vs] * 13,
        scratch_shapes=[VM((5,) + cin.shape, BF), pltpu.SemaphoreType.DMA((5,))],
        compiler_params=pltpu.CompilerParams(vmem_limit_bytes=62 * 2**20),
    )(vout, cin, premix, home, across, gx, gq, go, gu, gd, mix)

def fast_shards(inputs, history, seq_lengths, attn_gain, attn_shift, qkv_weight, qkv_bias, out_weight, out_bias, mlp_gain,
                mlp_shift, up_weight, up_bias, down_weight, down_bias, mix_weights, cotangent):
    seq, batch = lax.axis_index("seq"), lax.axis_index("batch")
    z, y, x, k = seq // 2, seq % 2, batch // 2, batch % 2
    vectors = (attn_gain, attn_shift, qkv_bias, out_bias, mlp_gain, mlp_shift, up_bias, down_bias)
    COS, SIN = (jnp.asarray(t) for t in rope_tables())
    X, actsT, Q, K, V, att, lse, WQ, WO, gmid, gup, pdown, bdown, block, home, premix, gain, vin = forward_call(
        qkv_weight, out_weight, up_weight, down_weight, inputs, cotangent, COS, SIN, history, vectors, mix_weights, seq_lengths)
    oq, oo, ou, od, vout, grad_inputs, across = backward_call(gup, pdown, bdown, block, gmid, X, actsT, Q, K, V, att, lse, WQ, WO, gain, COS, SIN, vin)
    layer_out, grad_inputs, grad_history, oq, oo, ou, od, *gv, grad_mix = finish_call(
        vectors, vout, cotangent, premix, home, across, grad_inputs, oq, oo, ou, od, mix_weights)
    return (layer_out, grad_inputs, grad_history, gv[0], gv[1], oq, gv[2], oo, gv[3], gv[4], gv[5], ou, gv[6], od, gv[7], grad_mix)


def fits(mesh, inputs):
    shape = dict(mesh.shape)
    return shape == {"seq": 8, "batch": 4} and inputs.shape == (8, 2048, 768)


def solution(mesh):
    def run(*args):
        body = fast_shards if fits(mesh, args[0]) else shards
        return placed(mesh, body)(*args)
    return run
```

```python
import functools
import math

import jax
import jax.numpy as jnp
import numpy as np
from jax import lax
from jax.experimental import pallas as pl
from jax.experimental.pallas import tpu as pltpu
from jax.sharding import PartitionSpec as P

HEADS = 12
HEAD_DIM = 64
LONG_LEN = 1024
SHORT_LEN = 256


eps = 1e-05
masked = -1e30


def block_size(row_count):
    chosen = 1
    for candidate in range(1, min(row_count, 512) + 1):
        if row_count % candidate == 0:
            chosen = candidate
    return chosen


def exact_gelu(values):
    return jax.nn.gelu(values, approximate=False)


def layer_norm(values, norm_gain, norm_shift):
    average = jnp.mean(values, axis=-1, keepdims=True)
    centred = values - average
    inverse = lax.rsqrt(jnp.mean(centred * centred, axis=-1, keepdims=True) + eps)
    normed = centred * inverse
    return (normed * norm_gain + norm_shift, normed, inverse)


def norm_back(grad_out, normed, inverse, norm_gain):
    grad_normed = grad_out * norm_gain
    mean_grad = jnp.mean(grad_normed, axis=-1, keepdims=True)
    mean_cross = jnp.mean(grad_normed * normed, axis=-1, keepdims=True)
    grad_in = inverse * (grad_normed - mean_grad - normed * mean_cross)
    return (grad_in, jnp.sum(grad_out * normed, axis=0), jnp.sum(grad_out, axis=0))


def token_layout(index, info):
    seq_len, tok_count, slice_len = info
    is_long = seq_len == LONG_LEN
    offset = index % tok_count
    device = index // tok_count
    doc_ids = jnp.where(is_long, offset // slice_len, index // SHORT_LEN).astype(jnp.int32)
    relative = jnp.where(
        is_long, device * slice_len + offset % slice_len, index % SHORT_LEN
    ).astype(jnp.int32)
    return (doc_ids, relative)


def rotary_tables(relative):
    half_dim = HEAD_DIM // 2
    frequency = jnp.exp(
        -math.log(10000.0) * (2.0 * jnp.arange(half_dim, dtype=jnp.float32) / HEAD_DIM)
    )
    angles = relative.astype(jnp.float32)[:, None] * frequency[None, :]
    return (jnp.cos(angles)[:, None, :], jnp.sin(angles)[:, None, :])


def rotate(values, cosine, sine_table):
    half_dim = values.shape[-1] // 2
    lower_half = values[..., :half_dim]
    upper_half = values[..., half_dim:]
    return jnp.concatenate(
        [
            lower_half * cosine - upper_half * sine_table,
            upper_half * cosine + lower_half * sine_table,
        ],
        axis=-1,
    )


def allowed_mask(query_places, key_places, info):
    query_docs, query_rel = token_layout(query_places, info)
    key_docs, key_rel = token_layout(key_places, info)
    return (key_docs[None, :] == query_docs[:, None]) & (key_rel[None, :] <= query_rel[:, None])


def online_block(current, query_b, key_block, value_block, query_places, key_places, info):
    running, denominator, weighted = current
    key_count = key_block.shape[0]
    allowed = allowed_mask(query_places, key_places, info)
    key_heads = key_block.reshape(key_count, HEADS, HEAD_DIM)
    scores = jnp.einsum(
        "qhd,khd->hqk", query_b, key_heads, preferred_element_type=jnp.float32
    ) * HEAD_DIM ** (-0.5)
    scores = jnp.where(allowed[None], scores, masked)
    new_max = jnp.maximum(running, jnp.max(scores, axis=-1))
    exp_scores = jnp.where(allowed[None], jnp.exp(scores - new_max[..., None]), 0.0)
    rescale = jnp.exp(running - new_max)
    denominator = denominator * rescale + jnp.sum(exp_scores, axis=-1)
    value_heads = value_block.reshape(key_count, HEADS, HEAD_DIM)
    weighted = weighted * rescale[..., None] + jnp.einsum(
        "hqk,khd->hqd",
        exp_scores.astype(jnp.bfloat16),
        value_heads,
        preferred_element_type=jnp.float32,
    )
    return (new_max, denominator, weighted)


def attend_rows(current, query_b, key_rows, value_rows, first_row, query_places, info, last_place):
    key_count = key_rows.shape[0]
    block_rows = block_size(key_count)

    def one_block(carried, block_index):
        start_place = first_row + block_index * block_rows
        key_block = lax.dynamic_slice_in_dim(key_rows, block_index * block_rows, block_rows, 0)
        value_block = lax.dynamic_slice_in_dim(value_rows, block_index * block_rows, block_rows, 0)
        key_places = start_place + jnp.arange(block_rows, dtype=jnp.int32)

        def one_compute(state_in):
            return online_block(
                state_in, query_b, key_block, value_block, query_places, key_places, info
            )

        def unchanged(state_in):
            return state_in

        return (lax.cond(start_place > last_place, unchanged, one_compute, carried), None)

    result, unused = lax.scan(
        one_block, current, jnp.arange(key_count // block_rows, dtype=jnp.int32)
    )
    return result


def block_probs(query_b, key_b, query_places, key_places, info, lse_rows):
    allowed = allowed_mask(query_places, key_places, info)
    scores = jnp.einsum(
        "qhd,khd->hqk", query_b, key_b, preferred_element_type=jnp.float32
    ) * HEAD_DIM ** (-0.5)
    return jnp.exp(jnp.where(allowed[None], scores - lse_rows[..., None], masked))


def block_dscores(probabilities, grad_b, value_b, delta_rows):
    dprobs = jnp.einsum("qhd,khd->hqk", grad_b, value_b, preferred_element_type=jnp.float32)
    return (probabilities * (dprobs - delta_rows[..., None])).astype(jnp.bfloat16)


def shards(
    inputs,
    history,
    seq_lengths,
    attn_gain,
    attn_shift,
    qkv_weight,
    qkv_bias,
    out_weight,
    out_bias,
    mlp_gain,
    mlp_shift,
    up_weight,
    up_bias,
    down_weight,
    down_bias,
    mix_weights,
    cotangent,
):
    group_count = inputs.shape[0]
    tok_count = inputs.shape[1]
    model_width = inputs.shape[2]
    seq_count = lax.axis_size("seq")
    group_rows = tok_count * seq_count
    slice_len = LONG_LEN // seq_count
    factor = HEAD_DIM ** (-0.5)
    seq_index = lax.axis_index("seq")
    first_place = seq_index * tok_count
    last_place = first_place + tok_count - 1
    places = first_place + jnp.arange(tok_count, dtype=jnp.int32)
    gathered = (
        lax.all_gather(attn_gain, ("seq", "batch"), axis=0, tiled=True),
        lax.all_gather(attn_shift, ("seq", "batch"), axis=0, tiled=True),
        lax.all_gather(qkv_weight, ("seq", "batch"), axis=0, tiled=True),
        lax.all_gather(qkv_bias, ("seq", "batch"), axis=0, tiled=True),
        lax.all_gather(out_weight, ("seq", "batch"), axis=0, tiled=True),
        lax.all_gather(out_bias, ("seq", "batch"), axis=0, tiled=True),
        lax.all_gather(mlp_gain, ("seq", "batch"), axis=0, tiled=True),
        lax.all_gather(mlp_shift, ("seq", "batch"), axis=0, tiled=True),
        lax.all_gather(up_weight, ("seq", "batch"), axis=0, tiled=True),
        lax.all_gather(up_bias, ("seq", "batch"), axis=0, tiled=True),
        lax.all_gather(down_weight, ("seq", "batch"), axis=0, tiled=True),
        lax.all_gather(down_bias, ("seq", "batch"), axis=0, tiled=True),
    )
    (
        gain_one,
        shift_one,
        qkv_full,
        qkv_vec,
        out_full,
        out_vec,
        gain_two,
        shift_two,
        up_full,
        up_vec,
        down_full,
        down_vec,
    ) = gathered
    saved = []
    block_outs = []
    for group in range(group_count):
        info = (seq_lengths[group], tok_count, slice_len)
        doc_ids, relative = token_layout(places, info)
        cosine, sine_table = rotary_tables(relative)
        residual_in = inputs[group].astype(jnp.float32)
        normed_out, normed_one, inverse_one = layer_norm(
            residual_in, gain_one.astype(jnp.float32), shift_one.astype(jnp.float32)
        )
        acts_one = normed_out.astype(jnp.bfloat16)
        projected = jnp.dot(
            acts_one, qkv_full, preferred_element_type=jnp.float32
        ) + qkv_vec.astype(jnp.float32)
        queries = rotate(
            projected[:, :model_width].reshape(tok_count, HEADS, HEAD_DIM), cosine, sine_table
        ).astype(jnp.bfloat16)
        key_flat = (
            rotate(
                projected[:, model_width : 2 * model_width].reshape(tok_count, HEADS, HEAD_DIM),
                cosine,
                sine_table,
            )
            .reshape(tok_count, model_width)
            .astype(jnp.bfloat16)
        )
        value_flat = projected[:, 2 * model_width :].astype(jnp.bfloat16)
        start_state = (
            jnp.full((HEADS, tok_count), masked, jnp.float32),
            jnp.zeros((HEADS, tok_count), jnp.float32),
            jnp.zeros((HEADS, tok_count, HEAD_DIM), jnp.float32),
        )
        key_all = None
        value_all = None
        running, denominator, weighted = attend_rows(
            start_state,
            queries,
            lax.all_gather(key_flat, "seq", axis=0, tiled=True),
            lax.all_gather(value_flat, "seq", axis=0, tiled=True),
            jnp.int32(0),
            places,
            info,
            last_place,
        )
        attended = jnp.transpose(weighted / denominator[..., None], (1, 0, 2))
        lse_rows = running + jnp.log(denominator)
        attended_b = attended.reshape(tok_count, model_width).astype(jnp.bfloat16)
        middle = (
            residual_in
            + jnp.dot(attended_b, out_full, preferred_element_type=jnp.float32)
            + out_vec.astype(jnp.float32)
        )
        normed_out_two, normed_two, inverse_two = layer_norm(
            middle, gain_two.astype(jnp.float32), shift_two.astype(jnp.float32)
        )
        acts_two = normed_out_two.astype(jnp.bfloat16)
        upward = jnp.dot(acts_two, up_full, preferred_element_type=jnp.float32) + up_vec.astype(
            jnp.float32
        )
        activated, gelu_back = jax.vjp(exact_gelu, upward)
        activated_b = activated.astype(jnp.bfloat16)
        block_out = (
            middle
            + jnp.dot(activated_b, down_full, preferred_element_type=jnp.float32)
            + down_vec.astype(jnp.float32)
        )
        block_outs.append(block_out)
        saved.append(
            (
                info,
                cosine,
                sine_table,
                normed_one,
                inverse_one,
                acts_one,
                queries,
                key_flat,
                value_flat,
                key_all,
                value_all,
                attended,
                lse_rows,
                attended_b,
                normed_two,
                inverse_two,
                acts_two,
                gelu_back,
                activated_b,
            )
        )
    block_stack = jnp.stack(block_outs, axis=0)
    earlier = history.astype(jnp.float32)
    grad_out_all = cotangent.astype(jnp.float32)
    mixed_out = (
        jnp.sum(mix_weights[:-1, None, None, None] * earlier, axis=0)
        + mix_weights[-1] * block_stack
    )
    mix_terms = jnp.concatenate(
        [
            jnp.sum(earlier * grad_out_all[None], axis=(1, 2, 3)),
            jnp.sum(block_stack * grad_out_all)[None],
        ]
    )
    grad_history = (mix_weights[:-1, None, None, None] * grad_out_all[None]).astype(jnp.bfloat16)
    back_gain_one, back_qkv, back_out, back_gain_two, back_up, back_down = (
        lax.all_gather(attn_gain, ("seq", "batch"), axis=0, tiled=True),
        lax.all_gather(qkv_weight, ("seq", "batch"), axis=0, tiled=True),
        lax.all_gather(out_weight, ("seq", "batch"), axis=0, tiled=True),
        lax.all_gather(mlp_gain, ("seq", "batch"), axis=0, tiled=True),
        lax.all_gather(up_weight, ("seq", "batch"), axis=0, tiled=True),
        lax.all_gather(down_weight, ("seq", "batch"), axis=0, tiled=True),
    )
    totals = None
    grad_input_list = []
    for group in range(group_count):
        (
            info,
            cosine,
            sine_table,
            normed_one,
            inverse_one,
            acts_one,
            queries,
            key_flat,
            value_flat,
            key_all,
            value_all,
            attended,
            lse_rows,
            attended_b,
            normed_two,
            inverse_two,
            acts_two,
            gelu_back,
            activated_b,
        ) = saved[group]
        grad_block = mix_weights[-1] * grad_out_all[group]
        down_grad_b = grad_block.astype(jnp.bfloat16)
        grad_w_down = jnp.einsum(
            "tf,td->fd", activated_b, down_grad_b, preferred_element_type=jnp.float32
        )
        grad_b_down = jnp.sum(down_grad_b.astype(jnp.float32), axis=0)
        grad_act = jnp.einsum(
            "td,fd->tf", down_grad_b, back_down, preferred_element_type=jnp.float32
        )
        up_grad_b = gelu_back(grad_act)[0].astype(jnp.bfloat16)
        grad_w_up = jnp.einsum("td,tf->df", acts_two, up_grad_b, preferred_element_type=jnp.float32)
        grad_b_up = jnp.sum(up_grad_b.astype(jnp.float32), axis=0)
        grad_acts_two = jnp.einsum(
            "tf,df->td", up_grad_b, back_up, preferred_element_type=jnp.float32
        )
        grad_middle_norm, grad_gain_two, grad_shift_two = norm_back(
            grad_acts_two, normed_two, inverse_two, back_gain_two.astype(jnp.float32)
        )
        grad_middle = grad_block + grad_middle_norm
        attn_grad_b = grad_middle.astype(jnp.bfloat16)
        grad_w_out = jnp.einsum(
            "te,td->ed", attended_b, attn_grad_b, preferred_element_type=jnp.float32
        )
        grad_b_out = jnp.sum(attn_grad_b.astype(jnp.float32), axis=0)
        grad_heads = (
            jnp.einsum("td,ed->te", attn_grad_b, back_out, preferred_element_type=jnp.float32)
            .astype(jnp.bfloat16)
            .reshape(tok_count, HEADS, HEAD_DIM)
        )
        delta_rows = jnp.transpose(jnp.sum(grad_heads.astype(jnp.float32) * attended, axis=-1))
        key_all, value_all = (
            lax.all_gather(key_flat, "seq", axis=0, tiled=True),
            lax.all_gather(value_flat, "seq", axis=0, tiled=True),
        )
        key_block_rows = block_size(group_rows)

        def query_grad_block(carried, block_index):
            start_place = block_index * key_block_rows
            key_block = lax.dynamic_slice_in_dim(key_all, start_place, key_block_rows, 0).reshape(
                key_block_rows, HEADS, HEAD_DIM
            )
            value_block = lax.dynamic_slice_in_dim(
                value_all, start_place, key_block_rows, 0
            ).reshape(key_block_rows, HEADS, HEAD_DIM)
            key_places = start_place + jnp.arange(key_block_rows, dtype=jnp.int32)

            def query_compute(summed):
                probabilities = block_probs(queries, key_block, places, key_places, info, lse_rows)
                dscores = block_dscores(probabilities, grad_heads, value_block, delta_rows)
                return (
                    summed
                    + jnp.einsum(
                        "hqk,khd->qhd", dscores, key_block, preferred_element_type=jnp.float32
                    )
                    * factor
                )

            return (
                lax.cond(start_place > last_place, lambda summed: summed, query_compute, carried),
                None,
            )

        grad_queries, unused = lax.scan(
            query_grad_block,
            jnp.zeros((tok_count, HEADS, HEAD_DIM), jnp.float32),
            jnp.arange(group_rows // key_block_rows, dtype=jnp.int32),
        )
        key_first_row = jnp.int32(0)
        key_rows = key_all
        value_rows = value_all
        inner_rows = block_size(lax.axis_size("seq") * tok_count)

        def key_grad_block(carried, block_index):
            offset = block_index * inner_rows
            start_place = key_first_row + offset
            key_block = lax.dynamic_slice_in_dim(key_rows, offset, inner_rows, 0).reshape(
                inner_rows, HEADS, HEAD_DIM
            )
            value_block = lax.dynamic_slice_in_dim(value_rows, offset, inner_rows, 0).reshape(
                inner_rows, HEADS, HEAD_DIM
            )
            key_places = start_place + jnp.arange(inner_rows, dtype=jnp.int32)

            def key_compute(unused_in):
                probabilities = block_probs(queries, key_block, places, key_places, info, lse_rows)
                dscores = block_dscores(probabilities, grad_heads, value_block, delta_rows)
                grad_keys = (
                    jnp.einsum("hqk,qhd->khd", dscores, queries, preferred_element_type=jnp.float32)
                    * factor
                )
                grad_values = jnp.einsum(
                    "hqk,qhd->khd",
                    probabilities.astype(jnp.bfloat16),
                    grad_heads,
                    preferred_element_type=jnp.float32,
                )
                return jnp.concatenate(
                    [
                        grad_keys.reshape(inner_rows, model_width),
                        grad_values.reshape(inner_rows, model_width),
                    ],
                    axis=1,
                )

            def nothing(unused_in):
                return jnp.zeros((inner_rows, 2 * model_width), jnp.float32)

            return (carried, lax.cond(start_place > last_place, nothing, key_compute, carried))

        unused_out, blocks = lax.scan(
            key_grad_block,
            jnp.int32(0),
            jnp.arange(lax.axis_size("seq") * tok_count // inner_rows, dtype=jnp.int32),
        )
        key_grads = lax.psum_scatter(
            blocks.reshape(lax.axis_size("seq") * tok_count, 2 * model_width).astype(jnp.bfloat16),
            "seq",
            scatter_dimension=0,
            tiled=True,
        ).astype(jnp.float32)
        grad_keys_own = key_grads[:, :model_width]
        grad_values_own = key_grads[:, model_width:]
        grad_q_turned = rotate(grad_queries, cosine, -sine_table).reshape(tok_count, model_width)
        grad_k_turned = rotate(
            grad_keys_own.reshape(tok_count, HEADS, HEAD_DIM), cosine, -sine_table
        ).reshape(tok_count, model_width)
        qkv_grad_b = jnp.concatenate(
            [grad_q_turned, grad_k_turned, grad_values_own], axis=1
        ).astype(jnp.bfloat16)
        grad_w_qkv = jnp.einsum(
            "td,te->de", acts_one, qkv_grad_b, preferred_element_type=jnp.float32
        )
        grad_b_qkv = jnp.sum(qkv_grad_b.astype(jnp.float32), axis=0)
        grad_acts_one = jnp.einsum(
            "te,de->td", qkv_grad_b, back_qkv, preferred_element_type=jnp.float32
        )
        grad_in_norm, grad_gain_one, grad_shift_one = norm_back(
            grad_acts_one, normed_one, inverse_one, back_gain_one.astype(jnp.float32)
        )
        grad_input_list.append((grad_middle + grad_in_norm).astype(jnp.bfloat16))
        terms = [
            grad_gain_one,
            grad_shift_one,
            grad_w_qkv,
            grad_b_qkv,
            grad_w_out,
            grad_b_out,
            grad_gain_two,
            grad_shift_two,
            grad_w_up,
            grad_b_up,
            grad_w_down,
            grad_b_down,
        ]
        if totals is None:
            totals = terms
        else:
            totals = [older + newer for older, newer in zip(totals, terms)]
    shares = (
        lax.psum_scatter(totals[0], ("seq", "batch"), scatter_dimension=0, tiled=True),
        lax.psum_scatter(totals[1], ("seq", "batch"), scatter_dimension=0, tiled=True),
        lax.psum_scatter(totals[2], ("seq", "batch"), scatter_dimension=0, tiled=True),
        lax.psum_scatter(totals[3], ("seq", "batch"), scatter_dimension=0, tiled=True),
        lax.psum_scatter(totals[4], ("seq", "batch"), scatter_dimension=0, tiled=True),
        lax.psum_scatter(totals[5], ("seq", "batch"), scatter_dimension=0, tiled=True),
        lax.psum_scatter(totals[6], ("seq", "batch"), scatter_dimension=0, tiled=True),
        lax.psum_scatter(totals[7], ("seq", "batch"), scatter_dimension=0, tiled=True),
        lax.psum_scatter(totals[8], ("seq", "batch"), scatter_dimension=0, tiled=True),
        lax.psum_scatter(totals[9], ("seq", "batch"), scatter_dimension=0, tiled=True),
        lax.psum_scatter(totals[10], ("seq", "batch"), scatter_dimension=0, tiled=True),
        lax.psum_scatter(totals[11], ("seq", "batch"), scatter_dimension=0, tiled=True),
    )
    grad_mix = lax.psum(mix_terms, ("seq", "batch"))
    grad_inputs = jnp.stack(grad_input_list, axis=0)
    return (
        mixed_out.astype(jnp.bfloat16),
        grad_inputs,
        grad_history,
        shares[0],
        shares[1],
        shares[2],
        shares[3],
        shares[4],
        shares[5],
        shares[6],
        shares[7],
        shares[8],
        shares[9],
        shares[10],
        shares[11],
        grad_mix,
    )


def placed(mesh, body):
    return jax.shard_map(
        body,
        mesh=mesh,
        in_specs=(
            P("batch", "seq", None),
            P(None, "batch", "seq", None),
            P("batch"),
            P(("seq", "batch")),
            P(("seq", "batch")),
            P(("seq", "batch"), None),
            P(("seq", "batch")),
            P(("seq", "batch"), None),
            P(("seq", "batch")),
            P(("seq", "batch")),
            P(("seq", "batch")),
            P(("seq", "batch"), None),
            P(("seq", "batch")),
            P(("seq", "batch"), None),
            P(("seq", "batch")),
            P(),
            P("batch", "seq", None),
        ),
        out_specs=(
            P("batch", "seq", None),
            P("batch", "seq", None),
            P(None, "batch", "seq", None),
            P(("seq", "batch")),
            P(("seq", "batch")),
            P(("seq", "batch"), None),
            P(("seq", "batch")),
            P(("seq", "batch"), None),
            P(("seq", "batch")),
            P(("seq", "batch")),
            P(("seq", "batch")),
            P(("seq", "batch"), None),
            P(("seq", "batch")),
            P(("seq", "batch"), None),
            P(("seq", "batch")),
            P(),
        ),
        check_vma=False,
    )

MESH = pl.DeviceIdType.MESH
BF, F32 = jnp.bfloat16, jnp.float32


def where_am_i():
    seq, batch = lax.axis_index("seq"), lax.axis_index("batch")
    return seq // 2, seq % 2, batch // 2, batch % 2


def dev(z, y, x, k):
    return (z * 2 + y, x * 2 + k)


def remote(src, dst, ssem, rsem, device):
    return pltpu.make_async_remote_copy(src_ref=src, dst_ref=dst, send_sem=ssem, recv_sem=rsem,
                                        device_id=device, device_id_type=MESH)


def chips_of(z, y, x):
    mine = (z * 2 + y) * 2 + x
    for step in range(1, 16):
        other = lax.rem(mine + step, 16)
        yield step, (other // 4, (other // 2) % 2, other % 2)


def greet(z, y, x, k):
    barrier = pltpu.get_barrier_semaphore()
    for _, chip in chips_of(z, y, x):
        pl.semaphore_signal(barrier, inc=1, device_id=dev(*chip, k), device_id_type=MESH)
    for step in range(8):
        other = lax.rem(z * 2 + y + step, 8)
        pl.semaphore_signal(barrier, inc=1, device_id=dev(other // 2, other % 2, x, 1 - k), device_id_type=MESH)
    pl.semaphore_wait(barrier, 23)


class Gather:
    STAGES = 7

    def __init__(self, part, send, recv, pos, both, hops):
        z, y, x, k = pos
        self.hops = hops
        turn = (k == 0) | both
        p2 = jnp.where(turn, 1 - y, y), jnp.where(turn, x, 1 - x)
        p3 = jnp.where(turn, y, 1 - y), jnp.where(turn, 1 - x, x)
        d4 = 1 - y, 1 - x
        one = lambda zz: part(pl.ds(zz, 1), y, x, k)
        allz = lambda yx: part(slice(None), yx[0], yx[1], k)
        self.mid = (z == 1) | (z == 2)
        end = jnp.where(z == 1, 0, 3)
        def cp(n, ref, device, r=None):
            return remote(ref, ref, send.at[n], recv.at[n if r is None else r], device)
        others = [lax.rem(z + d, 4) for d in (1, 2, 3)]
        self.three = [cp(d, one(o), dev(o, y, x, k), o) for d, o in enumerate(others)]
        if hops:
            self.direct = [cp(0, one(z), dev(jnp.where(z == 1, 0, 1), y, x, k), z), cp(1, one(z), dev(jnp.where(z == 2, 3, 2), y, x, k), z)]
        else:
            self.direct = [cp(d, one(z), dev(o, y, x, k), z) for d, o in enumerate(others)]
        self.passed = [cp(3 + n, one(f), dev(end, y, x, k), f) for n, f in enumerate((3 - z, 3 - end))]
        self.near = cp(0, one(end), dev(end, y, x, k), end)
        n2, n3 = dev(z, *p2, k), dev(z, *p3, k)
        blocks = [z] + others
        self.a2 = [cp(5 + n, one(b), n2, 4 + b) for n, b in enumerate(blocks)]
        self.a3 = [cp(9 + n, one(b), n3, 8 + b) for n, b in enumerate(blocks)]
        self.b3 = [cp(13 + n, part(pl.ds(b, 1), *p2, k), n3, 12 + b) for n, b in enumerate(blocks)]
        sib = dev(z, y, x, 1 - k)
        self.s = [cp(17 + n, allz(p), sib, 16 + n) for n, p in enumerate(((y, x), p2, p3, d4))]

    def early(self):
        self.a2[0].start(); self.a3[0].start()

    def early_on(self):
        self.a2[0].wait_recv()
        self.b3[0].start()

    def stage(self, n):
        if n == 0:
            for c in self.direct: c.start()
        elif n == 1:
            if self.hops:
                @pl.when(self.mid)
                def _():
                    for c in self.passed:
                        c.wait_recv()
                        c.start()
        elif n == 2:
            if self.hops:
                @pl.when(self.mid)
                def _():
                    self.near.wait_recv()
                @pl.when(jnp.logical_not(self.mid))
                def _():
                    for c in self.three: c.wait_recv()
            else:
                for c in self.three: c.wait_recv()
            for c in self.a2[1:] + self.a3[1:]: c.start()
            self.s[0].start()
        elif n == 3:
            for c in self.a2[1:]: c.wait_recv()
            for c in self.b3[1:]: c.start()
            self.s[1].start()
        elif n == 4:
            for c in self.a3: c.wait_recv()
            self.s[2].start()
        elif n == 5:
            for c in self.b3: c.wait_recv()
            self.s[3].start()
        elif n == 6:
            for c in self.s: c.wait_recv()

    def sent(self):
        for c in self.direct + self.a2 + self.a3 + self.b3 + self.s: c.wait_send()
        if self.hops:
            @pl.when(self.mid)
            def _():
                for c in self.passed: c.wait_send()


class Home:
    def __init__(self, buf, cross, sel, out_straight, out_crossed, length, sems, pos):
        self.__dict__.update(locals())
        z, y, x, k = pos
        self.esend, self.erecv, self.send, self.h0, self.hs = sems
        self.swap = [remote(buf.at[self.crossed(n)], cross.at[n], self.esend.at[n], self.erecv.at[n], dev(z, 1 - y, x, 1 - k))
                     for n in range(2)] if cross is not None else []
        self.sent = []

    def crossed(self, n):
        z, y, x, k = self.pos
        return lax.rem(1 - y + k, 2) + 2 * n

    def go(self, ref, i, out, sem, n):
        z, y, x, k = self.pos
        slot = lax.rem(z, 2)
        dst = out(slot)
        me = (i == z) & (z // 2 == k)
        cp = remote(ref, dst, self.send.at[n], sem.at[slot], dev(i, y, x, z // 2))
        @pl.when(me)
        def _():
            pltpu.make_async_copy(ref, dst, sem.at[slot]).start()
        @pl.when(jnp.logical_not(me))
        def _():
            cp.start()
        self.sent.append((cp, jnp.logical_not(me)))

    def first(self):
        for c in self.swap: c.start()

    def straight(self):
        z, y, x, k = self.pos
        for n in range(2):
            i = lax.rem(y + k, 2) + 2 * n
            self.go(self.buf.at[i], i, self.out_straight, self.h0, n)

    def second(self):
        for n in range(2):
            self.swap[n].wait_recv()
            i = self.crossed(n)
            far = jnp.broadcast_to(self.length, (128, 768)) > 512.0
            self.sel[n] = jnp.where(far, self.cross[n].astype(F32), self.buf[i].astype(F32)).astype(BF)
            self.go(self.sel.at[n], i, self.out_crossed, self.hs, 2 + n)

    def done(self):
        z, y, x, k = self.pos
        for g in range(2):
            for out, sem in ((self.out_straight, self.h0), (self.out_crossed, self.hs)):
                if out is not None:
                    remote(out(g), out(g), self.send.at[0], sem.at[g], dev(z, y, x, 1 - k)).wait_recv()
        for c in self.swap: c.wait_send()
        for cp, cond in self.sent:
            @pl.when(cond)
            def _():
                cp.wait_send()


class Scatter:
    STAGES = 7

    def __init__(self, mine, theirs, RA, RB, RC, RZ, put, finish, send, recv, pos, load=None, both=False, begun=False):
        self.mine, self.RA, self.RB, self.RC, self.RZ, self.put, self.finish, self.pos, self.load = mine, RA, RB, RC, RZ, put, finish, pos, load
        self.begun = begun
        z, y, x, k = pos
        self.own = (y, x)
        turn = (k == 0) | both
        self.p2 = jnp.where(turn, 1 - y, y), jnp.where(turn, x, 1 - x)
        self.p3 = jnp.where(turn, y, 1 - y), jnp.where(turn, 1 - x, x)
        self.d4 = 1 - y, 1 - x
        blk = lambda yx: mine(slice(None), yx[0], yx[1])
        n3, n2 = dev(z, *self.p3, k), dev(z, *self.p2, k)
        if not begun:
            self.pre = [remote(a, b, send.at[8 * n], recv.at[8 * n], dev(z, y, x, 1 - k)) for n, (a, b) in enumerate(theirs)]
            self.b1 = remote(blk(self.d4), RB.at[1], send.at[1], recv.at[1], n3)
            self.b0 = remote(blk(self.p3), RB.at[0], send.at[2], recv.at[2], n3)
        if RC is None: return
        self.c = remote(blk(self.p2), RC, send.at[3], recv.at[3], n2)
        self.mid = (z == 1) | (z == 2)
        end, near = jnp.where(z < 2, 0, 3), jnp.where(z < 2, 1, 2)
        self.far = (3 - near, 3 - end)
        zdev = lambda zz: dev(zz, y, x, k)
        def zcp(n, block, slot, to):
            return remote(mine(block, y, x), RZ.at[slot], send.at[4 + n], recv.at[4 + slot], zdev(to))
        self.up = [zcp(0, near, 0, near), zcp(1, self.far[0], 2, near), zcp(2, self.far[1], 3, near)]
        self.down = zcp(0, end, 0, end)
        self.on = [zcp(1, self.far[0], 1, self.far[0]), zcp(2, self.far[1], 1, self.far[1])]
        self.sends = [self.c] if begun else self.pre + [self.b1, self.b0, self.c]

    def add(self, yx, other):
        @pl.loop(0, 4)
        def _(i):
            ref = self.mine(i, yx[0], yx[1])
            ref[...] = (ref[...].astype(F32) + other[i].astype(F32)).astype(BF)

    def first(self, yx):
        for rows_of, part in self.RA:
            @pl.loop(0, 4)
            def _(i):
                ref = rows_of(self.mine(i, yx[0], yx[1]))
                ref[...] = (ref[...].astype(F32) + part.at[:, yx[0], yx[1]][i].astype(F32)).astype(BF)

    def stage(self, n):
        z, y, x, k = self.pos
        if n == 0:
            for c in self.load or (): c.start()
            for c in self.pre: c.start()
        elif n == 1:
            for c in self.pre: c.wait_recv()
            for c in self.load or (): c.wait()
            self.first(self.d4)
            self.b1.start()
            self.first(self.p3)
            self.b0.start()
            self.first(self.p2)
            self.first(self.own)
        elif n == 2:
            if self.begun:
                for c in self.load: c.wait()
            else:
                self.b1.wait_recv()
            self.add(self.p2, self.RB.at[1])
            self.c.start()
            if not self.begun: self.b0.wait_recv()
            self.add(self.own, self.RB.at[0])
        elif n == 3:
            self.c.wait_recv()
            self.add(self.own, self.RC)
            @pl.when(self.mid)
            def _():
                self.down.start()
            @pl.when(jnp.logical_not(self.mid))
            def _():
                for c in self.up: c.start()
        elif n == 4:
            @pl.when(self.mid)
            def _():
                for i, c in enumerate(self.on):
                    self.up[1 + i].wait_recv()
                    ref = self.mine(self.far[i], y, x)
                    ref[...] = (ref[...].astype(F32) + self.RZ[2 + i].astype(F32)).astype(BF)
                    c.start()
        elif n == 5:
            self.up[0].wait_recv()
            self.on[0].wait_recv()
            self.put(self.mine(z, y, x)[...].astype(F32) + self.RZ[0].astype(F32) + self.RZ[1].astype(F32))
        elif n == 6:
            self.finish()
            for c in self.sends: c.wait_send()
            @pl.when(self.mid)
            def _():
                for c in [self.down] + self.on: c.wait_send()
            @pl.when(jnp.logical_not(self.mid))
            def _():
                for c in self.up: c.wait_send()

EPS = 1e-5
NT = (((1,), (1,)), ((), ()))


def nt(a, b):
    return lax.dot_general(a, b, NT, preferred_element_type=F32)


def nn(a, b):
    return jnp.dot(a, b, preferred_element_type=F32)


def rope_tables():
    freq = np.exp(-math.log(10000.0) * (2.0 * np.arange(32, dtype=np.float32) / 64)).astype(np.float32)
    ang = np.arange(1024, dtype=np.float32)[:, None] * freq[None, :]
    c, s = np.cos(ang.astype(np.float64)), np.sin(ang.astype(np.float64))
    return (np.concatenate([c, c, c, c], 1).astype(np.float32), np.concatenate([-s, s, -s, s], 1).astype(np.float32))


def swap(u):
    low = lax.broadcasted_iota(jnp.int32, u.shape, 1) % 64 < 32
    return jnp.where(low, pltpu.roll(u, 96, 1), pltpu.roll(u, 32, 1))


def norm(v):
    mean = jnp.mean(v, axis=-1, keepdims=True)
    cen = v - mean
    inv = lax.rsqrt(jnp.mean(cen * cen, axis=-1, keepdims=True) + EPS)
    return cen * inv, inv


def norm_grad(e, n, inv, gain):
    g = e * gain
    return inv * (g - jnp.mean(g, axis=-1, keepdims=True) - n * jnp.mean(g * n, axis=-1, keepdims=True))


def own_block(i, k):
    return 2 * i + lax.rem(i + k, 2)


def rows(i, n=128):
    return pl.ds(pl.multiple_of(i * n, n), n)


def spread(p):
    low = lax.broadcasted_iota(jnp.int32, p.shape, 1) < 64
    zero = jnp.zeros_like(p)
    return jnp.concatenate([jnp.where(low, p, zero), jnp.where(low, zero, p)], axis=0)


def pick(o):
    low = lax.broadcasted_iota(jnp.int32, (128, 128), 0) < 64
    return jnp.where(low, o[:, :128], o[:, 128:]).T


def fill_bias(bias, is_long, k):
    at = 0
    for i in range(4):
        kk = 256 * (i + 1)
        key = lax.broadcasted_iota(jnp.int32, (kk, 256), 0)
        q = own_block(i, k) * 128 + lax.broadcasted_iota(jnp.int32, (kk, 256), 1) % 128
        first = jnp.where(is_long, 0, q - q % 256)
        bias[at:at + kk, :] = jnp.where((key <= q) & (key >= first), 0.0, -1e30)
        at += kk


def attn_fwd(flag, XM, XA, wqkv, wout, gain, shift, bqkv, bout, COS, SIN,
             acts, Q, K, V, att, lse, middle, bias, VT):
    z, y, x, k = where_am_i()
    is_long = flag[0] != 0
    fill_bias(bias, is_long, k)
    for j in range(8):
        alt = jnp.logical_and(jnp.logical_not(is_long), lax.rem(jnp.int32(j), 2) != y)
        blk = jnp.where(alt, XA[j // 2], XM[j]).astype(F32)
        n, _ = norm(blk)
        acts[j * 128:(j + 1) * 128, :] = (n * gain[...] + shift[...]).astype(BF)

    def tables(j):
        off = jnp.where(is_long, j, lax.rem(j, 2))
        return COS[rows(off), :], SIN[rows(off), :]

    @pl.loop(0, 8)
    def _(j):
        a = acts[rows(j), :]
        c, s = tables(j)
        for t in range(6):
            u = nn(a, wqkv[:, 768 + t * 128:896 + t * 128]) + bqkv[:, 768 + t * 128:896 + t * 128]
            K[rows(j), t * 128:(t + 1) * 128] = (u * c + swap(u) * s).astype(BF)
        V[rows(j), :] = (nn(a, wqkv[:, 1536:]) + bqkv[:, 1536:]).astype(BF)

    @pl.loop(0, 4)
    def _(i):
        j = own_block(i, k)
        a = acts[rows(j), :]
        c, s = tables(j)
        for t in range(6):
            u = nn(a, wqkv[:, t * 128:(t + 1) * 128]) + bqkv[:, t * 128:(t + 1) * 128]
            Q[rows(i), t * 128:(t + 1) * 128] = (u * c + swap(u) * s).astype(BF) * jnp.asarray(0.125, BF)

    @pl.loop(0, 6)
    def _(h):
        lanes = rows(h)
        VT[...] = V[:, lanes].T
        at = 0
        for i in range(4):
            kk = 256 * (i + 1)
            qb = spread(Q[i * 128:(i + 1) * 128, lanes])
            st = nt(K[0:kk, lanes], qb) + bias[at:at + kk, :]
            top = jnp.max(st, axis=0, keepdims=True)
            p = jnp.exp(st - top)
            den = jnp.sum(p, axis=0, keepdims=True)
            o = nn(VT[:, 0:kk], p.astype(BF)) * (1.0 / den)
            att[i * 128:(i + 1) * 128, lanes] = pick(o)
            lse[h, i:i + 1, :] = top + jnp.log(den)
            at += kk

    @pl.loop(0, 4)
    def _(i):
        j = own_block(i, k)
        alt = jnp.logical_and(jnp.logical_not(is_long), lax.rem(j, 2) != y)
        xb = jnp.where(alt, XA[i], XM[j]).astype(F32)
        middle[rows(i), :] = xb + (nn(att[rows(i), :].astype(BF), wout[...]) + bout[...])


def mlp(CH, flag, mix, middle, CM, CA, wup, wdown, gain, shift, bup, bdown,
        block, gmid, gup, gdown, g_gain, g_shift, g_bup, g_bdown, mixsum, acts2, actsT, dg, ga, cf):
    z, y, x, k = where_am_i()
    is_long = flag[0] != 0
    m5 = mix[5]
    for i in range(4):
        r = slice(i * 128, (i + 1) * 128)
        mid = middle[r, :]
        n, _ = norm(mid)
        acts2[r, :] = (n * gain[...] + shift[...]).astype(BF)
        j = own_block(jnp.int32(i), k)
        alt = jnp.logical_and(jnp.logical_not(is_long), lax.rem(j, 2) != y)
        c = jnp.where(alt, CA[i], CM[j]).astype(F32)
        cf[r, :] = c
        dg[r, :] = (m5 * c).astype(BF)
        block[r, :] = mid + bdown[...]
        ga[r, :] = jnp.zeros_like(mid)
        actsT[:, r] = acts2[r, :].T
    g_bdown[...] = jnp.sum(dg[...].astype(F32), axis=0, keepdims=True)

    @pl.loop(0, wup.shape[1] // CH)
    def _(f):
        cols = rows(f, CH)
        up = nn(acts2[...], wup[:, cols]) + bup[:, cols]
        half_erf = 0.5 * lax.erf(up * (2.0 ** -0.5)) + 0.5
        slope = half_erf + up * (jnp.exp(up * up * -0.5) * (1.0 / math.sqrt(2 * math.pi)))
        act = (up * half_erf).astype(BF)
        block[...] += nn(act, wdown[cols, :])
        upg = (nt(dg[...], wdown[cols, :]) * slope).astype(BF)
        g_bup[:, cols] = jnp.sum(upg.astype(F32), axis=0, keepdims=True)
        gdown[cols, :] = nn(act.T, dg[...]).astype(BF)
        gup[:, cols] = nn(actsT[...], upg).astype(BF)
        ga[...] += nt(upg, wup[:, cols])

    total = jnp.zeros((1, 768), F32)
    gg = jnp.zeros((1, 768), F32)
    gs = jnp.zeros((1, 768), F32)
    for i in range(4):
        r = slice(i * 128, (i + 1) * 128)
        n, inv = norm(middle[r, :])
        e = ga[r, :]
        gg += jnp.sum(e * n, axis=0, keepdims=True)
        gs += jnp.sum(e, axis=0, keepdims=True)
        gmid[r, :] = m5 * cf[r, :] + norm_grad(e, n, inv, gain[...])
        total += jnp.sum(cf[r, :] * block[r, :], axis=0, keepdims=True)
    g_gain[...] = gg
    g_shift[...] = gs
    mixsum[...] = total


def attn_bwd(flag, gmid, acts, Q, K, V, att, lse, wqkv, wout, COS, SIN,
             e, gqkv, gout, g_bqkv, g_bout, bias, KT, da, dQ, dK, dV, agrad, actsT, actsqT, KG, VG):
    z, y, x, k = where_am_i()
    is_long = flag[0] != 0
    fill_bias(bias, is_long, k)
    agrad[...] = gmid[...].astype(BF)
    g_bout[...] = jnp.sum(agrad[...].astype(F32), axis=0, keepdims=True)

    @pl.loop(0, 4)
    def _(i):
        da[rows(i), :] = nt(agrad[rows(i), :], wout[...]).astype(BF)

    for t in range(6):
        aT = att[:, t * 128:(t + 1) * 128].T.astype(BF)
        gout[t * 128:(t + 1) * 128, :] = nn(aT, agrad[...]).astype(BF)
    dK[...] = jnp.zeros_like(dK)
    dV[...] = jnp.zeros_like(dV)

    @pl.loop(0, 6)
    def _(h):
        lanes = rows(h)
        KT[...] = K[:, lanes].T
        at = 0
        for i in range(4):
            kk = 256 * (i + 1)
            r = slice(i * 128, (i + 1) * 128)
            d = da[r, lanes]
            qb, db = spread(Q[r, lanes]), spread(d)
            prod = (d.astype(F32) * att[r, lanes]).T
            delta = jnp.concatenate([jnp.sum(prod[:64], axis=0, keepdims=True), jnp.sum(prod[64:], axis=0, keepdims=True)], axis=1)
            st = nt(K[0:kk, lanes], qb) + bias[at:at + kk, :]
            p = jnp.exp(st - lse[h, i:i + 1, :])
            ds = (p * (nt(V[0:kk, lanes], db) - delta)).astype(BF)
            dV[0:kk, lanes] += nn(p.astype(BF), db)
            dK[0:kk, lanes] += nn(ds, qb)
            dQ[r, lanes] = pick(nn(KT[:, 0:kk], ds)) * 0.125
            at += kk

    def tables(j):
        off = jnp.where(is_long, j, lax.rem(j, 2))
        return COS[rows(off), :], SIN[rows(off), :]

    for j in range(8):
        actsT[:, j * 128:(j + 1) * 128] = acts[j * 128:(j + 1) * 128, :].T
    for i in range(4):
        j = own_block(jnp.int32(i), k)
        actsqT[:, i * 128:(i + 1) * 128] = acts[rows(j), :].T
        c, s = tables(j)
        for t in range(6):
            u = dQ[i * 128:(i + 1) * 128, t * 128:(t + 1) * 128]
            da[i * 128:(i + 1) * 128, t * 128:(t + 1) * 128] = (u * c - swap(u) * s).astype(BF)

    @pl.loop(0, 8)
    def _(j):
        c, s = tables(j)
        for t in range(6):
            u = dK[rows(j), t * 128:(t + 1) * 128]
            KG[rows(j), t * 128:(t + 1) * 128] = (u * c - swap(u) * s).astype(BF)
        VG[rows(j), :] = dV[rows(j), :].astype(BF)
        e[rows(j), :] = nt(KG[rows(j), :], wqkv[:, 768:1536]) + nt(VG[rows(j), :], wqkv[:, 1536:])

    @pl.loop(0, 4)
    def _(i):
        j = own_block(i, k)
        e[rows(j), :] += nt(da[rows(i), :], wqkv[:, :768])

    g_bqkv[:, :768] = jnp.sum(da[...].astype(F32), axis=0, keepdims=True)
    g_bqkv[:, 768:1536] = jnp.sum(KG[...].astype(F32), axis=0, keepdims=True)
    g_bqkv[:, 1536:] = jnp.sum(VG[...].astype(F32), axis=0, keepdims=True)

    @pl.loop(0, 6)
    def _(t):
        gqkv[rows(t), :768] = nn(actsqT[rows(t), :], da[...]).astype(BF)
        gqkv[rows(t), 768:1536] = nn(actsT[rows(t), :], KG[...]).astype(BF)
        gqkv[rows(t), 1536:] = nn(actsT[rows(t), :], VG[...]).astype(BF)


sd = jax.ShapeDtypeStruct
VM = pltpu.VMEM
vs = pl.BlockSpec(memory_space=pltpu.VMEM)
ss = pl.BlockSpec(memory_space=pltpu.SMEM)
CP = pltpu.CompilerParams(vmem_limit_bytes=60 * 2**20)


def attn_fwd_call(flag, *ins):
    return pl.pallas_call(attn_fwd,
        out_shape=[sd((1024, 768), BF), sd((512, 768), BF), sd((1024, 768), BF), sd((1024, 768), BF),
                   sd((512, 768), F32), sd((6, 4, 256), F32), sd((512, 768), F32)],
        in_specs=[ss] + [vs] * len(ins), out_specs=[vs] * 7,
        scratch_shapes=[VM((2560, 256), F32), VM((128, 1024), BF)],
        compiler_params=CP)(flag, *ins)


def mlp_call(flag, mix, *ins):
    r = sd((1, 768), F32)
    return pl.pallas_call(functools.partial(mlp, 512),
        out_shape=[sd((512, 768), F32), sd((512, 768), F32), sd((768, 3072), BF), sd((3072, 768), BF), r, r, sd((1, 3072), F32), r, r],
        in_specs=[ss, ss] + [vs] * len(ins), out_specs=[vs] * 9,
        scratch_shapes=[VM((512, 768), BF), VM((768, 512), BF), VM((512, 768), BF), VM((512, 768), F32), VM((512, 768), F32)],
        compiler_params=CP)(flag, mix, *ins)


def attn_bwd_call(flag, *ins):
    return pl.pallas_call(attn_bwd,
        out_shape=[sd((1024, 768), F32), sd((768, 2304), BF), sd((768, 768), BF), sd((1, 2304), F32), sd((1, 768), F32)],
        in_specs=[ss] + [vs] * len(ins), out_specs=[vs] * 5,
        scratch_shapes=[VM((2560, 256), F32), VM((128, 1024), BF), VM((512, 768), BF), VM((512, 768), F32), VM((1024, 768), F32),
                        VM((1024, 768), F32), VM((512, 768), BF), VM((768, 1024), BF), VM((768, 512), BF), VM((1024, 768), BF), VM((1024, 768), BF)],
        compiler_params=CP)(flag, *ins)


VROWS = (24, 24, 72, 24, 24, 24, 96, 24)


def widen(vecs, row, n):
    v = vecs[:, row, :].astype(BF)
    wide = 32 * n
    j = lax.broadcasted_iota(jnp.int32, (128, wide), 1)
    i = lax.broadcasted_iota(jnp.int32, (128, wide), 0)
    q = jnp.floor((j.astype(F32) + 0.5) * (1.0 / n)).astype(jnp.int32)
    hot = jnp.where(j - q * n == i, 1.0, 0.0).astype(BF)
    full = nn(v, hot)
    d = lax.broadcasted_iota(jnp.int32, (32, wide), 0)
    return jnp.sum(jnp.where(q[:32] == d, full, 0.0), axis=0, keepdims=True)


def lane(tile, row, at):
    r = lax.broadcasted_iota(jnp.int32, tile.shape, 0)
    c = lax.broadcasted_iota(jnp.int32, tile.shape, 1)
    v = jnp.sum(jnp.where((r == row) & (c == at), tile, 0.0), axis=1, keepdims=True)
    return jnp.sum(v, axis=0, keepdims=True)


def longer(length, shape):
    return jnp.broadcast_to(length, shape) > 512.0


def bias_rows(bias, length, k):
    at = 0
    for i in range(4):
        kk = 256 * (i + 1)
        key = lax.broadcasted_iota(jnp.int32, (kk, 128), 0)
        q = own_block(i, k) * 128 + lax.broadcasted_iota(jnp.int32, (kk, 128), 1)
        first = jnp.where(longer(length, (kk, 128)), 0, q - q % 256)
        bias[at:at + kk, :] = jnp.where((key <= q) & (key >= first), 0.0, -1e30)
        at += kk


def both_heads(bias, at, kk):
    b = bias[at:at + kk, :]
    return jnp.concatenate([b, b], axis=1)


def table_rows(COS, SIN, length, j):
    far = longer(length, (128, 128))
    near = lax.rem(j, 2)
    return (jnp.where(far, COS[rows(j), :], COS[rows(near), :]), jnp.where(far, SIN[rows(j), :], SIN[rows(near), :]))


def matrix(W, cols):
    w = W[:, :, :, :, cols]
    return w.reshape(768, w.shape[-1])


def forward_kernel(cols, qkv, out, up, down, xin, cin, COS, SIN, hist, v0, v1, v2, v3, v4, v5, v6, v7, mix, lens,
                   oX, oacts, oQ, oK, oV, oatt, olse, oWQ, oWO, ogmid, ogup, opd, orb, obl, ohome, opre, ogain, vgrad,
                   f_own, f_sib, block_w, WQ, WO, WU, WD, VEC, X, C, NB, SB,
                   Q, K, V, att, lse, middle, bias, VT, act, slope, block, ga, acts2, actsT, dg, gup, GD, a1T, bl,
                   vq, vg, vu, vec, mixrow,
                   psend, precv, lsem, gsend, grecv, asend, arecv, nsend, nrecv, fsend, frecv, xsem, csem, hsem, osem, vsend, vrecv, dsend, drecv, free, *home_sems):
    pos = z, y, x, k = where_am_i()
    sib = dev(z, y, x, 1 - k)
    greet(z, y, x, k)
    s = 2 * z + y
    own_s = lax.rem(y + z, 2)
    def neighbour(a, src):
        cps = []
        for i in range(2):
            hi = src.at[i, pl.ds(pl.multiple_of((1 - y) * 128, 128), 128)]
            cp = remote(hi, NB.at[a, i], nsend.at[a, i], nrecv.at[a, i], dev(z, 1 - y, x, k))
            cp.start()
            cps.append(cp)
        return cps

    tokens = []
    def along_z(a, i, n, ref, dst, core):
        g = 2 * k + i
        me = (g == z) & (core == k)
        cp = remote(ref, dst, asend.at[a, i, n], arecv.at[a, z], dev(g, y, x, core))
        @pl.when(me)
        def _():
            pltpu.make_async_copy(ref, dst, arecv.at[a, z]).start()
        @pl.when(jnp.logical_not(me))
        def _():
            cp.start()
        tokens.append((cp, jnp.logical_not(me)))

    def straight(a, src, dst):
        for i in range(2):
            along_z(a, i, 0, src.at[i, pl.ds(pl.multiple_of(y * 128, 128), 128)], dst(s), own_s)

    def crossed(a, src, dst, cps):
        for i in range(2):
            cps[i].wait_recv()
            mine = src[i, pl.ds(pl.multiple_of((1 - y) * 128, 128), 128), :]
            far = jnp.broadcast_to(lens[i].astype(F32), (128, 768)) > 512.0
            SB[a, i] = jnp.where(far, NB[a, i].astype(F32), mine.astype(F32)).astype(BF)
            along_z(a, i, 1, SB.at[a, i], dst(s + 1 - 2 * y), 1 - own_s)

    def arrived(a, dst, i):
        remote(dst, dst, asend.at[a, 0, 0], arecv.at[a, i], sib).wait_recv()

    def acts(j, low):
        return (acts2 if low else dg).at[rows(j if low else j - 4)]
    slots = [act.at[:, pl.ds(768 * n, 768)] for n in range(4)] + [dg]
    to_x = lambda j: X.at[j]
    to_c = lambda j: C.at[j // 2]
    vec[...] = jnp.zeros_like(vec)
    for r, v in enumerate((v0, v1, v2, v3, v4, v5, v6, v7)):
        vec[r:r + 1, 0:v.shape[1]] = v[...].astype(F32)
    place = lax.broadcasted_iota(jnp.int32, (1, 128), 1)
    first = vec[0:1, :]
    for i in range(2):
        first = jnp.where(place == 64 + i, lens[i].astype(F32), first)
    vec[0:1, :] = first
    at, offs = 0, []
    for n in cols:
        offs.append((at, n // 2))
        at += n // 2
    pres = []
    for i, ((at, half), ref) in enumerate(zip(offs, (qkv, out, up))):
        f_own[0, :, at:at + half] = ref[:, :half].astype(F32)
        f_own[1, :, at:at + half] = ref[:, half:].astype(F32)
        pre = remote(f_own.at[1 - k, :, pl.ds(at, half)], f_sib.at[:, pl.ds(at, half)], psend.at[i], precv.at[i], sib)
        pre.start()
        pres.append(pre)
    lvec = pltpu.make_async_copy(vec, VEC.at[z, y, x, k], lsem.at[4])
    ldown = pltpu.make_async_copy(down, WD.at[z, y, x, k], lsem.at[3])
    lvec.start(); ldown.start()

    def colpart(W, half):
        return lambda zz, yy, xx, kk: W.at[zz, yy, xx, :, pl.ds(pl.multiple_of(kk * half, 128), half)]
    def rowpart(W):
        return lambda zz, yy, xx, kk: W.at[zz, yy, xx, kk]
    gq, go, gu, gd = G = [Gather(p, gsend.at[i], grecv.at[i], pos, i in (1, 2), i > 1) for i, p in enumerate(
        [colpart(WQ, offs[0][1]), colpart(WO, offs[1][1]), colpart(WU, offs[2][1]), rowpart(WD)])]
    lvec.wait()
    vs_out = [remote(VEC.at[z, y, x, k], VEC.at[z, y, x, k], vsend.at[n], vrecv.at[15 - n], dev(*chip, k)) for n, chip in chips_of(z, y, x)]
    vs_in = [remote(VEC.at[chip[0], chip[1], chip[2], k], VEC.at[chip[0], chip[1], chip[2], k], vsend.at[n], vrecv.at[n - 1], dev(*chip, k)) for n, chip in chips_of(z, y, x)]
    v_sib = remote(VEC.at[:, :, :, k], VEC.at[:, :, :, k], vsend.at[0], vrecv.at[15], sib)
    for c in vs_out: c.start()

    def own_rows(i, W):
        at, half = offs[i]
        pres[i].wait_recv()
        mine = f_own[k, :, at:at + half]
        theirs = f_sib[:, at:at + half]
        block_w[:, at:at + half] = jnp.concatenate([jnp.where(k == 0, mine, theirs), jnp.where(k == 0, theirs, mine)], axis=0).astype(BF)
        c = pltpu.make_async_copy(block_w.at[:, pl.ds(at, half)], W.at[z, y, x, :, pl.ds(pl.multiple_of(k * half, 128), half)], lsem.at[i])
        c.start()
        return c

    own_rows(0, WQ).wait()
    gq.stage(0)
    gq.early()
    nx = neighbour(0, xin)
    lo, lu = own_rows(1, WO), own_rows(2, WU)
    hin = [[pltpu.make_async_copy(hist.at[j, g], slots[j].at[pl.ds(256 * g, 256)], hsem.at[j, g]) for g in range(2)] for j in range(5)]
    for c in hin: c[0].start(); c[1].start()
    block[...] = jnp.zeros_like(block)
    mixrow[...] = jnp.zeros_like(mixrow)

    def mix_in(js):
        for j in js:
            for g in range(2):
                hin[j][g].wait()
                for t in range(2):
                    q = slice(256 * g + 128 * t, 256 * g + 128 * t + 128)
                    h = slots[j][q, :].astype(F32)
                    c = cin[g, 128 * t:128 * t + 128, :].astype(F32)
                    mixrow[j:j + 1, :] += jnp.sum(h * c, axis=0, keepdims=True)
                    block[q, :] += mix[j] * h
    lo.wait(); lu.wait(); ldown.wait()
    go.early(); gu.early()
    mix_in((0, 1))
    for c in vs_in: c.wait_recv()
    v_sib.start()
    mix_in((2, 3))
    gq.early_on()
    gq.stage(2)
    gu.stage(0)
    go.stage(0)
    straight(0, xin, to_x)
    crossed(0, xin, to_x, nx)
    gd.early()
    go.early_on(); gu.early_on()
    mix_in((4,))
    opres = [pltpu.make_async_copy(block.at[pl.ds(256 * g, 256)], opre.at[g], osem.at[g]) for g in range(2)]
    for c in opres: c.start()
    v_sib.wait_recv()
    tiles = VEC[...].reshape(32, 8, 128)
    length = lane(VEC[0, 0, x, z // 2], 0, 64 + lax.rem(z, 2))
    vq[...] = widen(tiles, 2, 72)
    gq.stage(3)
    for n, r in enumerate((0, 1, 3, 4, 5, 7)):
        vg[n:n + 1, :] = widen(tiles, r, 24)
    a_gain, a_shift, bout, m_gain, m_shift, bdown = (vg[n:n + 1, :] for n in range(6))
    gu.stage(1)
    gd.early_on()
    gq.stage(4)
    vu[...] = widen(tiles, 6, 96)
    bias_rows(bias, length, k)
    fw = []
    def forward_x(i):
        j = own_block(jnp.int32(i), k)
        arrived(0, X.at[j], i)
        cp = remote(X.at[j], X.at[j], fsend.at[i], frecv.at[i], sib)
        cp.start(); fw.append(cp)
    def norm_block(i, core):
        j = own_block(jnp.int32(i), core)
        n, _ = norm(X[j].astype(F32))
        a = (n * a_gain + a_shift).astype(BF)
        acts(j, i < 2)[...] = a
        a1T[:, rows(j)] = a.T
    gq.stage(5)
    gu.stage(2)
    go.stage(2)
    nc = neighbour(1, cin)
    for i in range(4):
        forward_x(i)
        norm_block(i, k)
    gd.stage(0)
    gq.stage(6)
    for i in range(4):
        fw[i].wait_recv()
        norm_block(i, 1 - k)
    exports, turn = [], iter(range(16))
    def export(ref, dst):
        c = pltpu.make_async_copy(ref, dst, xsem.at[next(turn)])
        c.start(); exports.append(c)

    def keys(low, j):
        a = acts(j, low)[...]
        c, sn = table_rows(COS, SIN, length, j)
        for t in range(3):
            u2 = nn(a, matrix(WQ, slice(768 + t * 256, 1024 + t * 256))) + vq[:, 768 + t * 256:1024 + t * 256]
            for h in range(2):
                u = u2[:, h * 128:(h + 1) * 128]
                K[rows(j), t * 256 + h * 128:t * 256 + (h + 1) * 128] = (u * c + swap(u) * sn).astype(BF)
        V[rows(j), :] = (nn(a, matrix(WQ, slice(1536, 2304))) + vq[:, 1536:]).astype(BF)

    pl.loop(0, 4)(functools.partial(keys, True))
    gu.stage(3)
    go.stage(3)
    gd.stage(1)
    pl.loop(4, 8)(functools.partial(keys, False))
    def ask(low, i):
        j = own_block(i, k)
        a = acts(j, low)[...]
        c, sn = table_rows(COS, SIN, length, j)
        for t in range(3):
            u2 = nn(a, matrix(WQ, slice(t * 256, 256 + t * 256))) + vq[:, t * 256:256 + t * 256]
            for h in range(2):
                u = u2[:, h * 128:(h + 1) * 128]
                Q[rows(i), t * 256 + h * 128:t * 256 + (h + 1) * 128] = (u * c + swap(u) * sn).astype(BF) * jnp.asarray(0.125, BF)
    pl.loop(0, 2)(functools.partial(ask, True))
    pl.loop(2, 4)(functools.partial(ask, False))
    straight(1, cin, to_c)
    go.stage(4)
    gu.stage(4)
    for i in range(4):
        j = own_block(jnp.int32(i), k)
        export(X.at[j], oX.at[i])
    export(a1T, oacts); export(Q, oQ); export(K, oK); export(V, oV)
    export(WQ, oWQ)
    free_wq = exports.pop()

    def heads(h):
        lanes = rows(h)
        VT[...] = V[:, lanes].T
        at = 0
        for i in range(4):
            kk = 256 * (i + 1)
            qb = spread(Q[i * 128:(i + 1) * 128, lanes])
            st = nt(K[0:kk, lanes], qb) + both_heads(bias, at, kk)
            top = jnp.max(st, axis=0, keepdims=True)
            p = jnp.exp(st - top)
            den = jnp.sum(p, axis=0, keepdims=True)
            o = nn(VT[:, 0:kk], p.astype(BF)) * (1.0 / den)
            att[i * 128:(i + 1) * 128, lanes] = pick(o)
            lse[h, i:i + 1, :] = top + jnp.log(den)
            at += kk

    pl.loop(0, 1)(heads)
    crossed(1, cin, to_c, nc)
    pl.loop(1, 2)(heads)
    gd.stage(2)
    go.stage(5)
    pl.loop(2, 4)(heads)
    gu.stage(5)
    pl.loop(4, 6)(heads)
    go.stage(6)
    export(WO, oWO)
    gd.stage(3)
    export(att, oatt); export(lse, olse)

    for c in opres: c.wait()

    @pl.loop(0, 4)
    def _(i):
        j = own_block(i, k)
        middle[rows(i), :] = X[j].astype(F32) + (nn(att[rows(i), :].astype(BF), WO[...].reshape(768, 768)) + bout)
    m5 = mix[5]
    free_wq.wait()
    gq.sent()
    pl.semaphore_signal(free, inc=1, device_id=sib, device_id_type=MESH)
    for i in range(4):
        r = slice(i * 128, (i + 1) * 128)
        mid = middle[r, :]
        n, _ = norm(mid)
        a2 = (n * m_gain + m_shift).astype(BF)
        acts2[r, :] = a2
        actsT[:, r] = a2.T
        block[r, :] = mid + bdown
        ga[r, :] = jnp.zeros_like(mid)
    gu.stage(6)
    vgrad[...] = jnp.zeros_like(vgrad)

    def put_vec(row, v):
        for t in range(v.shape[1] // 128):
            vgrad[row + t:row + t + 1, :] = v[:, t * 128:(t + 1) * 128]

    def hidden(f):
        c = rows(f, 384)
        u = nn(acts2[...], matrix(WU, c)) + vu[:, c]
        half_erf = 0.5 * lax.erf(u * (2.0 ** -0.5)) + 0.5
        slope[:, c] = half_erf + u * (jnp.exp(u * u * -0.5) * (1.0 / math.sqrt(2 * math.pi)))
        act[:, c] = (u * half_erf).astype(BF)
    pl.loop(0, 4)(hidden)
    gd.stage(4)
    pl.loop(4, 8)(hidden)
    for i in range(4):
        arrived(1, C.at[i], i)
        dg[i * 128:(i + 1) * 128, :] = (m5 * C[i].astype(F32)).astype(BF)
    put_vec(72, jnp.sum(dg[...].astype(F32), axis=0, keepdims=True))
    sdn = Scatter(lambda zz, yy, xx: GD.at[zz, yy, xx, k],
                  [(GD.at[:, :, :, 1 - k, pl.ds(48 * n, 48)], WQ.at[:, :, :, :, pl.ds(768 * n, 768)]) for n in range(2)],
                  [(lambda r, n=n: r.at[pl.ds(48 * n, 48)], WQ.at[:, :, :, :, pl.ds(768 * n, 768)]) for n in range(2)],
                  orb, None, None, None, None, dsend, drecv, pos)

    gd.stage(5)

    @pl.loop(0, 4)
    def _(f):
        GD[f] = nn(act[:, rows(f, 768)].T, dg[...]).astype(BF).reshape(2, 2, 2, 96, 768)
    pl.semaphore_wait(free, 1)
    gd.stage(6)
    sdn.stage(0)

    @pl.loop(0, 4)
    def _(f):
        block[...] += nn(act[:, rows(f, 768)], WD[f].reshape(768, 768))

    total = jnp.zeros((1, 768), F32)
    for i in range(4):
        r = slice(i * 128, (i + 1) * 128)
        total += jnp.sum(C[i].astype(F32) * block[r, :], axis=0, keepdims=True)
        bl[i] = block[r, :].astype(BF)
    home = Home(bl, None, None, lambda slot: ohome.at[slot], None, length, home_sems, pos)
    home.straight()
    export(bl, obl)
    sdn.stage(1)
    export(GD.at[:, :, :, k], opd)

    def chunk(f):
        c = rows(f, 768)
        wd = WD[f].reshape(768, 768)
        upg = (nt(dg[...], wd) * slope[:, c]).astype(BF)
        g = jnp.sum(upg.astype(F32), axis=0, keepdims=True)
        for t in range(6):
            vgrad[pl.ds(48 + f * 6 + t, 1), :] = g[:, t * 128:(t + 1) * 128]
        gup[:, c] = nn(actsT[...], upg).astype(BF)
        pltpu.make_async_copy(gup.at[:, c], ogup.at[:, c], csem.at[1, f]).start()
        ga[...] += nt(upg, matrix(WU, c))

    pl.loop(0, 4)(chunk)
    gg = jnp.zeros((1, 768), F32)
    gs = jnp.zeros((1, 768), F32)
    for i in range(4):
        r = slice(i * 128, (i + 1) * 128)
        n, inv = norm(middle[r, :])
        e = ga[r, :]
        cf = C[i].astype(F32)
        gg += jnp.sum(e * n, axis=0, keepdims=True)
        gs += jnp.sum(e, axis=0, keepdims=True)
        ga[r, :] = m5 * cf + norm_grad(e, n, inv, m_gain)
    put_vec(36, gg); put_vec(42, gs)
    ogain[...] = jnp.broadcast_to(a_gain, (8, 768))
    whole = jnp.sum(total, axis=1, keepdims=True)
    row = jnp.where(place == 5, jnp.broadcast_to(whole, (1, 128)), 0.0)
    for j in range(5):
        row = jnp.where(place == j, jnp.broadcast_to(jnp.sum(mixrow[j:j + 1, :], axis=1, keepdims=True), (1, 128)), row)
    vgrad[78:79, :] = row
    vgrad[79:80, :] = jnp.broadcast_to(length, (1, 128))
    export(ga, ogmid)
    for f in range(4):
        c = slice(f * 768, (f + 1) * 768)
        pltpu.make_async_copy(gup.at[:, c], ogup.at[:, c], csem.at[1, f]).wait()
    for c in exports: c.wait()
    sdn.b1.wait_recv(); sdn.b0.wait_recv()
    for c in sdn.pre + [sdn.b1, sdn.b0]: c.wait_send()
    home.done()
    for c in fw + nx + nc: c.wait_send()
    for cp, cond in tokens:
        @pl.when(cond)
        def _():
            cp.wait_send()
    for c in pres: c.wait_send()
    for g in G[1:]: g.sent()
    for c in vs_out + [v_sib]: c.wait_send()


def forward_call(qkv, out, up, down, xin, cin, COS, SIN, hist, vectors, mix, lens):
    cols = (qkv.shape[1], out.shape[1], up.shape[1])
    H = sum(cols) // 2
    any_ = pl.BlockSpec(memory_space=pl.ANY)
    T = lambda n, t=BF: ((n, 768), t)
    shapes = [((4, 128, 768), BF), ((768, 1024), BF), T(512), T(1024), T(1024), T(512, F32), ((6, 4, 256), F32),
              ((4, 2, 2, 48, 2304), BF), ((4, 2, 2, 48, 768), BF), T(512, F32), ((768, 3072), BF), ((4, 2, 2, 96, 768), BF), ((2, 4, 96, 768), BF), ((4, 128, 768), BF),
              ((2, 128, 768), BF), (xin.shape, F32)]
    DS = pltpu.SemaphoreType.DMA
    return pl.pallas_call(functools.partial(forward_kernel, cols),
        out_shape=[sd(*t) for t in shapes] + [sd((8, 768), F32), sd((80, 128), F32)],
        in_specs=[vs] * 8 + [any_] + [vs] * 8 + [ss, ss], out_specs=[any_] * len(shapes) + [vs, vs],
        scratch_shapes=[VM((2, 24, H), F32), VM((24, H), F32), VM((48, H), BF),
                        VM((4, 2, 2, 48, 2304), BF), VM((4, 2, 2, 48, 768), BF), VM((4, 2, 2, 48, 3072), BF), VM((4, 2, 2, 2, 96, 768), BF),
                        VM((4, 2, 2, 2, 8, 128), F32), VM((8, 128, 768), BF), VM((4, 128, 768), BF), VM((2, 2, 128, 768), BF), VM((2, 2, 128, 768), BF),
                        VM((512, 768), BF), VM((1024, 768), BF), VM((1024, 768), BF), VM((512, 768), F32),
                        VM((6, 4, 256), F32), VM((512, 768), F32), VM((2560, 128), F32), VM((128, 1024), BF),
                        VM((512, 3072), BF), VM((512, 3072), F32), VM((512, 768), F32), VM((512, 768), F32), VM((512, 768), BF),
                        VM((768, 512), BF), VM((512, 768), BF), VM((768, 3072), BF), VM((4, 2, 2, 2, 96, 768), BF), VM((768, 1024), BF), VM((4, 128, 768), BF),
                        VM((1, 2304), F32), VM((8, 768), F32), VM((1, 3072), F32), VM((8, 128), F32), VM((8, 768), F32),
                        DS((3,)), DS((3,)), DS((5,)), DS((4, 21)), DS((4, 20)), DS((2, 2, 2)), DS((2, 4)), DS((2, 2)), DS((2, 2)), DS((4,)), DS((4,)),
                        DS((16,)), DS((2, 4)), DS((5, 2)), DS((2,)), DS((16,)), DS((16,)), DS((9,)), DS((9,)), pltpu.SemaphoreType.REGULAR, DS((2,)), DS((2,)), DS((4,)), DS((2,)), DS((2,))],
        compiler_params=pltpu.CompilerParams(collective_id=0, has_side_effects=True, vmem_limit_bytes=63 * 2**20),
    )(qkv, out, up, down, xin, cin, COS, SIN, hist, *[v.reshape(1, -1) for v in vectors], mix, lens)


def backward_kernel(gup, pdown, bdown, bl, gmid, X, actsT, Q, Kin, Vin, att, lse, WQ, WO, gain, COS, SIN, vin,
                    oq, oo, ou, od, vout, ox, ocross,
                    K, V, bias, KT, da, dQ, dK, dV, agrad, actsqT, GO, GQ, PU, PD,
                    AU, BU, CU, ZU, BD, CD, ZD, AO, BO, CO, ZO, AQ, BQ, CQ, ZQ,
                    fin, fsib, finu, fsibu, es, er, gx, cross, sel, cross_b, sel_b, vbuf, vrec,
                    ssem, rsem, ldsem, fsend, frecv, esem_s, esem_r, vsend, vrecv, csem, *home_sems):
    pos = z, y, x, k = where_am_i()
    sib = dev(z, y, x, 1 - k)
    greet(z, y, x, k)
    length = vin[79:80, 0:1]
    ck = pltpu.make_async_copy(Kin, K, csem.at[0])
    cv = pltpu.make_async_copy(Vin, V, csem.at[1])
    ck.start(); cv.start()
    half_of = lambda kk, half: pl.ds(pl.multiple_of(kk * half, 128), half)

    def col_scatter(a, G, half, bufs, n, out, at, width, fi, fs, hbm=None, both=False):
        def put(t):
            fi[n, 0] = t[:24]
            fi[n, 1] = t[24:]
            last.start()
        last = remote(fi.at[n, 1 - k], fs.at[n], fsend.at[a], frecv.at[a], sib)
        def finish():
            last.wait_recv()
            mine, theirs = fi[n, k], fs[n]
            out[:, at:at + half] = jnp.where(k == 0, mine, theirs)
            out[:, at + half:at + 2 * half] = jnp.where(k == 0, theirs, mine)
            last.wait_send()
        if hbm is None:
            mine = lambda zz, yy, xx: G.at[zz, yy, xx, :, half_of(k, half)]
            theirs = G.at[:, :, :, :, half_of(1 - k, half)]
            load = None
        else:
            mine = lambda zz, yy, xx: G.at[zz, yy, xx]
            theirs = hbm.at[:, :, :, :, half_of(1 - k, half)]
            load = [pltpu.make_async_copy(hbm.at[:, :, :, :, half_of(k, half)], G, ldsem.at[a])]
        RA, RB, RC, RZ = bufs
        return Scatter(mine, [(theirs, RA)], [(lambda r: r, RA)], RB, RC, RZ, put, finish, ssem.at[a], rsem.at[a], pos, load, both)

    def put_down(t):
        od[...] = t
    loads = [pltpu.make_async_copy(pdown, PD, ldsem.at[0]), pltpu.make_async_copy(bdown, BD, ldsem.at[2])]
    for c in loads: c.start()
    sdn = Scatter(lambda zz, yy, xx: PD.at[zz, yy, xx], None, None, BD, CD, ZD, put_down, lambda: None,
                  ssem.at[0], rsem.at[0], pos, loads, begun=True)
    sup = col_scatter(1, PU, 1536, (AU, BU, CU, ZU), 0, ou, 0, 3072, finu, fsibu, gup)
    sout = col_scatter(2, GO, 384, (AO, BO, CO, ZO), 0, oo, 0, 768, fin, fsib, both=True)
    sq, sk, sv = (col_scatter(3 + n, GQ.at[n], 384, (AQ.at[n], BQ.at[n], CQ.at[n], ZQ.at[n]), 1 + n, oq, 768 * n, 768, fin, fsib, both=n == 2)
                  for n in range(3))
    sup.stage(0)

    part_of = lambda half: lambda slot: ox.at[slot, pl.ds(pl.multiple_of(half * 128, 128), 128)]
    home = Home(gx, cross, sel, part_of(y), part_of(1 - y), length, home_sems[:5], pos)
    outs = Home(bl, cross_b, sel_b, None, lambda slot: ocross.at[slot], length, home_sems[5:], pos)
    outs.first()
    agrad[...] = gmid[...].astype(BF)
    vbuf[0] = vin[...]

    def put_vec(row, v):
        for t in range(v.shape[1] // 128):
            vbuf[0, row + t:row + t + 1, :] = v[:, t * 128:(t + 1) * 128]
    put_vec(30, jnp.sum(agrad[...].astype(F32), axis=0, keepdims=True))
    wo = lambda: WO[...].reshape(768, 768)

    da[...] = nt(agrad[...], wo()).astype(BF)
    for i in range(4):
        actsqT[:, i * 128:(i + 1) * 128] = actsT[:, rows(own_block(jnp.int32(i), k))]

    sdn.stage(2)

    def out_rows(t):
        aT = att[:, t * 384:(t + 1) * 384].T.astype(BF)
        g = nn(aT, agrad[...]).astype(BF)
        GO[2 * t:2 * t + 2] = g.reshape(2, 2, 2, 48, 768)
    sup.stage(1)
    for t in range(2): out_rows(t)
    sout.stage(0)
    outs.second()
    bias_rows(bias, length, k)
    dK[...] = jnp.zeros_like(dK)
    dV[...] = jnp.zeros_like(dV)
    ck.wait(); cv.wait()

    def heads(h):
        lanes = rows(h)
        KT[...] = K[:, lanes].T
        at = 0
        for i in range(4):
            kk = 256 * (i + 1)
            r = slice(i * 128, (i + 1) * 128)
            d = da[r, lanes]
            qb, db = spread(Q[r, lanes]), spread(d)
            prod = (d.astype(F32) * att[r, lanes]).T
            delta = jnp.concatenate([jnp.sum(prod[:64], axis=0, keepdims=True), jnp.sum(prod[64:], axis=0, keepdims=True)], axis=1)
            st = nt(K[0:kk, lanes], qb) + both_heads(bias, at, kk)
            p = jnp.exp(st - lse[h, i:i + 1, :])
            ds = (p * (nt(V[0:kk, lanes], db) - delta)).astype(BF)
            dV[0:kk, lanes] += nn(p.astype(BF), db)
            dK[0:kk, lanes] += nn(ds, qb)
            dQ[r, lanes] = pick(nn(KT[:, 0:kk], ds)) * 0.125
            at += kk

    pl.loop(0, 2)(heads)
    sout.stage(1)
    pl.loop(2, 4)(heads)
    sdn.stage(3)
    pl.loop(4, 6)(heads)
    V[...] = dV[...].astype(BF)
    put_vec(24, jnp.sum(V[...].astype(F32), axis=0, keepdims=True))

    def weight_rows(n, lhs, g):
        @pl.loop(0, 4)
        def _(t):
            GQ[n, t] = nn(lhs[rows(t, 192), :], g[...]).astype(BF).reshape(2, 2, 48, 768)
    @pl.loop(0, 8)
    def _(j):
        c, s = table_rows(COS, SIN, length, j)
        for t in range(6):
            u = dK[rows(j), t * 128:(t + 1) * 128]
            K[rows(j), t * 128:(t + 1) * 128] = (u * c - swap(u) * s).astype(BF)

    @pl.loop(0, 4)
    def _(i):
        j = own_block(i, k)
        c, s = table_rows(COS, SIN, length, j)
        for t in range(6):
            u = dQ[rows(i), t * 128:(t + 1) * 128]
            da[rows(i), t * 128:(t + 1) * 128] = (u * c - swap(u) * s).astype(BF)
    @pl.loop(0, 2)
    def _(j):
        r = rows(j, 512)
        dK[r, :] = nt(K[r, :], matrix(WQ, slice(768, 1536))) + nt(V[r, :], matrix(WQ, slice(1536, 2304)))
    dQ[...] = nt(da[...], matrix(WQ, slice(0, 768)))
    for i in range(4):
        dK[rows(own_block(jnp.int32(i), k)), :] += dQ[i * 128:(i + 1) * 128, :]
        es[i] = dK[rows(own_block(jnp.int32(i), 1 - k)), :].astype(BF)
    ecp = remote(es, er, esem_s, esem_r, sib)
    ecp.start()
    sup.stage(2)
    sout.stage(2)
    weight_rows(2, actsT, V)
    sv.stage(0)
    put_vec(18, jnp.sum(K[...].astype(F32), axis=0, keepdims=True))
    put_vec(12, jnp.sum(da[...].astype(F32), axis=0, keepdims=True))
    ecp.wait_recv()
    gg = jnp.zeros((1, 768), F32)
    gsh = jnp.zeros((1, 768), F32)
    for i in range(4):
        n, inv = norm(X[i].astype(F32))
        ee = dK[rows(own_block(jnp.int32(i), k)), :] + er[i].astype(F32)
        gg += jnp.sum(ee * n, axis=0, keepdims=True)
        gsh += jnp.sum(ee, axis=0, keepdims=True)
        gx[i] = (gmid[i * 128:(i + 1) * 128, :] + norm_grad(ee, n, inv, gain[0:1, :])).astype(BF)
    home.first(); home.straight()
    put_vec(0, gg); put_vec(6, gsh)
    vec_steps = [[sib], [dev(z, *sdn.p2, k)], [dev(z, *sdn.p3, k)], [dev(lax.rem(z + d, 4), y, x, k) for d in (1, 2, 3)]]
    vcp = []
    def vec_stage(n):
        if n > 0:
            for c in vcp[-1]: c.wait_recv()
            t = vbuf[n - 1]
            for r in range(len(vcp[-1])):
                t = t + vrec[n - 1 + r]
            if n < 4: vbuf[n] = t
            else: vout[...] = t
        if n < 4:
            vcp.append([remote(vbuf.at[n], vrec.at[n + i], vsend.at[n + i], vrecv.at[n + i], d) for i, d in enumerate(vec_steps[n])])
            for c in vcp[-1]: c.start()

    weight_rows(1, actsT, K)
    sk.stage(0)
    sv.stage(1)
    sdn.stage(4)
    weight_rows(0, actsqT, da)
    sq.stage(0)
    sk.stage(1)
    sq.stage(1)
    vec_stage(0)
    sout.stage(3)
    sup.stage(3)
    home.second()
    vec_stage(1)
    sv.stage(2)
    sk.stage(2)
    sq.stage(2)
    sup.stage(4)
    sv.stage(3)
    sout.stage(4)
    sk.stage(3)
    sdn.stage(5); sdn.stage(6)
    sv.stage(4)
    sq.stage(3)
    vec_stage(2)
    sk.stage(4)
    sq.stage(4)
    vec_stage(3)
    sup.stage(5); sout.stage(5)
    sv.stage(5); sk.stage(5); sq.stage(5)
    sup.stage(6); sout.stage(6)
    vec_stage(4)
    sv.stage(6); sk.stage(6); sq.stage(6)
    outs.done()
    home.done()
    ecp.wait_send()
    for cs in vcp:
        for c in cs: c.wait_send()


def backward_call(gup, pdown, bdown, *ins):
    n_up = gup.shape[1]
    gup = gup.reshape(4, 2, 2, 48, n_up)
    any_ = pl.BlockSpec(memory_space=pl.ANY)
    def bufs(r, n, lead=()):
        return [VM(lead + s + (r, n), BF) for s in ((4, 2, 2), (2, 4), (4,), (4,))]
    DS = pltpu.SemaphoreType.DMA
    home = sd((2, 256, 768), BF)
    return pl.pallas_call(backward_kernel,
        out_shape=[sd((24, 2304), F32), sd((24, 768), F32), sd((24, 3072), F32), sd((96, 768), F32), sd((80, 128), F32), home, sd((2, 128, 768), BF)],
        in_specs=[any_] * 3 + [vs] * 5 + [any_] * 2 + [vs] * 8, out_specs=[vs] * 5 + [any_] * 2,
        scratch_shapes=[VM((1024, 768), BF), VM((1024, 768), BF), VM((2560, 128), F32), VM((128, 1024), BF), VM((512, 768), BF), VM((512, 768), F32),
                        VM((1024, 768), F32), VM((1024, 768), F32), VM((512, 768), BF), VM((768, 512), BF),
                        VM((4, 2, 2, 48, 768), BF), VM((3, 4, 2, 2, 48, 768), BF), VM((4, 2, 2, 48, 1536), BF), VM((4, 2, 2, 96, 768), BF)]
        + bufs(48, 1536) + bufs(96, 768)[1:] + bufs(48, 384) + bufs(48, 384, (3,))
        + [VM((4, 2, 24, 384), F32), VM((4, 24, 384), F32), VM((1, 2, 24, 1536), F32), VM((1, 24, 1536), F32),
           VM((4, 128, 768), BF), VM((4, 128, 768), BF), VM((4, 128, 768), BF), VM((2, 128, 768), BF), VM((2, 128, 768), BF), VM((2, 128, 768), BF), VM((2, 128, 768), BF), VM((4, 80, 128), F32), VM((6, 80, 128), F32),
           DS((6, 9)), DS((6, 9)), DS((3,)), DS((6,)), DS((6,)), DS, DS, DS((6,)), DS((6,)), DS((2,)), DS((2,)), DS((2,)), DS((4,)), DS((2,)), DS((2,)), DS((2,)), DS((2,)), DS((4,)), DS((2,)), DS((2,))],
        compiler_params=pltpu.CompilerParams(collective_id=1, has_side_effects=True, vmem_limit_bytes=63 * 2**20),
    )(gup, pdown, bdown, *ins)


def finish_kernel(vout, cin, premix, home, across, gx, gq, go, gu, gd, mix,
                  lo, ox, gh, oq, oo, ou, od, v0, v1, v2, v3, v4, v5, v6, v7, gm, stage, sems):
    z, y, x, k = where_am_i()
    copies = []
    for j in range(5):
        stage[j] = (mix[j] * cin[...].astype(F32)).astype(BF)
        c = pltpu.make_async_copy(stage.at[j], gh.at[j], sems.at[j])
        c.start(); copies.append(c)
    for src, half in ((home, y), (across, 1 - y)):
        r = pl.ds(pl.multiple_of(half * 128, 128), 128)
        lo[:, r, :] = (premix[:, r, :] + mix[5] * src[...].astype(F32)).astype(BF)
    me = ((z * 2 + y) * 2 + x) * 2 + k
    spot = lax.broadcasted_iota(jnp.int32, (8, 128), 1)
    base = 0
    for v in (v0, v1, v2, v3, v4, v5, v6, v7):
        n = v.shape[0]
        first = me * n
        row, shift = first // 128, lax.rem(first, 128)
        a = jnp.broadcast_to(vout[pl.ds(base + row, 1), :], (8, 128))
        b = jnp.broadcast_to(vout[pl.ds(base + row + 1, 1), :], (8, 128))
        back = lax.rem(128 - shift, 128)
        both = jnp.where(spot < 128 - shift, pltpu.roll(a, back, 1), pltpu.roll(b, back, 1))
        v[...] = both[0, :n]
        base += n // 4
    gm[...] = vout[78, :6]
    for a, b in ((gx, ox), (gq, oq), (go, oo), (gu, ou), (gd, od)):
        b[...] = a[...]
    for c in copies: c.wait()


def finish_call(vectors, vout, cin, premix, home, across, gx, gq, go, gu, gd, mix):
    any_ = pl.BlockSpec(memory_space=pl.ANY)
    like = lambda a: sd(a.shape, a.dtype)
    return pl.pallas_call(finish_kernel,
        out_shape=[sd(cin.shape, BF), like(gx), sd((5,) + cin.shape, BF), like(gq), like(go), like(gu), like(gd)]
        + [sd(v.shape, F32) for v in vectors] + [sd((6,), F32)],
        in_specs=[vs] * 10 + [ss], out_specs=[vs, vs, any_] + [vs] * 13,
        scratch_shapes=[VM((5,) + cin.shape, BF), pltpu.SemaphoreType.DMA((5,))],
        compiler_params=pltpu.CompilerParams(vmem_limit_bytes=62 * 2**20),
    )(vout, cin, premix, home, across, gx, gq, go, gu, gd, mix)

def fast_shards(inputs, history, seq_lengths, attn_gain, attn_shift, qkv_weight, qkv_bias, out_weight, out_bias, mlp_gain,
                mlp_shift, up_weight, up_bias, down_weight, down_bias, mix_weights, cotangent):
    seq, batch = lax.axis_index("seq"), lax.axis_index("batch")
    z, y, x, k = seq // 2, seq % 2, batch // 2, batch % 2
    vectors = (attn_gain, attn_shift, qkv_bias, out_bias, mlp_gain, mlp_shift, up_bias, down_bias)
    COS, SIN = (jnp.asarray(t) for t in rope_tables())
    X, actsT, Q, K, V, att, lse, WQ, WO, gmid, gup, pdown, bdown, block, home, premix, gain, vin = forward_call(
        qkv_weight, out_weight, up_weight, down_weight, inputs, cotangent, COS, SIN, history, vectors, mix_weights, seq_lengths)
    oq, oo, ou, od, vout, grad_inputs, across = backward_call(gup, pdown, bdown, block, gmid, X, actsT, Q, K, V, att, lse, WQ, WO, gain, COS, SIN, vin)
    layer_out, grad_inputs, grad_history, oq, oo, ou, od, *gv, grad_mix = finish_call(
        vectors, vout, cotangent, premix, home, across, grad_inputs, oq, oo, ou, od, mix_weights)
    return (layer_out, grad_inputs, grad_history, gv[0], gv[1], oq, gv[2], oo, gv[3], gv[4], gv[5], ou, gv[6], od, gv[7], grad_mix)


def fits(mesh, inputs):
    shape = dict(mesh.shape)
    return shape == {"seq": 8, "batch": 4} and inputs.shape == (8, 2048, 768)


def solution(mesh):
    def run(*args):
        body = fast_shards if fits(mesh, args[0]) else shards
        return placed(mesh, body)(*args)
    return run
```

```python
import functools
import math

import jax
import jax.numpy as jnp
import numpy as np
from jax import lax
from jax.experimental import pallas as pl
from jax.experimental.pallas import tpu as pltpu
from jax.sharding import PartitionSpec as P

HEADS = 12
HEAD_DIM = 64
LONG_LEN = 1024
SHORT_LEN = 256


eps = 1e-05
masked = -1e30


def block_size(row_count):
    chosen = 1
    for candidate in range(1, min(row_count, 512) + 1):
        if row_count % candidate == 0:
            chosen = candidate
    return chosen


def exact_gelu(values):
    return jax.nn.gelu(values, approximate=False)


def layer_norm(values, norm_gain, norm_shift):
    average = jnp.mean(values, axis=-1, keepdims=True)
    centred = values - average
    inverse = lax.rsqrt(jnp.mean(centred * centred, axis=-1, keepdims=True) + eps)
    normed = centred * inverse
    return (normed * norm_gain + norm_shift, normed, inverse)


def norm_back(grad_out, normed, inverse, norm_gain):
    grad_normed = grad_out * norm_gain
    mean_grad = jnp.mean(grad_normed, axis=-1, keepdims=True)
    mean_cross = jnp.mean(grad_normed * normed, axis=-1, keepdims=True)
    grad_in = inverse * (grad_normed - mean_grad - normed * mean_cross)
    return (grad_in, jnp.sum(grad_out * normed, axis=0), jnp.sum(grad_out, axis=0))


def token_layout(index, info):
    seq_len, tok_count, slice_len = info
    is_long = seq_len == LONG_LEN
    offset = index % tok_count
    device = index // tok_count
    doc_ids = jnp.where(is_long, offset // slice_len, index // SHORT_LEN).astype(jnp.int32)
    relative = jnp.where(
        is_long, device * slice_len + offset % slice_len, index % SHORT_LEN
    ).astype(jnp.int32)
    return (doc_ids, relative)


def rotary_tables(relative):
    half_dim = HEAD_DIM // 2
    frequency = jnp.exp(
        -math.log(10000.0) * (2.0 * jnp.arange(half_dim, dtype=jnp.float32) / HEAD_DIM)
    )
    angles = relative.astype(jnp.float32)[:, None] * frequency[None, :]
    return (jnp.cos(angles)[:, None, :], jnp.sin(angles)[:, None, :])


def rotate(values, cosine, sine_table):
    half_dim = values.shape[-1] // 2
    lower_half = values[..., :half_dim]
    upper_half = values[..., half_dim:]
    return jnp.concatenate(
        [
            lower_half * cosine - upper_half * sine_table,
            upper_half * cosine + lower_half * sine_table,
        ],
        axis=-1,
    )


def allowed_mask(query_places, key_places, info):
    query_docs, query_rel = token_layout(query_places, info)
    key_docs, key_rel = token_layout(key_places, info)
    return (key_docs[None, :] == query_docs[:, None]) & (key_rel[None, :] <= query_rel[:, None])


def online_block(current, query_b, key_block, value_block, query_places, key_places, info):
    running, denominator, weighted = current
    key_count = key_block.shape[0]
    allowed = allowed_mask(query_places, key_places, info)
    key_heads = key_block.reshape(key_count, HEADS, HEAD_DIM)
    scores = jnp.einsum(
        "qhd,khd->hqk", query_b, key_heads, preferred_element_type=jnp.float32
    ) * HEAD_DIM ** (-0.5)
    scores = jnp.where(allowed[None], scores, masked)
    new_max = jnp.maximum(running, jnp.max(scores, axis=-1))
    exp_scores = jnp.where(allowed[None], jnp.exp(scores - new_max[..., None]), 0.0)
    rescale = jnp.exp(running - new_max)
    denominator = denominator * rescale + jnp.sum(exp_scores, axis=-1)
    value_heads = value_block.reshape(key_count, HEADS, HEAD_DIM)
    weighted = weighted * rescale[..., None] + jnp.einsum(
        "hqk,khd->hqd",
        exp_scores.astype(jnp.bfloat16),
        value_heads,
        preferred_element_type=jnp.float32,
    )
    return (new_max, denominator, weighted)


def attend_rows(current, query_b, key_rows, value_rows, first_row, query_places, info, last_place):
    key_count = key_rows.shape[0]
    block_rows = block_size(key_count)

    def one_block(carried, block_index):
        start_place = first_row + block_index * block_rows
        key_block = lax.dynamic_slice_in_dim(key_rows, block_index * block_rows, block_rows, 0)
        value_block = lax.dynamic_slice_in_dim(value_rows, block_index * block_rows, block_rows, 0)
        key_places = start_place + jnp.arange(block_rows, dtype=jnp.int32)

        def one_compute(state_in):
            return online_block(
                state_in, query_b, key_block, value_block, query_places, key_places, info
            )

        def unchanged(state_in):
            return state_in

        return (lax.cond(start_place > last_place, unchanged, one_compute, carried), None)

    result, unused = lax.scan(
        one_block, current, jnp.arange(key_count // block_rows, dtype=jnp.int32)
    )
    return result


def block_probs(query_b, key_b, query_places, key_places, info, lse_rows):
    allowed = allowed_mask(query_places, key_places, info)
    scores = jnp.einsum(
        "qhd,khd->hqk", query_b, key_b, preferred_element_type=jnp.float32
    ) * HEAD_DIM ** (-0.5)
    return jnp.exp(jnp.where(allowed[None], scores - lse_rows[..., None], masked))


def block_dscores(probabilities, grad_b, value_b, delta_rows):
    dprobs = jnp.einsum("qhd,khd->hqk", grad_b, value_b, preferred_element_type=jnp.float32)
    return (probabilities * (dprobs - delta_rows[..., None])).astype(jnp.bfloat16)


def shards(
    inputs,
    history,
    seq_lengths,
    attn_gain,
    attn_shift,
    qkv_weight,
    qkv_bias,
    out_weight,
    out_bias,
    mlp_gain,
    mlp_shift,
    up_weight,
    up_bias,
    down_weight,
    down_bias,
    mix_weights,
    cotangent,
):
    group_count = inputs.shape[0]
    tok_count = inputs.shape[1]
    model_width = inputs.shape[2]
    seq_count = lax.axis_size("seq")
    group_rows = tok_count * seq_count
    slice_len = LONG_LEN // seq_count
    factor = HEAD_DIM ** (-0.5)
    seq_index = lax.axis_index("seq")
    first_place = seq_index * tok_count
    last_place = first_place + tok_count - 1
    places = first_place + jnp.arange(tok_count, dtype=jnp.int32)
    gathered = (
        lax.all_gather(attn_gain, ("seq", "batch"), axis=0, tiled=True),
        lax.all_gather(attn_shift, ("seq", "batch"), axis=0, tiled=True),
        lax.all_gather(qkv_weight, ("seq", "batch"), axis=0, tiled=True),
        lax.all_gather(qkv_bias, ("seq", "batch"), axis=0, tiled=True),
        lax.all_gather(out_weight, ("seq", "batch"), axis=0, tiled=True),
        lax.all_gather(out_bias, ("seq", "batch"), axis=0, tiled=True),
        lax.all_gather(mlp_gain, ("seq", "batch"), axis=0, tiled=True),
        lax.all_gather(mlp_shift, ("seq", "batch"), axis=0, tiled=True),
        lax.all_gather(up_weight, ("seq", "batch"), axis=0, tiled=True),
        lax.all_gather(up_bias, ("seq", "batch"), axis=0, tiled=True),
        lax.all_gather(down_weight, ("seq", "batch"), axis=0, tiled=True),
        lax.all_gather(down_bias, ("seq", "batch"), axis=0, tiled=True),
    )
    (
        gain_one,
        shift_one,
        qkv_full,
        qkv_vec,
        out_full,
        out_vec,
        gain_two,
        shift_two,
        up_full,
        up_vec,
        down_full,
        down_vec,
    ) = gathered
    saved = []
    block_outs = []
    for group in range(group_count):
        info = (seq_lengths[group], tok_count, slice_len)
        doc_ids, relative = token_layout(places, info)
        cosine, sine_table = rotary_tables(relative)
        residual_in = inputs[group].astype(jnp.float32)
        normed_out, normed_one, inverse_one = layer_norm(
            residual_in, gain_one.astype(jnp.float32), shift_one.astype(jnp.float32)
        )
        acts_one = normed_out.astype(jnp.bfloat16)
        projected = jnp.dot(
            acts_one, qkv_full, preferred_element_type=jnp.float32
        ) + qkv_vec.astype(jnp.float32)
        queries = rotate(
            projected[:, :model_width].reshape(tok_count, HEADS, HEAD_DIM), cosine, sine_table
        ).astype(jnp.bfloat16)
        key_flat = (
            rotate(
                projected[:, model_width : 2 * model_width].reshape(tok_count, HEADS, HEAD_DIM),
                cosine,
                sine_table,
            )
            .reshape(tok_count, model_width)
            .astype(jnp.bfloat16)
        )
        value_flat = projected[:, 2 * model_width :].astype(jnp.bfloat16)
        start_state = (
            jnp.full((HEADS, tok_count), masked, jnp.float32),
            jnp.zeros((HEADS, tok_count), jnp.float32),
            jnp.zeros((HEADS, tok_count, HEAD_DIM), jnp.float32),
        )
        key_all = None
        value_all = None
        running, denominator, weighted = attend_rows(
            start_state,
            queries,
            lax.all_gather(key_flat, "seq", axis=0, tiled=True),
            lax.all_gather(value_flat, "seq", axis=0, tiled=True),
            jnp.int32(0),
            places,
            info,
            last_place,
        )
        attended = jnp.transpose(weighted / denominator[..., None], (1, 0, 2))
        lse_rows = running + jnp.log(denominator)
        attended_b = attended.reshape(tok_count, model_width).astype(jnp.bfloat16)
        middle = (
            residual_in
            + jnp.dot(attended_b, out_full, preferred_element_type=jnp.float32)
            + out_vec.astype(jnp.float32)
        )
        normed_out_two, normed_two, inverse_two = layer_norm(
            middle, gain_two.astype(jnp.float32), shift_two.astype(jnp.float32)
        )
        acts_two = normed_out_two.astype(jnp.bfloat16)
        upward = jnp.dot(acts_two, up_full, preferred_element_type=jnp.float32) + up_vec.astype(
            jnp.float32
        )
        activated, gelu_back = jax.vjp(exact_gelu, upward)
        activated_b = activated.astype(jnp.bfloat16)
        block_out = (
            middle
            + jnp.dot(activated_b, down_full, preferred_element_type=jnp.float32)
            + down_vec.astype(jnp.float32)
        )
        block_outs.append(block_out)
        saved.append(
            (
                info,
                cosine,
                sine_table,
                normed_one,
                inverse_one,
                acts_one,
                queries,
                key_flat,
                value_flat,
                key_all,
                value_all,
                attended,
                lse_rows,
                attended_b,
                normed_two,
                inverse_two,
                acts_two,
                gelu_back,
                activated_b,
            )
        )
    block_stack = jnp.stack(block_outs, axis=0)
    earlier = history.astype(jnp.float32)
    grad_out_all = cotangent.astype(jnp.float32)
    mixed_out = (
        jnp.sum(mix_weights[:-1, None, None, None] * earlier, axis=0)
        + mix_weights[-1] * block_stack
    )
    mix_terms = jnp.concatenate(
        [
            jnp.sum(earlier * grad_out_all[None], axis=(1, 2, 3)),
            jnp.sum(block_stack * grad_out_all)[None],
        ]
    )
    grad_history = (mix_weights[:-1, None, None, None] * grad_out_all[None]).astype(jnp.bfloat16)
    back_gain_one, back_qkv, back_out, back_gain_two, back_up, back_down = (
        lax.all_gather(attn_gain, ("seq", "batch"), axis=0, tiled=True),
        lax.all_gather(qkv_weight, ("seq", "batch"), axis=0, tiled=True),
        lax.all_gather(out_weight, ("seq", "batch"), axis=0, tiled=True),
        lax.all_gather(mlp_gain, ("seq", "batch"), axis=0, tiled=True),
        lax.all_gather(up_weight, ("seq", "batch"), axis=0, tiled=True),
        lax.all_gather(down_weight, ("seq", "batch"), axis=0, tiled=True),
    )
    totals = None
    grad_input_list = []
    for group in range(group_count):
        (
            info,
            cosine,
            sine_table,
            normed_one,
            inverse_one,
            acts_one,
            queries,
            key_flat,
            value_flat,
            key_all,
            value_all,
            attended,
            lse_rows,
            attended_b,
            normed_two,
            inverse_two,
            acts_two,
            gelu_back,
            activated_b,
        ) = saved[group]
        grad_block = mix_weights[-1] * grad_out_all[group]
        down_grad_b = grad_block.astype(jnp.bfloat16)
        grad_w_down = jnp.einsum(
            "tf,td->fd", activated_b, down_grad_b, preferred_element_type=jnp.float32
        )
        grad_b_down = jnp.sum(down_grad_b.astype(jnp.float32), axis=0)
        grad_act = jnp.einsum(
            "td,fd->tf", down_grad_b, back_down, preferred_element_type=jnp.float32
        )
        up_grad_b = gelu_back(grad_act)[0].astype(jnp.bfloat16)
        grad_w_up = jnp.einsum("td,tf->df", acts_two, up_grad_b, preferred_element_type=jnp.float32)
        grad_b_up = jnp.sum(up_grad_b.astype(jnp.float32), axis=0)
        grad_acts_two = jnp.einsum(
            "tf,df->td", up_grad_b, back_up, preferred_element_type=jnp.float32
        )
        grad_middle_norm, grad_gain_two, grad_shift_two = norm_back(
            grad_acts_two, normed_two, inverse_two, back_gain_two.astype(jnp.float32)
        )
        grad_middle = grad_block + grad_middle_norm
        attn_grad_b = grad_middle.astype(jnp.bfloat16)
        grad_w_out = jnp.einsum(
            "te,td->ed", attended_b, attn_grad_b, preferred_element_type=jnp.float32
        )
        grad_b_out = jnp.sum(attn_grad_b.astype(jnp.float32), axis=0)
        grad_heads = (
            jnp.einsum("td,ed->te", attn_grad_b, back_out, preferred_element_type=jnp.float32)
            .astype(jnp.bfloat16)
            .reshape(tok_count, HEADS, HEAD_DIM)
        )
        delta_rows = jnp.transpose(jnp.sum(grad_heads.astype(jnp.float32) * attended, axis=-1))
        key_all, value_all = (
            lax.all_gather(key_flat, "seq", axis=0, tiled=True),
            lax.all_gather(value_flat, "seq", axis=0, tiled=True),
        )
        key_block_rows = block_size(group_rows)

        def query_grad_block(carried, block_index):
            start_place = block_index * key_block_rows
            key_block = lax.dynamic_slice_in_dim(key_all, start_place, key_block_rows, 0).reshape(
                key_block_rows, HEADS, HEAD_DIM
            )
            value_block = lax.dynamic_slice_in_dim(
                value_all, start_place, key_block_rows, 0
            ).reshape(key_block_rows, HEADS, HEAD_DIM)
            key_places = start_place + jnp.arange(key_block_rows, dtype=jnp.int32)

            def query_compute(summed):
                probabilities = block_probs(queries, key_block, places, key_places, info, lse_rows)
                dscores = block_dscores(probabilities, grad_heads, value_block, delta_rows)
                return (
                    summed
                    + jnp.einsum(
                        "hqk,khd->qhd", dscores, key_block, preferred_element_type=jnp.float32
                    )
                    * factor
                )

            return (
                lax.cond(start_place > last_place, lambda summed: summed, query_compute, carried),
                None,
            )

        grad_queries, unused = lax.scan(
            query_grad_block,
            jnp.zeros((tok_count, HEADS, HEAD_DIM), jnp.float32),
            jnp.arange(group_rows // key_block_rows, dtype=jnp.int32),
        )
        key_first_row = jnp.int32(0)
        key_rows = key_all
        value_rows = value_all
        inner_rows = block_size(lax.axis_size("seq") * tok_count)

        def key_grad_block(carried, block_index):
            offset = block_index * inner_rows
            start_place = key_first_row + offset
            key_block = lax.dynamic_slice_in_dim(key_rows, offset, inner_rows, 0).reshape(
                inner_rows, HEADS, HEAD_DIM
            )
            value_block = lax.dynamic_slice_in_dim(value_rows, offset, inner_rows, 0).reshape(
                inner_rows, HEADS, HEAD_DIM
            )
            key_places = start_place + jnp.arange(inner_rows, dtype=jnp.int32)

            def key_compute(unused_in):
                probabilities = block_probs(queries, key_block, places, key_places, info, lse_rows)
                dscores = block_dscores(probabilities, grad_heads, value_block, delta_rows)
                grad_keys = (
                    jnp.einsum("hqk,qhd->khd", dscores, queries, preferred_element_type=jnp.float32)
                    * factor
                )
                grad_values = jnp.einsum(
                    "hqk,qhd->khd",
                    probabilities.astype(jnp.bfloat16),
                    grad_heads,
                    preferred_element_type=jnp.float32,
                )
                return jnp.concatenate(
                    [
                        grad_keys.reshape(inner_rows, model_width),
                        grad_values.reshape(inner_rows, model_width),
                    ],
                    axis=1,
                )

            def nothing(unused_in):
                return jnp.zeros((inner_rows, 2 * model_width), jnp.float32)

            return (carried, lax.cond(start_place > last_place, nothing, key_compute, carried))

        unused_out, blocks = lax.scan(
            key_grad_block,
            jnp.int32(0),
            jnp.arange(lax.axis_size("seq") * tok_count // inner_rows, dtype=jnp.int32),
        )
        key_grads = lax.psum_scatter(
            blocks.reshape(lax.axis_size("seq") * tok_count, 2 * model_width).astype(jnp.bfloat16),
            "seq",
            scatter_dimension=0,
            tiled=True,
        ).astype(jnp.float32)
        grad_keys_own = key_grads[:, :model_width]
        grad_values_own = key_grads[:, model_width:]
        grad_q_turned = rotate(grad_queries, cosine, -sine_table).reshape(tok_count, model_width)
        grad_k_turned = rotate(
            grad_keys_own.reshape(tok_count, HEADS, HEAD_DIM), cosine, -sine_table
        ).reshape(tok_count, model_width)
        qkv_grad_b = jnp.concatenate(
            [grad_q_turned, grad_k_turned, grad_values_own], axis=1
        ).astype(jnp.bfloat16)
        grad_w_qkv = jnp.einsum(
            "td,te->de", acts_one, qkv_grad_b, preferred_element_type=jnp.float32
        )
        grad_b_qkv = jnp.sum(qkv_grad_b.astype(jnp.float32), axis=0)
        grad_acts_one = jnp.einsum(
            "te,de->td", qkv_grad_b, back_qkv, preferred_element_type=jnp.float32
        )
        grad_in_norm, grad_gain_one, grad_shift_one = norm_back(
            grad_acts_one, normed_one, inverse_one, back_gain_one.astype(jnp.float32)
        )
        grad_input_list.append((grad_middle + grad_in_norm).astype(jnp.bfloat16))
        terms = [
            grad_gain_one,
            grad_shift_one,
            grad_w_qkv,
            grad_b_qkv,
            grad_w_out,
            grad_b_out,
            grad_gain_two,
            grad_shift_two,
            grad_w_up,
            grad_b_up,
            grad_w_down,
            grad_b_down,
        ]
        if totals is None:
            totals = terms
        else:
            totals = [older + newer for older, newer in zip(totals, terms)]
    shares = (
        lax.psum_scatter(totals[0], ("seq", "batch"), scatter_dimension=0, tiled=True),
        lax.psum_scatter(totals[1], ("seq", "batch"), scatter_dimension=0, tiled=True),
        lax.psum_scatter(totals[2], ("seq", "batch"), scatter_dimension=0, tiled=True),
        lax.psum_scatter(totals[3], ("seq", "batch"), scatter_dimension=0, tiled=True),
        lax.psum_scatter(totals[4], ("seq", "batch"), scatter_dimension=0, tiled=True),
        lax.psum_scatter(totals[5], ("seq", "batch"), scatter_dimension=0, tiled=True),
        lax.psum_scatter(totals[6], ("seq", "batch"), scatter_dimension=0, tiled=True),
        lax.psum_scatter(totals[7], ("seq", "batch"), scatter_dimension=0, tiled=True),
        lax.psum_scatter(totals[8], ("seq", "batch"), scatter_dimension=0, tiled=True),
        lax.psum_scatter(totals[9], ("seq", "batch"), scatter_dimension=0, tiled=True),
        lax.psum_scatter(totals[10], ("seq", "batch"), scatter_dimension=0, tiled=True),
        lax.psum_scatter(totals[11], ("seq", "batch"), scatter_dimension=0, tiled=True),
    )
    grad_mix = lax.psum(mix_terms, ("seq", "batch"))
    grad_inputs = jnp.stack(grad_input_list, axis=0)
    return (
        mixed_out.astype(jnp.bfloat16),
        grad_inputs,
        grad_history,
        shares[0],
        shares[1],
        shares[2],
        shares[3],
        shares[4],
        shares[5],
        shares[6],
        shares[7],
        shares[8],
        shares[9],
        shares[10],
        shares[11],
        grad_mix,
    )


def placed(mesh, body):
    return jax.shard_map(
        body,
        mesh=mesh,
        in_specs=(
            P("batch", "seq", None),
            P(None, "batch", "seq", None),
            P("batch"),
            P(("seq", "batch")),
            P(("seq", "batch")),
            P(("seq", "batch"), None),
            P(("seq", "batch")),
            P(("seq", "batch"), None),
            P(("seq", "batch")),
            P(("seq", "batch")),
            P(("seq", "batch")),
            P(("seq", "batch"), None),
            P(("seq", "batch")),
            P(("seq", "batch"), None),
            P(("seq", "batch")),
            P(),
            P("batch", "seq", None),
        ),
        out_specs=(
            P("batch", "seq", None),
            P("batch", "seq", None),
            P(None, "batch", "seq", None),
            P(("seq", "batch")),
            P(("seq", "batch")),
            P(("seq", "batch"), None),
            P(("seq", "batch")),
            P(("seq", "batch"), None),
            P(("seq", "batch")),
            P(("seq", "batch")),
            P(("seq", "batch")),
            P(("seq", "batch"), None),
            P(("seq", "batch")),
            P(("seq", "batch"), None),
            P(("seq", "batch")),
            P(),
        ),
        check_vma=False,
    )

MESH = pl.DeviceIdType.MESH
BF, F32 = jnp.bfloat16, jnp.float32


def where_am_i():
    seq, batch = lax.axis_index("seq"), lax.axis_index("batch")
    return seq // 2, seq % 2, batch // 2, batch % 2


def dev(z, y, x, k):
    return (z * 2 + y, x * 2 + k)


def remote(src, dst, ssem, rsem, device):
    return pltpu.make_async_remote_copy(src_ref=src, dst_ref=dst, send_sem=ssem, recv_sem=rsem,
                                        device_id=device, device_id_type=MESH)


def chips_of(z, y, x):
    mine = (z * 2 + y) * 2 + x
    for step in range(1, 16):
        other = lax.rem(mine + step, 16)
        yield step, (other // 4, (other // 2) % 2, other % 2)


def greet(z, y, x, k):
    barrier = pltpu.get_barrier_semaphore()
    for _, chip in chips_of(z, y, x):
        pl.semaphore_signal(barrier, inc=1, device_id=dev(*chip, k), device_id_type=MESH)
    for step in range(8):
        other = lax.rem(z * 2 + y + step, 8)
        pl.semaphore_signal(barrier, inc=1, device_id=dev(other // 2, other % 2, x, 1 - k), device_id_type=MESH)
    pl.semaphore_wait(barrier, 23)


class Gather:
    STAGES = 7

    def __init__(self, part, send, recv, pos, both, hops):
        z, y, x, k = pos
        self.hops = hops
        turn = (k == 0) | both
        p2 = jnp.where(turn, 1 - y, y), jnp.where(turn, x, 1 - x)
        p3 = jnp.where(turn, y, 1 - y), jnp.where(turn, 1 - x, x)
        d4 = 1 - y, 1 - x
        one = lambda zz: part(pl.ds(zz, 1), y, x, k)
        allz = lambda yx: part(slice(None), yx[0], yx[1], k)
        self.mid = (z == 1) | (z == 2)
        end = jnp.where(z == 1, 0, 3)
        def cp(n, ref, device, r=None):
            return remote(ref, ref, send.at[n], recv.at[n if r is None else r], device)
        others = [lax.rem(z + d, 4) for d in (1, 2, 3)]
        self.three = [cp(d, one(o), dev(o, y, x, k), o) for d, o in enumerate(others)]
        if hops:
            self.direct = [cp(0, one(z), dev(jnp.where(z == 1, 0, 1), y, x, k), z), cp(1, one(z), dev(jnp.where(z == 2, 3, 2), y, x, k), z)]
        else:
            self.direct = [cp(d, one(z), dev(o, y, x, k), z) for d, o in enumerate(others)]
        self.passed = [cp(3 + n, one(f), dev(end, y, x, k), f) for n, f in enumerate((3 - z, 3 - end))]
        self.near = cp(0, one(end), dev(end, y, x, k), end)
        n2, n3 = dev(z, *p2, k), dev(z, *p3, k)
        blocks = [z] + others
        self.a2 = [cp(5 + n, one(b), n2, 4 + b) for n, b in enumerate(blocks)]
        self.a3 = [cp(9 + n, one(b), n3, 8 + b) for n, b in enumerate(blocks)]
        self.b3 = [cp(13 + n, part(pl.ds(b, 1), *p2, k), n3, 12 + b) for n, b in enumerate(blocks)]
        sib = dev(z, y, x, 1 - k)
        self.s = [cp(17 + n, allz(p), sib, 16 + n) for n, p in enumerate(((y, x), p2, p3, d4))]

    def early(self):
        self.a2[0].start(); self.a3[0].start()

    def early_on(self):
        self.a2[0].wait_recv()
        self.b3[0].start()

    def stage(self, n):
        if n == 0:
            for c in self.direct: c.start()
        elif n == 1:
            if self.hops:
                @pl.when(self.mid)
                def _():
                    for c in self.passed:
                        c.wait_recv()
                        c.start()
        elif n == 2:
            if self.hops:
                @pl.when(self.mid)
                def _():
                    self.near.wait_recv()
                @pl.when(jnp.logical_not(self.mid))
                def _():
                    for c in self.three: c.wait_recv()
            else:
                for c in self.three: c.wait_recv()
            for c in self.a2[1:] + self.a3[1:]: c.start()
            self.s[0].start()
        elif n == 3:
            for c in self.a2[1:]: c.wait_recv()
            for c in self.b3[1:]: c.start()
            self.s[1].start()
        elif n == 4:
            for c in self.a3: c.wait_recv()
            self.s[2].start()
        elif n == 5:
            for c in self.b3: c.wait_recv()
            self.s[3].start()
        elif n == 6:
            for c in self.s: c.wait_recv()

    def sent(self):
        for c in self.direct + self.a2 + self.a3 + self.b3 + self.s: c.wait_send()
        if self.hops:
            @pl.when(self.mid)
            def _():
                for c in self.passed: c.wait_send()


class Home:
    def __init__(self, buf, cross, sel, out_straight, out_crossed, length, sems, pos):
        self.__dict__.update(locals())
        z, y, x, k = pos
        self.esend, self.erecv, self.send, self.h0, self.hs = sems
        self.swap = [remote(buf.at[self.crossed(n)], cross.at[n], self.esend.at[n], self.erecv.at[n], dev(z, 1 - y, x, 1 - k))
                     for n in range(2)] if cross is not None else []
        self.sent = []

    def crossed(self, n):
        z, y, x, k = self.pos
        return lax.rem(1 - y + k, 2) + 2 * n

    def go(self, ref, i, out, sem, n):
        z, y, x, k = self.pos
        slot = lax.rem(z, 2)
        dst = out(slot)
        me = (i == z) & (z // 2 == k)
        cp = remote(ref, dst, self.send.at[n], sem.at[slot], dev(i, y, x, z // 2))
        @pl.when(me)
        def _():
            pltpu.make_async_copy(ref, dst, sem.at[slot]).start()
        @pl.when(jnp.logical_not(me))
        def _():
            cp.start()
        self.sent.append((cp, jnp.logical_not(me)))

    def first(self):
        for c in self.swap: c.start()

    def straight(self):
        z, y, x, k = self.pos
        for n in range(2):
            i = lax.rem(y + k, 2) + 2 * n
            self.go(self.buf.at[i], i, self.out_straight, self.h0, n)

    def second(self):
        for n in range(2):
            self.swap[n].wait_recv()
            i = self.crossed(n)
            far = jnp.broadcast_to(self.length, (128, 768)) > 512.0
            self.sel[n] = jnp.where(far, self.cross[n].astype(F32), self.buf[i].astype(F32)).astype(BF)
            self.go(self.sel.at[n], i, self.out_crossed, self.hs, 2 + n)

    def done(self):
        z, y, x, k = self.pos
        for g in range(2):
            for out, sem in ((self.out_straight, self.h0), (self.out_crossed, self.hs)):
                if out is not None:
                    remote(out(g), out(g), self.send.at[0], sem.at[g], dev(z, y, x, 1 - k)).wait_recv()
        for c in self.swap: c.wait_send()
        for cp, cond in self.sent:
            @pl.when(cond)
            def _():
                cp.wait_send()


class Scatter:
    STAGES = 7

    def __init__(self, mine, theirs, RA, RB, RC, RZ, put, finish, send, recv, pos, load=None, both=False, begun=False):
        self.mine, self.RA, self.RB, self.RC, self.RZ, self.put, self.finish, self.pos, self.load = mine, RA, RB, RC, RZ, put, finish, pos, load
        self.begun = begun
        z, y, x, k = pos
        self.own = (y, x)
        turn = (k == 0) | both
        self.p2 = jnp.where(turn, 1 - y, y), jnp.where(turn, x, 1 - x)
        self.p3 = jnp.where(turn, y, 1 - y), jnp.where(turn, 1 - x, x)
        self.d4 = 1 - y, 1 - x
        blk = lambda yx: mine(slice(None), yx[0], yx[1])
        n3, n2 = dev(z, *self.p3, k), dev(z, *self.p2, k)
        if not begun:
            self.pre = [remote(a, b, send.at[8 * n], recv.at[8 * n], dev(z, y, x, 1 - k)) for n, (a, b) in enumerate(theirs)]
            self.b1 = remote(blk(self.d4), RB.at[1], send.at[1], recv.at[1], n3)
            self.b0 = remote(blk(self.p3), RB.at[0], send.at[2], recv.at[2], n3)
        if RC is None: return
        self.c = remote(blk(self.p2), RC, send.at[3], recv.at[3], n2)
        self.mid = (z == 1) | (z == 2)
        end, near = jnp.where(z < 2, 0, 3), jnp.where(z < 2, 1, 2)
        self.far = (3 - near, 3 - end)
        zdev = lambda zz: dev(zz, y, x, k)
        def zcp(n, block, slot, to):
            return remote(mine(block, y, x), RZ.at[slot], send.at[4 + n], recv.at[4 + slot], zdev(to))
        self.up = [zcp(0, near, 0, near), zcp(1, self.far[0], 2, near), zcp(2, self.far[1], 3, near)]
        self.down = zcp(0, end, 0, end)
        self.on = [zcp(1, self.far[0], 1, self.far[0]), zcp(2, self.far[1], 1, self.far[1])]
        self.sends = [self.c] if begun else self.pre + [self.b1, self.b0, self.c]

    def add(self, yx, other):
        @pl.loop(0, 4)
        def _(i):
            ref = self.mine(i, yx[0], yx[1])
            ref[...] = (ref[...].astype(F32) + other[i].astype(F32)).astype(BF)

    def first(self, yx):
        for rows_of, part in self.RA:
            @pl.loop(0, 4)
            def _(i):
                ref = rows_of(self.mine(i, yx[0], yx[1]))
                ref[...] = (ref[...].astype(F32) + part.at[:, yx[0], yx[1]][i].astype(F32)).astype(BF)

    def stage(self, n):
        z, y, x, k = self.pos
        if n == 0:
            for c in self.load or (): c.start()
            for c in self.pre: c.start()
        elif n == 1:
            for c in self.pre: c.wait_recv()
            for c in self.load or (): c.wait()
            self.first(self.d4)
            self.b1.start()
            self.first(self.p3)
            self.b0.start()
            self.first(self.p2)
            self.first(self.own)
        elif n == 2:
            if self.begun:
                for c in self.load: c.wait()
            else:
                self.b1.wait_recv()
            self.add(self.p2, self.RB.at[1])
            self.c.start()
            if not self.begun: self.b0.wait_recv()
            self.add(self.own, self.RB.at[0])
        elif n == 3:
            self.c.wait_recv()
            self.add(self.own, self.RC)
            @pl.when(self.mid)
            def _():
                self.down.start()
            @pl.when(jnp.logical_not(self.mid))
            def _():
                for c in self.up: c.start()
        elif n == 4:
            @pl.when(self.mid)
            def _():
                for i, c in enumerate(self.on):
                    self.up[1 + i].wait_recv()
                    ref = self.mine(self.far[i], y, x)
                    ref[...] = (ref[...].astype(F32) + self.RZ[2 + i].astype(F32)).astype(BF)
                    c.start()
        elif n == 5:
            self.up[0].wait_recv()
            self.on[0].wait_recv()
            self.put(self.mine(z, y, x)[...].astype(F32) + self.RZ[0].astype(F32) + self.RZ[1].astype(F32))
        elif n == 6:
            self.finish()
            for c in self.sends: c.wait_send()
            @pl.when(self.mid)
            def _():
                for c in [self.down] + self.on: c.wait_send()
            @pl.when(jnp.logical_not(self.mid))
            def _():
                for c in self.up: c.wait_send()

EPS = 1e-5
NT = (((1,), (1,)), ((), ()))


def nt(a, b):
    return lax.dot_general(a, b, NT, preferred_element_type=F32)


def nn(a, b):
    return jnp.dot(a, b, preferred_element_type=F32)


def rope_tables():
    freq = np.exp(-math.log(10000.0) * (2.0 * np.arange(32, dtype=np.float32) / 64)).astype(np.float32)
    ang = np.arange(1024, dtype=np.float32)[:, None] * freq[None, :]
    c, s = np.cos(ang.astype(np.float64)), np.sin(ang.astype(np.float64))
    return (np.concatenate([c, c, c, c], 1).astype(np.float32), np.concatenate([-s, s, -s, s], 1).astype(np.float32))


def swap(u):
    low = lax.broadcasted_iota(jnp.int32, u.shape, 1) % 64 < 32
    return jnp.where(low, pltpu.roll(u, 96, 1), pltpu.roll(u, 32, 1))


def norm(v):
    mean = jnp.mean(v, axis=-1, keepdims=True)
    cen = v - mean
    inv = lax.rsqrt(jnp.mean(cen * cen, axis=-1, keepdims=True) + EPS)
    return cen * inv, inv


def norm_grad(e, n, inv, gain):
    g = e * gain
    return inv * (g - jnp.mean(g, axis=-1, keepdims=True) - n * jnp.mean(g * n, axis=-1, keepdims=True))


def own_block(i, k):
    return 2 * i + lax.rem(i + k, 2)


def rows(i, n=128):
    return pl.ds(pl.multiple_of(i * n, n), n)


def spread(p):
    low = lax.broadcasted_iota(jnp.int32, p.shape, 1) < 64
    zero = jnp.zeros_like(p)
    return jnp.concatenate([jnp.where(low, p, zero), jnp.where(low, zero, p)], axis=0)


def pick(o):
    low = lax.broadcasted_iota(jnp.int32, (128, 128), 0) < 64
    return jnp.where(low, o[:, :128], o[:, 128:]).T


def fill_bias(bias, is_long, k):
    at = 0
    for i in range(4):
        kk = 256 * (i + 1)
        key = lax.broadcasted_iota(jnp.int32, (kk, 256), 0)
        q = own_block(i, k) * 128 + lax.broadcasted_iota(jnp.int32, (kk, 256), 1) % 128
        first = jnp.where(is_long, 0, q - q % 256)
        bias[at:at + kk, :] = jnp.where((key <= q) & (key >= first), 0.0, -1e30)
        at += kk


def attn_fwd(flag, XM, XA, wqkv, wout, gain, shift, bqkv, bout, COS, SIN,
             acts, Q, K, V, att, lse, middle, bias, VT):
    z, y, x, k = where_am_i()
    is_long = flag[0] != 0
    fill_bias(bias, is_long, k)
    for j in range(8):
        alt = jnp.logical_and(jnp.logical_not(is_long), lax.rem(jnp.int32(j), 2) != y)
        blk = jnp.where(alt, XA[j // 2], XM[j]).astype(F32)
        n, _ = norm(blk)
        acts[j * 128:(j + 1) * 128, :] = (n * gain[...] + shift[...]).astype(BF)

    def tables(j):
        off = jnp.where(is_long, j, lax.rem(j, 2))
        return COS[rows(off), :], SIN[rows(off), :]

    @pl.loop(0, 8)
    def _(j):
        a = acts[rows(j), :]
        c, s = tables(j)
        for t in range(6):
            u = nn(a, wqkv[:, 768 + t * 128:896 + t * 128]) + bqkv[:, 768 + t * 128:896 + t * 128]
            K[rows(j), t * 128:(t + 1) * 128] = (u * c + swap(u) * s).astype(BF)
        V[rows(j), :] = (nn(a, wqkv[:, 1536:]) + bqkv[:, 1536:]).astype(BF)

    @pl.loop(0, 4)
    def _(i):
        j = own_block(i, k)
        a = acts[rows(j), :]
        c, s = tables(j)
        for t in range(6):
            u = nn(a, wqkv[:, t * 128:(t + 1) * 128]) + bqkv[:, t * 128:(t + 1) * 128]
            Q[rows(i), t * 128:(t + 1) * 128] = (u * c + swap(u) * s).astype(BF) * jnp.asarray(0.125, BF)

    @pl.loop(0, 6)
    def _(h):
        lanes = rows(h)
        VT[...] = V[:, lanes].T
        at = 0
        for i in range(4):
            kk = 256 * (i + 1)
            qb = spread(Q[i * 128:(i + 1) * 128, lanes])
            st = nt(K[0:kk, lanes], qb) + bias[at:at + kk, :]
            top = jnp.max(st, axis=0, keepdims=True)
            p = jnp.exp(st - top)
            den = jnp.sum(p, axis=0, keepdims=True)
            o = nn(VT[:, 0:kk], p.astype(BF)) * (1.0 / den)
            att[i * 128:(i + 1) * 128, lanes] = pick(o)
            lse[h, i:i + 1, :] = top + jnp.log(den)
            at += kk

    @pl.loop(0, 4)
    def _(i):
        j = own_block(i, k)
        alt = jnp.logical_and(jnp.logical_not(is_long), lax.rem(j, 2) != y)
        xb = jnp.where(alt, XA[i], XM[j]).astype(F32)
        middle[rows(i), :] = xb + (nn(att[rows(i), :].astype(BF), wout[...]) + bout[...])


def mlp(CH, flag, mix, middle, CM, CA, wup, wdown, gain, shift, bup, bdown,
        block, gmid, gup, gdown, g_gain, g_shift, g_bup, g_bdown, mixsum, acts2, actsT, dg, ga, cf):
    z, y, x, k = where_am_i()
    is_long = flag[0] != 0
    m5 = mix[5]
    for i in range(4):
        r = slice(i * 128, (i + 1) * 128)
        mid = middle[r, :]
        n, _ = norm(mid)
        acts2[r, :] = (n * gain[...] + shift[...]).astype(BF)
        j = own_block(jnp.int32(i), k)
        alt = jnp.logical_and(jnp.logical_not(is_long), lax.rem(j, 2) != y)
        c = jnp.where(alt, CA[i], CM[j]).astype(F32)
        cf[r, :] = c
        dg[r, :] = (m5 * c).astype(BF)
        block[r, :] = mid + bdown[...]
        ga[r, :] = jnp.zeros_like(mid)
        actsT[:, r] = acts2[r, :].T
    g_bdown[...] = jnp.sum(dg[...].astype(F32), axis=0, keepdims=True)

    @pl.loop(0, wup.shape[1] // CH)
    def _(f):
        cols = rows(f, CH)
        up = nn(acts2[...], wup[:, cols]) + bup[:, cols]
        half_erf = 0.5 * lax.erf(up * (2.0 ** -0.5)) + 0.5
        slope = half_erf + up * (jnp.exp(up * up * -0.5) * (1.0 / math.sqrt(2 * math.pi)))
        act = (up * half_erf).astype(BF)
        block[...] += nn(act, wdown[cols, :])
        upg = (nt(dg[...], wdown[cols, :]) * slope).astype(BF)
        g_bup[:, cols] = jnp.sum(upg.astype(F32), axis=0, keepdims=True)
        gdown[cols, :] = nn(act.T, dg[...]).astype(BF)
        gup[:, cols] = nn(actsT[...], upg).astype(BF)
        ga[...] += nt(upg, wup[:, cols])

    total = jnp.zeros((1, 768), F32)
    gg = jnp.zeros((1, 768), F32)
    gs = jnp.zeros((1, 768), F32)
    for i in range(4):
        r = slice(i * 128, (i + 1) * 128)
        n, inv = norm(middle[r, :])
        e = ga[r, :]
        gg += jnp.sum(e * n, axis=0, keepdims=True)
        gs += jnp.sum(e, axis=0, keepdims=True)
        gmid[r, :] = m5 * cf[r, :] + norm_grad(e, n, inv, gain[...])
        total += jnp.sum(cf[r, :] * block[r, :], axis=0, keepdims=True)
    g_gain[...] = gg
    g_shift[...] = gs
    mixsum[...] = total


def attn_bwd(flag, gmid, acts, Q, K, V, att, lse, wqkv, wout, COS, SIN,
             e, gqkv, gout, g_bqkv, g_bout, bias, KT, da, dQ, dK, dV, agrad, actsT, actsqT, KG, VG):
    z, y, x, k = where_am_i()
    is_long = flag[0] != 0
    fill_bias(bias, is_long, k)
    agrad[...] = gmid[...].astype(BF)
    g_bout[...] = jnp.sum(agrad[...].astype(F32), axis=0, keepdims=True)

    @pl.loop(0, 4)
    def _(i):
        da[rows(i), :] = nt(agrad[rows(i), :], wout[...]).astype(BF)

    for t in range(6):
        aT = att[:, t * 128:(t + 1) * 128].T.astype(BF)
        gout[t * 128:(t + 1) * 128, :] = nn(aT, agrad[...]).astype(BF)
    dK[...] = jnp.zeros_like(dK)
    dV[...] = jnp.zeros_like(dV)

    @pl.loop(0, 6)
    def _(h):
        lanes = rows(h)
        KT[...] = K[:, lanes].T
        at = 0
        for i in range(4):
            kk = 256 * (i + 1)
            r = slice(i * 128, (i + 1) * 128)
            d = da[r, lanes]
            qb, db = spread(Q[r, lanes]), spread(d)
            prod = (d.astype(F32) * att[r, lanes]).T
            delta = jnp.concatenate([jnp.sum(prod[:64], axis=0, keepdims=True), jnp.sum(prod[64:], axis=0, keepdims=True)], axis=1)
            st = nt(K[0:kk, lanes], qb) + bias[at:at + kk, :]
            p = jnp.exp(st - lse[h, i:i + 1, :])
            ds = (p * (nt(V[0:kk, lanes], db) - delta)).astype(BF)
            dV[0:kk, lanes] += nn(p.astype(BF), db)
            dK[0:kk, lanes] += nn(ds, qb)
            dQ[r, lanes] = pick(nn(KT[:, 0:kk], ds)) * 0.125
            at += kk

    def tables(j):
        off = jnp.where(is_long, j, lax.rem(j, 2))
        return COS[rows(off), :], SIN[rows(off), :]

    for j in range(8):
        actsT[:, j * 128:(j + 1) * 128] = acts[j * 128:(j + 1) * 128, :].T
    for i in range(4):
        j = own_block(jnp.int32(i), k)
        actsqT[:, i * 128:(i + 1) * 128] = acts[rows(j), :].T
        c, s = tables(j)
        for t in range(6):
            u = dQ[i * 128:(i + 1) * 128, t * 128:(t + 1) * 128]
            da[i * 128:(i + 1) * 128, t * 128:(t + 1) * 128] = (u * c - swap(u) * s).astype(BF)

    @pl.loop(0, 8)
    def _(j):
        c, s = tables(j)
        for t in range(6):
            u = dK[rows(j), t * 128:(t + 1) * 128]
            KG[rows(j), t * 128:(t + 1) * 128] = (u * c - swap(u) * s).astype(BF)
        VG[rows(j), :] = dV[rows(j), :].astype(BF)
        e[rows(j), :] = nt(KG[rows(j), :], wqkv[:, 768:1536]) + nt(VG[rows(j), :], wqkv[:, 1536:])

    @pl.loop(0, 4)
    def _(i):
        j = own_block(i, k)
        e[rows(j), :] += nt(da[rows(i), :], wqkv[:, :768])

    g_bqkv[:, :768] = jnp.sum(da[...].astype(F32), axis=0, keepdims=True)
    g_bqkv[:, 768:1536] = jnp.sum(KG[...].astype(F32), axis=0, keepdims=True)
    g_bqkv[:, 1536:] = jnp.sum(VG[...].astype(F32), axis=0, keepdims=True)

    @pl.loop(0, 6)
    def _(t):
        gqkv[rows(t), :768] = nn(actsqT[rows(t), :], da[...]).astype(BF)
        gqkv[rows(t), 768:1536] = nn(actsT[rows(t), :], KG[...]).astype(BF)
        gqkv[rows(t), 1536:] = nn(actsT[rows(t), :], VG[...]).astype(BF)


sd = jax.ShapeDtypeStruct
VM = pltpu.VMEM
vs = pl.BlockSpec(memory_space=pltpu.VMEM)
ss = pl.BlockSpec(memory_space=pltpu.SMEM)
CP = pltpu.CompilerParams(vmem_limit_bytes=60 * 2**20)


def attn_fwd_call(flag, *ins):
    return pl.pallas_call(attn_fwd,
        out_shape=[sd((1024, 768), BF), sd((512, 768), BF), sd((1024, 768), BF), sd((1024, 768), BF),
                   sd((512, 768), F32), sd((6, 4, 256), F32), sd((512, 768), F32)],
        in_specs=[ss] + [vs] * len(ins), out_specs=[vs] * 7,
        scratch_shapes=[VM((2560, 256), F32), VM((128, 1024), BF)],
        compiler_params=CP)(flag, *ins)


def mlp_call(flag, mix, *ins):
    r = sd((1, 768), F32)
    return pl.pallas_call(functools.partial(mlp, 512),
        out_shape=[sd((512, 768), F32), sd((512, 768), F32), sd((768, 3072), BF), sd((3072, 768), BF), r, r, sd((1, 3072), F32), r, r],
        in_specs=[ss, ss] + [vs] * len(ins), out_specs=[vs] * 9,
        scratch_shapes=[VM((512, 768), BF), VM((768, 512), BF), VM((512, 768), BF), VM((512, 768), F32), VM((512, 768), F32)],
        compiler_params=CP)(flag, mix, *ins)


def attn_bwd_call(flag, *ins):
    return pl.pallas_call(attn_bwd,
        out_shape=[sd((1024, 768), F32), sd((768, 2304), BF), sd((768, 768), BF), sd((1, 2304), F32), sd((1, 768), F32)],
        in_specs=[ss] + [vs] * len(ins), out_specs=[vs] * 5,
        scratch_shapes=[VM((2560, 256), F32), VM((128, 1024), BF), VM((512, 768), BF), VM((512, 768), F32), VM((1024, 768), F32),
                        VM((1024, 768), F32), VM((512, 768), BF), VM((768, 1024), BF), VM((768, 512), BF), VM((1024, 768), BF), VM((1024, 768), BF)],
        compiler_params=CP)(flag, *ins)


VROWS = (24, 24, 72, 24, 24, 24, 96, 24)


def widen(vecs, row, n):
    v = vecs[:, row, :].astype(BF)
    wide = 32 * n
    j = lax.broadcasted_iota(jnp.int32, (128, wide), 1)
    i = lax.broadcasted_iota(jnp.int32, (128, wide), 0)
    q = jnp.floor((j.astype(F32) + 0.5) * (1.0 / n)).astype(jnp.int32)
    hot = jnp.where(j - q * n == i, 1.0, 0.0).astype(BF)
    full = nn(v, hot)
    d = lax.broadcasted_iota(jnp.int32, (32, wide), 0)
    return jnp.sum(jnp.where(q[:32] == d, full, 0.0), axis=0, keepdims=True)


def lane(tile, row, at):
    r = lax.broadcasted_iota(jnp.int32, tile.shape, 0)
    c = lax.broadcasted_iota(jnp.int32, tile.shape, 1)
    v = jnp.sum(jnp.where((r == row) & (c == at), tile, 0.0), axis=1, keepdims=True)
    return jnp.sum(v, axis=0, keepdims=True)


def longer(length, shape):
    return jnp.broadcast_to(length, shape) > 512.0


def bias_rows(bias, length, k):
    at = 0
    for i in range(4):
        kk = 256 * (i + 1)
        key = lax.broadcasted_iota(jnp.int32, (kk, 128), 0)
        q = own_block(i, k) * 128 + lax.broadcasted_iota(jnp.int32, (kk, 128), 1)
        first = jnp.where(longer(length, (kk, 128)), 0, q - q % 256)
        bias[at:at + kk, :] = jnp.where((key <= q) & (key >= first), 0.0, -1e30)
        at += kk


def both_heads(bias, at, kk):
    b = bias[at:at + kk, :]
    return jnp.concatenate([b, b], axis=1)


def table_rows(COS, SIN, length, j):
    far = longer(length, (128, 128))
    near = lax.rem(j, 2)
    return (jnp.where(far, COS[rows(j), :], COS[rows(near), :]), jnp.where(far, SIN[rows(j), :], SIN[rows(near), :]))


def matrix(W, cols):
    w = W[:, :, :, :, cols]
    return w.reshape(768, w.shape[-1])


def forward_kernel(cols, qkv, out, up, down, xin, cin, COS, SIN, hist, v0, v1, v2, v3, v4, v5, v6, v7, mix, lens,
                   oX, oacts, oQ, oK, oV, oatt, olse, oWQ, oWO, ogmid, ogup, opd, orb, obl, ohome, opre, ogain, vgrad,
                   f_own, f_sib, block_w, WQ, WO, WU, WD, VEC, X, C, NB, SB,
                   Q, K, V, att, lse, middle, bias, VT, act, slope, block, ga, acts2, actsT, dg, gup, GD, a1T, bl,
                   vq, vg, vu, vec, mixrow,
                   psend, precv, lsem, gsend, grecv, asend, arecv, nsend, nrecv, fsend, frecv, xsem, csem, hsem, osem, vsend, vrecv, dsend, drecv, free, *home_sems):
    pos = z, y, x, k = where_am_i()
    sib = dev(z, y, x, 1 - k)
    greet(z, y, x, k)
    s = 2 * z + y
    own_s = lax.rem(y + z, 2)
    def neighbour(a, src):
        cps = []
        for i in range(2):
            hi = src.at[i, pl.ds(pl.multiple_of((1 - y) * 128, 128), 128)]
            cp = remote(hi, NB.at[a, i], nsend.at[a, i], nrecv.at[a, i], dev(z, 1 - y, x, k))
            cp.start()
            cps.append(cp)
        return cps

    tokens = []
    def along_z(a, i, n, ref, dst, core):
        g = 2 * k + i
        me = (g == z) & (core == k)
        cp = remote(ref, dst, asend.at[a, i, n], arecv.at[a, z], dev(g, y, x, core))
        @pl.when(me)
        def _():
            pltpu.make_async_copy(ref, dst, arecv.at[a, z]).start()
        @pl.when(jnp.logical_not(me))
        def _():
            cp.start()
        tokens.append((cp, jnp.logical_not(me)))

    def straight(a, src, dst):
        for i in range(2):
            along_z(a, i, 0, src.at[i, pl.ds(pl.multiple_of(y * 128, 128), 128)], dst(s), own_s)

    def crossed(a, src, dst, cps):
        for i in range(2):
            cps[i].wait_recv()
            mine = src[i, pl.ds(pl.multiple_of((1 - y) * 128, 128), 128), :]
            far = jnp.broadcast_to(lens[i].astype(F32), (128, 768)) > 512.0
            SB[a, i] = jnp.where(far, NB[a, i].astype(F32), mine.astype(F32)).astype(BF)
            along_z(a, i, 1, SB.at[a, i], dst(s + 1 - 2 * y), 1 - own_s)

    def arrived(a, dst, i):
        remote(dst, dst, asend.at[a, 0, 0], arecv.at[a, i], sib).wait_recv()

    def acts(j, low):
        return (acts2 if low else dg).at[rows(j if low else j - 4)]
    slots = [act.at[:, pl.ds(768 * n, 768)] for n in range(4)] + [dg]
    to_x = lambda j: X.at[j]
    to_c = lambda j: C.at[j // 2]
    vec[...] = jnp.zeros_like(vec)
    for r, v in enumerate((v0, v1, v2, v3, v4, v5, v6, v7)):
        vec[r:r + 1, 0:v.shape[1]] = v[...].astype(F32)
    place = lax.broadcasted_iota(jnp.int32, (1, 128), 1)
    first = vec[0:1, :]
    for i in range(2):
        first = jnp.where(place == 64 + i, lens[i].astype(F32), first)
    vec[0:1, :] = first
    at, offs = 0, []
    for n in cols:
        offs.append((at, n // 2))
        at += n // 2
    pres = []
    for i, ((at, half), ref) in enumerate(zip(offs, (qkv, out, up))):
        f_own[0, :, at:at + half] = ref[:, :half].astype(F32)
        f_own[1, :, at:at + half] = ref[:, half:].astype(F32)
        pre = remote(f_own.at[1 - k, :, pl.ds(at, half)], f_sib.at[:, pl.ds(at, half)], psend.at[i], precv.at[i], sib)
        pre.start()
        pres.append(pre)
    lvec = pltpu.make_async_copy(vec, VEC.at[z, y, x, k], lsem.at[4])
    ldown = pltpu.make_async_copy(down, WD.at[z, y, x, k], lsem.at[3])
    lvec.start(); ldown.start()

    def colpart(W, half):
        return lambda zz, yy, xx, kk: W.at[zz, yy, xx, :, pl.ds(pl.multiple_of(kk * half, 128), half)]
    def rowpart(W):
        return lambda zz, yy, xx, kk: W.at[zz, yy, xx, kk]
    gq, go, gu, gd = G = [Gather(p, gsend.at[i], grecv.at[i], pos, i in (1, 2), i > 1) for i, p in enumerate(
        [colpart(WQ, offs[0][1]), colpart(WO, offs[1][1]), colpart(WU, offs[2][1]), rowpart(WD)])]
    lvec.wait()
    vs_out = [remote(VEC.at[z, y, x, k], VEC.at[z, y, x, k], vsend.at[n], vrecv.at[15 - n], dev(*chip, k)) for n, chip in chips_of(z, y, x)]
    vs_in = [remote(VEC.at[chip[0], chip[1], chip[2], k], VEC.at[chip[0], chip[1], chip[2], k], vsend.at[n], vrecv.at[n - 1], dev(*chip, k)) for n, chip in chips_of(z, y, x)]
    v_sib = remote(VEC.at[:, :, :, k], VEC.at[:, :, :, k], vsend.at[0], vrecv.at[15], sib)
    for c in vs_out: c.start()

    def own_rows(i, W):
        at, half = offs[i]
        pres[i].wait_recv()
        mine = f_own[k, :, at:at + half]
        theirs = f_sib[:, at:at + half]
        block_w[:, at:at + half] = jnp.concatenate([jnp.where(k == 0, mine, theirs), jnp.where(k == 0, theirs, mine)], axis=0).astype(BF)
        c = pltpu.make_async_copy(block_w.at[:, pl.ds(at, half)], W.at[z, y, x, :, pl.ds(pl.multiple_of(k * half, 128), half)], lsem.at[i])
        c.start()
        return c

    own_rows(0, WQ).wait()
    gq.stage(0)
    gq.early()
    nx = neighbour(0, xin)
    lo, lu = own_rows(1, WO), own_rows(2, WU)
    hin = [[pltpu.make_async_copy(hist.at[j, g], slots[j].at[pl.ds(256 * g, 256)], hsem.at[j, g]) for g in range(2)] for j in range(5)]
    for c in hin: c[0].start(); c[1].start()
    block[...] = jnp.zeros_like(block)
    mixrow[...] = jnp.zeros_like(mixrow)

    def mix_in(js):
        for j in js:
            for g in range(2):
                hin[j][g].wait()
                for t in range(2):
                    q = slice(256 * g + 128 * t, 256 * g + 128 * t + 128)
                    h = slots[j][q, :].astype(F32)
                    c = cin[g, 128 * t:128 * t + 128, :].astype(F32)
                    mixrow[j:j + 1, :] += jnp.sum(h * c, axis=0, keepdims=True)
                    block[q, :] += mix[j] * h
    lo.wait(); lu.wait(); ldown.wait()
    go.early(); gu.early()
    mix_in((0, 1))
    for c in vs_in: c.wait_recv()
    v_sib.start()
    mix_in((2, 3))
    gq.early_on()
    gq.stage(2)
    gu.stage(0)
    go.stage(0)
    straight(0, xin, to_x)
    crossed(0, xin, to_x, nx)
    gd.early()
    go.early_on(); gu.early_on()
    mix_in((4,))
    opres = [pltpu.make_async_copy(block.at[pl.ds(256 * g, 256)], opre.at[g], osem.at[g]) for g in range(2)]
    for c in opres: c.start()
    v_sib.wait_recv()
    tiles = VEC[...].reshape(32, 8, 128)
    length = lane(VEC[0, 0, x, z // 2], 0, 64 + lax.rem(z, 2))
    vq[...] = widen(tiles, 2, 72)
    gq.stage(3)
    for n, r in enumerate((0, 1, 3, 4, 5, 7)):
        vg[n:n + 1, :] = widen(tiles, r, 24)
    a_gain, a_shift, bout, m_gain, m_shift, bdown = (vg[n:n + 1, :] for n in range(6))
    gu.stage(1)
    gd.early_on()
    gq.stage(4)
    vu[...] = widen(tiles, 6, 96)
    bias_rows(bias, length, k)
    fw = []
    def forward_x(i):
        j = own_block(jnp.int32(i), k)
        arrived(0, X.at[j], i)
        cp = remote(X.at[j], X.at[j], fsend.at[i], frecv.at[i], sib)
        cp.start(); fw.append(cp)
    def norm_block(i, core):
        j = own_block(jnp.int32(i), core)
        n, _ = norm(X[j].astype(F32))
        a = (n * a_gain + a_shift).astype(BF)
        acts(j, i < 2)[...] = a
        a1T[:, rows(j)] = a.T
    gq.stage(5)
    gu.stage(2)
    go.stage(2)
    nc = neighbour(1, cin)
    for i in range(4):
        forward_x(i)
        norm_block(i, k)
    gd.stage(0)
    gq.stage(6)
    for i in range(4):
        fw[i].wait_recv()
        norm_block(i, 1 - k)
    exports, turn = [], iter(range(16))
    def export(ref, dst):
        c = pltpu.make_async_copy(ref, dst, xsem.at[next(turn)])
        c.start(); exports.append(c)

    def keys(low, j):
        a = acts(j, low)[...]
        c, sn = table_rows(COS, SIN, length, j)
        for t in range(3):
            u2 = nn(a, matrix(WQ, slice(768 + t * 256, 1024 + t * 256))) + vq[:, 768 + t * 256:1024 + t * 256]
            for h in range(2):
                u = u2[:, h * 128:(h + 1) * 128]
                K[rows(j), t * 256 + h * 128:t * 256 + (h + 1) * 128] = (u * c + swap(u) * sn).astype(BF)
        V[rows(j), :] = (nn(a, matrix(WQ, slice(1536, 2304))) + vq[:, 1536:]).astype(BF)

    pl.loop(0, 4)(functools.partial(keys, True))
    gu.stage(3)
    go.stage(3)
    gd.stage(1)
    pl.loop(4, 8)(functools.partial(keys, False))
    def ask(low, i):
        j = own_block(i, k)
        a = acts(j, low)[...]
        c, sn = table_rows(COS, SIN, length, j)
        for t in range(3):
            u2 = nn(a, matrix(WQ, slice(t * 256, 256 + t * 256))) + vq[:, t * 256:256 + t * 256]
            for h in range(2):
                u = u2[:, h * 128:(h + 1) * 128]
                Q[rows(i), t * 256 + h * 128:t * 256 + (h + 1) * 128] = (u * c + swap(u) * sn).astype(BF) * jnp.asarray(0.125, BF)
    pl.loop(0, 2)(functools.partial(ask, True))
    pl.loop(2, 4)(functools.partial(ask, False))
    straight(1, cin, to_c)
    go.stage(4)
    gu.stage(4)
    for i in range(4):
        j = own_block(jnp.int32(i), k)
        export(X.at[j], oX.at[i])
    export(a1T, oacts); export(Q, oQ); export(K, oK); export(V, oV)
    export(WQ, oWQ)
    free_wq = exports.pop()

    def heads(h):
        lanes = rows(h)
        VT[...] = V[:, lanes].T
        at = 0
        for i in range(4):
            kk = 256 * (i + 1)
            qb = spread(Q[i * 128:(i + 1) * 128, lanes])
            st = nt(K[0:kk, lanes], qb) + both_heads(bias, at, kk)
            top = jnp.max(st, axis=0, keepdims=True)
            p = jnp.exp(st - top)
            den = jnp.sum(p, axis=0, keepdims=True)
            o = nn(VT[:, 0:kk], p.astype(BF)) * (1.0 / den)
            att[i * 128:(i + 1) * 128, lanes] = pick(o)
            lse[h, i:i + 1, :] = top + jnp.log(den)
            at += kk

    pl.loop(0, 1)(heads)
    crossed(1, cin, to_c, nc)
    pl.loop(1, 2)(heads)
    gd.stage(2)
    go.stage(5)
    pl.loop(2, 4)(heads)
    gu.stage(5)
    pl.loop(4, 6)(heads)
    go.stage(6)
    export(WO, oWO)
    gd.stage(3)
    export(att, oatt); export(lse, olse)

    for c in opres: c.wait()

    @pl.loop(0, 4)
    def _(i):
        j = own_block(i, k)
        middle[rows(i), :] = X[j].astype(F32) + (nn(att[rows(i), :].astype(BF), WO[...].reshape(768, 768)) + bout)
    m5 = mix[5]
    free_wq.wait()
    gq.sent()
    pl.semaphore_signal(free, inc=1, device_id=sib, device_id_type=MESH)
    for i in range(4):
        r = slice(i * 128, (i + 1) * 128)
        mid = middle[r, :]
        n, _ = norm(mid)
        a2 = (n * m_gain + m_shift).astype(BF)
        acts2[r, :] = a2
        actsT[:, r] = a2.T
        block[r, :] = mid + bdown
        ga[r, :] = jnp.zeros_like(mid)
    gu.stage(6)
    vgrad[...] = jnp.zeros_like(vgrad)

    def put_vec(row, v):
        for t in range(v.shape[1] // 128):
            vgrad[row + t:row + t + 1, :] = v[:, t * 128:(t + 1) * 128]

    def hidden(f):
        c = rows(f, 384)
        u = nn(acts2[...], matrix(WU, c)) + vu[:, c]
        half_erf = 0.5 * lax.erf(u * (2.0 ** -0.5)) + 0.5
        slope[:, c] = half_erf + u * (jnp.exp(u * u * -0.5) * (1.0 / math.sqrt(2 * math.pi)))
        act[:, c] = (u * half_erf).astype(BF)
    pl.loop(0, 4)(hidden)
    gd.stage(4)
    pl.loop(4, 8)(hidden)
    for i in range(4):
        arrived(1, C.at[i], i)
        dg[i * 128:(i + 1) * 128, :] = (m5 * C[i].astype(F32)).astype(BF)
    put_vec(72, jnp.sum(dg[...].astype(F32), axis=0, keepdims=True))
    sdn = Scatter(lambda zz, yy, xx: GD.at[zz, yy, xx, k],
                  [(GD.at[:, :, :, 1 - k, pl.ds(48 * n, 48)], WQ.at[:, :, :, :, pl.ds(768 * n, 768)]) for n in range(2)],
                  [(lambda r, n=n: r.at[pl.ds(48 * n, 48)], WQ.at[:, :, :, :, pl.ds(768 * n, 768)]) for n in range(2)],
                  orb, None, None, None, None, dsend, drecv, pos)

    gd.stage(5)

    @pl.loop(0, 4)
    def _(f):
        GD[f] = nn(act[:, rows(f, 768)].T, dg[...]).astype(BF).reshape(2, 2, 2, 96, 768)
    pl.semaphore_wait(free, 1)
    gd.stage(6)
    sdn.stage(0)

    @pl.loop(0, 4)
    def _(f):
        block[...] += nn(act[:, rows(f, 768)], WD[f].reshape(768, 768))

    total = jnp.zeros((1, 768), F32)
    for i in range(4):
        r = slice(i * 128, (i + 1) * 128)
        total += jnp.sum(C[i].astype(F32) * block[r, :], axis=0, keepdims=True)
        bl[i] = block[r, :].astype(BF)
    home = Home(bl, None, None, lambda slot: ohome.at[slot], None, length, home_sems, pos)
    home.straight()
    export(bl, obl)
    sdn.stage(1)
    export(GD.at[:, :, :, k], opd)

    def chunk(f):
        c = rows(f, 768)
        wd = WD[f].reshape(768, 768)
        upg = (nt(dg[...], wd) * slope[:, c]).astype(BF)
        g = jnp.sum(upg.astype(F32), axis=0, keepdims=True)
        for t in range(6):
            vgrad[pl.ds(48 + f * 6 + t, 1), :] = g[:, t * 128:(t + 1) * 128]
        gup[:, c] = nn(actsT[...], upg).astype(BF)
        pltpu.make_async_copy(gup.at[:, c], ogup.at[:, c], csem.at[1, f]).start()
        ga[...] += nt(upg, matrix(WU, c))

    pl.loop(0, 4)(chunk)
    gg = jnp.zeros((1, 768), F32)
    gs = jnp.zeros((1, 768), F32)
    for i in range(4):
        r = slice(i * 128, (i + 1) * 128)
        n, inv = norm(middle[r, :])
        e = ga[r, :]
        cf = C[i].astype(F32)
        gg += jnp.sum(e * n, axis=0, keepdims=True)
        gs += jnp.sum(e, axis=0, keepdims=True)
        ga[r, :] = m5 * cf + norm_grad(e, n, inv, m_gain)
    put_vec(36, gg); put_vec(42, gs)
    ogain[...] = jnp.broadcast_to(a_gain, (8, 768))
    whole = jnp.sum(total, axis=1, keepdims=True)
    row = jnp.where(place == 5, jnp.broadcast_to(whole, (1, 128)), 0.0)
    for j in range(5):
        row = jnp.where(place == j, jnp.broadcast_to(jnp.sum(mixrow[j:j + 1, :], axis=1, keepdims=True), (1, 128)), row)
    vgrad[78:79, :] = row
    vgrad[79:80, :] = jnp.broadcast_to(length, (1, 128))
    export(ga, ogmid)
    for f in range(4):
        c = slice(f * 768, (f + 1) * 768)
        pltpu.make_async_copy(gup.at[:, c], ogup.at[:, c], csem.at[1, f]).wait()
    for c in exports: c.wait()
    sdn.b1.wait_recv(); sdn.b0.wait_recv()
    for c in sdn.pre + [sdn.b1, sdn.b0]: c.wait_send()
    home.done()
    for c in fw + nx + nc: c.wait_send()
    for cp, cond in tokens:
        @pl.when(cond)
        def _():
            cp.wait_send()
    for c in pres: c.wait_send()
    for g in G[1:]: g.sent()
    for c in vs_out + [v_sib]: c.wait_send()


def forward_call(qkv, out, up, down, xin, cin, COS, SIN, hist, vectors, mix, lens):
    cols = (qkv.shape[1], out.shape[1], up.shape[1])
    H = sum(cols) // 2
    any_ = pl.BlockSpec(memory_space=pl.ANY)
    T = lambda n, t=BF: ((n, 768), t)
    shapes = [((4, 128, 768), BF), ((768, 1024), BF), T(512), T(1024), T(1024), T(512, F32), ((6, 4, 256), F32),
              ((4, 2, 2, 48, 2304), BF), ((4, 2, 2, 48, 768), BF), T(512, F32), ((768, 3072), BF), ((4, 2, 2, 96, 768), BF), ((2, 4, 96, 768), BF), ((4, 128, 768), BF),
              ((2, 128, 768), BF), (xin.shape, F32)]
    DS = pltpu.SemaphoreType.DMA
    return pl.pallas_call(functools.partial(forward_kernel, cols),
        out_shape=[sd(*t) for t in shapes] + [sd((8, 768), F32), sd((80, 128), F32)],
        in_specs=[vs] * 8 + [any_] + [vs] * 8 + [ss, ss], out_specs=[any_] * len(shapes) + [vs, vs],
        scratch_shapes=[VM((2, 24, H), F32), VM((24, H), F32), VM((48, H), BF),
                        VM((4, 2, 2, 48, 2304), BF), VM((4, 2, 2, 48, 768), BF), VM((4, 2, 2, 48, 3072), BF), VM((4, 2, 2, 2, 96, 768), BF),
                        VM((4, 2, 2, 2, 8, 128), F32), VM((8, 128, 768), BF), VM((4, 128, 768), BF), VM((2, 2, 128, 768), BF), VM((2, 2, 128, 768), BF),
                        VM((512, 768), BF), VM((1024, 768), BF), VM((1024, 768), BF), VM((512, 768), F32),
                        VM((6, 4, 256), F32), VM((512, 768), F32), VM((2560, 128), F32), VM((128, 1024), BF),
                        VM((512, 3072), BF), VM((512, 3072), F32), VM((512, 768), F32), VM((512, 768), F32), VM((512, 768), BF),
                        VM((768, 512), BF), VM((512, 768), BF), VM((768, 3072), BF), VM((4, 2, 2, 2, 96, 768), BF), VM((768, 1024), BF), VM((4, 128, 768), BF),
                        VM((1, 2304), F32), VM((8, 768), F32), VM((1, 3072), F32), VM((8, 128), F32), VM((8, 768), F32),
                        DS((3,)), DS((3,)), DS((5,)), DS((4, 21)), DS((4, 20)), DS((2, 2, 2)), DS((2, 4)), DS((2, 2)), DS((2, 2)), DS((4,)), DS((4,)),
                        DS((16,)), DS((2, 4)), DS((5, 2)), DS((2,)), DS((16,)), DS((16,)), DS((9,)), DS((9,)), pltpu.SemaphoreType.REGULAR, DS((2,)), DS((2,)), DS((4,)), DS((2,)), DS((2,))],
        compiler_params=pltpu.CompilerParams(collective_id=0, has_side_effects=True, vmem_limit_bytes=63 * 2**20),
    )(qkv, out, up, down, xin, cin, COS, SIN, hist, *[v.reshape(1, -1) for v in vectors], mix, lens)


def backward_kernel(gup, pdown, bdown, bl, gmid, X, actsT, Q, Kin, Vin, att, lse, WQ, WO, gain, COS, SIN, vin,
                    oq, oo, ou, od, vout, ox, ocross,
                    K, V, bias, KT, da, dQ, dK, dV, agrad, actsqT, GO, GQ, PU, PD,
                    AU, BU, CU, ZU, BD, CD, ZD, AO, BO, CO, ZO, AQ, BQ, CQ, ZQ,
                    fin, fsib, finu, fsibu, es, er, gx, cross, sel, cross_b, sel_b, vbuf, vrec,
                    ssem, rsem, ldsem, fsend, frecv, esem_s, esem_r, vsend, vrecv, csem, *home_sems):
    pos = z, y, x, k = where_am_i()
    sib = dev(z, y, x, 1 - k)
    greet(z, y, x, k)
    length = vin[79:80, 0:1]
    ck = pltpu.make_async_copy(Kin, K, csem.at[0])
    cv = pltpu.make_async_copy(Vin, V, csem.at[1])
    ck.start(); cv.start()
    half_of = lambda kk, half: pl.ds(pl.multiple_of(kk * half, 128), half)

    def col_scatter(a, G, half, bufs, n, out, at, width, fi, fs, hbm=None, both=False):
        def put(t):
            fi[n, 0] = t[:24]
            fi[n, 1] = t[24:]
            last.start()
        last = remote(fi.at[n, 1 - k], fs.at[n], fsend.at[a], frecv.at[a], sib)
        def finish():
            last.wait_recv()
            mine, theirs = fi[n, k], fs[n]
            out[:, at:at + half] = jnp.where(k == 0, mine, theirs)
            out[:, at + half:at + 2 * half] = jnp.where(k == 0, theirs, mine)
            last.wait_send()
        if hbm is None:
            mine = lambda zz, yy, xx: G.at[zz, yy, xx, :, half_of(k, half)]
            theirs = G.at[:, :, :, :, half_of(1 - k, half)]
            load = None
        else:
            mine = lambda zz, yy, xx: G.at[zz, yy, xx]
            theirs = hbm.at[:, :, :, :, half_of(1 - k, half)]
            load = [pltpu.make_async_copy(hbm.at[:, :, :, :, half_of(k, half)], G, ldsem.at[a])]
        RA, RB, RC, RZ = bufs
        return Scatter(mine, [(theirs, RA)], [(lambda r: r, RA)], RB, RC, RZ, put, finish, ssem.at[a], rsem.at[a], pos, load, both)

    def put_down(t):
        od[...] = t
    loads = [pltpu.make_async_copy(pdown, PD, ldsem.at[0]), pltpu.make_async_copy(bdown, BD, ldsem.at[2])]
    for c in loads: c.start()
    sdn = Scatter(lambda zz, yy, xx: PD.at[zz, yy, xx], None, None, BD, CD, ZD, put_down, lambda: None,
                  ssem.at[0], rsem.at[0], pos, loads, begun=True)
    sup = col_scatter(1, PU, 1536, (AU, BU, CU, ZU), 0, ou, 0, 3072, finu, fsibu, gup)
    sout = col_scatter(2, GO, 384, (AO, BO, CO, ZO), 0, oo, 0, 768, fin, fsib, both=True)
    sq, sk, sv = (col_scatter(3 + n, GQ.at[n], 384, (AQ.at[n], BQ.at[n], CQ.at[n], ZQ.at[n]), 1 + n, oq, 768 * n, 768, fin, fsib, both=n == 2)
                  for n in range(3))
    sup.stage(0)

    part_of = lambda half: lambda slot: ox.at[slot, pl.ds(pl.multiple_of(half * 128, 128), 128)]
    home = Home(gx, cross, sel, part_of(y), part_of(1 - y), length, home_sems[:5], pos)
    outs = Home(bl, cross_b, sel_b, None, lambda slot: ocross.at[slot], length, home_sems[5:], pos)
    outs.first()
    agrad[...] = gmid[...].astype(BF)
    vbuf[0] = vin[...]

    def put_vec(row, v):
        for t in range(v.shape[1] // 128):
            vbuf[0, row + t:row + t + 1, :] = v[:, t * 128:(t + 1) * 128]
    put_vec(30, jnp.sum(agrad[...].astype(F32), axis=0, keepdims=True))
    wo = lambda: WO[...].reshape(768, 768)

    da[...] = nt(agrad[...], wo()).astype(BF)
    for i in range(4):
        actsqT[:, i * 128:(i + 1) * 128] = actsT[:, rows(own_block(jnp.int32(i), k))]

    sdn.stage(2)

    def out_rows(t):
        aT = att[:, t * 384:(t + 1) * 384].T.astype(BF)
        g = nn(aT, agrad[...]).astype(BF)
        GO[2 * t:2 * t + 2] = g.reshape(2, 2, 2, 48, 768)
    sup.stage(1)
    for t in range(2): out_rows(t)
    sout.stage(0)
    outs.second()
    bias_rows(bias, length, k)
    dK[...] = jnp.zeros_like(dK)
    dV[...] = jnp.zeros_like(dV)
    ck.wait(); cv.wait()

    def heads(h):
        lanes = rows(h)
        KT[...] = K[:, lanes].T
        at = 0
        for i in range(4):
            kk = 256 * (i + 1)
            r = slice(i * 128, (i + 1) * 128)
            d = da[r, lanes]
            qb, db = spread(Q[r, lanes]), spread(d)
            prod = (d.astype(F32) * att[r, lanes]).T
            delta = jnp.concatenate([jnp.sum(prod[:64], axis=0, keepdims=True), jnp.sum(prod[64:], axis=0, keepdims=True)], axis=1)
            st = nt(K[0:kk, lanes], qb) + both_heads(bias, at, kk)
            p = jnp.exp(st - lse[h, i:i + 1, :])
            ds = (p * (nt(V[0:kk, lanes], db) - delta)).astype(BF)
            dV[0:kk, lanes] += nn(p.astype(BF), db)
            dK[0:kk, lanes] += nn(ds, qb)
            dQ[r, lanes] = pick(nn(KT[:, 0:kk], ds)) * 0.125
            at += kk

    pl.loop(0, 2)(heads)
    sout.stage(1)
    pl.loop(2, 4)(heads)
    pl.loop(4, 6)(heads)
    sdn.stage(3)
    V[...] = dV[...].astype(BF)
    put_vec(24, jnp.sum(V[...].astype(F32), axis=0, keepdims=True))

    def weight_rows(n, lhs, g):
        @pl.loop(0, 4)
        def _(t):
            GQ[n, t] = nn(lhs[rows(t, 192), :], g[...]).astype(BF).reshape(2, 2, 48, 768)
    @pl.loop(0, 8)
    def _(j):
        c, s = table_rows(COS, SIN, length, j)
        for t in range(6):
            u = dK[rows(j), t * 128:(t + 1) * 128]
            K[rows(j), t * 128:(t + 1) * 128] = (u * c - swap(u) * s).astype(BF)

    @pl.loop(0, 4)
    def _(i):
        j = own_block(i, k)
        c, s = table_rows(COS, SIN, length, j)
        for t in range(6):
            u = dQ[rows(i), t * 128:(t + 1) * 128]
            da[rows(i), t * 128:(t + 1) * 128] = (u * c - swap(u) * s).astype(BF)
    @pl.loop(0, 2)
    def _(j):
        r = rows(j, 512)
        dK[r, :] = nt(K[r, :], matrix(WQ, slice(768, 1536))) + nt(V[r, :], matrix(WQ, slice(1536, 2304)))
    dQ[...] = nt(da[...], matrix(WQ, slice(0, 768)))
    for i in range(4):
        dK[rows(own_block(jnp.int32(i), k)), :] += dQ[i * 128:(i + 1) * 128, :]
        es[i] = dK[rows(own_block(jnp.int32(i), 1 - k)), :].astype(BF)
    ecp = remote(es, er, esem_s, esem_r, sib)
    ecp.start()
    sup.stage(2)
    sout.stage(2)
    weight_rows(2, actsT, V)
    sv.stage(0)
    put_vec(18, jnp.sum(K[...].astype(F32), axis=0, keepdims=True))
    put_vec(12, jnp.sum(da[...].astype(F32), axis=0, keepdims=True))
    ecp.wait_recv()
    gg = jnp.zeros((1, 768), F32)
    gsh = jnp.zeros((1, 768), F32)
    for i in range(4):
        n, inv = norm(X[i].astype(F32))
        ee = dK[rows(own_block(jnp.int32(i), k)), :] + er[i].astype(F32)
        gg += jnp.sum(ee * n, axis=0, keepdims=True)
        gsh += jnp.sum(ee, axis=0, keepdims=True)
        gx[i] = (gmid[i * 128:(i + 1) * 128, :] + norm_grad(ee, n, inv, gain[0:1, :])).astype(BF)
    home.first(); home.straight()
    put_vec(0, gg); put_vec(6, gsh)
    vec_steps = [[sib], [dev(z, *sdn.p2, k)], [dev(z, *sdn.p3, k)], [dev(lax.rem(z + d, 4), y, x, k) for d in (1, 2, 3)]]
    vcp = []
    def vec_stage(n):
        if n > 0:
            for c in vcp[-1]: c.wait_recv()
            t = vbuf[n - 1]
            for r in range(len(vcp[-1])):
                t = t + vrec[n - 1 + r]
            if n < 4: vbuf[n] = t
            else: vout[...] = t
        if n < 4:
            vcp.append([remote(vbuf.at[n], vrec.at[n + i], vsend.at[n + i], vrecv.at[n + i], d) for i, d in enumerate(vec_steps[n])])
            for c in vcp[-1]: c.start()

    weight_rows(1, actsT, K)
    sk.stage(0)
    sv.stage(1)
    sdn.stage(4)
    weight_rows(0, actsqT, da)
    sq.stage(0)
    sk.stage(1)
    sq.stage(1)
    vec_stage(0)
    sout.stage(3)
    sup.stage(3)
    home.second()
    vec_stage(1)
    sv.stage(2)
    sk.stage(2)
    sq.stage(2)
    sup.stage(4)
    sv.stage(3)
    sout.stage(4)
    sk.stage(3)
    sdn.stage(5); sdn.stage(6)
    sv.stage(4)
    sq.stage(3)
    vec_stage(2)
    sk.stage(4)
    sq.stage(4)
    vec_stage(3)
    sup.stage(5); sout.stage(5)
    sv.stage(5); sk.stage(5); sq.stage(5)
    sup.stage(6); sout.stage(6)
    vec_stage(4)
    sv.stage(6); sk.stage(6); sq.stage(6)
    outs.done()
    home.done()
    ecp.wait_send()
    for cs in vcp:
        for c in cs: c.wait_send()


def backward_call(gup, pdown, bdown, *ins):
    n_up = gup.shape[1]
    gup = gup.reshape(4, 2, 2, 48, n_up)
    any_ = pl.BlockSpec(memory_space=pl.ANY)
    def bufs(r, n, lead=()):
        return [VM(lead + s + (r, n), BF) for s in ((4, 2, 2), (2, 4), (4,), (4,))]
    DS = pltpu.SemaphoreType.DMA
    home = sd((2, 256, 768), BF)
    return pl.pallas_call(backward_kernel,
        out_shape=[sd((24, 2304), F32), sd((24, 768), F32), sd((24, 3072), F32), sd((96, 768), F32), sd((80, 128), F32), home, sd((2, 128, 768), BF)],
        in_specs=[any_] * 3 + [vs] * 5 + [any_] * 2 + [vs] * 8, out_specs=[vs] * 5 + [any_] * 2,
        scratch_shapes=[VM((1024, 768), BF), VM((1024, 768), BF), VM((2560, 128), F32), VM((128, 1024), BF), VM((512, 768), BF), VM((512, 768), F32),
                        VM((1024, 768), F32), VM((1024, 768), F32), VM((512, 768), BF), VM((768, 512), BF),
                        VM((4, 2, 2, 48, 768), BF), VM((3, 4, 2, 2, 48, 768), BF), VM((4, 2, 2, 48, 1536), BF), VM((4, 2, 2, 96, 768), BF)]
        + bufs(48, 1536) + bufs(96, 768)[1:] + bufs(48, 384) + bufs(48, 384, (3,))
        + [VM((4, 2, 24, 384), F32), VM((4, 24, 384), F32), VM((1, 2, 24, 1536), F32), VM((1, 24, 1536), F32),
           VM((4, 128, 768), BF), VM((4, 128, 768), BF), VM((4, 128, 768), BF), VM((2, 128, 768), BF), VM((2, 128, 768), BF), VM((2, 128, 768), BF), VM((2, 128, 768), BF), VM((4, 80, 128), F32), VM((6, 80, 128), F32),
           DS((6, 9)), DS((6, 9)), DS((3,)), DS((6,)), DS((6,)), DS, DS, DS((6,)), DS((6,)), DS((2,)), DS((2,)), DS((2,)), DS((4,)), DS((2,)), DS((2,)), DS((2,)), DS((2,)), DS((4,)), DS((2,)), DS((2,))],
        compiler_params=pltpu.CompilerParams(collective_id=1, has_side_effects=True, vmem_limit_bytes=63 * 2**20),
    )(gup, pdown, bdown, *ins)


def finish_kernel(vout, cin, premix, home, across, gx, gq, go, gu, gd, mix,
                  lo, ox, gh, oq, oo, ou, od, v0, v1, v2, v3, v4, v5, v6, v7, gm, stage, sems):
    z, y, x, k = where_am_i()
    copies = []
    for j in range(5):
        stage[j] = (mix[j] * cin[...].astype(F32)).astype(BF)
        c = pltpu.make_async_copy(stage.at[j], gh.at[j], sems.at[j])
        c.start(); copies.append(c)
    for src, half in ((home, y), (across, 1 - y)):
        r = pl.ds(pl.multiple_of(half * 128, 128), 128)
        lo[:, r, :] = (premix[:, r, :] + mix[5] * src[...].astype(F32)).astype(BF)
    me = ((z * 2 + y) * 2 + x) * 2 + k
    spot = lax.broadcasted_iota(jnp.int32, (8, 128), 1)
    base = 0
    for v in (v0, v1, v2, v3, v4, v5, v6, v7):
        n = v.shape[0]
        first = me * n
        row, shift = first // 128, lax.rem(first, 128)
        a = jnp.broadcast_to(vout[pl.ds(base + row, 1), :], (8, 128))
        b = jnp.broadcast_to(vout[pl.ds(base + row + 1, 1), :], (8, 128))
        back = lax.rem(128 - shift, 128)
        both = jnp.where(spot < 128 - shift, pltpu.roll(a, back, 1), pltpu.roll(b, back, 1))
        v[...] = both[0, :n]
        base += n // 4
    gm[...] = vout[78, :6]
    for a, b in ((gx, ox), (gq, oq), (go, oo), (gu, ou), (gd, od)):
        b[...] = a[...]
    for c in copies: c.wait()


def finish_call(vectors, vout, cin, premix, home, across, gx, gq, go, gu, gd, mix):
    any_ = pl.BlockSpec(memory_space=pl.ANY)
    like = lambda a: sd(a.shape, a.dtype)
    return pl.pallas_call(finish_kernel,
        out_shape=[sd(cin.shape, BF), like(gx), sd((5,) + cin.shape, BF), like(gq), like(go), like(gu), like(gd)]
        + [sd(v.shape, F32) for v in vectors] + [sd((6,), F32)],
        in_specs=[vs] * 10 + [ss], out_specs=[vs, vs, any_] + [vs] * 13,
        scratch_shapes=[VM((5,) + cin.shape, BF), pltpu.SemaphoreType.DMA((5,))],
        compiler_params=pltpu.CompilerParams(vmem_limit_bytes=62 * 2**20),
    )(vout, cin, premix, home, across, gx, gq, go, gu, gd, mix)

def fast_shards(inputs, history, seq_lengths, attn_gain, attn_shift, qkv_weight, qkv_bias, out_weight, out_bias, mlp_gain,
                mlp_shift, up_weight, up_bias, down_weight, down_bias, mix_weights, cotangent):
    seq, batch = lax.axis_index("seq"), lax.axis_index("batch")
    z, y, x, k = seq // 2, seq % 2, batch // 2, batch % 2
    vectors = (attn_gain, attn_shift, qkv_bias, out_bias, mlp_gain, mlp_shift, up_bias, down_bias)
    COS, SIN = (jnp.asarray(t) for t in rope_tables())
    X, actsT, Q, K, V, att, lse, WQ, WO, gmid, gup, pdown, bdown, block, home, premix, gain, vin = forward_call(
        qkv_weight, out_weight, up_weight, down_weight, inputs, cotangent, COS, SIN, history, vectors, mix_weights, seq_lengths)
    oq, oo, ou, od, vout, grad_inputs, across = backward_call(gup, pdown, bdown, block, gmid, X, actsT, Q, K, V, att, lse, WQ, WO, gain, COS, SIN, vin)
    layer_out, grad_inputs, grad_history, oq, oo, ou, od, *gv, grad_mix = finish_call(
        vectors, vout, cotangent, premix, home, across, grad_inputs, oq, oo, ou, od, mix_weights)
    return (layer_out, grad_inputs, grad_history, gv[0], gv[1], oq, gv[2], oo, gv[3], gv[4], gv[5], ou, gv[6], od, gv[7], grad_mix)


def fits(mesh, inputs):
    shape = dict(mesh.shape)
    return shape == {"seq": 8, "batch": 4} and inputs.shape == (8, 2048, 768)


def solution(mesh):
    def run(*args):
        body = fast_shards if fits(mesh, args[0]) else shards
        return placed(mesh, body)(*args)
    return run
```
